32 devices in a mesh: dp: 16 (over z, y, x), ctx: 2 (over core).
Axes of the slice: x: 2, y: 2, z: 4, core: 2. Of those that a mesh axis runs over, the one named last changes fastest.
Arguments:
- inputs: bfloat16 [2, 16, 1024, 960], P(None, 'dp', 'ctx'), may hold values from -6 to 6
- segment_ids: int32 [2, 16, 1024], P(None, 'dp'), may hold values from 0 to 3, as said below
- positions: int32 [2, 16, 1024], P(None, 'dp'), may hold values from 0 to 767, as said below
- w_query: bfloat16 [960, 960], P('dp', 'ctx'), may hold values from -0.1875 to 0.1875
- w_key: bfloat16 [960, 320], P('dp', 'ctx'), may hold values from -0.1875 to 0.1875
- w_value: bfloat16 [960, 320], P('dp', 'ctx'), may hold values from -0.1875 to 0.1875
- w_out: bfloat16 [960, 960], P('dp', 'ctx'), may hold values from -0.5 to 0.5
- w_gate: bfloat16 [960, 2560], P('dp', 'ctx'), may hold values from -0.1875 to 0.1875
- w_up: bfloat16 [960, 2560], P('dp', 'ctx'), may hold values from -0.1875 to 0.1875
- w_down: bfloat16 [2560, 960], P('dp', 'ctx'), may hold values from -0.125 to 0.125
- gain_attn: bfloat16 [960], P('dp'), may hold values from 0.5 to 1.5
- gain_ffn: bfloat16 [960], P('dp'), may hold values from 0.5 to 1.5
- cotangent: bfloat16 [2, 16, 1024, 960], P(None, 'dp', 'ctx'), may hold values from -6 to 6
Outputs:
- outputs: bfloat16 [2, 16, 1024, 960], P(None, 'dp', 'ctx')
- grad_inputs: float32 [2, 16, 1024, 960], P(None, 'dp', 'ctx')
- grad_w_query: float32 [960, 960], P('dp', 'ctx')
- grad_w_key: float32 [960, 320], P('dp', 'ctx')
- grad_w_value: float32 [960, 320], P('dp', 'ctx')
- grad_w_out: float32 [960, 960], P('dp', 'ctx')
- grad_w_gate: float32 [960, 2560], P('dp', 'ctx')
- grad_w_up: float32 [960, 2560], P('dp', 'ctx')
- grad_w_down: float32 [2560, 960], P('dp', 'ctx')
- grad_gain_attn: float32 [960], P('dp')
- grad_gain_ffn: float32 [960], P('dp')
The draws below stay inside these ranges and needn't reach their ends.
Inputs may be any that keep to these rules, and one draw needn't show every extreme that they name: `segment_ids`: along each sequence the ids never fall, each of the 4 ids is used, and one document has exactly 768 tokens. `positions`: the number of earlier tokens of the same document in the sequence.
All inputs are finite; a program needn't handle non-finite values.
Results may differ from the reference program's by a relative error of at most 0.02.
Values may be sent and summed in bfloat16 or wider, within the bound.
No kernel may reach another device: no remote copies, remote signals or barrier semaphores. Data moves between devices by JAX's collectives and lax.ppermute only.
A program may use at most 192 MiB of HBM per device.

```python
import jax
import jax.numpy as jnp
from jax import lax

D = 960
HEADS = 15
KV_HEADS = 5
HEAD = 64
FF = 2560
SEQ = 1024
MICRO = 2
USES = 1
DOCS = 4
BATCH = 16
GROUP = 3
DOC_MOST = 768


def doc_layout(key):
    base_key = jax.random.fold_in(key, 7)
    weight_key, slot_key = jax.random.split(base_key)
    row_total = MICRO * BATCH
    rest_tokens = SEQ - DOC_MOST
    draws = jax.random.randint(weight_key, (row_total, DOCS - 1), 1, 100)
    spare = rest_tokens - (DOCS - 1)
    smaller = 1 + spare * draws // jnp.sum(draws, axis=1, keepdims=True)
    smaller = smaller.at[:, DOCS - 2].add(rest_tokens - jnp.sum(smaller, axis=1))
    big_slot = jax.random.randint(slot_key, (row_total, 1), 0, DOCS)
    doc_index = jnp.arange(DOCS, dtype=jnp.int32)[None, :]
    zero_col = jnp.zeros((row_total, 1), jnp.int32)
    after_pad = jnp.concatenate([smaller, zero_col], axis=1)
    before_pad = jnp.concatenate([zero_col, smaller], axis=1)
    lengths = jnp.where(doc_index < big_slot, after_pad, jnp.where(doc_index == big_slot, DOC_MOST, before_pad))
    ends = jnp.cumsum(lengths, axis=1)
    starts = ends - lengths
    token_index = jnp.arange(SEQ, dtype=jnp.int32)
    seg_table = jnp.sum((token_index[None, :, None] >= ends[:, None, :]).astype(jnp.int32), axis=-1)
    onehot = (seg_table[:, :, None] == doc_index[:, None, :]).astype(jnp.int32)
    start_of = jnp.sum(onehot * starts[:, None, :], axis=-1)
    pos_table = token_index[None, :] - start_of
    return (seg_table.reshape(MICRO, BATCH, SEQ), pos_table.reshape(MICRO, BATCH, SEQ))


def draw_segment_ids(key, part):
    return doc_layout(key)[0].astype(jnp.int32)


def draw_positions(key, part):
    return doc_layout(key)[1].astype(jnp.int32)


def steps_of(stream_key, dims, cuts, smallest, top_value):
    def one(dim, shards_of):
        steps = jax.random.uniform(jax.random.fold_in(jax.random.fold_in(stream_key, 6), dim), (shards_of,), jnp.float32, smallest / len(cuts), top_value / len(cuts))
        return jnp.repeat(jnp.exp(steps), dims[dim] // shards_of).reshape((-1,) + (1,) * (len(dims) - dim - 1))

    factor_of = one(*cuts[0])
    for cut in cuts[1:]:
        factor_of = factor_of * one(*cut)
    return factor_of


def noise(stream_key, shape, scale, bound, cuts=(), kind=jnp.bfloat16):
    values = scale * jax.random.normal(stream_key, shape, jnp.float32)
    if cuts:
        values = values * steps_of(stream_key, shape, cuts, -0.22, 0.18)
    return jnp.clip(values, -bound, bound).astype(kind)


def setup_inputs(seed: int = 0) -> dict:
    arg_keys = jax.random.split(jax.random.key(seed), 14)
    return {
        "inputs": noise(arg_keys[0], (MICRO, BATCH, SEQ, D), 1.0, 6.0, ((1, 16), (2, 2))),
        "segment_ids": draw_segment_ids(jax.random.fold_in(arg_keys[13], 71), 0),
        "positions": draw_positions(jax.random.fold_in(arg_keys[13], 71), 0),
        "w_query": noise(arg_keys[3], (D, HEADS * HEAD), D ** -0.5, 0.1875, ((0, 16), (1, 2))),
        "w_key": noise(arg_keys[4], (D, KV_HEADS * HEAD), D ** -0.5, 0.1875, ((0, 16), (1, 2))),
        "w_value": noise(arg_keys[5], (D, KV_HEADS * HEAD), D ** -0.5, 0.1875, ((0, 16), (1, 2))),
        "w_out": noise(arg_keys[6], (HEADS * HEAD, D), (HEADS * HEAD // 8) ** -0.5, 0.5, ((0, 16), (1, 2))),
        "w_gate": noise(arg_keys[7], (D, FF), D ** -0.5, 0.1875, ((0, 16), (1, 2))),
        "w_up": noise(arg_keys[8], (D, FF), D ** -0.5, 0.1875, ((0, 16), (1, 2))),
        "w_down": noise(arg_keys[9], (FF, D), FF ** -0.5, 0.125, ((0, 16), (1, 2))),
        "gain_attn": jnp.clip(1.0 + 0.1 * jax.random.normal(arg_keys[10], (D,), jnp.float32), 0.5, 1.5).astype(jnp.bfloat16),
        "gain_ffn": jnp.clip(1.0 + 0.1 * jax.random.normal(arg_keys[11], (D,), jnp.float32), 0.5, 1.5).astype(jnp.bfloat16),
        "cotangent": noise(arg_keys[12], (MICRO, BATCH, SEQ, D), 1.0, 6.0, ((1, 16), (2, 2))),
    }


EPSILON = 1e-05
MASKED = -1e+30
HIGH = lax.Precision.HIGHEST

@jax.custom_vjp
def low(v):
    return lax.optimization_barrier(v.astype(jnp.bfloat16)).astype(jnp.float32)

@jax.custom_vjp
def low_back(v):
    return v

def low_keep(v):
    return (low(v), None)

def low_pass(kept, grad):
    return (grad,)

def back_keep(v):
    return (v, None)

def back_low(kept, grad):
    return (low(grad),)
low.defvjp(low_keep, low_pass)
low_back.defvjp(back_keep, back_low)

def dot_high(left, right):
    return jnp.dot(left, right, precision=HIGH)

def rms_norm(hidden, gain_vec):
    return hidden * lax.rsqrt(lax.optimization_barrier(jnp.mean(hidden * hidden, axis=-1, keepdims=True)) + EPSILON) * gain_vec

def rotary_tables(seq_positions):
    half_width = HEAD // 2
    frequency = 10000.0 ** (-(jnp.arange(half_width, dtype=jnp.float32) * 2.0 / HEAD))
    angles = seq_positions.astype(jnp.float32)[:, None] * frequency[None, :]
    return (jnp.cos(angles)[:, None, :], jnp.sin(angles)[:, None, :])

def rotate(values, cos_table, sin_table):
    half_width = values.shape[-1] // 2
    front_half = values[..., :half_width]
    back_half = values[..., half_width:]
    return jnp.concatenate([front_half * cos_table - back_half * sin_table, back_half * cos_table + front_half * sin_table], axis=-1)

def attention(queries, key_rows, values, segments):
    seq_len = queries.shape[0]
    block_rows = min(512, seq_len)
    block_count = seq_len // block_rows
    grouped = queries.reshape(block_count, block_rows, KV_HEADS, GROUP, HEAD)
    block_starts = jnp.arange(block_count, dtype=jnp.int32) * block_rows
    key_index = jnp.arange(seq_len, dtype=jnp.int32)

    def one_block(operands):
        query_block, block_start = operands
        query_index = block_start + jnp.arange(block_rows, dtype=jnp.int32)
        query_seg = lax.dynamic_slice_in_dim(segments, block_start, block_rows)
        allowed = (key_index[None, :] <= query_index[:, None]) & (segments[None, :] == query_seg[:, None])
        scores = low_back(jnp.einsum('bngd,snd->ngbs', query_block, key_rows, precision=HIGH) * HEAD ** (-0.5))
        scores = jnp.where(allowed, scores, MASKED)
        row_top = lax.optimization_barrier(jnp.max(scores, axis=-1, keepdims=True))
        weights = jnp.exp(scores - row_top) * allowed
        weights_low = low(weights / lax.optimization_barrier(jnp.sum(weights, axis=-1, keepdims=True)))
        return jnp.einsum('ngbs,snd->bngd', weights_low, values, precision=HIGH)
    attended = lax.map(jax.checkpoint(one_block), (grouped, block_starts))
    return attended.reshape(seq_len, HEADS * HEAD)

def apply_layer(hidden, params, segments, cos_table, sin_table):
    w_query, w_key, w_value, w_out, w_gate, w_up, w_down, gain_attn, gain_ffn = params
    seq_len = hidden.shape[0]
    normed = low(rms_norm(hidden, gain_attn))
    queries = low(rotate(low_back(dot_high(normed, w_query)).reshape(seq_len, HEADS, HEAD), cos_table, sin_table))
    key_rows = low(rotate(low_back(dot_high(normed, w_key)).reshape(seq_len, KV_HEADS, HEAD), cos_table, sin_table))
    values = low(low_back(dot_high(normed, w_value)).reshape(seq_len, KV_HEADS, HEAD))
    attended = low(low_back(attention(queries, key_rows, values, segments)))
    middle = hidden + low_back(dot_high(attended, w_out))
    normed_ffn = low(rms_norm(middle, gain_ffn))
    gate_pre = low_back(dot_high(normed_ffn, w_gate))
    up_pre = low_back(dot_high(normed_ffn, w_up))
    activated = low(jax.nn.silu(gate_pre) * up_pre)
    return middle + low_back(dot_high(activated, w_down))

def reference(inputs, segment_ids, positions, w_query, w_key, w_value, w_out, w_gate, w_up, w_down, gain_attn, gain_ffn, cotangent):
    weights = tuple((item.astype(jnp.float32) for item in (w_query, w_key, w_value, w_out, w_gate, w_up, w_down, gain_attn, gain_ffn)))
    row_total = MICRO * BATCH
    flat_in = inputs.reshape(row_total, SEQ, D).astype(jnp.float32)
    flat_ct = cotangent.reshape(row_total, SEQ, D).astype(jnp.float32)
    flat_seg = segment_ids.reshape(row_total, SEQ)
    flat_pos = positions.reshape(row_total, SEQ)

    def one_sequence(totals, operands):
        seq_in, seq_seg, seq_pos, seq_ct = operands
        cos_table, sin_table = rotary_tables(seq_pos)

        def forward(hidden, params):
            for use_index in range(USES):
                hidden = apply_layer(hidden, params, seq_seg, cos_table, sin_table)
            return hidden
        result, pullback = jax.vjp(forward, seq_in, weights)
        grad_in, grad_params = pullback(seq_ct)
        totals = jax.tree.map(lambda left, right: left + right, totals, grad_params)
        return (totals, (result.astype(jnp.bfloat16), grad_in))
    zero_grads = jax.tree.map(jnp.zeros_like, weights)
    totals, (results, grads_in) = lax.scan(one_sequence, zero_grads, (flat_in, flat_seg, flat_pos, flat_ct))
    return (results.reshape(MICRO, BATCH, SEQ, D), grads_in.reshape(MICRO, BATCH, SEQ, D), totals[0], totals[1], totals[2], totals[3], totals[4], totals[5], totals[6], totals[7], totals[8])
```

```python
import functools

import jax
import jax.numpy as jnp
from jax import lax
from jax.experimental import pallas as pl
from jax.experimental.pallas import tpu as pltpu
from jax.sharding import PartitionSpec as P

HEADS = 15
KV_HEADS = 5
HEAD = 64
MICRO = 2
GROUP = 3
DOCS = 4

EPSILON = 1e-05
MASKED = -1e30
LANES = 128
QKV = (HEADS + 2 * KV_HEADS) * HEAD
QKV_PAD = 1664
VMEM_LIMIT = 60 * 1024 * 1024
F32 = jnp.float32
BF16 = jnp.bfloat16


def up(value, step):
    return -(-value // step) * step


def mm(left, right):
    return lax.dot_general(left, right, (((1,), (0,)), ((), ())), preferred_element_type=F32)


def mm_nt(left, right):
    return lax.dot_general(left, right, (((1,), (1,)), ((), ())), preferred_element_type=F32)


def mm_tn(left, right):
    return lax.dot_general(left, right, (((0,), (0,)), ((), ())), preferred_element_type=F32)


def call(body, out_shape, grid, in_specs, out_specs, scratch=(), flops=0, moved=0, prefetch=0, alias=None):
    return pl.pallas_call(
        body,
        out_shape=out_shape,
        grid_spec=pltpu.PrefetchScalarGridSpec(
            num_scalar_prefetch=prefetch,
            grid=grid,
            in_specs=in_specs,
            out_specs=out_specs,
            scratch_shapes=scratch,
        ),
        input_output_aliases=alias or {},
        compiler_params=pltpu.CompilerParams(vmem_limit_bytes=VMEM_LIMIT),
        cost_estimate=pl.CostEstimate(flops=flops, bytes_accessed=moved, transcendentals=0),
    )


def whole(shape):
    return pl.BlockSpec(shape, lambda *_: (0,) * len(shape))


def lane_of(rows):
    return lax.broadcasted_iota(jnp.int32, (rows, LANES), 1)


def three_terms(column):
    high = column.astype(BF16).astype(F32)
    rest = column - high
    mid = rest.astype(BF16).astype(F32)
    return high, mid, rest - mid


def put_terms(base, column, lane, first):
    high, mid, low = three_terms(column)
    base = jnp.where(lane == first, high, base)
    base = jnp.where(lane == first + 1, mid, base)
    return jnp.where(lane == first + 2, low, base)


def pre_body(width, x_ref, e_ref, w_ref, gain_ref, cos_ref, sa_ref, sb_ref, aq_ref, ak_ref,
             xp_ref, a_ref, q_ref, k_ref, v_ref):
    xp = mm(x_ref[...], e_ref[:width, :])
    scale = lax.rsqrt(jnp.sum(xp * xp, axis=-1, keepdims=True) / width + EPSILON)
    a = (xp * scale * gain_ref[...]).astype(BF16)
    xp_ref[...] = xp.astype(BF16)
    a_ref[...] = a
    t = mm(a, w_ref[...])
    lane = lane_of(t.shape[0])
    low = lane < HEAD
    cos, sa, sb, aq, ak = cos_ref[...], sa_ref[...], sb_ref[...], aq_ref[...], ak_ref[...]
    for pair in range((HEADS + KV_HEADS) // 2):
        tt = t[:, LANES * pair : LANES * (pair + 1)]
        rot = tt * cos + pltpu.roll(tt, 32, 1) * sa + pltpu.roll(tt, 96, 1) * sb
        for half in range(2):
            head = 2 * pair + half
            val = rot if half == 0 else pltpu.roll(rot, 64, 1)
            if head < HEADS:
                q_ref[head] = jnp.where(low, val * HEAD ** -0.5, aq).astype(BF16)
            else:
                k_ref[head - HEADS] = jnp.where(low, val, ak).astype(BF16)
    av = jnp.where(lane < HEAD + 3, -1.0, 0.0)
    for head in range(KV_HEADS):
        first = (HEADS + KV_HEADS) * HEAD + LANES * (head // 2)
        tt = t[:, first : first + LANES]
        val = tt if head % 2 == 0 else pltpu.roll(tt, 64, 1)
        v_ref[head] = jnp.where(low, val, av).astype(BF16)


def pre_attention(x, spread, w_qkv, gain, cos, sa, sb, aq, ak, block=256):
    seq, width = x.shape
    wide = spread.shape[1]
    rows = lambda n: pl.BlockSpec((block, n), lambda i: (i, 0))
    heads = lambda n: pl.BlockSpec((n, block, LANES), lambda i: (0, i, 0))
    return call(
        functools.partial(pre_body, width),
        [
            jax.ShapeDtypeStruct((seq, wide), BF16),
            jax.ShapeDtypeStruct((seq, wide), BF16),
            jax.ShapeDtypeStruct((HEADS, seq, LANES), BF16),
            jax.ShapeDtypeStruct((KV_HEADS, seq, LANES), BF16),
            jax.ShapeDtypeStruct((KV_HEADS, seq, LANES), BF16),
        ],
        (seq // block,),
        [rows(width), whole(spread.shape), whole(w_qkv.shape), whole((1, wide))]
        + [rows(LANES)] * 5,
        [rows(wide), rows(wide), heads(HEADS), heads(KV_HEADS), heads(KV_HEADS)],
        flops=2 * seq * wide * (width + QKV_PAD),
        moved=20_000_000,
    )(x, spread, w_qkv, gain, cos, sa, sb, aq, ak)


def attend_body(block, q_ref, k_ref, v_ref, o_ref, q2_ref):
    seq = k_ref.shape[1]
    rows = GROUP * block
    below = lax.broadcasted_iota(jnp.int32, (block, block), 0) >= lax.broadcasted_iota(
        jnp.int32, (block, block), 1
    )
    below = jnp.concatenate([below.astype(F32)] * GROUP, axis=0) > 0.5
    lane = lane_of(rows)
    for i in range(seq // block):
        span = slice(block * i, block * (i + 1))
        q = q_ref[:, span, :].reshape(rows, LANES)
        s_in = jnp.where(below, mm_nt(q, k_ref[0, span, :]), MASKED)
        top = jnp.max(s_in, axis=-1, keepdims=True)
        if i:
            s_left = mm_nt(q, k_ref[0, : block * i, :])
            top = jnp.maximum(top, jnp.max(s_left, axis=-1, keepdims=True))
        ext = mm(jnp.exp(s_in - top).astype(BF16), v_ref[0, span, :])
        if i:
            ext = ext + mm(jnp.exp(s_left - top).astype(BF16), v_ref[0, : block * i, :])
        total = -ext[:, HEAD : HEAD + 1]
        o = ext / total
        o = jnp.where(lane < HEAD, o, pltpu.roll(o, 64, 1))
        o_ref[:, span, :] = o.reshape(GROUP, block, LANES).astype(BF16)
        q2 = put_terms(q.astype(F32), top + jnp.log(total), lane, HEAD + DOCS)
        q2_ref[:, span, :] = q2.reshape(GROUP, block, LANES).astype(BF16)


def attend(q, k, v, block=256):
    seq = q.shape[1]
    group = pl.BlockSpec((GROUP, seq, LANES), lambda n: (n, 0, 0))
    one = pl.BlockSpec((1, seq, LANES), lambda n: (n, 0, 0))
    shape = jax.ShapeDtypeStruct(q.shape, BF16)
    return call(
        functools.partial(attend_body, block),
        [shape, shape],
        (KV_HEADS,),
        [group, one, one],
        [group, group],
        flops=4 * HEADS * seq * seq * LANES,
        moved=15_000_000,
    )(q, k, v)


def attend_back_body(block, q_ref, k_ref, v_ref, do_ref, cos_ref, sa_ref, sb_ref,
                     dq_ref, dk_ref, dv_ref, acc_ref):
    seq = k_ref.shape[1]
    above = lax.broadcasted_iota(jnp.int32, (block, block), 0) <= lax.broadcasted_iota(
        jnp.int32, (block, block), 1
    )
    lane = lane_of(seq)

    def unrotate(t, span):
        rows = span.stop - span.start
        rot = (
            t * cos_ref[span, :]
            - pltpu.roll(t, 32, 1) * sa_ref[span, :]
            - pltpu.roll(t, 96, 1) * sb_ref[span, :]
        )
        return twice(rot, rows)

    def twice(t, rows):
        return jnp.where(lane[:rows] < HEAD, t, pltpu.roll(t, 64, 1)).astype(BF16)

    for j in range(seq // block):
        span = slice(block * j, block * (j + 1))
        k, v = k_ref[0, span, :], v_ref[0, span, :]
        dk = jnp.zeros((block, LANES), F32)
        dv = jnp.zeros((block, LANES), F32)
        for g in range(GROUP):
            q, do = q_ref[g, block * j :, :], do_ref[g, block * j :, :]
            p = jnp.exp(mm_nt(k, q))
            inner = jnp.where(above, p[:, :block], 0.0)
            p = inner if p.shape[1] == block else jnp.concatenate([inner, p[:, block:]], axis=1)
            ds = (p * mm_nt(v, do)).astype(BF16)
            dv = dv + mm(p.astype(BF16), do)
            dk = dk + mm(ds, q)
            dq = mm_tn(ds, k)
            if j == 0:
                acc_ref[g] = dq
            else:
                acc_ref[g, block * j :, :] += dq
        dk_ref[0, span, :] = unrotate(dk, span)
        dv_ref[0, span, :] = twice(dv, block)
    for g in range(GROUP):
        dq_ref[g] = unrotate(acc_ref[g] * HEAD ** -0.5, slice(0, seq))


def attend_back(q, k, v, do, cos, sa, sb, block=256):
    seq = q.shape[1]
    group = pl.BlockSpec((GROUP, seq, LANES), lambda n: (n, 0, 0))
    one = pl.BlockSpec((1, seq, LANES), lambda n: (n, 0, 0))
    return call(
        functools.partial(attend_back_body, block),
        [
            jax.ShapeDtypeStruct(q.shape, BF16),
            jax.ShapeDtypeStruct(k.shape, BF16),
            jax.ShapeDtypeStruct(k.shape, BF16),
        ],
        (KV_HEADS,),
        [group, one, one, group] + [whole((seq, LANES))] * 3,
        [group, one, one],
        scratch=[pltpu.VMEM((GROUP, seq, LANES), F32)],
        flops=10 * HEADS * seq * seq * LANES,
        moved=20_000_000,
    )(q, k, v, do, cos, sa, sb)


def columns_of(w_refs, part):
    w = w_refs[part % 2][:, part // 2]
    return w.reshape(w.shape[0] * w.shape[1], w.shape[2])


def pairs_to(ref, get, heads, first=0):
    for pair in range((heads + 1) // 2):
        left = get(2 * pair)
        lane = lane_of(left.shape[0])
        right = get(2 * pair + 1).astype(F32) if 2 * pair + 1 < heads else 0.0
        both = jnp.where(lane < HEAD, left.astype(F32), right)
        ref[:, first + LANES * pair : first + LANES * (pair + 1)] = both.astype(BF16)


def mid_body(width, o_ref, ct_ref, e_ref, wo0_ref, wo1_ref, xp_ref, gain_ref,
             op_ref, m_ref, b_ref, df_ref, nat_ref):
    pairs_to(nat_ref, lambda h: o_ref[h], HEADS)
    op = mm(nat_ref[...], e_ref[...]).astype(BF16)
    op_ref[...] = op
    square = 0.0
    for part in range(4):
        w = columns_of((wo0_ref, wo1_ref), part)
        cols = slice(w.shape[1] * part, w.shape[1] * (part + 1))
        m = xp_ref[:, cols].astype(F32) + mm(op, w)
        m_ref[:, cols] = m
        square = square + jnp.sum(m * m, axis=-1, keepdims=True)
    b_ref[...] = (m_ref[...] * lax.rsqrt(square / width + EPSILON) * gain_ref[...]).astype(BF16)
    df_ref[...] = mm(ct_ref[...], e_ref[:width, :]).astype(BF16)


def out_spec_of(packed, which):
    return pl.BlockSpec((packed.shape[0], 2, 64, 256), lambda *_: (0, 0, 15 + which, 0))


def middle(o, ct, spread, packed, xp, gain, block=256):
    seq, width = ct.shape
    wide = spread.shape[1]
    rows = lambda n: pl.BlockSpec((block, n), lambda i: (i, 0))
    return call(
        functools.partial(mid_body, width),
        [
            jax.ShapeDtypeStruct((seq, wide), BF16),
            jax.ShapeDtypeStruct((seq, wide), F32),
            jax.ShapeDtypeStruct((seq, wide), BF16),
            jax.ShapeDtypeStruct((seq, wide), BF16),
        ],
        (seq // block,),
        [
            pl.BlockSpec((HEADS, block, LANES), lambda i: (0, i, 0)),
            rows(width),
            whole(spread.shape),
            out_spec_of(packed, 0),
            out_spec_of(packed, 1),
            rows(wide),
            whole((1, wide)),
        ],
        [rows(wide)] * 4,
        scratch=[pltpu.VMEM((block, wide), BF16)],
        flops=2 * seq * wide * 3 * wide,
        moved=22_000_000,
    )(o, ct, spread, packed, packed, xp, gain)


def ffn_body(b_ref, df_ref, g_ref, u_ref, d00_ref, d01_ref, d10_ref, d11_ref,
             out_ref, db_ref, dwg_ref, dwu_ref, dwd_ref, wd_ref):
    half, s = pl.program_id(0), pl.program_id(1)
    chunk = g_ref.shape[3]

    @pl.when(s == 0)
    def _():
        for part, ref in enumerate((d00_ref, d01_ref, d10_ref, d11_ref)):
            w = ref[:, 0]
            wd_ref[:, chunk * part : chunk * (part + 1)] = w.reshape(-1, chunk)

    b, df = b_ref[...], df_ref[...]
    wg = g_ref[:, 0].reshape(-1, chunk)
    wu = u_ref[:, 0].reshape(-1, chunk)
    wd = wd_ref[pl.ds(pl.multiple_of(chunk * s, chunk), chunk), :]
    gate = mm(b, wg)
    upper = mm(b, wu)
    sig = jax.nn.sigmoid(gate)
    act = gate * sig
    z = (act * upper).astype(BF16)
    dz = mm_nt(df, wd)
    dg = (dz * upper * sig * (1.0 + gate * (1.0 - sig))).astype(BF16)
    du = (dz * act).astype(BF16)

    first = jnp.logical_and(half == 0, s == 0)

    @pl.when(first)
    def _():
        out_ref[...] = mm(z, wd)
        db_ref[...] = mm_nt(dg, wg) + mm_nt(du, wu)

    @pl.when(jnp.logical_not(first))
    def _():
        out_ref[...] += mm(z, wd)
        db_ref[...] += mm_nt(dg, wg) + mm_nt(du, wu)

    dwg_ref[0, 0] = mm_tn(b, dg).astype(BF16).reshape(dwg_ref.shape[2:])
    dwu_ref[0, 0] = mm_tn(b, du).astype(BF16).reshape(dwu_ref.shape[2:])
    dwd = mm_tn(z, df).astype(BF16)
    for part in range(4):
        dwd_ref[part] = dwd[:, chunk * part : chunk * (part + 1)]


def feed_forward(b, df, packed):
    seq, wide = b.shape
    blocks = packed.shape[0]
    halves, chunks, chunk = 2, 5, 256
    hidden = halves * chunks * chunk
    gate = pl.BlockSpec((blocks, 1, 64, chunk), lambda h, s: (0, h, s, 0))
    upper = pl.BlockSpec((blocks, 1, 64, chunk), lambda h, s: (0, h, chunks + s, 0))
    down = lambda j, q: pl.BlockSpec((blocks // 2, 1, 160, chunk), lambda h, s: (h, j, 4 + q, 0))
    return call(
        ffn_body,
        [
            jax.ShapeDtypeStruct((seq, wide), F32),
            jax.ShapeDtypeStruct((seq, wide), F32),
            jax.ShapeDtypeStruct((halves, chunks, blocks, 64, chunk), BF16),
            jax.ShapeDtypeStruct((halves, chunks, blocks, 64, chunk), BF16),
            jax.ShapeDtypeStruct((4, hidden, chunk), BF16),
        ],
        (halves, chunks),
        [whole(b.shape), whole(df.shape), gate, upper, down(0, 0), down(0, 1), down(1, 0), down(1, 1)],
        [
            whole((seq, wide)),
            whole((seq, wide)),
            pl.BlockSpec((1, 1, blocks, 64, chunk), lambda h, s: (h, s, 0, 0, 0)),
            pl.BlockSpec((1, 1, blocks, 64, chunk), lambda h, s: (h, s, 0, 0, 0)),
            pl.BlockSpec((4, chunk, chunk), lambda h, s: (0, h * chunks + s, 0)),
        ],
        scratch=[pltpu.VMEM((chunks * chunk, wide), BF16)],
        flops=18 * seq * wide * hidden,
        moved=50_000_000,
    )(b, df, *([packed] * 6))


def post_body(width, m_ref, acc_ref, db_ref, df_ref, gain_ref, e_ref, wo0_ref, wo1_ref, o_ref, op_ref,
              out_ref, em_ref, do_ref, dwo_ref, dgain_ref, nat_ref, dwo_acc):
    i = pl.program_id(0)
    m, db = m_ref[...], db_ref[...]
    out_ref[...] = mm_nt((m + acc_ref[...]).astype(BF16), e_ref[:width, :]).astype(BF16)
    scale = lax.rsqrt(jnp.sum(m * m, axis=-1, keepdims=True) / width + EPSILON)
    n = m * scale
    c = db * gain_ref[...]
    mean = jnp.sum(c * n, axis=-1, keepdims=True) / width
    em = df_ref[...].astype(F32) + scale * (c - n * mean)
    em_ref[...] = em
    da = em.astype(BF16)
    dgain = jnp.sum(db * n, axis=0, keepdims=True)
    dwo = mm_tn(op_ref[...], da)

    @pl.when(i == 0)
    def _():
        dgain_ref[...] = dgain
        dwo_acc[...] = dwo

    @pl.when(i > 0)
    def _():
        dgain_ref[...] += dgain
        dwo_acc[...] += dwo

    @pl.when(i == pl.num_programs(0) - 1)
    def _():
        for part in range(4):
            w = dwo_acc[:, 256 * part : 256 * (part + 1)].astype(BF16)
            dwo_ref[part] = w.reshape(dwo_ref.shape[1:])

    dop = 0.0
    for part in range(4):
        w = columns_of((wo0_ref, wo1_ref), part)
        dop = dop + mm_nt(da[:, 256 * part : 256 * (part + 1)], w)
    nat_ref[...] = mm_nt(dop.astype(BF16), e_ref[...])
    lane = lane_of(m.shape[0])
    low = lane < HEAD
    for head in range(HEADS):
        val = nat_ref[:, LANES * (head // 2) : LANES * (head // 2 + 1)]
        if head % 2:
            val = pltpu.roll(val, 64, 1)
        val = jnp.where(low, val, 0.0)
        delta = jnp.sum(val * o_ref[head].astype(F32), axis=-1, keepdims=True)
        do_ref[head] = put_terms(val, delta, lane, HEAD).astype(BF16)


def after(m, acc, db, df, gain, spread, packed, o, op, width, block=256):
    seq, wide = m.shape
    blocks = packed.shape[0]
    rows = lambda n: pl.BlockSpec((block, n), lambda i: (i, 0))
    heads = pl.BlockSpec((HEADS, block, LANES), lambda i: (0, i, 0))
    return call(
        functools.partial(post_body, width),
        [
            jax.ShapeDtypeStruct((seq, width), BF16),
            jax.ShapeDtypeStruct((seq, wide), F32),
            jax.ShapeDtypeStruct((HEADS, seq, LANES), BF16),
            jax.ShapeDtypeStruct((4, blocks, wide // blocks, 256), BF16),
            jax.ShapeDtypeStruct((1, wide), F32),
        ],
        (seq // block,),
        [rows(wide)] * 4
        + [whole((1, wide)), whole(spread.shape), out_spec_of(packed, 0), out_spec_of(packed, 1), heads, rows(wide)],
        [
            rows(width),
            rows(wide),
            heads,
            whole((4, blocks, wide // blocks, 256)),
            whole((1, wide)),
        ],
        scratch=[pltpu.VMEM((block, wide), F32), pltpu.VMEM((wide, wide), F32)],
        flops=2 * seq * wide * 4 * wide,
        moved=35_000_000,
    )(m, acc, db, df, gain, spread, packed, packed, o, op)


def last_body(width, dq_ref, dk_ref, dv_ref, w_ref, a_ref, xp_ref, em_ref, gain_ref, e_ref,
              gi_ref, dw_ref, dgain_ref, flat_ref, dw_acc):
    i = pl.program_id(0)
    heads = HEADS + KV_HEADS
    pairs_to(flat_ref, lambda h: dq_ref[h] if h < HEADS else dk_ref[h - HEADS], heads)
    pairs_to(flat_ref, lambda h: dv_ref[h], KV_HEADS, heads * HEAD)
    flat = flat_ref[...]
    dw = mm_tn(a_ref[...], flat)
    da = mm_nt(flat, w_ref[...])
    xp = xp_ref[...].astype(F32)
    scale = lax.rsqrt(jnp.sum(xp * xp, axis=-1, keepdims=True) / width + EPSILON)
    n = xp * scale
    c = da * gain_ref[...]
    mean = jnp.sum(c * n, axis=-1, keepdims=True) / width
    grad = em_ref[...] + scale * (c - n * mean)
    dgain = jnp.sum(da * n, axis=0, keepdims=True)

    @pl.when(i == 0)
    def _():
        dgain_ref[...] = dgain
        dw_acc[...] = dw

    @pl.when(i > 0)
    def _():
        dgain_ref[...] += dgain
        dw_acc[...] += dw

    @pl.when(i == pl.num_programs(0) - 1)
    def _():
        dw_ref[...] = dw_acc[...].astype(BF16)

    e = e_ref[:width, :]
    high = grad.astype(BF16)
    gi_ref[...] = mm_nt(high, e) + mm_nt((grad - high.astype(F32)).astype(BF16), e)


def last(dq, dk, dv, w_qkv, a, xp, em, gain, spread, width, block=256):
    seq, wide = a.shape
    rows = lambda n: pl.BlockSpec((block, n), lambda i: (i, 0))
    heads = lambda n: pl.BlockSpec((n, block, LANES), lambda i: (0, i, 0))
    return call(
        functools.partial(last_body, width),
        [
            jax.ShapeDtypeStruct((seq, width), F32),
            jax.ShapeDtypeStruct((wide, QKV_PAD), BF16),
            jax.ShapeDtypeStruct((1, wide), F32),
        ],
        (seq // block,),
        [heads(HEADS), heads(KV_HEADS), heads(KV_HEADS), whole(w_qkv.shape), rows(wide), rows(wide), rows(wide)]
        + [whole((1, wide)), whole(spread.shape)],
        [rows(width), whole((wide, QKV_PAD)), whole((1, wide))],
        scratch=[pltpu.VMEM((block, QKV_PAD), BF16), pltpu.VMEM((wide, QKV_PAD), F32)],
        flops=4 * seq * wide * (QKV_PAD + width),
        moved=30_000_000,
    )(dq, dk, dv, w_qkv, a, xp, em, gain, spread)


def spread_matrix(width, blocks, wide):
    row = jnp.arange(wide, dtype=jnp.int32)
    per, step = width // blocks, wide // blocks
    place = (row // per) * step + row % per
    hit = (place[:, None] == jnp.arange(wide, dtype=jnp.int32)[None, :]) & (row < width)[:, None]
    return hit.astype(BF16)


def tables(positions, segments):
    lane = jnp.arange(LANES, dtype=jnp.int32)
    frequency = 10000.0 ** (-((lane % 32).astype(F32) * 2.0 / HEAD))
    angles = positions.astype(F32)[:, None] * frequency[None, :]
    cos, sin = jnp.cos(angles), jnp.sin(angles)
    high = (lane % HEAD >= 32)[None, :]
    sa = jnp.where(high, sin, 0.0)
    sb = jnp.where(high, 0.0, -sin)
    doc = (lane - HEAD)[None, :]
    mine = segments[:, None] == doc
    in_doc = (doc >= 0) & (doc < DOCS)
    aq = jnp.where(mine & in_doc, MASKED, 0.0)
    ak = jnp.where(in_doc & ~mine, 1.0, 0.0)
    ak = jnp.where((doc >= DOCS) & (doc < DOCS + 3), -1.0, ak)
    return cos, sa, sb, aq, ak


def layer(x, ct, segments, positions, w_qkv, get_packed, gain_attn, gain_ffn, spread, reduce_first):
    width = x.shape[1]
    cos, sa, sb, aq, ak = tables(positions, segments)
    xp, a, q, k, v = pre_attention(x, spread, w_qkv, gain_attn, cos, sa, sb, aq, ak)
    o, q2 = attend(q, k, v)
    packed = get_packed
    op, m, b, df = middle(o, ct, spread, packed, xp, gain_ffn)
    acc, db, dwg, dwu, dwd = feed_forward(b, df, packed)
    out, em, do, dwo, dgain_ffn = after(m, acc, db, df, gain_ffn, spread, packed, o, op, width)
    first = reduce_first(dwg, dwu, dwd, dwo)
    dq, dk, dv = attend_back(q2, k, v, do, cos, sa, sb)
    gi, dw, dgain_attn = last(dq, dk, dv, w_qkv, a, xp, em, gain_attn, spread, width)
    return out, gi, first, dw, dgain_attn, dgain_ffn


def pad_rows(w, blocks, step=64):
    per = w.shape[0] // blocks
    return jnp.pad(w.reshape(blocks, per, w.shape[1]), ((0, 0), (0, step - per), (0, 0)))


def pad_cols(w, blocks, step=64):
    per = w.shape[1] // blocks
    w = jnp.pad(w.reshape(w.shape[0], blocks, per), ((0, 0), (0, 0), (0, step - per)))
    return w.reshape(w.shape[0], blocks * step)


def cut_rows(w, per):
    return w[:, :per].reshape(w.shape[0] * per, w.shape[2])


def cut_cols(w, per, step=64):
    blocks = w.shape[1] // step
    return w.reshape(w.shape[0], blocks, step)[:, :, :per].reshape(w.shape[0], blocks * per)


def chunked(w, chunk=256):
    blocks, rows, cols = w.shape
    w = w.reshape(blocks, rows, cols // chunk, chunk).transpose(0, 2, 1, 3)
    return w.reshape(blocks, cols // chunk * rows, chunk)


def joined(w, rows):
    blocks, total, chunk = w.shape
    w = w.reshape(blocks, total // rows, rows, chunk).transpose(0, 2, 1, 3)
    return w.reshape(blocks, rows, total // rows * chunk)


def pack_half(w_gate, w_up, w_down, w_out, blocks, groups):
    down = pad_cols(w_down, groups)
    down = down.reshape(blocks, w_down.shape[0] // blocks, down.shape[1])
    return jnp.concatenate(
        [
            chunked(pad_rows(w_gate, blocks)),
            chunked(pad_rows(w_up, blocks)),
            chunked(down),
            chunked(pad_rows(pad_cols(w_out, groups), blocks)),
        ],
        axis=1,
    )


def add(left, right):
    return (left.astype(F32) + right.astype(F32)).astype(BF16)


def swap(x):
    return lax.ppermute(x, "ctx", [(0, 1), (1, 0)])


def across(x, bit, count):
    return lax.ppermute(x, "dp", [(i, i ^ (1 << bit)) for i in range(count)])


def pick(x, index, axis=0):
    return lax.dynamic_index_in_dim(x, index, axis, keepdims=False)


def in_order(own, other, index):
    return jnp.where(index == 0, jnp.stack([own, other]), jnp.stack([other, own]))


def gather_projections(shard, bits):
    count = 1 << len(bits)
    grow = lambda buf, bit: in_order(buf, across(buf, bit, count), bits[bit])
    buf = grow(grow(shard, 2), 3)
    half = shard.shape[0] // 2
    first = grow(grow(buf[:, :, :half], 0), 1)
    second = grow(grow(buf[:, :, half:], 1), 0)
    first = first.transpose(2, 3, 0, 1, 4, 5).reshape(count, half, -1)
    second = second.transpose(2, 3, 1, 0, 4, 5).reshape(count, half, -1)
    return jnp.concatenate([first, second], axis=1)


def reduce_rows(first, second, bits):
    count = 1 << len(bits)
    cube = (2,) * len(bits)

    def step(buf, bit, axis):
        got = across(pick(buf, 1 - bits[bit], axis), bit, count)
        return add(pick(buf, bits[bit], axis), got)

    first = step(step(first.reshape(cube + first.shape[1:]), 0, 3), 1, 2)
    second = step(step(second.reshape(cube + second.shape[1:]), 1, 2), 0, 2)
    both = jnp.stack([first, second], axis=2)
    return step(step(both, 3, 0), 2, 0)


def shards_of_two(inputs, segment_ids, positions, w_query, w_key, w_value, w_out, w_gate, w_up,
                  w_down, gain_attn, gain_ffn, cotangent):
    count = lax.axis_size("dp")
    me, core = lax.axis_index("dp"), lax.axis_index("ctx")
    bits = [(me >> bit) & 1 for bit in range(count.bit_length() - 1)]
    per = gain_attn.shape[0]
    width = per * count
    groups = w_out.shape[1] // per
    hidden = w_down.shape[0]
    n_q, n_k = w_query.shape[1], w_key.shape[1]
    n_qkv = n_q + 2 * n_k

    shard = jnp.concatenate(
        [w_query, w_key, w_value, gain_attn[:, None], gain_ffn[:, None]], axis=1
    )
    shard = jnp.pad(shard, ((0, 64 - per), (0, 896 - n_qkv - 2)))
    mine = gather_projections(shard, bits)
    packed = pack_half(w_gate, w_up, w_down, w_out, 1, groups)[0]
    packed = lax.all_gather(packed, ("dp", "ctx"), axis=0, tiled=False)
    packed = packed.reshape((count, 2) + packed.shape[1:])

    pair = in_order(mine, swap(mine), core).reshape(2, count * 64, 896)
    cut = lambda a, b: [pair[0, :, a:b], pair[1, :, a:b]]
    w_qkv = jnp.concatenate(
        cut(0, n_q) + cut(n_q, n_q + n_k) + cut(n_q + n_k, n_qkv)
        + [jnp.zeros((count * 64, QKV_PAD - QKV), BF16)],
        axis=1,
    )
    gains = mine[:, :, n_qkv : n_qkv + 2].astype(F32).reshape(count * 64, 2).T

    def sequence(x):
        own, other = pick(x[:, 0], core), swap(pick(x[:, 0], 1 - core))
        return in_order(own, other, core).reshape(-1, x.shape[3])

    x, ct = sequence(inputs), sequence(cotangent)

    def sum_first(dwg, dwu, dwd, dwo):
        def core_sum(t):
            return add(pick(t, core), swap(pick(t, 1 - core)))

        g, u = core_sum(dwg), core_sum(dwu)
        d = core_sum(dwd.reshape(2, 2, count, hidden, 256))
        o = core_sum(dwo.reshape((2, 2) + dwo.shape[1:]))
        flat = lambda t: t.transpose(1, 0, 2, 3).reshape(count, -1, 256)
        return reduce_rows(
            jnp.concatenate([flat(g), d[0], o[0]], axis=1),
            jnp.concatenate([flat(u), d[1], o[1]], axis=1),
            bits,
        )

    out, gi, first, dw, dga, dgf = layer(
        x, ct, pick(segment_ids[:, 0], core), pick(positions[:, 0], core),
        w_qkv, packed, gains[:1], gains[1:], spread_matrix(width, count, count * 64), sum_first,
    )

    def part_of(j):
        cols = lambda a, n: dw[:, a + n * j : a + n * (j + 1)]
        parts = [cols(0, n_q), cols(2 * n_q, n_k), cols(2 * (n_q + n_k), n_k)]
        parts += [dga.astype(BF16).T, dgf.astype(BF16).T]
        part = jnp.concatenate(parts, axis=1)
        return jnp.pad(part, ((0, 0), (0, 896 - part.shape[1]))).reshape(count, 64, 896)

    both = jnp.stack([part_of(0), part_of(1)])
    total = add(pick(both, core), swap(pick(both, 1 - core)))
    last_sum = reduce_rows(total[:, :32], total[:, 32:], bits)
    last_sum = last_sum.reshape(64, 896)[:per].astype(F32)

    def tokens(seq):
        halves = seq.reshape(2, seq.shape[0] // 2, seq.shape[1])
        own, other = pick(halves, core), swap(pick(halves, 1 - core))
        return in_order(own, other, core)[:, None]

    rows = 5 * 64
    gate = joined(first[:1, :rows], 64)[0, :per]
    upper = joined(first[1:, :rows], 64)[0, :per]
    down = first[:, rows : rows + hidden].transpose(1, 0, 2).reshape(hidden, -1)
    outer = first[:, rows + hidden :].transpose(1, 0, 2).reshape(64, -1)[:per]
    return (
        tokens(out),
        tokens(gi),
        last_sum[:, :n_q],
        last_sum[:, n_q : n_q + n_k],
        last_sum[:, n_q + n_k : n_qkv],
        cut_cols(outer.astype(F32), per),
        gate.astype(F32),
        upper.astype(F32),
        cut_cols(down.astype(F32), per),
        last_sum[:, n_qkv],
        last_sum[:, n_qkv + 1],
    )


def shards_of_many(inputs, segment_ids, positions, w_query, w_key, w_value, w_out, w_gate, w_up,
                   w_down, gain_attn, gain_ffn, cotangent):
    count, cores = lax.axis_size("dp"), lax.axis_size("ctx")
    core = lax.axis_index("ctx")
    share = cores // MICRO
    per = gain_attn.shape[0]
    width = per * count

    def gathered(w):
        return lax.all_gather(lax.all_gather(w, "dp", axis=0, tiled=True), "ctx", axis=1, tiled=True)

    full = [gathered(w) for w in (w_query, w_key, w_value, w_out, w_gate, w_up, w_down)]
    gain_pair = lax.all_gather(jnp.stack([gain_attn, gain_ffn]), "dp", axis=1, tiled=True)
    gains = pad_cols(gain_pair.astype(F32), count)
    w_qkv = pad_rows(jnp.concatenate(full[:3], axis=1), count).reshape(count * 64, QKV)
    w_qkv = jnp.pad(w_qkv, ((0, 0), (0, QKV_PAD - QKV)))
    w_o, w_g, w_u, w_d = full[3:]
    half = lambda w, j: w[:, w.shape[1] // 2 * j : w.shape[1] // 2 * (j + 1)]
    packed = jnp.stack(
        [pack_half(half(w_g, j), half(w_u, j), half(w_d, j), half(w_o, j), count, count // 2) for j in range(2)],
        axis=1,
    )
    which = core // share
    sequence = lambda x: pick(lax.all_gather(x[:, 0], "ctx", axis=1, tiled=True), which)
    out, gi, first, dw, dga, dgf = layer(
        sequence(inputs), sequence(cotangent),
        pick(segment_ids[:, 0], which), pick(positions[:, 0], which),
        w_qkv, packed, gains[:1], gains[1:], spread_matrix(width, count, count * 64), lambda *t: t,
    )
    dwg, dwu, dwd, dwo = first
    wide_of = lambda t: jnp.concatenate(
        [cut_rows(t[j].transpose(1, 2, 0, 3).reshape(count, 64, -1), per) for j in range(2)], axis=1
    )
    side = lambda t: jnp.concatenate([t[q] for q in range(4)], axis=-1)
    d_qkv = cut_rows(dw.reshape(count, 64, QKV_PAD), per)
    n_q, n_k = HEADS * HEAD, KV_HEADS * HEAD
    grads = [
        d_qkv[:, :n_q],
        d_qkv[:, n_q : n_q + n_k],
        d_qkv[:, n_q + n_k : QKV],
        cut_cols(cut_rows(side(dwo), per), per),
        wide_of(dwg),
        wide_of(dwu),
        cut_cols(side(dwd), per),
    ]

    def summed(g):
        g = lax.psum_scatter(g * (1.0 / share), "dp", scatter_dimension=0, tiled=True)
        return lax.psum_scatter(g, "ctx", scatter_dimension=1, tiled=True).astype(F32)

    sums = [summed(g.astype(BF16)) for g in grads]
    dgain = cut_cols(jnp.concatenate([dga, dgf]), per) * (1.0 / share)
    dgain = lax.psum_scatter(lax.psum(dgain, "ctx"), "dp", scatter_dimension=1, tiled=True)

    def tokens(seq):
        rows = seq.shape[0] // cores
        every = lax.all_gather(seq, "ctx", axis=0, tiled=False)
        return lax.dynamic_slice_in_dim(every[::share], core * rows, rows, axis=1)[:, None]

    return (tokens(out), tokens(gi), *sums, dgain[0], dgain[1])


def solution(mesh):
    two = mesh.shape["ctx"] == MICRO and mesh.shape["dp"] == 16
    matrices = (P("dp", "ctx"),) * 7 + (P("dp"), P("dp"))
    tokens = P(None, "dp", "ctx", None)
    return jax.shard_map(
        shards_of_two if two else shards_of_many,
        mesh=mesh,
        in_specs=(tokens, P(None, "dp", None), P(None, "dp", None)) + matrices + (tokens,),
        out_specs=(tokens, tokens) + matrices,
        check_vma=False,
    )
```

```python
import functools

import jax
import jax.numpy as jnp
from jax import lax
from jax.experimental import pallas as pl
from jax.experimental.pallas import tpu as pltpu
from jax.sharding import PartitionSpec as P

HEADS = 15
KV_HEADS = 5
HEAD = 64
MICRO = 2
GROUP = 3
DOCS = 4

EPSILON = 1e-05
MASKED = -1e30
LANES = 128
QKV = (HEADS + 2 * KV_HEADS) * HEAD
QKV_PAD = 1664
VMEM_LIMIT = 60 * 1024 * 1024
F32 = jnp.float32
BF16 = jnp.bfloat16


def up(value, step):
    return -(-value // step) * step


def mm(left, right):
    return lax.dot_general(left, right, (((1,), (0,)), ((), ())), preferred_element_type=F32)


def mm_nt(left, right):
    return lax.dot_general(left, right, (((1,), (1,)), ((), ())), preferred_element_type=F32)


def mm_tn(left, right):
    return lax.dot_general(left, right, (((0,), (0,)), ((), ())), preferred_element_type=F32)


def call(body, out_shape, grid, in_specs, out_specs, scratch=(), flops=0, moved=0, prefetch=0, alias=None):
    return pl.pallas_call(
        body,
        out_shape=out_shape,
        grid_spec=pltpu.PrefetchScalarGridSpec(
            num_scalar_prefetch=prefetch,
            grid=grid,
            in_specs=in_specs,
            out_specs=out_specs,
            scratch_shapes=scratch,
        ),
        input_output_aliases=alias or {},
        compiler_params=pltpu.CompilerParams(vmem_limit_bytes=VMEM_LIMIT),
        cost_estimate=pl.CostEstimate(flops=flops, bytes_accessed=moved, transcendentals=0),
    )


def whole(shape):
    return pl.BlockSpec(shape, lambda *_: (0,) * len(shape))


def lane_of(rows):
    return lax.broadcasted_iota(jnp.int32, (rows, LANES), 1)


def three_terms(column):
    high = column.astype(BF16).astype(F32)
    rest = column - high
    mid = rest.astype(BF16).astype(F32)
    return high, mid, rest - mid


def put_terms(base, column, lane, first):
    high, mid, low = three_terms(column)
    base = jnp.where(lane == first, high, base)
    base = jnp.where(lane == first + 1, mid, base)
    return jnp.where(lane == first + 2, low, base)


def build_weights(place_ref, piece_refs, stage_ref, w_ref):
    core, z, y, x = (place_ref[n] for n in range(4))
    for swapped in range(2):
        near_a, far_a, near_b, far_b = piece_refs[4 * swapped : 4 * swapped + 4]
        to = jnp.bitwise_xor(core, swapped)
        for dy in range(2):
            for dx in range(2):
                for k in range(4):
                    block = lax.rem(z + 4 - k, 4) * 4 + (y ^ dy) * 2 + (x ^ dx)
                    row = pl.multiple_of(block * 64, 64)
                    stage_ref[to, pl.ds(row, 32), :] = (far_a if dy else near_a)[4 * dx + k]
                    stage_ref[to, pl.ds(row + 32, 32), :] = (far_b if dx else near_b)[4 * dy + k]
    n_q, n_k = HEADS * HEAD // 2, KV_HEADS * HEAD // 2
    for j in range(2):
        w_ref[:, n_q * j : n_q * (j + 1)] = stage_ref[j, :, :n_q]
        for part in range(2):
            to, at = 2 * n_q + n_k * (2 * part + j), n_q + n_k * part
            w_ref[:, to : to + n_k] = stage_ref[j, :, at : at + n_k]
    w_ref[:, QKV:] = jnp.zeros((w_ref.shape[0], QKV_PAD - QKV), BF16)


def projections(xp, scale, w_ref, gain_ref, cos_ref, sa_ref, sb_ref, aq_ref, ak_ref,
                xp_ref, a_ref, q_ref, k_ref, v_ref):
    a = (xp * scale * gain_ref[:1]).astype(BF16)
    xp_ref[...] = xp.astype(BF16)
    a_ref[...] = a
    t = mm(a, w_ref[...])
    lane = lane_of(t.shape[0])
    low = lane < HEAD
    cos, sa, sb, aq, ak = cos_ref[...], sa_ref[...], sb_ref[...], aq_ref[...], ak_ref[...]
    for pair in range((HEADS + KV_HEADS) // 2):
        tt = t[:, LANES * pair : LANES * (pair + 1)]
        rot = tt * cos + pltpu.roll(tt, 32, 1) * sa + pltpu.roll(tt, 96, 1) * sb
        for half in range(2):
            head = 2 * pair + half
            val = rot if half == 0 else pltpu.roll(rot, 64, 1)
            if head < HEADS:
                q_ref[head] = jnp.where(low, val * HEAD ** -0.5, aq).astype(BF16)
            else:
                k_ref[head - HEADS] = jnp.where(low, val, ak).astype(BF16)
    av = jnp.where(lane < HEAD + 3, -1.0, 0.0)
    for head in range(KV_HEADS):
        first = (HEADS + KV_HEADS) * HEAD + LANES * (head // 2)
        tt = t[:, first : first + LANES]
        val = tt if head % 2 == 0 else pltpu.roll(tt, 64, 1)
        v_ref[head] = jnp.where(low, val, av).astype(BF16)


def own_or_other(place_ref, own_ref, other_ref):
    first = pl.program_id(0) < pl.num_programs(0) // 2
    mine = first == (place_ref[0] == 0)
    return jnp.where(mine, own_ref[...], other_ref[...])


def pre_body(width, place_ref, own_ref, other_ref, e_ref, *refs):
    pieces, refs = refs[:8], refs[8:]
    *rest, w_ref, gain_ref, stage_ref = refs

    @pl.when(pl.program_id(0) == 0)
    def _():
        build_weights(place_ref, pieces, stage_ref, w_ref)
        gain_ref[...] = stage_ref[0, :, 768:].astype(F32).T[32:40]

    xp = mm(own_or_other(place_ref, own_ref, other_ref), e_ref[:width, :])
    scale = lax.rsqrt(jnp.sum(xp * xp, axis=-1, keepdims=True) / width + EPSILON)
    projections(xp, scale, w_ref, gain_ref, *rest)


def pre_whole_body(width, place_ref, own_ref, other_ref, e_ref, w_ref, gain_ref, *rest):
    xp = mm(own_or_other(place_ref, own_ref, other_ref), e_ref[:width, :])
    scale = lax.rsqrt(jnp.sum(xp * xp, axis=-1, keepdims=True) / width + EPSILON)
    projections(xp, scale, w_ref, gain_ref, *rest)


def halves_specs(rows, width, block):
    steps = rows // block
    return [pl.BlockSpec((block, width), lambda i, *_: (i % steps, 0))] * 2


def pre_attention(place, own, other, spread, weights, cos, sa, sb, aq, ak, block=256):
    half, width = own.shape
    seq, wide = 2 * half, spread.shape[1]
    pieces = len(weights) == 8
    rows = lambda n: pl.BlockSpec((block, n), lambda i, *_: (i, 0))
    heads = lambda n: pl.BlockSpec((n, block, LANES), lambda i, *_: (0, i, 0))
    shapes = [
        jax.ShapeDtypeStruct((seq, wide), BF16),
        jax.ShapeDtypeStruct((seq, wide), BF16),
        jax.ShapeDtypeStruct((HEADS, seq, LANES), BF16),
        jax.ShapeDtypeStruct((KV_HEADS, seq, LANES), BF16),
        jax.ShapeDtypeStruct((KV_HEADS, seq, LANES), BF16),
    ]
    specs = [rows(wide), rows(wide), heads(HEADS), heads(KV_HEADS), heads(KV_HEADS)]
    if pieces:
        shapes += [jax.ShapeDtypeStruct((wide, QKV_PAD), BF16), jax.ShapeDtypeStruct((8, wide), F32)]
        specs += [whole((wide, QKV_PAD)), whole((8, wide))]
    results = call(
        functools.partial(pre_body if pieces else pre_whole_body, width),
        shapes,
        (seq // block,),
        halves_specs(half, width, block)
        + [whole(spread.shape)]
        + [whole(w.shape) for w in weights]
        + [rows(LANES)] * 5,
        specs,
        scratch=[pltpu.VMEM((2, wide, weights[0].shape[-1]), BF16)] if pieces else (),
        flops=2 * seq * wide * (width + QKV_PAD),
        moved=20_000_000,
        prefetch=1,
    )(place, own, other, spread, *weights, cos, sa, sb, aq, ak)
    return results if pieces else (*results, *weights)


def attend_body(block, q_ref, k_ref, v_ref, o_ref, q2_ref):
    seq = k_ref.shape[1]
    rows = GROUP * block
    below = lax.broadcasted_iota(jnp.int32, (block, block), 0) >= lax.broadcasted_iota(
        jnp.int32, (block, block), 1
    )
    below = jnp.concatenate([below.astype(F32)] * GROUP, axis=0) > 0.5
    lane = lane_of(rows)
    for i in range(seq // block):
        span = slice(block * i, block * (i + 1))
        q = q_ref[:, span, :].reshape(rows, LANES)
        s_in = jnp.where(below, mm_nt(q, k_ref[0, span, :]), MASKED)
        top = jnp.max(s_in, axis=-1, keepdims=True)
        if i:
            s_left = mm_nt(q, k_ref[0, : block * i, :])
            top = jnp.maximum(top, jnp.max(s_left, axis=-1, keepdims=True))
        ext = mm(jnp.exp(s_in - top).astype(BF16), v_ref[0, span, :])
        if i:
            ext = ext + mm(jnp.exp(s_left - top).astype(BF16), v_ref[0, : block * i, :])
        total = -ext[:, HEAD : HEAD + 1]
        o = ext / total
        o = jnp.where(lane < HEAD, o, pltpu.roll(o, 64, 1))
        o_ref[:, span, :] = o.reshape(GROUP, block, LANES).astype(BF16)
        q2 = put_terms(q.astype(F32), top + jnp.log(total), lane, HEAD + DOCS)
        q2_ref[:, span, :] = q2.reshape(GROUP, block, LANES).astype(BF16)


def attend(q, k, v, block=256):
    seq = q.shape[1]
    group = pl.BlockSpec((GROUP, seq, LANES), lambda n: (n, 0, 0))
    one = pl.BlockSpec((1, seq, LANES), lambda n: (n, 0, 0))
    shape = jax.ShapeDtypeStruct(q.shape, BF16)
    return call(
        functools.partial(attend_body, block),
        [shape, shape],
        (KV_HEADS,),
        [group, one, one],
        [group, group],
        flops=4 * HEADS * seq * seq * LANES,
        moved=15_000_000,
    )(q, k, v)


def attend_back_body(block, q_ref, k_ref, v_ref, do_ref, cos_ref, sa_ref, sb_ref,
                     dq_ref, dk_ref, dv_ref, acc_ref):
    seq = k_ref.shape[1]
    above = lax.broadcasted_iota(jnp.int32, (block, block), 0) <= lax.broadcasted_iota(
        jnp.int32, (block, block), 1
    )
    lane = lane_of(seq)

    def unrotate(t, span):
        rows = span.stop - span.start
        rot = (
            t * cos_ref[span, :]
            - pltpu.roll(t, 32, 1) * sa_ref[span, :]
            - pltpu.roll(t, 96, 1) * sb_ref[span, :]
        )
        return twice(rot, rows)

    def twice(t, rows):
        return jnp.where(lane[:rows] < HEAD, t, pltpu.roll(t, 64, 1)).astype(BF16)

    for j in range(seq // block):
        span = slice(block * j, block * (j + 1))
        k, v = k_ref[0, span, :], v_ref[0, span, :]
        dk = jnp.zeros((block, LANES), F32)
        dv = jnp.zeros((block, LANES), F32)
        for g in range(GROUP):
            q, do = q_ref[g, block * j :, :], do_ref[g, block * j :, :]
            p = jnp.exp(mm_nt(k, q))
            inner = jnp.where(above, p[:, :block], 0.0)
            p = inner if p.shape[1] == block else jnp.concatenate([inner, p[:, block:]], axis=1)
            ds = (p * mm_nt(v, do)).astype(BF16)
            dv = dv + mm(p.astype(BF16), do)
            dk = dk + mm(ds, q)
            dq = mm_tn(ds, k)
            if j == 0:
                acc_ref[g] = dq
            else:
                acc_ref[g, block * j :, :] += dq
        dk_ref[0, span, :] = unrotate(dk, span)
        dv_ref[0, span, :] = twice(dv, block)
    for g in range(GROUP):
        dq_ref[g] = unrotate(acc_ref[g] * HEAD ** -0.5, slice(0, seq))


def attend_back(q, k, v, do, cos, sa, sb, first, count, block=256):
    seq = q.shape[1]
    group = lambda at: pl.BlockSpec((GROUP, seq, LANES), lambda n: (n + at, 0, 0))
    one = lambda at: pl.BlockSpec((1, seq, LANES), lambda n: (n + at, 0, 0))
    return call(
        functools.partial(attend_back_body, block),
        [
            jax.ShapeDtypeStruct((GROUP * count, seq, LANES), BF16),
            jax.ShapeDtypeStruct((count, seq, LANES), BF16),
            jax.ShapeDtypeStruct((count, seq, LANES), BF16),
        ],
        (count,),
        [group(first), one(first), one(first), group(first)] + [whole((seq, LANES))] * 3,
        [group(0), one(0), one(0)],
        scratch=[pltpu.VMEM((GROUP, seq, LANES), F32)],
        flops=10 * GROUP * count * seq * seq * LANES,
        moved=4_000_000 * count,
    )(q, k, v, do, cos, sa, sb)


def columns_of(w_refs, part):
    w = w_refs[part % 2][:, part // 2]
    return w.reshape(w.shape[0] * w.shape[1], w.shape[2])


def pairs_to(ref, get, heads, first=0):
    for pair in range((heads + 1) // 2):
        left = get(2 * pair)
        lane = lane_of(left.shape[0])
        right = get(2 * pair + 1).astype(F32) if 2 * pair + 1 < heads else 0.0
        both = jnp.where(lane < HEAD, left.astype(F32), right)
        ref[:, first + LANES * pair : first + LANES * (pair + 1)] = both.astype(BF16)


def mid_body(width, place_ref, o_ref, own_ref, other_ref, e_ref, wo0_ref, wo1_ref, xp_ref, gain_ref,
             op_ref, m_ref, b_ref, df_ref, nat_ref):
    pairs_to(nat_ref, lambda h: o_ref[h], HEADS)
    op = mm(nat_ref[...], e_ref[...]).astype(BF16)
    op_ref[...] = op
    square = 0.0
    for part in range(4):
        w = columns_of((wo0_ref, wo1_ref), part)
        cols = slice(w.shape[1] * part, w.shape[1] * (part + 1))
        m = xp_ref[:, cols].astype(F32) + mm(op, w)
        m_ref[:, cols] = m
        square = square + jnp.sum(m * m, axis=-1, keepdims=True)
    b_ref[...] = (m_ref[...] * lax.rsqrt(square / width + EPSILON) * gain_ref[1:2]).astype(BF16)
    ct = own_or_other(place_ref, own_ref, other_ref)
    df_ref[...] = mm(ct, e_ref[:width, :]).astype(BF16)


def out_spec_of(packed, which):
    return pl.BlockSpec((packed.shape[0], 2, 64, 256), lambda *_: (0, 0, 15 + which, 0))


def middle(place, o, own, other, spread, packed, xp, gain, block=256):
    half, width = own.shape
    seq, wide = 2 * half, spread.shape[1]
    rows = lambda n: pl.BlockSpec((block, n), lambda i, *_: (i, 0))
    return call(
        functools.partial(mid_body, width),
        [
            jax.ShapeDtypeStruct((seq, wide), BF16),
            jax.ShapeDtypeStruct((seq, wide), F32),
            jax.ShapeDtypeStruct((seq, wide), BF16),
            jax.ShapeDtypeStruct((seq, wide), BF16),
        ],
        (seq // block,),
        [
            pl.BlockSpec((HEADS, block, LANES), lambda i, *_: (0, i, 0)),
            *halves_specs(half, width, block),
            whole(spread.shape),
            out_spec_of(packed, 0),
            out_spec_of(packed, 1),
            rows(wide),
            whole((8, wide)),
        ],
        [rows(wide)] * 4,
        scratch=[pltpu.VMEM((block, wide), BF16)],
        flops=2 * seq * wide * 3 * wide,
        moved=22_000_000,
        prefetch=1,
    )(place, o, own, other, spread, packed, packed, xp, gain)


def ffn_body(chunks, start, place_ref, b_ref, df_ref, g_ref, u_ref, d00_ref, d01_ref, d10_ref, d11_ref,
             out_ref, db_ref, gu_send, gu_keep, d_send, d_keep, wd_ref):
    half, s = pl.program_id(0), pl.program_id(1)
    core = place_ref[0]
    chunk = g_ref.shape[3]

    @pl.when(s == 0)
    def _():
        for part, ref in enumerate((d00_ref, d01_ref, d10_ref, d11_ref)):
            w = ref[:, 0]
            wd_ref[:, chunk * part : chunk * (part + 1)] = w.reshape(-1, chunk)

    b, df = b_ref[...], df_ref[...]
    wg = g_ref[:, 0].reshape(-1, chunk)
    wu = u_ref[:, 0].reshape(-1, chunk)
    wd = wd_ref[pl.ds(pl.multiple_of(chunk * (s + start), chunk), chunk), :]
    gate = mm(b, wg)
    upper = mm(b, wu)
    sig = jax.nn.sigmoid(gate)
    act = gate * sig
    z = (act * upper).astype(BF16)
    dz = mm_nt(df, wd)
    dg = (dz * upper * sig * (1.0 + gate * (1.0 - sig))).astype(BF16)
    du = (dz * act).astype(BF16)

    first = jnp.logical_and(half == 0, s == 0)

    @pl.when(first)
    def _():
        out_ref[...] = mm(z, wd)
        db_ref[...] = mm_nt(dg, wg) + mm_nt(du, wu)

    @pl.when(jnp.logical_not(first))
    def _():
        out_ref[...] += mm(z, wd)
        db_ref[...] += mm_nt(dg, wg) + mm_nt(du, wu)

    dwg = mm_tn(b, dg).astype(BF16).reshape(gu_send.shape[0], 64, chunk)
    dwu = mm_tn(b, du).astype(BF16).reshape(gu_send.shape[0], 64, chunk)
    for to, ref in ((0, gu_send), (1, gu_keep)):

        @pl.when(half == to)
        def _():
            ref[:, :64] = dwg
            ref[:, 64:] = dwu

    dwd = mm_tn(z, df).astype(BF16)
    for j in range(2):
        for ref, here in ((d_keep, core == j), (d_send, core != j)):

            @pl.when(here)
            def _():
                for q in range(2):
                    part = 2 * j + q
                    ref[q] = dwd[:, chunk * part : chunk * (part + 1)]


def feed_forward(place, b, df, packed, start, count):
    seq, wide = b.shape
    blocks = packed.shape[0]
    chunks, chunk = 5, 256
    half_of = lambda h, place: jnp.bitwise_xor(place[0], 1 - h)
    columns = lambda at: pl.BlockSpec(
        (blocks, 1, 64, chunk), lambda h, s, place: (0, half_of(h, place), at + start + s, 0)
    )
    down = lambda j, q: pl.BlockSpec(
        (blocks // 2, 1, 160, chunk), lambda h, s, place: (half_of(h, place), j, 4 + q, 0)
    )
    gu = lambda at: pl.BlockSpec(
        (blocks, 128, chunk), lambda h, s, place: (0, jnp.clip(h * count + s - at, 0, count - 1), 0)
    )
    gu_shape = jax.ShapeDtypeStruct((blocks, 128 * count, chunk), BF16)
    d_shape = jax.ShapeDtypeStruct((2, 2 * count * chunk, chunk), BF16)
    d_spec = pl.BlockSpec((2, chunk, chunk), lambda h, s, place: (0, half_of(h, place) * count + s, 0))
    return call(
        functools.partial(ffn_body, chunks, start),
        [
            jax.ShapeDtypeStruct((seq, wide), F32),
            jax.ShapeDtypeStruct((seq, wide), F32),
            gu_shape,
            gu_shape,
            d_shape,
            d_shape,
        ],
        (2, count),
        [whole(b.shape), whole(df.shape), columns(0), columns(chunks)]
        + [down(0, 0), down(0, 1), down(1, 0), down(1, 1)],
        [whole((seq, wide)), whole((seq, wide)), gu(0), gu(count), d_spec, d_spec],
        scratch=[pltpu.VMEM((chunks * chunk, wide), BF16)],
        flops=18 * seq * wide * 2 * count * chunk,
        moved=10_000_000 * count,
        prefetch=1,
    )(place, b, df, *([packed] * 6))


def token_block(steps):
    def at(i, place):
        return jnp.where(i < steps // 2, (1 - place[0]) * (steps // 2) + i, place[0] * (steps // 2) + i - steps // 2)

    return at


def token_specs(steps, block, width):
    half = steps // 2
    return [
        pl.BlockSpec((block, width), lambda i, place: (jnp.minimum(i, half - 1), 0)),
        pl.BlockSpec((1, block, width), lambda i, place: (place[0], jnp.maximum(i - half, 0), 0)),
    ]


def put_tokens(send_ref, keep_ref, value):
    early = pl.program_id(0) < pl.num_programs(0) // 2

    @pl.when(early)
    def _():
        send_ref[...] = value

    @pl.when(jnp.logical_not(early))
    def _():
        keep_ref[0] = value


def post_body(width, place_ref, m_ref, acc0_ref, acc1_ref, db0_ref, db1_ref, df_ref, gain_ref, e_ref,
              wo0_ref, wo1_ref, o_ref, op_ref,
              send_ref, keep_ref, em_ref, do_ref, dwo_send, dwo_keep, dgain_ref, nat_ref, dwo_acc):
    i = pl.program_id(0)
    m, db = m_ref[...], db0_ref[...] + db1_ref[...]
    out = (m + (acc0_ref[...] + acc1_ref[...])).astype(BF16)
    put_tokens(send_ref, keep_ref, mm_nt(out, e_ref[:width, :]).astype(BF16))
    scale = lax.rsqrt(jnp.sum(m * m, axis=-1, keepdims=True) / width + EPSILON)
    n = m * scale
    c = db * gain_ref[1:2]
    mean = jnp.sum(c * n, axis=-1, keepdims=True) / width
    em = df_ref[...].astype(F32) + scale * (c - n * mean)
    em_ref[...] = em
    da = em.astype(BF16)
    dgain = jnp.sum(db * n, axis=0, keepdims=True)
    dwo = mm_tn(op_ref[...], da)

    @pl.when(i == 0)
    def _():
        dgain_ref[...] = dgain
        dwo_acc[...] = dwo

    @pl.when(i > 0)
    def _():
        dgain_ref[...] += dgain
        dwo_acc[...] += dwo

    @pl.when(i == pl.num_programs(0) - 1)
    def _():
        for j in range(2):
            for ref, here in ((dwo_keep, place_ref[0] == j), (dwo_send, place_ref[0] != j)):

                @pl.when(here)
                def _():
                    for q in range(2):
                        at = 512 * j + 256 * q
                        ref[q] = dwo_acc[:, at : at + 256].astype(BF16).reshape(ref.shape[1:])

    dop = 0.0
    for part in range(4):
        w = columns_of((wo0_ref, wo1_ref), part)
        dop = dop + mm_nt(da[:, 256 * part : 256 * (part + 1)], w)
    nat_ref[...] = mm_nt(dop.astype(BF16), e_ref[...])
    lane = lane_of(m.shape[0])
    low = lane < HEAD
    for head in range(HEADS):
        val = nat_ref[:, LANES * (head // 2) : LANES * (head // 2 + 1)]
        if head % 2:
            val = pltpu.roll(val, 64, 1)
        val = jnp.where(low, val, 0.0)
        delta = jnp.sum(val * o_ref[head].astype(F32), axis=-1, keepdims=True)
        do_ref[head] = put_terms(val, delta, lane, HEAD).astype(BF16)


def after(place, m, accs, dbs, df, gain, spread, packed, o, op, width, block=256):
    seq, wide = m.shape
    blocks = packed.shape[0]
    steps = seq // block
    at = token_block(steps)
    rows = lambda n: pl.BlockSpec((block, n), lambda i, place: (at(i, place), 0))
    heads = pl.BlockSpec((HEADS, block, LANES), lambda i, place: (0, at(i, place), 0))
    dwo_shape = (2, blocks, wide // blocks, 256)
    return call(
        functools.partial(post_body, width),
        [
            jax.ShapeDtypeStruct((seq // 2, width), BF16),
            jax.ShapeDtypeStruct((2, seq // 2, width), BF16),
            jax.ShapeDtypeStruct((seq, wide), F32),
            jax.ShapeDtypeStruct((HEADS, seq, LANES), BF16),
            jax.ShapeDtypeStruct(dwo_shape, BF16),
            jax.ShapeDtypeStruct(dwo_shape, BF16),
            jax.ShapeDtypeStruct((1, wide), F32),
        ],
        (steps,),
        [rows(wide)] * 6
        + [whole((8, wide)), whole(spread.shape), out_spec_of(packed, 0), out_spec_of(packed, 1), heads, rows(wide)],
        token_specs(steps, block, width)
        + [rows(wide), heads, whole(dwo_shape), whole(dwo_shape), whole((1, wide))],
        scratch=[pltpu.VMEM((block, wide), F32), pltpu.VMEM((wide, wide), F32)],
        flops=2 * seq * wide * 4 * wide,
        moved=45_000_000,
        prefetch=1,
    )(place, m, *accs, *dbs, df, gain, spread, packed, packed, o, op)


def weights_body(place_ref, dq0_ref, dq1_ref, dk0_ref, dk1_ref, dv0_ref, dv1_ref, a_ref, w_ref, gain_ref,
                 dgain_ref, flat_ref, send_ref, keep_ref, dw_acc, part_ref):
    i = pl.program_id(0)
    heads = HEADS + KV_HEADS

    def head(h, first, second):
        return first[h] if h < first.shape[0] else second[h - first.shape[0]]

    def query_or_key(h):
        return head(h, dq0_ref, dq1_ref) if h < HEADS else head(h - HEADS, dk0_ref, dk1_ref)

    pairs_to(flat_ref, query_or_key, heads)
    pairs_to(flat_ref, lambda h: head(h, dv0_ref, dv1_ref), KV_HEADS, heads * HEAD)
    dw = mm_tn(a_ref[...], flat_ref[...])

    @pl.when(i == 0)
    def _():
        dw_acc[...] = dw

    @pl.when(i > 0)
    def _():
        dw_acc[...] += dw

    @pl.when(i == pl.num_programs(0) - 1)
    def _():
        wide = dw_acc.shape[0]
        total = jnp.sum(dw_acc[...] * w_ref[...].astype(F32), axis=-1, keepdims=True)
        column = lambda row: jnp.broadcast_to(row, (LANES, wide)).T
        gain = column(gain_ref[:1])
        attn = jnp.broadcast_to(total, (wide, LANES)) / jnp.where(gain == 0.0, 1.0, gain)
        lane = lane_of(wide)
        gains = jnp.where(lane == 32, attn, 0.0) + jnp.where(lane == 33, column(dgain_ref[...]), 0.0)
        n_q, n_k = HEADS * HEAD // 2, KV_HEADS * HEAD // 2
        for j in range(2):
            part_ref[:, 768:] = gains.astype(BF16)
            part_ref[:, :n_q] = dw_acc[:, n_q * j : n_q * (j + 1)].astype(BF16)
            for part in range(2):
                at, to = 2 * n_q + n_k * (2 * part + j), n_q + n_k * part
                part_ref[:, to : to + n_k] = dw_acc[:, at : at + n_k].astype(BF16)
            for ref, here in ((keep_ref, place_ref[0] == j), (send_ref, place_ref[0] != j)):

                @pl.when(here)
                def _():
                    ref[...] = part_ref[...].reshape(ref.shape)


def projections_back(place, firsts, seconds, a, w_qkv, gain, dgain_ffn, block=512):
    seq, wide = a.shape
    blocks = 16
    rows = lambda n: pl.BlockSpec((block, n), lambda i, *_: (i, 0))
    heads = lambda t: pl.BlockSpec((t.shape[0], block, LANES), lambda i, *_: (0, i, 0))
    parts = [t for pair in zip(firsts, seconds) for t in pair]
    shape = (blocks, wide // blocks, 896)
    return call(
        weights_body,
        [
            jax.ShapeDtypeStruct((seq, QKV_PAD), BF16),
            jax.ShapeDtypeStruct(shape, BF16),
            jax.ShapeDtypeStruct(shape, BF16),
        ],
        (seq // block,),
        [heads(t) for t in parts] + [rows(wide), whole(w_qkv.shape), whole((8, wide)), whole((1, wide))],
        [rows(QKV_PAD), whole(shape), whole(shape)],
        scratch=[pltpu.VMEM((wide, QKV_PAD), F32), pltpu.VMEM((wide, 896), BF16)],
        flops=2 * seq * wide * QKV_PAD,
        moved=20_000_000,
        prefetch=1,
    )(place, *parts, a, w_qkv, gain, dgain_ffn)


def input_body(width, place_ref, flat_ref, w_ref, xp_ref, em_ref, gain_ref, e_ref, send_ref, keep_ref):
    da = mm_nt(flat_ref[...], w_ref[...])
    xp = xp_ref[...].astype(F32)
    scale = lax.rsqrt(jnp.sum(xp * xp, axis=-1, keepdims=True) / width + EPSILON)
    n = xp * scale
    c = da * gain_ref[:1]
    mean = jnp.sum(c * n, axis=-1, keepdims=True) / width
    grad = em_ref[...] + scale * (c - n * mean)
    e = e_ref[:width, :]
    high = grad.astype(BF16)
    value = mm_nt(high, e) + mm_nt((grad - high.astype(F32)).astype(BF16), e)
    put_tokens(send_ref, keep_ref, value)


def input_back(place, flat, w_qkv, xp, em, gain, spread, width, block=256):
    seq, wide = xp.shape
    steps = seq // block
    at = token_block(steps)
    rows = lambda n: pl.BlockSpec((block, n), lambda i, place: (at(i, place), 0))
    return call(
        functools.partial(input_body, width),
        [
            jax.ShapeDtypeStruct((seq // 2, width), F32),
            jax.ShapeDtypeStruct((2, seq // 2, width), F32),
        ],
        (steps,),
        [rows(QKV_PAD), whole(w_qkv.shape), rows(wide), rows(wide), whole((8, wide)), whole(spread.shape)],
        token_specs(steps, block, width),
        flops=2 * seq * wide * (QKV_PAD + 2 * width),
        moved=20_000_000,
        prefetch=1,
    )(place, flat, w_qkv, xp, em, gain, spread)


def spread_matrix(width, blocks, wide):
    row = jnp.arange(wide, dtype=jnp.int32)
    per, step = width // blocks, wide // blocks
    place = (row // per) * step + row % per
    hit = (place[:, None] == jnp.arange(wide, dtype=jnp.int32)[None, :]) & (row < width)[:, None]
    return hit.astype(BF16)


def tables(positions, segments):
    lane = jnp.arange(LANES, dtype=jnp.int32)
    frequency = 10000.0 ** (-((lane % 32).astype(F32) * 2.0 / HEAD))
    angles = positions.astype(F32)[:, None] * frequency[None, :]
    cos, sin = jnp.cos(angles), jnp.sin(angles)
    high = (lane % HEAD >= 32)[None, :]
    sa = jnp.where(high, sin, 0.0)
    sb = jnp.where(high, 0.0, -sin)
    doc = (lane - HEAD)[None, :]
    mine = segments[:, None] == doc
    in_doc = (doc >= 0) & (doc < DOCS)
    aq = jnp.where(mine & in_doc, MASKED, 0.0)
    ak = jnp.where(in_doc & ~mine, 1.0, 0.0)
    ak = jnp.where((doc >= DOCS) & (doc < DOCS + 3), -1.0, ak)
    return cos, sa, sb, aq, ak


def pad_rows(w, blocks, step=64):
    per = w.shape[0] // blocks
    return jnp.pad(w.reshape(blocks, per, w.shape[1]), ((0, 0), (0, step - per), (0, 0)))


def pad_cols(w, blocks, step=64):
    per = w.shape[1] // blocks
    w = jnp.pad(w.reshape(w.shape[0], blocks, per), ((0, 0), (0, 0), (0, step - per)))
    return w.reshape(w.shape[0], blocks * step)


def cut_rows(w, per):
    return w[:, :per].reshape(w.shape[0] * per, w.shape[2])


def cut_cols(w, per, step=64):
    blocks = w.shape[1] // step
    return w.reshape(w.shape[0], blocks, step)[:, :, :per].reshape(w.shape[0], blocks * per)


def chunked(w, chunk=256):
    blocks, rows, cols = w.shape
    w = w.reshape(blocks, rows, cols // chunk, chunk).transpose(0, 2, 1, 3)
    return w.reshape(blocks, cols // chunk * rows, chunk)


def joined(w, rows):
    blocks, total, chunk = w.shape
    w = w.reshape(blocks, total // rows, rows, chunk).transpose(0, 2, 1, 3)
    return w.reshape(blocks, rows, total // rows * chunk)


def pack_half(w_gate, w_up, w_down, w_out, blocks, groups):
    down = pad_cols(w_down, groups)
    down = down.reshape(blocks, w_down.shape[0] // blocks, down.shape[1])
    return jnp.concatenate(
        [
            chunked(pad_rows(w_gate, blocks)),
            chunked(pad_rows(w_up, blocks)),
            chunked(down),
            chunked(pad_rows(pad_cols(w_out, groups), blocks)),
        ],
        axis=1,
    )


def add(left, right):
    return (left.astype(F32) + right.astype(F32)).astype(BF16)


def swap(x):
    return lax.ppermute(x, "ctx", [(0, 1), (1, 0)])


def across(x, bit, count):
    return lax.ppermute(x, "dp", [(i, i ^ (1 << bit)) for i in range(count)])


def pick(x, index, axis=0):
    return lax.dynamic_index_in_dim(x, index, axis, keepdims=False)


def tie(value, *others):
    return lax.optimization_barrier((value, *others))[0]


def along_z(x, step, count):
    return lax.ppermute(x, "dp", [(i, (i + 4 * step) % count) for i in range(count)])


def gather_pieces(shard, count):
    stack = jnp.stack([shard] + [along_z(shard, k, count) for k in (1, 2, 3)])
    half = shard.shape[0] // 2
    first, second = stack[:, :half], stack[:, half:]
    first = jnp.concatenate([first, across(first, 0, count)])
    second = jnp.concatenate([second, across(second, 1, count)])
    pieces = (first, across(first, 1, count), second, across(second, 0, count))
    return pieces + tuple(swap(piece) for piece in pieces)


class RowSum:
    def __init__(self, first, second, place, count):
        _, z, y, x = place
        self.count, self.z, self.y, self.x = count, z, y, x
        cube = (4, 2, 2)
        first = first.reshape(cube + first.shape[1:])
        second = second.reshape(cube + second.shape[1:])
        self.sent = [pick(first, 1 - x, 2), pick(second, 1 - y, 1)]
        self.kept = [pick(first, x, 2), pick(second, y, 1)]

    def move(self):
        self.got = [across(self.sent[0], 0, self.count), across(self.sent[1], 1, self.count)]

    def wait(self, other):
        self.got = list(lax.optimization_barrier((*self.got, other))[:-1])

    def turn(self, other):
        self.wait(other)
        first, second = (add(k, g) for k, g in zip(self.kept, self.got))
        self.sent = [pick(first, 1 - self.y, 1), pick(second, 1 - self.x, 1)]
        self.kept = [pick(first, self.y, 1), pick(second, self.x, 1)]

    def move_again(self):
        self.got = [across(self.sent[0], 1, self.count), across(self.sent[1], 0, self.count)]

    def climb(self, other):
        self.wait(other)
        both = jnp.stack([add(k, g) for k, g in zip(self.kept, self.got)], axis=1)
        self.sent = [pick(both, lax.rem(self.z + k, 4), 0) for k in (1, 2, 3)]
        self.kept = [pick(both, self.z, 0)]

    def move_up(self):
        self.got = [along_z(self.sent[k - 1], k, self.count) for k in (1, 2, 3)]

    def total(self):
        total = self.kept[0].astype(F32)
        for got in self.got:
            total = total + got.astype(F32)
        return total


def split_rows(x, at):
    return x[:, :at], x[:, at:]


def join(early, late, count):
    early = early.reshape(2, 2, early.shape[1] // 2, 256)
    late = late.reshape(2, 2, late.shape[1] // 2, 256)
    return jnp.concatenate([early, late], axis=2).reshape(2, count, -1, 256)


def put_other(both, got, core):
    return lax.dynamic_update_slice(both, got[None], (1 - core, 0, 0))


def shards_of_two(inputs, segment_ids, positions, w_query, w_key, w_value, w_out, w_gate, w_up,
                  w_down, gain_attn, gain_ffn, cotangent):
    count = lax.axis_size("dp")
    me, core = lax.axis_index("dp"), lax.axis_index("ctx")
    place = (core, me // 4, (me >> 1) & 1, me & 1)
    place_of = jnp.stack(place).astype(jnp.int32)
    per = gain_attn.shape[0]
    width = per * count
    groups = w_out.shape[1] // per
    hidden = w_down.shape[0]
    n_q, n_k = w_query.shape[1], w_key.shape[1]
    n_qkv = n_q + 2 * n_k

    packed = pack_half(w_gate, w_up, w_down, w_out, 1, groups)[0]
    packed = lax.all_gather(packed, ("dp", "ctx"), axis=0, tiled=False)
    packed = packed.reshape((count, 2) + packed.shape[1:])

    shard = jnp.concatenate(
        [w_query, w_key, w_value, gain_attn[:, None], gain_ffn[:, None]], axis=1
    )
    shard = jnp.pad(shard, ((0, 64 - per), (0, 896 - n_qkv - 2)))
    pieces = gather_pieces(shard, count)

    def halves(x):
        return pick(x[:, 0], core), swap(pick(x[:, 0], 1 - core))

    spread = spread_matrix(width, count, count * 64)
    cos, sa, sb, aq, ak = tables(pick(positions[:, 0], core), pick(segment_ids[:, 0], core))
    xp, a, q, k, v, w_qkv, gains = pre_attention(
        place_of, *halves(inputs), spread, pieces, cos, sa, sb, aq, ak
    )
    o, q2 = attend(q, k, v)
    op, m, b, df = middle(place_of, o, *halves(cotangent), spread, packed, xp, gains)

    acc0, db0, gu_send, gu_keep, d_send0, d_keep0 = feed_forward(place_of, b, df, packed, 0, 3)
    gu_got = swap(gu_send)
    b = tie(b, acc0, gu_send)
    acc1, db1, gu1_send, gu1_keep, d_send1, d_keep1 = feed_forward(place_of, b, df, packed, 3, 2)
    one = RowSum(*split_rows(add(gu_keep, tie(gu_got, acc1)), 192), place, count)
    d_send = join(d_send0, d_send1, count)
    gu1_got, d_got = swap(gu1_send), swap(d_send)
    one.move()
    m = tie(m, *one.sent, gu1_send, d_send)
    out_send, outs, em, do, o_send, o_keep, dgf = after(
        place_of, m, (acc0, acc1), (db0, db1), df, gains, spread, packed, o, op, width
    )
    o_got = swap(o_send)
    outs = put_other(outs, swap(out_send), core)

    one.turn(em)
    gu1 = add(gu1_keep, tie(gu1_got, em))
    down = add(join(d_keep0, d_keep1, count), tie(d_got, em))
    outer = add(o_keep, o_got)
    two = RowSum(
        jnp.concatenate([gu1[:, :128], down[0], outer[0]], axis=1),
        jnp.concatenate([gu1[:, 128:], down[1], outer[1]], axis=1),
        place, count,
    )
    one.move_again()
    two.move()
    do = tie(do, *one.sent, *two.sent)
    firsts = attend_back(q2, k, v, do, cos, sa, sb, 0, 3)
    one.climb(firsts[0])
    one.move_up()
    do = tie(do, *one.sent)
    seconds = attend_back(q2, k, v, do, cos, sa, sb, 3, 2)
    two.turn(seconds[0])
    two.move_again()
    a = tie(a, *two.sent)
    flat, p_send, p_keep = projections_back(place_of, firsts, seconds, a, w_qkv, gains, dgf)
    three = RowSum(*split_rows(add(p_keep, swap(p_send)), 32), place, count)
    two.climb(flat)
    two.move_up()
    three.move()
    flat = tie(flat, *two.sent, *three.sent)
    gi_send, gis = input_back(place_of, flat, w_qkv, xp, em, gains, spread, width)
    three.turn(gis)
    three.move_again()
    gis = put_other(gis, swap(gi_send), core)
    three.climb(gis)
    three.move_up()

    first, second, third = one.total(), two.total(), three.total()
    third = third.reshape(64, 896)[:per]
    gu = jnp.concatenate([first.reshape(3, 2, 64, 256), second[:, :128].reshape(2, 2, 64, 256)])
    wide_of = lambda t: t.transpose(1, 0, 2).reshape(t.shape[1], -1)
    return (
        outs[:, None],
        gis[:, None],
        third[:, :n_q],
        third[:, n_q : n_q + n_k],
        third[:, n_q + n_k : n_qkv],
        cut_cols(wide_of(second[:, 288:])[:per], per),
        wide_of(gu[:, 0])[:per],
        wide_of(gu[:, 1])[:per],
        cut_cols(wide_of(second[:, 128:288]), per),
        third[:, n_qkv],
        third[:, n_qkv + 1],
    )


def shards_of_many(inputs, segment_ids, positions, w_query, w_key, w_value, w_out, w_gate, w_up,
                   w_down, gain_attn, gain_ffn, cotangent):
    count, cores = lax.axis_size("dp"), lax.axis_size("ctx")
    core = lax.axis_index("ctx")
    share = cores // MICRO
    per = gain_attn.shape[0]
    width = per * count

    def gathered(w):
        return lax.all_gather(lax.all_gather(w, "dp", axis=0, tiled=True), "ctx", axis=1, tiled=True)

    full = [gathered(w) for w in (w_query, w_key, w_value, w_out, w_gate, w_up, w_down)]
    gain_pair = lax.all_gather(jnp.stack([gain_attn, gain_ffn]), "dp", axis=1, tiled=True)
    gains = jnp.pad(pad_cols(gain_pair.astype(F32), count), ((0, 6), (0, 0)))
    w_qkv = pad_rows(jnp.concatenate(full[:3], axis=1), count).reshape(count * 64, QKV)
    w_qkv = jnp.pad(w_qkv, ((0, 0), (0, QKV_PAD - QKV)))
    w_o, w_g, w_u, w_d = full[3:]
    half = lambda w, j: w[:, w.shape[1] // 2 * j : w.shape[1] // 2 * (j + 1)]
    packed = jnp.stack(
        [pack_half(half(w_g, j), half(w_u, j), half(w_d, j), half(w_o, j), count, count // 2) for j in range(2)],
        axis=1,
    )
    which = core // share

    def sequence(x):
        whole_one = pick(lax.all_gather(x[:, 0], "ctx", axis=1, tiled=True), which)
        return whole_one[: whole_one.shape[0] // 2], whole_one[whole_one.shape[0] // 2 :]

    place = jnp.zeros((4,), jnp.int32)
    spread = spread_matrix(width, count, count * 64)
    cos, sa, sb, aq, ak = tables(pick(positions[:, 0], which), pick(segment_ids[:, 0], which))
    xp, a, q, k, v, w_qkv, gains = pre_attention(
        place, *sequence(inputs), spread, (w_qkv, gains), cos, sa, sb, aq, ak
    )
    o, q2 = attend(q, k, v)
    op, m, b, df = middle(place, o, *sequence(cotangent), spread, packed, xp, gains)
    acc0, db0, gu_send, gu_keep, d_send, d_keep = feed_forward(place, b, df, packed, 0, 3)
    acc1, db1, gu1_send, gu1_keep, d1_send, d1_keep = feed_forward(place, b, df, packed, 3, 2)
    out_send, outs, em, do, o_send, o_keep, dgf = after(
        place, m, (acc0, acc1), (db0, db1), df, gains, spread, packed, o, op, width
    )
    firsts = attend_back(q2, k, v, do, cos, sa, sb, 0, 3)
    seconds = attend_back(q2, k, v, do, cos, sa, sb, 3, 2)
    flat, p_send, p_keep = projections_back(place, firsts, seconds, a, w_qkv, gains, dgf)
    gi_send, gis = input_back(place, flat, w_qkv, xp, em, gains, spread, width)

    parts = [cut_rows(p, per) for p in (p_keep, p_send)]
    n_q, n_k = HEADS * HEAD // 2, KV_HEADS * HEAD // 2
    both = lambda at, n: jnp.concatenate([p[:, at : at + n] for p in parts], axis=1)
    side = lambda t: jnp.concatenate([t[0], t[1]], axis=-1)

    def wide_of(index):
        every = []
        for early, late in ((gu_keep, gu1_keep), (gu_send, gu1_send)):
            t = jnp.concatenate([early, late], axis=1).reshape(count, 5, 2, 64, 256)[:, :, index]
            every.append(cut_rows(t.transpose(0, 2, 1, 3).reshape(count, 64, -1), per))
        return jnp.concatenate(every, axis=1)

    grads = [
        both(0, n_q),
        both(n_q * 1, n_k),
        both(n_q + n_k, n_k),
        cut_cols(cut_rows(jnp.concatenate([side(o_keep), side(o_send)], axis=-1), per), per),
        wide_of(0),
        wide_of(1),
        cut_cols(
            jnp.concatenate([side(join(d_keep, d1_keep, count)), side(join(d_send, d1_send, count))], axis=-1)
            .reshape(-1, 4 * 256),
            per,
        ),
    ]

    def summed(g):
        g = lax.psum_scatter(g * (1.0 / share), "dp", scatter_dimension=0, tiled=True)
        return lax.psum_scatter(g, "ctx", scatter_dimension=1, tiled=True).astype(F32)

    sums = [summed(g.astype(BF16)) for g in grads]
    dgain = parts[0][:, 2 * n_k + n_q : 2 * n_k + n_q + 2].astype(F32).T * (1.0 / share)
    dgain = lax.psum_scatter(lax.psum(dgain, "ctx"), "dp", scatter_dimension=1, tiled=True)

    def tokens(seq):
        rows = seq.shape[0] // cores
        every = lax.all_gather(seq, "ctx", axis=0, tiled=False)
        return lax.dynamic_slice_in_dim(every[::share], core * rows, rows, axis=1)[:, None]

    out = jnp.concatenate([outs[0], out_send])
    gi = jnp.concatenate([gis[0], gi_send])
    return (tokens(out), tokens(gi), *sums, dgain[0], dgain[1])


def solution(mesh):
    two = mesh.shape["ctx"] == MICRO and mesh.shape["dp"] == 16
    matrices = (P("dp", "ctx"),) * 7 + (P("dp"), P("dp"))
    tokens = P(None, "dp", "ctx", None)
    return jax.shard_map(
        shards_of_two if two else shards_of_many,
        mesh=mesh,
        in_specs=(tokens, P(None, "dp", None), P(None, "dp", None)) + matrices + (tokens,),
        out_specs=(tokens, tokens) + matrices,
        check_vma=False,
    )
```

```python
import functools

import jax
import jax.numpy as jnp
from jax import lax
from jax.experimental import pallas as pl
from jax.experimental.pallas import tpu as pltpu
from jax.sharding import PartitionSpec as P

HEADS = 15
KV_HEADS = 5
HEAD = 64
MICRO = 2
GROUP = 3
DOCS = 4

EPSILON = 1e-05
MASKED = -1e30
LANES = 128
QKV = (HEADS + 2 * KV_HEADS) * HEAD
QKV_PAD = 1664
VMEM_LIMIT = 48 * 1024 * 1024
PACK = 1408
VMEM_SMALL = 24 * 1024 * 1024
WIDE_HEADS = HEADS * LANES
F32 = jnp.float32
BF16 = jnp.bfloat16


def up(value, step):
    return -(-value // step) * step


def mm(left, right):
    return lax.dot_general(left, right, (((1,), (0,)), ((), ())), preferred_element_type=F32)


def mm_nt(left, right):
    return lax.dot_general(left, right, (((1,), (1,)), ((), ())), preferred_element_type=F32)


def mm_tn(left, right):
    return lax.dot_general(left, right, (((0,), (0,)), ((), ())), preferred_element_type=F32)


def call(body, out_shape, grid, in_specs, out_specs, scratch=(), flops=0, moved=0, prefetch=0, alias=None,
         vmem=VMEM_LIMIT):
    return pl.pallas_call(
        body,
        out_shape=out_shape,
        grid_spec=pltpu.PrefetchScalarGridSpec(
            num_scalar_prefetch=prefetch,
            grid=grid,
            in_specs=in_specs,
            out_specs=out_specs,
            scratch_shapes=scratch,
        ),
        input_output_aliases=alias or {},
        compiler_params=pltpu.CompilerParams(vmem_limit_bytes=vmem),
        cost_estimate=pl.CostEstimate(flops=flops, bytes_accessed=moved, transcendentals=0),
    )


def whole(shape):
    return pl.BlockSpec(shape, lambda *_: (0,) * len(shape))


def lane_of(rows):
    return lax.broadcasted_iota(jnp.int32, (rows, LANES), 1)


def three_terms(column):
    high = column.astype(BF16).astype(F32)
    rest = column - high
    mid = rest.astype(BF16).astype(F32)
    return high, mid, rest - mid


def put_terms(base, column, lane, first):
    high, mid, low = three_terms(column)
    base = jnp.where(lane == first, high, base)
    base = jnp.where(lane == first + 1, mid, base)
    return jnp.where(lane == first + 2, low, base)


def build_weights(place_ref, piece_refs, stage_ref, w_ref, wo_ref):
    core, z, y, x = (place_ref[n] for n in range(4))
    for swapped in range(2):
        near_a, far_a, near_b, far_b = piece_refs[4 * swapped : 4 * swapped + 4]
        to = jnp.bitwise_xor(core, swapped)
        for dy in range(2):
            for dx in range(2):
                for k in range(4):
                    block = lax.rem(z + 4 - k, 4) * 4 + (y ^ dy) * 2 + (x ^ dx)
                    row = pl.multiple_of(block * 64, 64)
                    stage_ref[to, pl.ds(row, 32), :] = (far_a if dy else near_a)[4 * dx + k]
                    stage_ref[to, pl.ds(row + 32, 32), :] = (far_b if dx else near_b)[4 * dy + k]
    n_q, n_k = HEADS * HEAD // 2, KV_HEADS * HEAD // 2
    for j in range(2):
        w_ref[:, n_q * j : n_q * (j + 1)] = stage_ref[j, :, :n_q]
        for part in range(2):
            to, at = 2 * n_q + n_k * (2 * part + j), n_q + n_k * part
            w_ref[:, to : to + n_k] = stage_ref[j, :, at : at + n_k]
        half = wo_ref.shape[1] // 2
        wo_ref[:, half * j : half * (j + 1)] = stage_ref[j, :, PACK - half :]
    w_ref[:, QKV:] = jnp.zeros((w_ref.shape[0], QKV_PAD - QKV), BF16)


def projections(xp, scale, w_ref, gain_ref, cos_ref, sa_ref, sb_ref, aq_ref, ak_ref,
                xp_ref, a_ref, q_ref, k_ref, v_ref):
    a = (xp * scale * gain_ref[:1]).astype(BF16)
    xp_ref[...] = xp.astype(BF16)
    a_ref[...] = a
    t = mm(a, w_ref[...])
    lane = lane_of(t.shape[0])
    low = lane < HEAD
    cos, sa, sb, aq, ak = cos_ref[...], sa_ref[...], sb_ref[...], aq_ref[...], ak_ref[...]
    for pair in range((HEADS + KV_HEADS) // 2):
        tt = t[:, LANES * pair : LANES * (pair + 1)]
        rot = tt * cos + pltpu.roll(tt, 32, 1) * sa + pltpu.roll(tt, 96, 1) * sb
        for half in range(2):
            head = 2 * pair + half
            val = rot if half == 0 else pltpu.roll(rot, 64, 1)
            if head < HEADS:
                q_ref[head] = jnp.where(low, val * HEAD ** -0.5, aq).astype(BF16)
            else:
                k_ref[head - HEADS] = jnp.where(low, val, ak).astype(BF16)
    av = jnp.where(lane < HEAD + 3, -1.0, 0.0)
    for head in range(KV_HEADS):
        first = (HEADS + KV_HEADS) * HEAD + LANES * (head // 2)
        tt = t[:, first : first + LANES]
        val = tt if head % 2 == 0 else pltpu.roll(tt, 64, 1)
        v_ref[head] = jnp.where(low, val, av).astype(BF16)


def own_or_other(place_ref, own_ref, other_ref):
    first = pl.program_id(0) < pl.num_programs(0) // 2
    mine = first == (place_ref[0] == 0)
    return jnp.where(mine, own_ref[...], other_ref[...])


def pre_body(width, place_ref, own_ref, other_ref, e_ref, *refs):
    pieces, refs = refs[:8], refs[8:]
    *rest, w_ref, wo_ref, gain_ref, stage_ref = refs

    @pl.when(pl.program_id(0) == 0)
    def _():
        build_weights(place_ref, pieces, stage_ref, w_ref, wo_ref)
        gain_ref[...] = stage_ref[0, :, 768:896].astype(F32).T[32:40]

    xp = mm_tn(own_or_other(place_ref, own_ref, other_ref), e_ref[:width, :])
    scale = lax.rsqrt(jnp.sum(xp * xp, axis=-1, keepdims=True) / width + EPSILON)
    projections(xp, scale, w_ref, gain_ref, *rest)


def pre_whole_body(width, place_ref, own_ref, other_ref, e_ref, w_ref, wo_ref, gain_ref, *rest):
    xp = mm_tn(own_or_other(place_ref, own_ref, other_ref), e_ref[:width, :])
    scale = lax.rsqrt(jnp.sum(xp * xp, axis=-1, keepdims=True) / width + EPSILON)
    projections(xp, scale, w_ref, gain_ref, *rest)


def halves_specs(rows, width, block):
    steps = rows // block
    return [pl.BlockSpec((width, block), lambda i, *_: (0, i % steps))] * 2


def pre_attention(place, own, other, spread, weights, cos, sa, sb, aq, ak, block=256):
    width, half = own.shape
    seq, wide = 2 * half, spread.shape[1]
    pieces = len(weights) == 8
    rows = lambda n: pl.BlockSpec((block, n), lambda i, *_: (i, 0))
    heads = lambda n: pl.BlockSpec((n, block, LANES), lambda i, *_: (0, i, 0))
    shapes = [
        jax.ShapeDtypeStruct((seq, wide), BF16),
        jax.ShapeDtypeStruct((seq, wide), BF16),
        jax.ShapeDtypeStruct((HEADS, seq, LANES), BF16),
        jax.ShapeDtypeStruct((KV_HEADS, seq, LANES), BF16),
        jax.ShapeDtypeStruct((KV_HEADS, seq, LANES), BF16),
    ]
    specs = [rows(wide), rows(wide), heads(HEADS), heads(KV_HEADS), heads(KV_HEADS)]
    if pieces:
        shapes += [jax.ShapeDtypeStruct((wide, QKV_PAD), BF16), jax.ShapeDtypeStruct((wide, wide), BF16)]
        shapes += [jax.ShapeDtypeStruct((8, wide), F32)]
        specs += [whole((wide, QKV_PAD)), whole((wide, wide)), whole((8, wide))]
    results = call(
        functools.partial(pre_body if pieces else pre_whole_body, width),
        shapes,
        (seq // block,),
        halves_specs(half, width, block)
        + [whole(spread.shape)]
        + [whole(w.shape) for w in weights]
        + [rows(LANES)] * 5,
        specs,
        scratch=[pltpu.VMEM((2, wide, weights[0].shape[-1]), BF16)] if pieces else (),
        flops=2 * seq * wide * (width + QKV_PAD),
        moved=20_000_000,
        prefetch=1,
    )(place, own, other, spread, *weights, cos, sa, sb, aq, ak)
    return results if pieces else (*results, *weights)


def attend_body(block, q_ref, k_ref, v_ref, o_ref, q2_ref):
    seq = k_ref.shape[1]
    rows = GROUP * block
    below = lax.broadcasted_iota(jnp.int32, (block, block), 0) >= lax.broadcasted_iota(
        jnp.int32, (block, block), 1
    )
    below = jnp.concatenate([below.astype(F32)] * GROUP, axis=0) > 0.5
    lane = lane_of(rows)
    for i in range(seq // block):
        span = slice(block * i, block * (i + 1))
        q = q_ref[:, span, :].reshape(rows, LANES)
        s_in = jnp.where(below, mm_nt(q, k_ref[0, span, :]), MASKED)
        top = jnp.max(s_in, axis=-1, keepdims=True)
        if i:
            s_left = mm_nt(q, k_ref[0, : block * i, :])
            top = jnp.maximum(top, jnp.max(s_left, axis=-1, keepdims=True))
        ext = mm(jnp.exp(s_in - top).astype(BF16), v_ref[0, span, :])
        if i:
            ext = ext + mm(jnp.exp(s_left - top).astype(BF16), v_ref[0, : block * i, :])
        total = -ext[:, HEAD : HEAD + 1]
        o = ext / total
        o = jnp.where(lane < HEAD, o, pltpu.roll(o, 64, 1))
        o_ref[:, span, :] = o.reshape(GROUP, block, LANES).astype(BF16)
        q2 = put_terms(q.astype(F32), top + jnp.log(total), lane, HEAD + DOCS)
        q2_ref[:, span, :] = q2.reshape(GROUP, block, LANES).astype(BF16)


def attend(q, k, v, block=256):
    seq = q.shape[1]
    group = pl.BlockSpec((GROUP, seq, LANES), lambda n: (n, 0, 0))
    one = pl.BlockSpec((1, seq, LANES), lambda n: (n, 0, 0))
    shape = jax.ShapeDtypeStruct(q.shape, BF16)
    return call(
        functools.partial(attend_body, block),
        [shape, shape],
        (KV_HEADS,),
        [group, one, one],
        [group, group],
        flops=4 * HEADS * seq * seq * LANES,
        moved=15_000_000,
    )(q, k, v)


def attend_back_body(block, q_ref, k_ref, v_ref, do_ref, cos_ref, sa_ref, sb_ref,
                     dq_ref, dk_ref, dv_ref, acc_ref):
    seq = k_ref.shape[1]
    above = lax.broadcasted_iota(jnp.int32, (block, block), 0) <= lax.broadcasted_iota(
        jnp.int32, (block, block), 1
    )
    lane = lane_of(seq)

    def unrotate(t, span):
        rows = span.stop - span.start
        rot = (
            t * cos_ref[span, :]
            - pltpu.roll(t, 32, 1) * sa_ref[span, :]
            - pltpu.roll(t, 96, 1) * sb_ref[span, :]
        )
        return twice(rot, rows)

    def twice(t, rows):
        return jnp.where(lane[:rows] < HEAD, t, pltpu.roll(t, 64, 1)).astype(BF16)

    for j in range(seq // block):
        span = slice(block * j, block * (j + 1))
        k, v = k_ref[0, span, :], v_ref[0, span, :]
        dk = jnp.zeros((block, LANES), F32)
        dv = jnp.zeros((block, LANES), F32)
        for g in range(GROUP):
            q, do = q_ref[g, block * j :, :], do_ref[g, block * j :, :]
            p = jnp.exp(mm_nt(k, q))
            inner = jnp.where(above, p[:, :block], 0.0)
            p = inner if p.shape[1] == block else jnp.concatenate([inner, p[:, block:]], axis=1)
            ds = (p * mm_nt(v, do)).astype(BF16)
            dv = dv + mm(p.astype(BF16), do)
            dk = dk + mm(ds, q)
            dq = mm_tn(ds, k)
            if j == 0:
                acc_ref[g] = dq
            else:
                acc_ref[g, block * j :, :] += dq
        dk_ref[0, span, :] = unrotate(dk, span)
        dv_ref[0, span, :] = twice(dv, block)
    for g in range(GROUP):
        dq_ref[g] = unrotate(acc_ref[g] * HEAD ** -0.5, slice(0, seq))


def attend_back(q, k, v, do, cos, sa, sb, first, count, block=256):
    seq = q.shape[1]
    group = lambda at: pl.BlockSpec((GROUP, seq, LANES), lambda n: (n + at, 0, 0))
    one = lambda at: pl.BlockSpec((1, seq, LANES), lambda n: (n + at, 0, 0))
    return call(
        functools.partial(attend_back_body, block),
        [
            jax.ShapeDtypeStruct((GROUP * count, seq, LANES), BF16),
            jax.ShapeDtypeStruct((count, seq, LANES), BF16),
            jax.ShapeDtypeStruct((count, seq, LANES), BF16),
        ],
        (count,),
        [group(first), one(first), one(first), group(first)] + [whole((seq, LANES))] * 3,
        [group(0), one(0), one(0)],
        scratch=[pltpu.VMEM((GROUP, seq, LANES), F32)],
        flops=10 * GROUP * count * seq * seq * LANES,
        moved=4_000_000 * count,
    )(q, k, v, do, cos, sa, sb)


def pairs_to(ref, get, heads, first=0):
    for pair in range((heads + 1) // 2):
        left = get(2 * pair)
        lane = lane_of(left.shape[0])
        right = get(2 * pair + 1).astype(F32) if 2 * pair + 1 < heads else 0.0
        both = jnp.where(lane < HEAD, left.astype(F32), right)
        ref[:, first + LANES * pair : first + LANES * (pair + 1)] = both.astype(BF16)


def mid_body(width, place_ref, o_ref, own_ref, other_ref, e_ref, u_ref, wo_ref, xp_ref, gain_ref,
             op_ref, m_ref, b_ref, df_ref):
    flat = jnp.concatenate([o_ref[head] for head in range(HEADS)], axis=1)
    op = mm_nt(flat, u_ref[...]).astype(BF16)
    op_ref[...] = op
    m = xp_ref[...].astype(F32) + mm(op, wo_ref[...])
    m_ref[...] = m
    scale = lax.rsqrt(jnp.sum(m * m, axis=-1, keepdims=True) / width + EPSILON)
    b_ref[...] = (m * scale * gain_ref[1:2]).astype(BF16)
    ct = own_or_other(place_ref, own_ref, other_ref)
    df_ref[...] = mm_tn(ct, e_ref[:width, :]).astype(BF16)


def middle(place, o, own, other, spread, unpack, w_out, xp, gain, block=256):
    width, half = own.shape
    seq, wide = 2 * half, spread.shape[1]
    rows = lambda n: pl.BlockSpec((block, n), lambda i, *_: (i, 0))
    return call(
        functools.partial(mid_body, width),
        [
            jax.ShapeDtypeStruct((seq, wide), BF16),
            jax.ShapeDtypeStruct((seq, wide), F32),
            jax.ShapeDtypeStruct((seq, wide), BF16),
            jax.ShapeDtypeStruct((seq, wide), BF16),
        ],
        (seq // block,),
        [
            pl.BlockSpec((HEADS, block, LANES), lambda i, *_: (0, i, 0)),
            *halves_specs(half, width, block),
            whole(spread.shape),
            whole(unpack.shape),
            whole(w_out.shape),
            rows(wide),
            whole((8, wide)),
        ],
        [rows(wide)] * 4,
        flops=2 * seq * wide * 4 * wide,
        moved=22_000_000,
        prefetch=1,
    )(place, o, own, other, spread, unpack, w_out, xp, gain)


def ffn_body(turn, place_ref, b_ref, df_ref, g_ref, u_ref, d00_ref, d01_ref, d10_ref, d11_ref, *refs):
    out_ref, db_ref, gu_ref, d_send, d_keep, wd_ref = refs[2 * turn :]
    s = pl.program_id(0)
    core = place_ref[0]
    chunk = g_ref.shape[3]

    @pl.when(s == 0)
    def _():
        for part, ref in enumerate((d00_ref, d01_ref, d10_ref, d11_ref)):
            w = ref[:, 0]
            wd_ref[:, chunk * part : chunk * (part + 1)] = w.reshape(-1, chunk)

    b, df = b_ref[...], df_ref[...]
    wg = g_ref[:, 0].reshape(-1, chunk)
    wu = u_ref[:, 0].reshape(-1, chunk)
    wd = wd_ref[pl.ds(pl.multiple_of(chunk * s, chunk), chunk), :]
    gate = mm(b, wg)
    upper = mm(b, wu)
    sig = jax.nn.sigmoid(gate)
    act = gate * sig
    z = (act * upper).astype(BF16)
    dz = mm_nt(df, wd)
    dg = (dz * upper * sig * (1.0 + gate * (1.0 - sig))).astype(BF16)
    du = (dz * act).astype(BF16)

    @pl.when(s == 0)
    def _():
        out_ref[...] = mm(z, wd)
        db_ref[...] = mm_nt(dg, wg) + mm_nt(du, wu)

    @pl.when(s > 0)
    def _():
        out_ref[...] += mm(z, wd)
        db_ref[...] += mm_nt(dg, wg) + mm_nt(du, wu)

    gu_ref[:, :64] = mm_tn(b, dg).astype(BF16).reshape(gu_ref.shape[0], 64, chunk)
    gu_ref[:, 64:] = mm_tn(b, du).astype(BF16).reshape(gu_ref.shape[0], 64, chunk)
    half = df.shape[1] // 2
    for ref, j in ((d_send, 1 - core), (d_keep, core)):
        dwd = mm_tn(z, df_ref[:, pl.ds(pl.multiple_of(half * j, half), half)]).astype(BF16)
        ref[0] = dwd[:, :chunk]
        ref[1] = dwd[:, chunk:]


def feed_forward(place, b, df, packed, turn, before=()):
    seq, wide = b.shape
    blocks = packed.shape[0]
    chunks, chunk = 5, 256
    half_of = lambda place: place[0] if turn else 1 - place[0]
    columns = lambda at: pl.BlockSpec((blocks, 1, 64, chunk), lambda s, place: (0, half_of(place), at + s, 0))
    down = lambda j, q: pl.BlockSpec((blocks // 2, 1, 160, chunk), lambda s, place: (half_of(place), j, 4 + q, 0))
    d_shape = jax.ShapeDtypeStruct((2, 2 * chunks * chunk, chunk), BF16)
    d_spec = pl.BlockSpec((2, chunk, chunk), lambda s, place: (0, half_of(place) * chunks + s, 0))
    return call(
        functools.partial(ffn_body, turn),
        [
            jax.ShapeDtypeStruct((seq, wide), F32),
            jax.ShapeDtypeStruct((seq, wide), F32),
            jax.ShapeDtypeStruct((blocks, 128 * chunks, chunk), BF16),
            d_shape,
            d_shape,
        ],
        (chunks,),
        [whole(b.shape), whole(df.shape), columns(0), columns(chunks)]
        + [down(0, 0), down(0, 1), down(1, 0), down(1, 1)]
        + [pl.BlockSpec(memory_space=pl.ANY)] * len(before),
        [
            whole((seq, wide)),
            whole((seq, wide)),
            pl.BlockSpec((blocks, 128, chunk), lambda s, place: (0, s, 0)),
            d_spec,
            d_spec,
        ],
        scratch=[pltpu.VMEM((chunks * chunk, wide), BF16)],
        flops=18 * seq * wide * chunks * chunk,
        moved=40_000_000,
        prefetch=1,
        alias={9: 3, 10: 4} if before else None,
    )(place, b, df, *([packed] * 6), *before)


def token_block(steps):
    def at(i, place):
        return jnp.where(i < steps // 2, (1 - place[0]) * (steps // 2) + i, place[0] * (steps // 2) + i - steps // 2)

    return at


def token_specs(steps, block, width):
    half = steps // 2
    return [
        pl.BlockSpec((width, block), lambda i, place: (0, jnp.minimum(i, half - 1))),
        pl.BlockSpec((1, width, block), lambda i, place: (place[0], 0, jnp.maximum(i - half, 0))),
    ]


def put_tokens(send_ref, keep_ref, value):
    early = pl.program_id(0) < pl.num_programs(0) // 2

    @pl.when(early)
    def _():
        send_ref[...] = value.astype(send_ref.dtype)

    @pl.when(jnp.logical_not(early))
    def _():
        keep_ref[0] = value.astype(keep_ref.dtype)


def post_body(width, place_ref, m_ref, acc0_ref, acc1_ref, db0_ref, db1_ref, df_ref, gain_ref, e_ref, u_ref,
              sum_ref, put_ref, wo_ref, o_ref, op_ref,
              send_ref, keep_ref, em_ref, do_ref, dwo_send, dwo_keep, dgain_ref, dwo_acc):
    i = pl.program_id(0)
    m, db = m_ref[...], db0_ref[...] + db1_ref[...]
    out = (m + (acc0_ref[...] + acc1_ref[...])).astype(BF16)
    put_tokens(send_ref, keep_ref, mm_nt(e_ref[:width, :], out))
    scale = lax.rsqrt(jnp.sum(m * m, axis=-1, keepdims=True) / width + EPSILON)
    n = m * scale
    c = db * gain_ref[1:2]
    mean = jnp.sum(c * n, axis=-1, keepdims=True) / width
    em = df_ref[...].astype(F32) + scale * (c - n * mean)
    em_ref[...] = em
    da = em.astype(BF16)
    dgain = jnp.sum(db * n, axis=0, keepdims=True)
    dwo = mm_tn(op_ref[...], da)

    @pl.when(i == 0)
    def _():
        dgain_ref[...] = dgain
        dwo_acc[...] = dwo

    @pl.when(i > 0)
    def _():
        dgain_ref[...] += dgain
        dwo_acc[...] += dwo

    @pl.when(i == pl.num_programs(0) - 1)
    def _():
        half = dwo_acc.shape[1] // 2
        for ref, j in ((dwo_send, 1 - place_ref[0]), (dwo_keep, place_ref[0])):
            for q in range(2):
                at = pl.multiple_of(half * j + 256 * q, 256)
                ref[q] = dwo_acc[:, pl.ds(at, 256)].astype(BF16).reshape(ref.shape[1:])

    do = mm(mm_nt(da, wo_ref[...]).astype(BF16), u_ref[...])
    flat = jnp.concatenate([o_ref[head] for head in range(HEADS)], axis=1)
    product = do * flat.astype(F32)
    high = product.astype(BF16)
    low = (product - high.astype(F32)).astype(BF16)
    delta = mm(high, sum_ref[...]) + mm(low, sum_ref[...])
    terms = jnp.concatenate([t.astype(BF16) for t in three_terms(delta)], axis=1)
    do = (do + mm(terms, put_ref[...])).astype(BF16)
    for head in range(HEADS):
        do_ref[head] = do[:, LANES * head : LANES * (head + 1)]


def after(place, m, accs, dbs, df, gain, spread, unpack, delta_sum, delta_put, w_out, o, op, width, block=256):
    seq, wide = m.shape
    blocks = 16
    steps = seq // block
    at = token_block(steps)
    rows = lambda n: pl.BlockSpec((block, n), lambda i, place: (at(i, place), 0))
    heads = pl.BlockSpec((HEADS, block, LANES), lambda i, place: (0, at(i, place), 0))
    dwo_shape = (2, blocks, wide // blocks, 256)
    consts = (gain, spread, unpack, delta_sum, delta_put, w_out)
    return call(
        functools.partial(post_body, width),
        [
            jax.ShapeDtypeStruct((width, seq // 2), BF16),
            jax.ShapeDtypeStruct((2, width, seq // 2), BF16),
            jax.ShapeDtypeStruct((seq, wide), F32),
            jax.ShapeDtypeStruct((HEADS, seq, LANES), BF16),
            jax.ShapeDtypeStruct(dwo_shape, BF16),
            jax.ShapeDtypeStruct(dwo_shape, BF16),
            jax.ShapeDtypeStruct((1, wide), F32),
        ],
        (steps,),
        [rows(wide)] * 6 + [whole(t.shape) for t in consts] + [heads, rows(wide)],
        token_specs(steps, block, width)
        + [rows(wide), heads, whole(dwo_shape), whole(dwo_shape), whole((1, wide))],
        scratch=[pltpu.VMEM((wide, wide), F32)],
        flops=2 * seq * wide * 6 * wide,
        moved=45_000_000,
        prefetch=1,
    )(place, m, *accs, *dbs, df, *consts, o, op)


def weights_body(place_ref, dq_ref, dk_ref, dv_ref, a_ref, w_ref, gain_ref,
                 dgain_ref, flat_ref, send_ref, keep_ref, dw_acc, part_ref):
    i = pl.program_id(0)
    heads = HEADS + KV_HEADS

    pairs_to(flat_ref, lambda h: dq_ref[h] if h < HEADS else dk_ref[h - HEADS], heads)
    pairs_to(flat_ref, lambda h: dv_ref[h], KV_HEADS, heads * HEAD)
    dw = mm_tn(a_ref[...], flat_ref[...])

    @pl.when(i == 0)
    def _():
        dw_acc[...] = dw

    @pl.when(i > 0)
    def _():
        dw_acc[...] += dw

    @pl.when(i == pl.num_programs(0) - 1)
    def _():
        wide = dw_acc.shape[0]
        total = jnp.sum(dw_acc[...] * w_ref[...].astype(F32), axis=-1, keepdims=True)
        column = lambda row: jnp.broadcast_to(row, (LANES, wide)).T
        gain = column(gain_ref[:1])
        attn = jnp.broadcast_to(total, (wide, LANES)) / jnp.where(gain == 0.0, 1.0, gain)
        lane = lane_of(wide)
        gains = jnp.where(lane == 32, attn, 0.0) + jnp.where(lane == 33, column(dgain_ref[...]), 0.0)
        n_q, n_k = HEADS * HEAD // 2, KV_HEADS * HEAD // 2
        for j in range(2):
            part_ref[:, 768:] = gains.astype(BF16)
            part_ref[:, :n_q] = dw_acc[:, n_q * j : n_q * (j + 1)].astype(BF16)
            for part in range(2):
                at, to = 2 * n_q + n_k * (2 * part + j), n_q + n_k * part
                part_ref[:, to : to + n_k] = dw_acc[:, at : at + n_k].astype(BF16)
            for ref, here in ((keep_ref, place_ref[0] == j), (send_ref, place_ref[0] != j)):

                @pl.when(here)
                def _():
                    ref[...] = part_ref[...].reshape(ref.shape)


def projections_back(place, parts, a, w_qkv, gain, dgain_ffn, block=512):
    seq, wide = a.shape
    blocks = 16
    rows = lambda n: pl.BlockSpec((block, n), lambda i, *_: (i, 0))
    heads = lambda t: pl.BlockSpec((t.shape[0], block, LANES), lambda i, *_: (0, i, 0))
    shape = (blocks, wide // blocks, 896)
    return call(
        weights_body,
        [
            jax.ShapeDtypeStruct((seq, QKV_PAD), BF16),
            jax.ShapeDtypeStruct(shape, BF16),
            jax.ShapeDtypeStruct(shape, BF16),
        ],
        (seq // block,),
        [heads(t) for t in parts] + [rows(wide), whole(w_qkv.shape), whole((8, wide)), whole((1, wide))],
        [rows(QKV_PAD), whole(shape), whole(shape)],
        scratch=[pltpu.VMEM((wide, QKV_PAD), F32), pltpu.VMEM((wide, 896), BF16)],
        flops=2 * seq * wide * QKV_PAD,
        moved=20_000_000,
        prefetch=1,
    )(place, *parts, a, w_qkv, gain, dgain_ffn)


def input_body(width, place_ref, flat_ref, w_ref, xp_ref, em_ref, gain_ref, e_ref, send_ref, keep_ref):
    da = mm_nt(flat_ref[...], w_ref[...])
    xp = xp_ref[...].astype(F32)
    scale = lax.rsqrt(jnp.sum(xp * xp, axis=-1, keepdims=True) / width + EPSILON)
    n = xp * scale
    c = da * gain_ref[:1]
    mean = jnp.sum(c * n, axis=-1, keepdims=True) / width
    grad = em_ref[...] + scale * (c - n * mean)
    put_tokens(send_ref, keep_ref, mm_nt(e_ref[:width, :], grad.astype(BF16)))


def input_back(place, flat, w_qkv, xp, em, gain, spread, width, block=256):
    seq, wide = xp.shape
    steps = seq // block
    at = token_block(steps)
    rows = lambda n: pl.BlockSpec((block, n), lambda i, place: (at(i, place), 0))
    return call(
        functools.partial(input_body, width),
        [
            jax.ShapeDtypeStruct((width, seq // 2), BF16),
            jax.ShapeDtypeStruct((2, width, seq // 2), F32),
        ],
        (steps,),
        [rows(QKV_PAD), whole(w_qkv.shape), rows(wide), rows(wide), whole((8, wide)), whole(spread.shape)],
        token_specs(steps, block, width),
        flops=2 * seq * wide * (QKV_PAD + 2 * width),
        moved=20_000_000,
        prefetch=1,
    )(place, flat, w_qkv, xp, em, gain, spread)


def begin_body(reader, n_in, place_ref, *refs):
    ins, outs = refs[:n_in], refs[n_in:]
    _, _, y, x = (place_ref[n] for n in range(4))
    for side in range(2):
        mine = y if side else x
        for other in range(2):
            for ref, bit in ((outs[2 * side], 1 - mine), (outs[2 * side + 1], mine)):
                block = 2 * bit + other if side else 2 * other + bit
                for row, keep, got in reader(ins, side, block):
                    ref[other, row : row + keep.shape[0]] = add(keep, got)


def begin(place, arrays, reader, rows, count=4):
    n = arrays[0].shape[-1]

    def spec(t):
        lead = t.shape[:-3]
        return pl.BlockSpec((*lead, 4, *t.shape[-2:]), lambda i, place: (0,) * len(lead) + (i, 0, 0))

    shape = jax.ShapeDtypeStruct((2 * count, rows, n), BF16)
    return call(
        functools.partial(begin_body, reader, len(arrays)),
        [shape] * 4,
        (count,),
        [spec(t) for t in arrays],
        [pl.BlockSpec((2, rows, n), lambda i, place: (i, 0, 0))] * 4,
        flops=1,
        moved=16 * count * rows * n * 6,
        prefetch=1,
        vmem=VMEM_SMALL,
    )(place, *arrays)


def turn_body(place_ref, *refs):
    y, x = place_ref[2], place_ref[3]
    for side in range(2):
        keep, got = refs[2 * side : 2 * side + 2]
        mine = x if side else y
        for ref, bit in ((refs[4 + 2 * side], 1 - mine), (refs[5 + 2 * side], mine)):
            ref[0] = add(keep[bit], got[bit])


def turn(place, keeps, gots):
    blocks, rows, n = keeps[0].shape
    shape = jax.ShapeDtypeStruct((blocks // 2, rows, n), BF16)
    return call(
        turn_body,
        [shape] * 4,
        (blocks // 2,),
        [pl.BlockSpec((2, rows, n), lambda i, place: (i, 0, 0))] * 4,
        [pl.BlockSpec((1, rows, n), lambda i, place: (i, 0, 0))] * 4,
        flops=1,
        moved=blocks * rows * n * 12,
        prefetch=1,
        vmem=VMEM_SMALL,
    )(place, keeps[0], gots[0], keeps[1], gots[1])


def climb_body(place_ref, a_keep, a_got, b_keep, b_got, total_ref, *sent):
    for step in range(4):
        block = lax.rem(place_ref[1] + step, 4)
        for side, (keep, got) in enumerate(((a_keep, a_got), (b_keep, b_got))):
            value = keep[block].astype(F32) + got[block].astype(F32)
            if step:
                sent[step - 1][side] = value.astype(BF16)
            else:
                total_ref[side] = value


def climb(place, keeps, gots):
    _, rows, n = keeps[0].shape
    return call(
        climb_body,
        [jax.ShapeDtypeStruct((2, rows, n), F32)] + [jax.ShapeDtypeStruct((2, rows, n), BF16)] * 3,
        (1,),
        [whole(keeps[0].shape)] * 4,
        [whole((2, rows, n))] * 4,
        flops=1,
        moved=rows * n * 50,
        prefetch=1,
        vmem=VMEM_SMALL,
    )(place, keeps[0], gots[0], keeps[1], gots[1])


def unpack_matrix(width, blocks, wide):
    per, step = width // blocks, wide // blocks
    col = jnp.arange(WIDE_HEADS, dtype=jnp.int32)
    feature = col // LANES * HEAD + col % LANES
    place = jnp.where(col % LANES < HEAD, feature // per * step + feature % per, -1)
    return (jnp.arange(wide, dtype=jnp.int32)[:, None] == place[None, :]).astype(BF16)


def delta_matrices():
    row = jnp.arange(WIDE_HEADS, dtype=jnp.int32)
    lane = jnp.arange(LANES, dtype=jnp.int32)
    total = (row[:, None] // LANES == lane[None, :]).astype(BF16)
    term = jnp.arange(3 * LANES, dtype=jnp.int32)
    to = jnp.where(term % LANES < HEADS, term % LANES * LANES + HEAD + term // LANES, -1)
    return total, (to[:, None] == row[None, :]).astype(BF16)


def spread_matrix(width, blocks, wide):
    row = jnp.arange(wide, dtype=jnp.int32)
    per, step = width // blocks, wide // blocks
    place = (row // per) * step + row % per
    hit = (place[:, None] == jnp.arange(wide, dtype=jnp.int32)[None, :]) & (row < width)[:, None]
    return hit.astype(BF16)


def tables(positions, segments):
    lane = jnp.arange(LANES, dtype=jnp.int32)
    frequency = 10000.0 ** (-((lane % 32).astype(F32) * 2.0 / HEAD))
    angles = positions.astype(F32)[:, None] * frequency[None, :]
    cos, sin = jnp.cos(angles), jnp.sin(angles)
    high = (lane % HEAD >= 32)[None, :]
    sa = jnp.where(high, sin, 0.0)
    sb = jnp.where(high, 0.0, -sin)
    doc = (lane - HEAD)[None, :]
    mine = segments[:, None] == doc
    in_doc = (doc >= 0) & (doc < DOCS)
    aq = jnp.where(mine & in_doc, MASKED, 0.0)
    ak = jnp.where(in_doc & ~mine, 1.0, 0.0)
    ak = jnp.where((doc >= DOCS) & (doc < DOCS + 3), -1.0, ak)
    return cos, sa, sb, aq, ak


def pad_rows(w, blocks, step=64):
    per = w.shape[0] // blocks
    return jnp.pad(w.reshape(blocks, per, w.shape[1]), ((0, 0), (0, step - per), (0, 0)))


def pad_cols(w, blocks, step=64):
    per = w.shape[1] // blocks
    w = jnp.pad(w.reshape(w.shape[0], blocks, per), ((0, 0), (0, 0), (0, step - per)))
    return w.reshape(w.shape[0], blocks * step)


def cut_rows(w, per):
    return w[:, :per].reshape(w.shape[0] * per, w.shape[2])


def cut_cols(w, per, step=64):
    blocks = w.shape[1] // step
    return w.reshape(w.shape[0], blocks, step)[:, :, :per].reshape(w.shape[0], blocks * per)


def chunked(w, chunk=256):
    blocks, rows, cols = w.shape
    w = w.reshape(blocks, rows, cols // chunk, chunk).transpose(0, 2, 1, 3)
    return w.reshape(blocks, cols // chunk * rows, chunk)


def joined(w, rows):
    blocks, total, chunk = w.shape
    w = w.reshape(blocks, total // rows, rows, chunk).transpose(0, 2, 1, 3)
    return w.reshape(blocks, rows, total // rows * chunk)


def pack_half(w_gate, w_up, w_down, blocks, groups):
    down = pad_cols(w_down, groups)
    down = down.reshape(blocks, w_down.shape[0] // blocks, down.shape[1])
    return jnp.concatenate(
        [
            chunked(pad_rows(w_gate, blocks)),
            chunked(pad_rows(w_up, blocks)),
            chunked(down),
        ],
        axis=1,
    )


def add(left, right):
    return (left.astype(F32) + right.astype(F32)).astype(BF16)


def swap(x):
    return lax.ppermute(x, "ctx", [(0, 1), (1, 0)])


def across(x, bit, count):
    return lax.ppermute(x, "dp", [(i, i ^ (1 << bit)) for i in range(count)])


def pick(x, index, axis=0):
    return lax.dynamic_index_in_dim(x, index, axis, keepdims=False)


def tie(value, *others):
    return lax.optimization_barrier((value, *others))[0]


def along_z(x, step, count):
    return lax.ppermute(x, "dp", [(i, (i + 4 * step) % count) for i in range(count)])


def gather_pieces(shard, count):
    stack = jnp.stack([shard] + [along_z(shard, k, count) for k in (1, 2, 3)])
    half = shard.shape[0] // 2
    first, second = stack[:, :half], stack[:, half:]
    first = jnp.concatenate([first, across(first, 0, count)])
    second = jnp.concatenate([second, across(second, 1, count)])
    pieces = (first, across(first, 1, count), second, across(second, 0, count))
    return pieces + tuple(swap(piece) for piece in pieces)


class RowSum:
    def __init__(self, place, count, arrays, reader, rows):
        self.place, self.count = place, count
        a_sent, a_kept, b_sent, b_kept = begin(place, arrays, reader, rows)
        self.sent, self.kept = [a_sent, b_sent], [a_kept, b_kept]

    def move(self):
        self.got = [across(self.sent[0], 0, self.count), across(self.sent[1], 1, self.count)]

    def wait(self, other):
        self.got = list(lax.optimization_barrier((*self.got, other))[:-1])

    def turn(self, other):
        self.wait(other)
        a_sent, a_kept, b_sent, b_kept = turn(self.place, self.kept, self.got)
        self.sent, self.kept = [a_sent, b_sent], [a_kept, b_kept]

    def move_again(self):
        self.got = [across(self.sent[0], 1, self.count), across(self.sent[1], 0, self.count)]

    def climb(self, other):
        self.wait(other)
        self.kept, *self.sent = climb(self.place, self.kept, self.got)

    def move_up(self):
        self.got = [along_z(self.sent[k - 1], k, self.count) for k in (1, 2, 3)]

    def total(self):
        total = self.kept
        for got in self.got:
            total = total + got.astype(F32)
        return total


def read_rows(ins, side, block):
    half = ins[0].shape[1] // 2
    rows = slice(half * side, half * (side + 1))
    return [(0, ins[0][block, rows], ins[1][block, rows])]


def read_quarters(ins, side, block):
    first = ins[0].shape[2]
    return [(0, ins[0][side, block], ins[1][side, block]), (first, ins[2][side, block], ins[3][side, block])]


def put_other(both, got, core):
    return lax.dynamic_update_slice(both, got[None], (1 - core, 0, 0))


def shards_of_two(inputs, segment_ids, positions, w_query, w_key, w_value, w_out, w_gate, w_up,
                  w_down, gain_attn, gain_ffn, cotangent):
    count = lax.axis_size("dp")
    me, core = lax.axis_index("dp"), lax.axis_index("ctx")
    place = (core, me // 4, (me >> 1) & 1, me & 1)
    place_of = jnp.stack(place).astype(jnp.int32)
    per = gain_attn.shape[0]
    width = per * count
    groups = w_out.shape[1] // per
    hidden = w_down.shape[0]
    n_q, n_k = w_query.shape[1], w_key.shape[1]
    n_qkv = n_q + 2 * n_k

    packed = pack_half(w_gate, w_up, w_down, 1, groups)[0]
    packed = lax.all_gather(packed, ("dp", "ctx"), axis=0, tiled=False)
    packed = packed.reshape((count, 2) + packed.shape[1:])

    shard = jnp.concatenate(
        [w_query, w_key, w_value, gain_attn[:, None], gain_ffn[:, None]], axis=1
    )
    shard = jnp.pad(shard, ((0, 0), (0, 896 - n_qkv - 2)))
    shard = jnp.concatenate([shard, pad_cols(w_out, groups)], axis=1)
    pieces = gather_pieces(jnp.pad(shard, ((0, 64 - per), (0, 0))), count)

    def halves(x):
        x = jnp.swapaxes(x[:, 0], 1, 2)
        return pick(x, core), swap(pick(x, 1 - core))

    wide = count * 64
    spread, unpack = spread_matrix(width, count, wide), unpack_matrix(width, count, wide)
    delta_sum, delta_put = delta_matrices()
    cos, sa, sb, aq, ak = tables(pick(positions[:, 0], core), pick(segment_ids[:, 0], core))
    xp, a, q, k, v, w_qkv, w_o, gains = pre_attention(
        place_of, *halves(inputs), spread, pieces, cos, sa, sb, aq, ak
    )
    o, q2 = attend(q, k, v)
    op, m, b, df = middle(place_of, o, *halves(cotangent), spread, unpack, w_o, xp, gains)

    acc0, db0, gu_send, d_send, d_keep = feed_forward(place_of, b, df, packed, 0)
    gu_got = swap(gu_send)
    acc1, db1, gu_keep, d_send, d_keep = feed_forward(
        place_of, tie(b, gu_send), df, packed, 1, (d_send, d_keep)
    )
    one = RowSum(place_of, count, (gu_keep, tie(gu_got, acc1)), read_rows, 320)
    one.move()
    blocked = lambda t: t.reshape(2, count, hidden, 256)
    d_got = swap(d_send)
    m = tie(m, *one.sent, d_send)
    out_send, outs, em, do, o_send, o_keep, dgf = after(
        place_of, m, (acc0, acc1), (db0, db1), df, gains, spread, unpack, delta_sum, delta_put, w_o, o, op, width
    )
    o_got = swap(o_send)
    one.turn(em)
    one.move_again()
    two = RowSum(
        place_of, count, (blocked(d_keep), blocked(tie(d_got, em)), o_keep, o_got), read_quarters, 224
    )
    two.move()
    do = tie(do, *one.sent, *two.sent)
    parts = attend_back(q2, k, v, do, cos, sa, sb, 0, KV_HEADS)
    outs = put_other(outs, tie(swap(out_send), parts[0]), core)
    one.climb(parts[0])
    one.move_up()
    two.turn(parts[0])
    two.move_again()
    a = tie(a, *one.sent, *two.sent)
    flat, p_send, p_keep = projections_back(place_of, parts, a, w_qkv, gains, dgf)
    p_got = swap(p_send)
    two.climb(flat)
    two.move_up()
    three = RowSum(place_of, count, (p_keep, p_got), read_rows, 32)
    three.move()
    flat = tie(flat, *two.sent, *three.sent)
    gi_send, gis = input_back(place_of, flat, w_qkv, xp, em, gains, spread, width)
    gi_got = swap(gi_send)
    three.turn(gis)
    three.move_again()
    gis = put_other(gis, gi_got.astype(F32), core)
    three.climb(gis)
    three.move_up()

    first, second, third = one.total(), two.total(), three.total()
    third = third.reshape(64, 896)[:per]
    gu = first.reshape(5, 2, 64, 256)
    wide_of = lambda t: t.transpose(1, 0, 2).reshape(t.shape[1], -1)
    tokens = lambda t: jnp.swapaxes(t, 1, 2)[:, None]
    return (
        tokens(outs),
        tokens(gis),
        third[:, :n_q],
        third[:, n_q : n_q + n_k],
        third[:, n_q + n_k : n_qkv],
        cut_cols(wide_of(second[:, 160:])[:per], per),
        wide_of(gu[:, 0])[:per],
        wide_of(gu[:, 1])[:per],
        cut_cols(wide_of(second[:, :160]), per),
        third[:, n_qkv],
        third[:, n_qkv + 1],
    )


def shards_of_many(inputs, segment_ids, positions, w_query, w_key, w_value, w_out, w_gate, w_up,
                   w_down, gain_attn, gain_ffn, cotangent):
    count, cores = lax.axis_size("dp"), lax.axis_size("ctx")
    core = lax.axis_index("ctx")
    share = cores // MICRO
    per = gain_attn.shape[0]
    width = per * count

    def gathered(w):
        return lax.all_gather(lax.all_gather(w, "dp", axis=0, tiled=True), "ctx", axis=1, tiled=True)

    full = [gathered(w) for w in (w_query, w_key, w_value, w_out, w_gate, w_up, w_down)]
    gain_pair = lax.all_gather(jnp.stack([gain_attn, gain_ffn]), "dp", axis=1, tiled=True)
    gains = jnp.pad(pad_cols(gain_pair.astype(F32), count), ((0, 6), (0, 0)))
    w_qkv = pad_rows(jnp.concatenate(full[:3], axis=1), count).reshape(count * 64, QKV)
    w_qkv = jnp.pad(w_qkv, ((0, 0), (0, QKV_PAD - QKV)))
    w_o, w_g, w_u, w_d = full[3:]
    half = lambda w, j: w[:, w.shape[1] // 2 * j : w.shape[1] // 2 * (j + 1)]
    packed = jnp.stack(
        [pack_half(half(w_g, j), half(w_u, j), half(w_d, j), count, count // 2) for j in range(2)],
        axis=1,
    )
    which = core // share

    def sequence(x):
        whole_one = pick(lax.all_gather(x[:, 0], "ctx", axis=1, tiled=True), which).T
        return whole_one[:, : whole_one.shape[1] // 2], whole_one[:, whole_one.shape[1] // 2 :]

    place = jnp.zeros((4,), jnp.int32)
    wide = count * 64
    w_o = pad_rows(pad_cols(w_o, count), count).reshape(wide, wide)
    spread, unpack = spread_matrix(width, count, wide), unpack_matrix(width, count, wide)
    delta_sum, delta_put = delta_matrices()
    cos, sa, sb, aq, ak = tables(pick(positions[:, 0], which), pick(segment_ids[:, 0], which))
    xp, a, q, k, v, w_qkv, w_o, gains = pre_attention(
        place, *sequence(inputs), spread, (w_qkv, w_o, gains), cos, sa, sb, aq, ak
    )
    o, q2 = attend(q, k, v)
    op, m, b, df = middle(place, o, *sequence(cotangent), spread, unpack, w_o, xp, gains)
    acc0, db0, gu_send, d_send, d_keep = feed_forward(place, b, df, packed, 0)
    acc1, db1, gu_keep, d_send, d_keep = feed_forward(place, b, df, packed, 1, (d_send, d_keep))
    out_send, outs, em, do, o_send, o_keep, dgf = after(
        place, m, (acc0, acc1), (db0, db1), df, gains, spread, unpack, delta_sum, delta_put, w_o, o, op, width
    )
    parts = attend_back(q2, k, v, do, cos, sa, sb, 0, KV_HEADS)
    flat, p_send, p_keep = projections_back(place, parts, a, w_qkv, gains, dgf)
    gi_send, gis = input_back(place, flat, w_qkv, xp, em, gains, spread, width)

    parts = [cut_rows(p, per) for p in (p_keep, p_send)]
    n_q, n_k = HEADS * HEAD // 2, KV_HEADS * HEAD // 2
    both = lambda at, n: jnp.concatenate([p[:, at : at + n] for p in parts], axis=1)
    side = lambda t: jnp.concatenate([t[0], t[1]], axis=-1)

    def wide_of(index):
        every = []
        for t in (gu_keep, gu_send):
            t = t.reshape(count, 5, 2, 64, 256)[:, :, index]
            every.append(cut_rows(t.transpose(0, 2, 1, 3).reshape(count, 64, -1), per))
        return jnp.concatenate(every, axis=1)

    grads = [
        both(0, n_q),
        both(n_q * 1, n_k),
        both(n_q + n_k, n_k),
        cut_cols(cut_rows(jnp.concatenate([side(o_keep), side(o_send)], axis=-1), per), per),
        wide_of(0),
        wide_of(1),
        cut_cols(
            jnp.concatenate([side(d_keep), side(d_send)], axis=-1),
            per,
        ),
    ]

    def summed(g):
        g = lax.psum_scatter(g * (1.0 / share), "dp", scatter_dimension=0, tiled=True)
        return lax.psum_scatter(g, "ctx", scatter_dimension=1, tiled=True).astype(F32)

    sums = [summed(g.astype(BF16)) for g in grads]
    dgain = parts[0][:, 2 * n_k + n_q : 2 * n_k + n_q + 2].astype(F32).T * (1.0 / share)
    dgain = lax.psum_scatter(lax.psum(dgain, "ctx"), "dp", scatter_dimension=1, tiled=True)

    def tokens(seq):
        rows = seq.shape[0] // cores
        every = lax.all_gather(seq, "ctx", axis=0, tiled=False)
        return lax.dynamic_slice_in_dim(every[::share], core * rows, rows, axis=1)[:, None]

    out = jnp.concatenate([outs[0], out_send], axis=1).T
    gi = jnp.concatenate([gis[0], gi_send.astype(F32)], axis=1).T
    return (tokens(out), tokens(gi), *sums, dgain[0], dgain[1])


def solution(mesh):
    two = mesh.shape["ctx"] == MICRO and mesh.shape["dp"] == 16
    matrices = (P("dp", "ctx"),) * 7 + (P("dp"), P("dp"))
    tokens = P(None, "dp", "ctx", None)
    return jax.shard_map(
        shards_of_two if two else shards_of_many,
        mesh=mesh,
        in_specs=(tokens, P(None, "dp", None), P(None, "dp", None)) + matrices + (tokens,),
        out_specs=(tokens, tokens) + matrices,
        check_vma=False,
    )
```

```python
import functools

import jax
import jax.numpy as jnp
from jax import lax
from jax.experimental import pallas as pl
from jax.experimental.pallas import tpu as pltpu
from jax.sharding import PartitionSpec as P

HEADS = 15
KV_HEADS = 5
HEAD = 64
MICRO = 2
GROUP = 3
DOCS = 4

EPSILON = 1e-05
MASKED = -1e30
LANES = 128
QKV = (HEADS + 2 * KV_HEADS) * HEAD
QKV_PAD = 1664
VMEM_LIMIT = 48 * 1024 * 1024
PACK = 1408
VMEM_SMALL = 24 * 1024 * 1024
WIDE_HEADS = HEADS * LANES
F32 = jnp.float32
BF16 = jnp.bfloat16


def up(value, step):
    return -(-value // step) * step


def mm(left, right):
    return lax.dot_general(left, right, (((1,), (0,)), ((), ())), preferred_element_type=F32)


def mm_nt(left, right):
    return lax.dot_general(left, right, (((1,), (1,)), ((), ())), preferred_element_type=F32)


def mm_tn(left, right):
    return lax.dot_general(left, right, (((0,), (0,)), ((), ())), preferred_element_type=F32)


def call(body, out_shape, grid, in_specs, out_specs, scratch=(), flops=0, moved=0, prefetch=0, alias=None,
         vmem=VMEM_LIMIT):
    return pl.pallas_call(
        body,
        out_shape=out_shape,
        grid_spec=pltpu.PrefetchScalarGridSpec(
            num_scalar_prefetch=prefetch,
            grid=grid,
            in_specs=in_specs,
            out_specs=out_specs,
            scratch_shapes=scratch,
        ),
        input_output_aliases=alias or {},
        compiler_params=pltpu.CompilerParams(vmem_limit_bytes=vmem),
        cost_estimate=pl.CostEstimate(flops=flops, bytes_accessed=moved, transcendentals=0),
    )


def whole(shape):
    return pl.BlockSpec(shape, lambda *_: (0,) * len(shape))


def lane_of(rows):
    return lax.broadcasted_iota(jnp.int32, (rows, LANES), 1)


def three_terms(column):
    high = column.astype(BF16).astype(F32)
    rest = column - high
    mid = rest.astype(BF16).astype(F32)
    return high, mid, rest - mid


def put_terms(base, column, lane, first):
    high, mid, low = three_terms(column)
    base = jnp.where(lane == first, high, base)
    base = jnp.where(lane == first + 1, mid, base)
    return jnp.where(lane == first + 2, low, base)


def build_weights(place_ref, piece_refs, stage_ref, w_ref, wo_ref):
    core, z, y, x = (place_ref[n] for n in range(4))
    for swapped in range(2):
        near_a, far_a, near_b, far_b = piece_refs[4 * swapped : 4 * swapped + 4]
        to = jnp.bitwise_xor(core, swapped)
        for dy in range(2):
            for dx in range(2):
                for k in range(4):
                    block = lax.rem(z + 4 - k, 4) * 4 + (y ^ dy) * 2 + (x ^ dx)
                    row = pl.multiple_of(block * 64, 64)
                    stage_ref[to, pl.ds(row, 32), :] = (far_a if dy else near_a)[4 * dx + k]
                    stage_ref[to, pl.ds(row + 32, 32), :] = (far_b if dx else near_b)[4 * dy + k]
    n_q, n_k = HEADS * HEAD // 2, KV_HEADS * HEAD // 2
    for j in range(2):
        w_ref[:, n_q * j : n_q * (j + 1)] = stage_ref[j, :, :n_q]
        for part in range(2):
            to, at = 2 * n_q + n_k * (2 * part + j), n_q + n_k * part
            w_ref[:, to : to + n_k] = stage_ref[j, :, at : at + n_k]
        half = wo_ref.shape[1] // 2
        wo_ref[:, half * j : half * (j + 1)] = stage_ref[j, :, PACK - half :]
    w_ref[:, QKV:] = jnp.zeros((w_ref.shape[0], QKV_PAD - QKV), BF16)


def projections(xp, scale, w_ref, gain_ref, cos_ref, sa_ref, sb_ref, aq_ref, ak_ref,
                xp_ref, a_ref, q_ref, k_ref, v_ref):
    a = (xp * scale * gain_ref[:1]).astype(BF16)
    xp_ref[...] = xp.astype(BF16)
    a_ref[...] = a
    t = mm(a, w_ref[...])
    lane = lane_of(t.shape[0])
    low = lane < HEAD
    cos, sa, sb, aq, ak = cos_ref[...], sa_ref[...], sb_ref[...], aq_ref[...], ak_ref[...]
    for pair in range((HEADS + KV_HEADS) // 2):
        tt = t[:, LANES * pair : LANES * (pair + 1)]
        rot = tt * cos + pltpu.roll(tt, 32, 1) * sa + pltpu.roll(tt, 96, 1) * sb
        for half in range(2):
            head = 2 * pair + half
            val = rot if half == 0 else pltpu.roll(rot, 64, 1)
            if head < HEADS:
                q_ref[head] = jnp.where(low, val * HEAD ** -0.5, aq).astype(BF16)
            else:
                k_ref[head - HEADS] = jnp.where(low, val, ak).astype(BF16)
    av = jnp.where(lane < HEAD + 3, -1.0, 0.0)
    for head in range(KV_HEADS):
        first = (HEADS + KV_HEADS) * HEAD + LANES * (head // 2)
        tt = t[:, first : first + LANES]
        val = tt if head % 2 == 0 else pltpu.roll(tt, 64, 1)
        v_ref[head] = jnp.where(low, val, av).astype(BF16)


def own_or_other(place_ref, own_ref, other_ref):
    first = pl.program_id(0) < pl.num_programs(0) // 2
    mine = first == (place_ref[0] == 0)
    return jnp.where(mine, own_ref[...], other_ref[...])


def pre_body(width, place_ref, own_ref, other_ref, e_ref, *refs):
    pieces, refs = refs[:8], refs[8:]
    *rest, w_ref, wo_ref, gain_ref, stage_ref = refs

    @pl.when(pl.program_id(0) == 0)
    def _():
        build_weights(place_ref, pieces, stage_ref, w_ref, wo_ref)
        gain_ref[...] = stage_ref[0, :, 768:896].astype(F32).T[32:40]

    xp = mm_tn(own_or_other(place_ref, own_ref, other_ref), e_ref[:width, :])
    scale = lax.rsqrt(jnp.sum(xp * xp, axis=-1, keepdims=True) / width + EPSILON)
    projections(xp, scale, w_ref, gain_ref, *rest)


def halves_specs(rows, width, block):
    steps = rows // block
    return [pl.BlockSpec((width, block), lambda i, *_: (0, i % steps))] * 2


def pre_attention(place, own, other, spread, pieces, cos, sa, sb, aq, ak, block=256):
    width, half = own.shape
    seq, wide = 2 * half, spread.shape[1]
    rows = lambda n: pl.BlockSpec((block, n), lambda i, *_: (i, 0))
    heads = lambda n: pl.BlockSpec((n, block, LANES), lambda i, *_: (0, i, 0))
    return call(
        functools.partial(pre_body, width),
        [
            jax.ShapeDtypeStruct((seq, wide), BF16),
            jax.ShapeDtypeStruct((seq, wide), BF16),
            jax.ShapeDtypeStruct((HEADS, seq, LANES), BF16),
            jax.ShapeDtypeStruct((KV_HEADS, seq, LANES), BF16),
            jax.ShapeDtypeStruct((KV_HEADS, seq, LANES), BF16),
            jax.ShapeDtypeStruct((wide, QKV_PAD), BF16),
            jax.ShapeDtypeStruct((wide, wide), BF16),
            jax.ShapeDtypeStruct((8, wide), F32),
        ],
        (seq // block,),
        halves_specs(half, width, block)
        + [whole(spread.shape)]
        + [whole(w.shape) for w in pieces]
        + [rows(LANES)] * 5,
        [rows(wide), rows(wide), heads(HEADS), heads(KV_HEADS), heads(KV_HEADS)]
        + [whole((wide, QKV_PAD)), whole((wide, wide)), whole((8, wide))],
        scratch=[pltpu.VMEM((2, wide, PACK), BF16)],
        flops=2 * seq * wide * (width + QKV_PAD),
        moved=20_000_000,
        prefetch=1,
    )(place, own, other, spread, *pieces, cos, sa, sb, aq, ak)


def attend_body(block, q_ref, k_ref, v_ref, o_ref, q2_ref):
    seq = k_ref.shape[1]
    rows = GROUP * block
    below = lax.broadcasted_iota(jnp.int32, (block, block), 0) >= lax.broadcasted_iota(
        jnp.int32, (block, block), 1
    )
    below = jnp.concatenate([below.astype(F32)] * GROUP, axis=0) > 0.5
    lane = lane_of(rows)
    for i in range(seq // block):
        span = slice(block * i, block * (i + 1))
        q = q_ref[:, span, :].reshape(rows, LANES)
        s_in = jnp.where(below, mm_nt(q, k_ref[0, span, :]), MASKED)
        top = jnp.max(s_in, axis=-1, keepdims=True)
        if i:
            s_left = mm_nt(q, k_ref[0, : block * i, :])
            top = jnp.maximum(top, jnp.max(s_left, axis=-1, keepdims=True))
        ext = mm(jnp.exp(s_in - top).astype(BF16), v_ref[0, span, :])
        if i:
            ext = ext + mm(jnp.exp(s_left - top).astype(BF16), v_ref[0, : block * i, :])
        total = -ext[:, HEAD : HEAD + 1]
        o = ext / total
        o = jnp.where(lane < HEAD, o, pltpu.roll(o, 64, 1))
        o_ref[:, span, :] = o.reshape(GROUP, block, LANES).astype(BF16)
        q2 = put_terms(q.astype(F32), top + jnp.log(total), lane, HEAD + DOCS)
        q2_ref[:, span, :] = q2.reshape(GROUP, block, LANES).astype(BF16)


def attend(q, k, v, block=256):
    seq = q.shape[1]
    group = pl.BlockSpec((GROUP, seq, LANES), lambda n: (n, 0, 0))
    one = pl.BlockSpec((1, seq, LANES), lambda n: (n, 0, 0))
    shape = jax.ShapeDtypeStruct(q.shape, BF16)
    return call(
        functools.partial(attend_body, block),
        [shape, shape],
        (KV_HEADS,),
        [group, one, one],
        [group, group],
        flops=4 * HEADS * seq * seq * LANES,
        moved=15_000_000,
    )(q, k, v)


def attend_back_body(block, q_ref, k_ref, v_ref, do_ref, cos_ref, sa_ref, sb_ref,
                     dq_ref, dk_ref, dv_ref, acc_ref):
    seq = k_ref.shape[1]
    above = lax.broadcasted_iota(jnp.int32, (block, block), 0) <= lax.broadcasted_iota(
        jnp.int32, (block, block), 1
    )
    lane = lane_of(seq)

    def unrotate(t, span):
        rows = span.stop - span.start
        rot = (
            t * cos_ref[span, :]
            - pltpu.roll(t, 32, 1) * sa_ref[span, :]
            - pltpu.roll(t, 96, 1) * sb_ref[span, :]
        )
        return twice(rot, rows)

    def twice(t, rows):
        return jnp.where(lane[:rows] < HEAD, t, pltpu.roll(t, 64, 1)).astype(BF16)

    for j in range(seq // block):
        span = slice(block * j, block * (j + 1))
        k, v = k_ref[0, span, :], v_ref[0, span, :]
        dk = jnp.zeros((block, LANES), F32)
        dv = jnp.zeros((block, LANES), F32)
        for g in range(GROUP):
            q, do = q_ref[g, block * j :, :], do_ref[g, block * j :, :]
            p = jnp.exp(mm_nt(k, q))
            inner = jnp.where(above, p[:, :block], 0.0)
            p = inner if p.shape[1] == block else jnp.concatenate([inner, p[:, block:]], axis=1)
            ds = (p * mm_nt(v, do)).astype(BF16)
            dv = dv + mm(p.astype(BF16), do)
            dk = dk + mm(ds, q)
            dq = mm_tn(ds, k)
            if j == 0:
                acc_ref[g] = dq
            else:
                acc_ref[g, block * j :, :] += dq
        dk_ref[0, span, :] = unrotate(dk, span)
        dv_ref[0, span, :] = twice(dv, block)
    for g in range(GROUP):
        dq_ref[g] = unrotate(acc_ref[g] * HEAD ** -0.5, slice(0, seq))


def attend_back(q, k, v, do, cos, sa, sb, first, count, block=256):
    seq = q.shape[1]
    group = lambda at: pl.BlockSpec((GROUP, seq, LANES), lambda n: (n + at, 0, 0))
    one = lambda at: pl.BlockSpec((1, seq, LANES), lambda n: (n + at, 0, 0))
    return call(
        functools.partial(attend_back_body, block),
        [
            jax.ShapeDtypeStruct((GROUP * count, seq, LANES), BF16),
            jax.ShapeDtypeStruct((count, seq, LANES), BF16),
            jax.ShapeDtypeStruct((count, seq, LANES), BF16),
        ],
        (count,),
        [group(first), one(first), one(first), group(first)] + [whole((seq, LANES))] * 3,
        [group(0), one(0), one(0)],
        scratch=[pltpu.VMEM((GROUP, seq, LANES), F32)],
        flops=10 * GROUP * count * seq * seq * LANES,
        moved=4_000_000 * count,
    )(q, k, v, do, cos, sa, sb)


def pairs_to(ref, get, heads, first=0):
    for pair in range((heads + 1) // 2):
        left = get(2 * pair)
        lane = lane_of(left.shape[0])
        right = get(2 * pair + 1).astype(F32) if 2 * pair + 1 < heads else 0.0
        both = jnp.where(lane < HEAD, left.astype(F32), right)
        ref[:, first + LANES * pair : first + LANES * (pair + 1)] = both.astype(BF16)


def mid_body(width, place_ref, o_ref, own_ref, other_ref, e_ref, u_ref, wo_ref, xp_ref, gain_ref,
             op_ref, m_ref, b_ref, df_ref):
    flat = jnp.concatenate([o_ref[head] for head in range(HEADS)], axis=1)
    op = mm_nt(flat, u_ref[...]).astype(BF16)
    op_ref[...] = op
    m = xp_ref[...].astype(F32) + mm(op, wo_ref[...])
    m_ref[...] = m
    scale = lax.rsqrt(jnp.sum(m * m, axis=-1, keepdims=True) / width + EPSILON)
    b_ref[...] = (m * scale * gain_ref[1:2]).astype(BF16)
    ct = own_or_other(place_ref, own_ref, other_ref)
    df_ref[...] = mm_tn(ct, e_ref[:width, :]).astype(BF16)


def middle(place, o, own, other, spread, unpack, w_out, xp, gain, block=256):
    width, half = own.shape
    seq, wide = 2 * half, spread.shape[1]
    rows = lambda n: pl.BlockSpec((block, n), lambda i, *_: (i, 0))
    return call(
        functools.partial(mid_body, width),
        [
            jax.ShapeDtypeStruct((seq, wide), BF16),
            jax.ShapeDtypeStruct((seq, wide), F32),
            jax.ShapeDtypeStruct((seq, wide), BF16),
            jax.ShapeDtypeStruct((seq, wide), BF16),
        ],
        (seq // block,),
        [
            pl.BlockSpec((HEADS, block, LANES), lambda i, *_: (0, i, 0)),
            *halves_specs(half, width, block),
            whole(spread.shape),
            whole(unpack.shape),
            whole(w_out.shape),
            rows(wide),
            whole((8, wide)),
        ],
        [rows(wide)] * 4,
        flops=2 * seq * wide * 4 * wide,
        moved=22_000_000,
        prefetch=1,
    )(place, o, own, other, spread, unpack, w_out, xp, gain)


def ffn_body(turn, place_ref, b_ref, df_ref, *refs):
    near_g, far_g, near_u, far_u = refs[:4]
    downs, refs = (refs[4:8], refs[8:12]), refs[12:]
    out_ref, db_ref, gu_ref, d_send, d_keep, wg_ref, wu_ref, wd_ref = refs[2 * turn :]
    s = pl.program_id(0)
    core, z_me, y_me, x_me = (place_ref[n] for n in range(4))
    chunk = wg_ref.shape[1]
    half = core if turn else 1 - core

    @pl.when(s == 0)
    def _():
        rows = downs[0][0].shape[2]
        for swapped in range(2):
            for k in range(4):
                z = lax.rem(z_me + 4 - k, 4)

                @pl.when(z // 2 == half)
                def _():
                    ref = downs[swapped][k]
                    for q in range(2):
                        col = pl.multiple_of(2 * chunk * (core ^ swapped) + chunk * q, chunk)
                        for dy in range(2):
                            for dx in range(2):
                                block = lax.rem(z, 2) * 4 + (y_me ^ dy) * 2 + (x_me ^ dx)
                                row = pl.multiple_of(rows * block, 16)
                                piece = ref[q, 2 * dx + dy if q else 2 * dy + dx]
                                wd_ref[pl.ds(row, rows), pl.ds(col, chunk)] = piece

    for dy in range(2):
        for dx in range(2):
            for k in range(4):
                block = lax.rem(z_me + 4 - k, 4) * 4 + (y_me ^ dy) * 2 + (x_me ^ dx)
                row = pl.multiple_of(block * 64, 64)
                wg_ref[pl.ds(row, 64), :] = (far_g if dy else near_g)[4 * dx + k]
                wu_ref[pl.ds(row, 64), :] = (far_u if dx else near_u)[4 * dy + k]

    b, df = b_ref[...], df_ref[...]
    wg, wu = wg_ref[...], wu_ref[...]
    wd = wd_ref[pl.ds(pl.multiple_of(chunk * s, chunk), chunk), :]
    gate = mm(b, wg)
    upper = mm(b, wu)
    sig = jax.nn.sigmoid(gate)
    act = gate * sig
    z = (act * upper).astype(BF16)
    dz = mm_nt(df, wd)
    dg = (dz * upper * sig * (1.0 + gate * (1.0 - sig))).astype(BF16)
    du = (dz * act).astype(BF16)

    @pl.when(s == 0)
    def _():
        out_ref[...] = mm(z, wd)
        db_ref[...] = mm_nt(dg, wg) + mm_nt(du, wu)

    @pl.when(s > 0)
    def _():
        out_ref[...] += mm(z, wd)
        db_ref[...] += mm_nt(dg, wg) + mm_nt(du, wu)

    gu_ref[:, :64] = mm_tn(b, dg).astype(BF16).reshape(gu_ref.shape[0], 64, chunk)
    gu_ref[:, 64:] = mm_tn(b, du).astype(BF16).reshape(gu_ref.shape[0], 64, chunk)
    side = df.shape[1] // 2
    for ref, j in ((d_send, 1 - core), (d_keep, core)):
        dwd = mm_tn(z, df_ref[:, pl.ds(pl.multiple_of(side * j, side), side)]).astype(BF16)
        ref[0] = dwd[:, :chunk]
        ref[1] = dwd[:, chunk:]


def feed_forward(place, b, df, columns, downs, turn, before=()):
    seq, wide = b.shape
    blocks, chunks, chunk = 16, 5, 256
    half_of = lambda place: place[0] if turn else 1 - place[0]
    d_shape = jax.ShapeDtypeStruct((2, 2 * chunks * chunk, chunk), BF16)
    d_spec = pl.BlockSpec((2, chunk, chunk), lambda s, place: (0, half_of(place) * chunks + s, 0))
    return call(
        functools.partial(ffn_body, turn),
        [
            jax.ShapeDtypeStruct((seq, wide), F32),
            jax.ShapeDtypeStruct((seq, wide), F32),
            jax.ShapeDtypeStruct((blocks, 128 * chunks, chunk), BF16),
            d_shape,
            d_shape,
        ],
        (chunks,),
        [whole(b.shape), whole(df.shape)]
        + [pl.BlockSpec((blocks // 2, 64, chunk), lambda s, place: (0, s, 0))] * 4
        + [whole(t.shape) for t in downs]
        + [pl.BlockSpec(memory_space=pl.ANY)] * len(before),
        [
            whole((seq, wide)),
            whole((seq, wide)),
            pl.BlockSpec((blocks, 128, chunk), lambda s, place: (0, s, 0)),
            d_spec,
            d_spec,
        ],
        scratch=[
            pltpu.VMEM((wide, chunk), BF16),
            pltpu.VMEM((wide, chunk), BF16),
            pltpu.VMEM((chunks * chunk, wide), BF16),
        ],
        flops=18 * seq * wide * chunks * chunk,
        moved=40_000_000,
        prefetch=1,
        alias={15: 3, 16: 4} if before else None,
    )(place, b, df, *columns, *downs, *before)


def token_block(steps):
    def at(i, place):
        return jnp.where(i < steps // 2, (1 - place[0]) * (steps // 2) + i, place[0] * (steps // 2) + i - steps // 2)

    return at


def token_specs(steps, block, width):
    half = steps // 2
    return [
        pl.BlockSpec((width, block), lambda i, place: (0, jnp.minimum(i, half - 1))),
        pl.BlockSpec((1, width, block), lambda i, place: (place[0], 0, jnp.maximum(i - half, 0))),
    ]


def put_tokens(send_ref, keep_ref, value):
    early = pl.program_id(0) < pl.num_programs(0) // 2

    @pl.when(early)
    def _():
        send_ref[...] = value.astype(send_ref.dtype)

    @pl.when(jnp.logical_not(early))
    def _():
        keep_ref[0] = value.astype(keep_ref.dtype)


def post_body(width, place_ref, m_ref, acc0_ref, acc1_ref, db0_ref, db1_ref, df_ref, gain_ref, e_ref, u_ref,
              sum_ref, put_ref, wo_ref, o_ref, op_ref,
              send_ref, keep_ref, em_ref, do_ref, dwo_send, dwo_keep, dgain_ref, dwo_acc):
    i = pl.program_id(0)
    m, db = m_ref[...], db0_ref[...] + db1_ref[...]
    out = (m + (acc0_ref[...] + acc1_ref[...])).astype(BF16)
    put_tokens(send_ref, keep_ref, mm_nt(e_ref[:width, :], out))
    scale = lax.rsqrt(jnp.sum(m * m, axis=-1, keepdims=True) / width + EPSILON)
    n = m * scale
    c = db * gain_ref[1:2]
    mean = jnp.sum(c * n, axis=-1, keepdims=True) / width
    em = df_ref[...].astype(F32) + scale * (c - n * mean)
    em_ref[...] = em
    da = em.astype(BF16)
    dgain = jnp.sum(db * n, axis=0, keepdims=True)
    dwo = mm_tn(op_ref[...], da)

    @pl.when(i == 0)
    def _():
        dgain_ref[...] = dgain
        dwo_acc[...] = dwo

    @pl.when(i > 0)
    def _():
        dgain_ref[...] += dgain
        dwo_acc[...] += dwo

    @pl.when(i == pl.num_programs(0) - 1)
    def _():
        half = dwo_acc.shape[1] // 2
        for ref, j in ((dwo_send, 1 - place_ref[0]), (dwo_keep, place_ref[0])):
            for q in range(2):
                at = pl.multiple_of(half * j + 256 * q, 256)
                ref[q] = dwo_acc[:, pl.ds(at, 256)].astype(BF16).reshape(ref.shape[1:])

    do = mm(mm_nt(da, wo_ref[...]).astype(BF16), u_ref[...])
    flat = jnp.concatenate([o_ref[head] for head in range(HEADS)], axis=1)
    product = do * flat.astype(F32)
    high = product.astype(BF16)
    low = (product - high.astype(F32)).astype(BF16)
    delta = mm(high, sum_ref[...]) + mm(low, sum_ref[...])
    terms = jnp.concatenate([t.astype(BF16) for t in three_terms(delta)], axis=1)
    do = (do + mm(terms, put_ref[...])).astype(BF16)
    for head in range(HEADS):
        do_ref[head] = do[:, LANES * head : LANES * (head + 1)]


def after(place, m, accs, dbs, df, gain, spread, unpack, delta_sum, delta_put, w_out, o, op, width, block=256):
    seq, wide = m.shape
    blocks = 16
    steps = seq // block
    at = token_block(steps)
    rows = lambda n: pl.BlockSpec((block, n), lambda i, place: (at(i, place), 0))
    heads = pl.BlockSpec((HEADS, block, LANES), lambda i, place: (0, at(i, place), 0))
    dwo_shape = (2, blocks, wide // blocks, 256)
    consts = (gain, spread, unpack, delta_sum, delta_put, w_out)
    return call(
        functools.partial(post_body, width),
        [
            jax.ShapeDtypeStruct((width, seq // 2), BF16),
            jax.ShapeDtypeStruct((2, width, seq // 2), BF16),
            jax.ShapeDtypeStruct((seq, wide), F32),
            jax.ShapeDtypeStruct((HEADS, seq, LANES), BF16),
            jax.ShapeDtypeStruct(dwo_shape, BF16),
            jax.ShapeDtypeStruct(dwo_shape, BF16),
            jax.ShapeDtypeStruct((1, wide), F32),
        ],
        (steps,),
        [rows(wide)] * 6 + [whole(t.shape) for t in consts] + [heads, rows(wide)],
        token_specs(steps, block, width)
        + [rows(wide), heads, whole(dwo_shape), whole(dwo_shape), whole((1, wide))],
        scratch=[pltpu.VMEM((wide, wide), F32)],
        flops=2 * seq * wide * 6 * wide,
        moved=45_000_000,
        prefetch=1,
    )(place, m, *accs, *dbs, df, *consts, o, op)


def weights_body(place_ref, dq_ref, dk_ref, dv_ref, a_ref, w_ref, gain_ref,
                 dgain_ref, flat_ref, send_ref, keep_ref, dw_acc, part_ref):
    i = pl.program_id(0)
    heads = HEADS + KV_HEADS

    pairs_to(flat_ref, lambda h: dq_ref[h] if h < HEADS else dk_ref[h - HEADS], heads)
    pairs_to(flat_ref, lambda h: dv_ref[h], KV_HEADS, heads * HEAD)
    dw = mm_tn(a_ref[...], flat_ref[...])

    @pl.when(i == 0)
    def _():
        dw_acc[...] = dw

    @pl.when(i > 0)
    def _():
        dw_acc[...] += dw

    @pl.when(i == pl.num_programs(0) - 1)
    def _():
        wide = dw_acc.shape[0]
        total = jnp.sum(dw_acc[...] * w_ref[...].astype(F32), axis=-1, keepdims=True)
        column = lambda row: jnp.broadcast_to(row, (LANES, wide)).T
        gain = column(gain_ref[:1])
        attn = jnp.broadcast_to(total, (wide, LANES)) / jnp.where(gain == 0.0, 1.0, gain)
        lane = lane_of(wide)
        gains = jnp.where(lane == 32, attn, 0.0) + jnp.where(lane == 33, column(dgain_ref[...]), 0.0)
        n_q, n_k = HEADS * HEAD // 2, KV_HEADS * HEAD // 2
        for j in range(2):
            part_ref[:, 768:] = gains.astype(BF16)
            part_ref[:, :n_q] = dw_acc[:, n_q * j : n_q * (j + 1)].astype(BF16)
            for part in range(2):
                at, to = 2 * n_q + n_k * (2 * part + j), n_q + n_k * part
                part_ref[:, to : to + n_k] = dw_acc[:, at : at + n_k].astype(BF16)
            for ref, here in ((keep_ref, place_ref[0] == j), (send_ref, place_ref[0] != j)):

                @pl.when(here)
                def _():
                    ref[...] = part_ref[...].reshape(ref.shape)


def projections_back(place, parts, a, w_qkv, gain, dgain_ffn, block=512):
    seq, wide = a.shape
    blocks = 16
    rows = lambda n: pl.BlockSpec((block, n), lambda i, *_: (i, 0))
    heads = lambda t: pl.BlockSpec((t.shape[0], block, LANES), lambda i, *_: (0, i, 0))
    shape = (blocks, wide // blocks, 896)
    return call(
        weights_body,
        [
            jax.ShapeDtypeStruct((seq, QKV_PAD), BF16),
            jax.ShapeDtypeStruct(shape, BF16),
            jax.ShapeDtypeStruct(shape, BF16),
        ],
        (seq // block,),
        [heads(t) for t in parts] + [rows(wide), whole(w_qkv.shape), whole((8, wide)), whole((1, wide))],
        [rows(QKV_PAD), whole(shape), whole(shape)],
        scratch=[pltpu.VMEM((wide, QKV_PAD), F32), pltpu.VMEM((wide, 896), BF16)],
        flops=2 * seq * wide * QKV_PAD,
        moved=20_000_000,
        prefetch=1,
    )(place, *parts, a, w_qkv, gain, dgain_ffn)


def input_body(width, place_ref, flat_ref, w_ref, xp_ref, em_ref, gain_ref, e_ref, send_ref, keep_ref):
    da = mm_nt(flat_ref[...], w_ref[...])
    xp = xp_ref[...].astype(F32)
    scale = lax.rsqrt(jnp.sum(xp * xp, axis=-1, keepdims=True) / width + EPSILON)
    n = xp * scale
    c = da * gain_ref[:1]
    mean = jnp.sum(c * n, axis=-1, keepdims=True) / width
    grad = em_ref[...] + scale * (c - n * mean)
    put_tokens(send_ref, keep_ref, mm_nt(e_ref[:width, :], grad.astype(BF16)))


def input_back(place, flat, w_qkv, xp, em, gain, spread, width, block=256):
    seq, wide = xp.shape
    steps = seq // block
    at = token_block(steps)
    rows = lambda n: pl.BlockSpec((block, n), lambda i, place: (at(i, place), 0))
    return call(
        functools.partial(input_body, width),
        [
            jax.ShapeDtypeStruct((width, seq // 2), BF16),
            jax.ShapeDtypeStruct((2, width, seq // 2), F32),
        ],
        (steps,),
        [rows(QKV_PAD), whole(w_qkv.shape), rows(wide), rows(wide), whole((8, wide)), whole(spread.shape)],
        token_specs(steps, block, width),
        flops=2 * seq * wide * (QKV_PAD + 2 * width),
        moved=20_000_000,
        prefetch=1,
    )(place, flat, w_qkv, xp, em, gain, spread)


def begin_body(reader, n_in, place_ref, *refs):
    ins, outs = refs[:n_in], refs[n_in:]
    _, _, y, x = (place_ref[n] for n in range(4))
    for side in range(2):
        mine = y if side else x
        for other in range(2):
            for ref, bit in ((outs[2 * side], 1 - mine), (outs[2 * side + 1], mine)):
                block = 2 * bit + other if side else 2 * other + bit
                for row, keep, got in reader(ins, side, block):
                    ref[other, row : row + keep.shape[0]] = add(keep, got)


def begin(place, arrays, reader, rows, count=4):
    n = arrays[0].shape[-1]

    def spec(t):
        lead = t.shape[:-3]
        return pl.BlockSpec((*lead, 4, *t.shape[-2:]), lambda i, place: (0,) * len(lead) + (i, 0, 0))

    shape = jax.ShapeDtypeStruct((2 * count, rows, n), BF16)
    return call(
        functools.partial(begin_body, reader, len(arrays)),
        [shape] * 4,
        (count,),
        [spec(t) for t in arrays],
        [pl.BlockSpec((2, rows, n), lambda i, place: (i, 0, 0))] * 4,
        flops=1,
        moved=16 * count * rows * n * 6,
        prefetch=1,
        vmem=VMEM_SMALL,
    )(place, *arrays)


def turn_body(place_ref, *refs):
    y, x = place_ref[2], place_ref[3]
    for side in range(2):
        keep, got = refs[2 * side : 2 * side + 2]
        mine = x if side else y
        for ref, bit in ((refs[4 + 2 * side], 1 - mine), (refs[5 + 2 * side], mine)):
            ref[0] = add(keep[bit], got[bit])


def turn(place, keeps, gots):
    blocks, rows, n = keeps[0].shape
    shape = jax.ShapeDtypeStruct((blocks // 2, rows, n), BF16)
    return call(
        turn_body,
        [shape] * 4,
        (blocks // 2,),
        [pl.BlockSpec((2, rows, n), lambda i, place: (i, 0, 0))] * 4,
        [pl.BlockSpec((1, rows, n), lambda i, place: (i, 0, 0))] * 4,
        flops=1,
        moved=blocks * rows * n * 12,
        prefetch=1,
        vmem=VMEM_SMALL,
    )(place, keeps[0], gots[0], keeps[1], gots[1])


def climb_body(place_ref, a_keep, a_got, b_keep, b_got, total_ref, *sent):
    for step in range(4):
        block = lax.rem(place_ref[1] + step, 4)
        for side, (keep, got) in enumerate(((a_keep, a_got), (b_keep, b_got))):
            value = keep[block].astype(F32) + got[block].astype(F32)
            if step:
                sent[step - 1][side] = value.astype(BF16)
            else:
                total_ref[side] = value


def climb(place, keeps, gots):
    _, rows, n = keeps[0].shape
    return call(
        climb_body,
        [jax.ShapeDtypeStruct((2, rows, n), F32)] + [jax.ShapeDtypeStruct((2, rows, n), BF16)] * 3,
        (1,),
        [whole(keeps[0].shape)] * 4,
        [whole((2, rows, n))] * 4,
        flops=1,
        moved=rows * n * 50,
        prefetch=1,
        vmem=VMEM_SMALL,
    )(place, keeps[0], gots[0], keeps[1], gots[1])


def unpack_matrix(width, blocks, wide):
    per, step = width // blocks, wide // blocks
    col = jnp.arange(WIDE_HEADS, dtype=jnp.int32)
    feature = col // LANES * HEAD + col % LANES
    place = jnp.where(col % LANES < HEAD, feature // per * step + feature % per, -1)
    return (jnp.arange(wide, dtype=jnp.int32)[:, None] == place[None, :]).astype(BF16)


def delta_matrices():
    row = jnp.arange(WIDE_HEADS, dtype=jnp.int32)
    lane = jnp.arange(LANES, dtype=jnp.int32)
    total = (row[:, None] // LANES == lane[None, :]).astype(BF16)
    term = jnp.arange(3 * LANES, dtype=jnp.int32)
    to = jnp.where(term % LANES < HEADS, term % LANES * LANES + HEAD + term // LANES, -1)
    return total, (to[:, None] == row[None, :]).astype(BF16)


def spread_matrix(width, blocks, wide):
    row = jnp.arange(wide, dtype=jnp.int32)
    per, step = width // blocks, wide // blocks
    place = (row // per) * step + row % per
    hit = (place[:, None] == jnp.arange(wide, dtype=jnp.int32)[None, :]) & (row < width)[:, None]
    return hit.astype(BF16)


def tables(positions, segments):
    lane = jnp.arange(LANES, dtype=jnp.int32)
    frequency = 10000.0 ** (-((lane % 32).astype(F32) * 2.0 / HEAD))
    angles = positions.astype(F32)[:, None] * frequency[None, :]
    cos, sin = jnp.cos(angles), jnp.sin(angles)
    high = (lane % HEAD >= 32)[None, :]
    sa = jnp.where(high, sin, 0.0)
    sb = jnp.where(high, 0.0, -sin)
    doc = (lane - HEAD)[None, :]
    mine = segments[:, None] == doc
    in_doc = (doc >= 0) & (doc < DOCS)
    aq = jnp.where(mine & in_doc, MASKED, 0.0)
    ak = jnp.where(in_doc & ~mine, 1.0, 0.0)
    ak = jnp.where((doc >= DOCS) & (doc < DOCS + 3), -1.0, ak)
    return cos, sa, sb, aq, ak


def pad_rows(w, blocks, step=64):
    per = w.shape[0] // blocks
    return jnp.pad(w.reshape(blocks, per, w.shape[1]), ((0, 0), (0, step - per), (0, 0)))


def pad_cols(w, blocks, step=64):
    per = w.shape[1] // blocks
    w = jnp.pad(w.reshape(w.shape[0], blocks, per), ((0, 0), (0, 0), (0, step - per)))
    return w.reshape(w.shape[0], blocks * step)


def cut_rows(w, per):
    return w[:, :per].reshape(w.shape[0] * per, w.shape[2])


def cut_cols(w, per, step=64):
    blocks = w.shape[1] // step
    return w.reshape(w.shape[0], blocks, step)[:, :, :per].reshape(w.shape[0], blocks * per)


def chunked(w, chunk=256):
    blocks, rows, cols = w.shape
    w = w.reshape(blocks, rows, cols // chunk, chunk).transpose(0, 2, 1, 3)
    return w.reshape(blocks, cols // chunk * rows, chunk)


def joined(w, rows):
    blocks, total, chunk = w.shape
    w = w.reshape(blocks, total // rows, rows, chunk).transpose(0, 2, 1, 3)
    return w.reshape(blocks, rows, total // rows * chunk)


def pack_half(w_gate, w_up, w_down, blocks, groups):
    down = pad_cols(w_down, groups)
    down = down.reshape(blocks, w_down.shape[0] // blocks, 2, -1).transpose(0, 2, 1, 3)
    columns = [chunked(pad_rows(w_gate, blocks)), chunked(pad_rows(w_up, blocks))]
    return jnp.concatenate(columns, axis=1), down


def add(left, right):
    return (left.astype(F32) + right.astype(F32)).astype(BF16)


def swap(x):
    return lax.ppermute(x, "ctx", [(0, 1), (1, 0)])


def across(x, bit, count):
    return lax.ppermute(x, "dp", [(i, i ^ (1 << bit)) for i in range(count)])


def pick(x, index, axis=0):
    return lax.dynamic_index_in_dim(x, index, axis, keepdims=False)


def tie(value, *others):
    return lax.optimization_barrier((value, *others))[0]


def tie_all(values, *others):
    return lax.optimization_barrier((*values, *others))[: len(values)]


def along_z(x, step, count):
    return lax.ppermute(x, "dp", [(i, (i + 4 * step) % count) for i in range(count)])


def rise(x, count):
    return [x] + [along_z(x, k, count) for k in (1, 2, 3)]


def spread_first(stack, count):
    half = stack.shape[1] // 2
    first, second = stack[:, :half], stack[:, half:]
    return first, across(first, 0, count), second, across(second, 1, count)


def spread_second(first, first_got, second, second_got, count):
    first, second = jnp.concatenate([first, first_got]), jnp.concatenate([second, second_got])
    return first, across(first, 1, count), second, across(second, 0, count)


def pieces_of(whole_one):
    n = whole_one.shape[1] // 2
    cube = whole_one.reshape(4, 2, 2, 2 * n, -1)
    cube = jnp.stack([cube[(4 - k) % 4] for k in range(4)])
    first, second = cube[:, :, :, :n], cube[:, :, :, n:]
    first, second = first.transpose(1, 2, 0, 3, 4), second.transpose(2, 1, 0, 3, 4)
    flat = lambda t: t.reshape(8, n, -1)
    return flat(first[0]), flat(first[1]), flat(second[0]), flat(second[1])


def downs_of(whole_one):
    cube = whole_one.reshape(4, 2, 2, 2, *whole_one.shape[2:])
    result = []
    for k in range(4):
        first, second = cube[(4 - k) % 4, :, :, 0], cube[(4 - k) % 4, :, :, 1].transpose(1, 0, 2, 3)
        result.append(jnp.stack([first, second]).reshape(2, 4, *whole_one.shape[2:]))
    return result


class RowSum:
    def __init__(self, place, count, arrays, reader, rows):
        self.place, self.count = place, count
        a_sent, a_kept, b_sent, b_kept = begin(place, arrays, reader, rows)
        self.sent, self.kept = [a_sent, b_sent], [a_kept, b_kept]

    def move(self):
        self.got = [across(self.sent[0], 0, self.count), across(self.sent[1], 1, self.count)]

    def wait(self, other):
        self.got = list(lax.optimization_barrier((*self.got, other))[:-1])

    def turn(self, other):
        self.wait(other)
        a_sent, a_kept, b_sent, b_kept = turn(self.place, self.kept, self.got)
        self.sent, self.kept = [a_sent, b_sent], [a_kept, b_kept]

    def move_again(self):
        self.got = [across(self.sent[0], 1, self.count), across(self.sent[1], 0, self.count)]

    def climb(self, other):
        self.wait(other)
        self.kept, *self.sent = climb(self.place, self.kept, self.got)

    def move_up(self):
        self.got = [along_z(self.sent[k - 1], k, self.count) for k in (1, 2, 3)]

    def total(self):
        total = self.kept
        for got in self.got:
            total = total + got.astype(F32)
        return total


def read_rows(ins, side, block):
    half = ins[0].shape[1] // 2
    rows = slice(half * side, half * (side + 1))
    return [(0, ins[0][block, rows], ins[1][block, rows])]


def read_quarters(ins, side, block):
    first = ins[0].shape[2]
    return [(0, ins[0][side, block], ins[1][side, block]), (first, ins[2][side, block], ins[3][side, block])]


def put_other(both, got, core):
    return lax.dynamic_update_slice(both, got[None], (1 - core, 0, 0))


def shards_of_two(inputs, segment_ids, positions, w_query, w_key, w_value, w_out, w_gate, w_up,
                  w_down, gain_attn, gain_ffn, cotangent):
    count = lax.axis_size("dp")
    me, core = lax.axis_index("dp"), lax.axis_index("ctx")
    place = (core, me // 4, (me >> 1) & 1, me & 1)
    place_of = jnp.stack(place).astype(jnp.int32)
    per = gain_attn.shape[0]
    width = per * count
    groups = w_out.shape[1] // per
    hidden = w_down.shape[0]
    n_q, n_k = w_query.shape[1], w_key.shape[1]
    n_qkv = n_q + 2 * n_k

    shard = jnp.concatenate(
        [w_query, w_key, w_value, gain_attn[:, None], gain_ffn[:, None]], axis=1
    )
    shard = jnp.pad(shard, ((0, 0), (0, 896 - n_qkv - 2)))
    shard = jnp.concatenate([shard, pad_cols(w_out, groups)], axis=1)
    shard = jnp.pad(shard, ((0, 64 - per), (0, 0)))
    columns, down = pack_half(w_gate, w_up, w_down, 1, groups)
    columns, down = columns[0], down[0]

    level = rise(shard, count)
    d_first, d_second = down[:1], down[1:]
    d_first = jnp.concatenate([d_first, across(d_first, 0, count)])
    d_second = jnp.concatenate([d_second, across(d_second, 1, count)])
    d_first = jnp.concatenate([d_first, across(d_first, 1, count)])
    d_second = jnp.concatenate([d_second, across(d_second, 0, count)])
    down = jnp.stack([d_first, d_second])
    part = spread_first(jnp.stack(level), count)
    c_level = rise(tie(columns, *level), count)
    near_far = spread_second(*part, count)
    c_level = list(tie_all(c_level, *near_far))
    c_part = spread_first(jnp.stack(c_level), count)
    downs = rise(tie(down, *c_level), count)
    pieces = near_far + tuple(swap(t) for t in near_far)

    def halves(x):
        x = jnp.swapaxes(x[:, 0], 1, 2)
        return pick(x, core), swap(pick(x, 1 - core))

    wide = count * 64
    spread, unpack = spread_matrix(width, count, wide), unpack_matrix(width, count, wide)
    delta_sum, delta_put = delta_matrices()
    cos, sa, sb, aq, ak = tables(pick(positions[:, 0], core), pick(segment_ids[:, 0], core))
    xp, a, q, k, v, w_qkv, w_o, gains = pre_attention(
        place_of, *halves(inputs), spread, tie_all(pieces, c_part[0], c_part[2], down), cos, sa, sb, aq, ak
    )
    columns = spread_second(*tie_all(c_part, q), count)
    q = tie(q, *columns[::2])
    near_got = [swap(t) for t in columns[::2]]
    o, q2 = attend(q, k, v)
    downs = list(tie_all(downs, o))
    down_got = [swap(t) for t in downs]
    op, m, b, df = middle(
        place_of, tie(o, *downs), *halves(cotangent), spread, unpack, w_o, xp, gains
    )
    far_got = [swap(t) for t in tie_all(columns[1::2], b)]
    other = (near_got[0], far_got[0], near_got[1], far_got[1])
    downs = downs + down_got

    acc0, db0, gu_send, d_send, d_keep = feed_forward(place_of, b, df, other, downs, 0)
    gu_got = swap(gu_send)
    acc1, db1, gu_keep, d_send, d_keep = feed_forward(
        place_of, tie(b, gu_send), df, columns, downs, 1, (d_send, d_keep)
    )
    one = RowSum(place_of, count, (gu_keep, tie(gu_got, acc1)), read_rows, 320)
    one.move()
    blocked = lambda t: t.reshape(2, count, hidden, 256)
    d_got = swap(d_send)
    m = tie(m, *one.sent, d_send)
    out_send, outs, em, do, o_send, o_keep, dgf = after(
        place_of, m, (acc0, acc1), (db0, db1), df, gains, spread, unpack, delta_sum, delta_put, w_o, o, op, width
    )
    o_got = swap(o_send)
    one.turn(em)
    one.move_again()
    two = RowSum(
        place_of, count, (blocked(d_keep), blocked(tie(d_got, em)), o_keep, o_got), read_quarters, 224
    )
    two.move()
    do = tie(do, *one.sent, *two.sent)
    parts = attend_back(q2, k, v, do, cos, sa, sb, 0, KV_HEADS)
    outs = put_other(outs, tie(swap(out_send), parts[0]), core)
    one.climb(parts[0])
    one.move_up()
    two.turn(parts[0])
    two.move_again()
    a = tie(a, *one.sent, *two.sent)
    flat, p_send, p_keep = projections_back(place_of, parts, a, w_qkv, gains, dgf)
    p_got = swap(p_send)
    two.climb(flat)
    two.move_up()
    one.got[1:] = tie_all(one.got[1:], flat)
    three = RowSum(place_of, count, (p_keep, p_got), read_rows, 32)
    three.move()
    flat = tie(flat, *two.sent, *three.sent, *one.got[1:])
    gi_send, gis = input_back(place_of, flat, w_qkv, xp, em, gains, spread, width)
    gi_got = swap(gi_send)
    one.wait(gis)
    first = one.total()
    three.turn(first)
    three.move_again()
    gis = put_other(gis, gi_got.astype(F32), core)
    three.climb(gis)
    three.move_up()
    second, third = two.total(), three.total()
    third = third.reshape(64, 896)[:per]
    gu = first.reshape(5, 2, 64, 256)
    wide_of = lambda t: t.transpose(1, 0, 2).reshape(t.shape[1], -1)
    tokens = lambda t: jnp.swapaxes(t, 1, 2)[:, None]
    return (
        tokens(outs),
        tokens(gis),
        third[:, :n_q],
        third[:, n_q : n_q + n_k],
        third[:, n_q + n_k : n_qkv],
        cut_cols(wide_of(second[:, 160:])[:per], per),
        wide_of(gu[:, 0])[:per],
        wide_of(gu[:, 1])[:per],
        cut_cols(wide_of(second[:, :160]), per),
        third[:, n_qkv],
        third[:, n_qkv + 1],
    )


def shards_of_many(inputs, segment_ids, positions, w_query, w_key, w_value, w_out, w_gate, w_up,
                   w_down, gain_attn, gain_ffn, cotangent):
    count, cores = lax.axis_size("dp"), lax.axis_size("ctx")
    core = lax.axis_index("ctx")
    share = cores // MICRO
    per = gain_attn.shape[0]
    width = per * count

    def gathered(w):
        return lax.all_gather(lax.all_gather(w, "dp", axis=0, tiled=True), "ctx", axis=1, tiled=True)

    full = [gathered(w) for w in (w_query, w_key, w_value, w_out, w_gate, w_up, w_down)]
    gain_pair = lax.all_gather(jnp.stack([gain_attn, gain_ffn]), "dp", axis=1, tiled=True)
    w_o, w_g, w_u, w_d = full[3:]
    half = lambda w, j: w[:, w.shape[1] // 2 * j : w.shape[1] // 2 * (j + 1)]
    packs = [pack_half(half(w_g, j), half(w_u, j), half(w_d, j), count, count // 2) for j in range(2)]
    columns = [pieces_of(p[0]) for p in packs]
    downs = [t for p in packs for t in downs_of(p[1])]
    pieces = []
    for j in range(2):
        parts = [half(w, j) for w in full[:3]] + [gain_pair.T]
        part = jnp.concatenate(parts, axis=1)
        part = jnp.pad(part, ((0, 0), (0, 896 - part.shape[1])))
        part = jnp.concatenate([part, pad_cols(half(w_o, j), count // 2)], axis=1)
        pieces += pieces_of(pad_rows(part, count))
    which = core // share

    def sequence(x):
        whole_one = pick(lax.all_gather(x[:, 0], "ctx", axis=1, tiled=True), which).T
        return whole_one[:, : whole_one.shape[1] // 2], whole_one[:, whole_one.shape[1] // 2 :]

    place = jnp.zeros((4,), jnp.int32)
    wide = count * 64
    spread, unpack = spread_matrix(width, count, wide), unpack_matrix(width, count, wide)
    delta_sum, delta_put = delta_matrices()
    cos, sa, sb, aq, ak = tables(pick(positions[:, 0], which), pick(segment_ids[:, 0], which))
    xp, a, q, k, v, w_qkv, w_o, gains = pre_attention(
        place, *sequence(inputs), spread, pieces, cos, sa, sb, aq, ak
    )
    o, q2 = attend(q, k, v)
    op, m, b, df = middle(place, o, *sequence(cotangent), spread, unpack, w_o, xp, gains)
    acc0, db0, gu_send, d_send, d_keep = feed_forward(place, b, df, columns[1], downs, 0)
    acc1, db1, gu_keep, d_send, d_keep = feed_forward(place, b, df, columns[0], downs, 1, (d_send, d_keep))
    out_send, outs, em, do, o_send, o_keep, dgf = after(
        place, m, (acc0, acc1), (db0, db1), df, gains, spread, unpack, delta_sum, delta_put, w_o, o, op, width
    )
    parts = attend_back(q2, k, v, do, cos, sa, sb, 0, KV_HEADS)
    flat, p_send, p_keep = projections_back(place, parts, a, w_qkv, gains, dgf)
    gi_send, gis = input_back(place, flat, w_qkv, xp, em, gains, spread, width)

    parts = [cut_rows(p, per) for p in (p_keep, p_send)]
    n_q, n_k = HEADS * HEAD // 2, KV_HEADS * HEAD // 2
    both = lambda at, n: jnp.concatenate([p[:, at : at + n] for p in parts], axis=1)
    side = lambda t: jnp.concatenate([t[0], t[1]], axis=-1)

    def wide_of(index):
        every = []
        for t in (gu_keep, gu_send):
            t = t.reshape(count, 5, 2, 64, 256)[:, :, index]
            every.append(cut_rows(t.transpose(0, 2, 1, 3).reshape(count, 64, -1), per))
        return jnp.concatenate(every, axis=1)

    grads = [
        both(0, n_q),
        both(n_q * 1, n_k),
        both(n_q + n_k, n_k),
        cut_cols(cut_rows(jnp.concatenate([side(o_keep), side(o_send)], axis=-1), per), per),
        wide_of(0),
        wide_of(1),
        cut_cols(
            jnp.concatenate([side(d_keep), side(d_send)], axis=-1),
            per,
        ),
    ]

    def summed(g):
        g = lax.psum_scatter(g * (1.0 / share), "dp", scatter_dimension=0, tiled=True)
        return lax.psum_scatter(g, "ctx", scatter_dimension=1, tiled=True).astype(F32)

    sums = [summed(g.astype(BF16)) for g in grads]
    dgain = parts[0][:, 2 * n_k + n_q : 2 * n_k + n_q + 2].astype(F32).T * (1.0 / share)
    dgain = lax.psum_scatter(lax.psum(dgain, "ctx"), "dp", scatter_dimension=1, tiled=True)

    def tokens(seq):
        rows = seq.shape[0] // cores
        every = lax.all_gather(seq, "ctx", axis=0, tiled=False)
        return lax.dynamic_slice_in_dim(every[::share], core * rows, rows, axis=1)[:, None]

    out = jnp.concatenate([outs[0], out_send], axis=1).T
    gi = jnp.concatenate([gis[0], gi_send.astype(F32)], axis=1).T
    return (tokens(out), tokens(gi), *sums, dgain[0], dgain[1])


def solution(mesh):
    two = mesh.shape["ctx"] == MICRO and mesh.shape["dp"] == 16
    matrices = (P("dp", "ctx"),) * 7 + (P("dp"), P("dp"))
    tokens = P(None, "dp", "ctx", None)
    return jax.shard_map(
        shards_of_two if two else shards_of_many,
        mesh=mesh,
        in_specs=(tokens, P(None, "dp", None), P(None, "dp", None)) + matrices + (tokens,),
        out_specs=(tokens, tokens) + matrices,
        check_vma=False,
    )
```

```python
import functools

import jax
import jax.numpy as jnp
from jax import lax
from jax.experimental import pallas as pl
from jax.experimental.pallas import tpu as pltpu
from jax.sharding import PartitionSpec as P

HEADS = 15
KV_HEADS = 5
HEAD = 64
MICRO = 2
GROUP = 3
DOCS = 4

EPSILON = 1e-05
MASKED = -1e30
LANES = 128
QKV = (HEADS + 2 * KV_HEADS) * HEAD
QKV_PAD = 1664
VMEM_LIMIT = 56 * 1024 * 1024
PACK = 1408
VMEM_SMALL = 24 * 1024 * 1024
WIDE_HEADS = HEADS * LANES
F32 = jnp.float32
BF16 = jnp.bfloat16


def up(value, step):
    return -(-value // step) * step


def mm(left, right):
    return lax.dot_general(left, right, (((1,), (0,)), ((), ())), preferred_element_type=F32)


def mm_nt(left, right):
    return lax.dot_general(left, right, (((1,), (1,)), ((), ())), preferred_element_type=F32)


def mm_tn(left, right):
    return lax.dot_general(left, right, (((0,), (0,)), ((), ())), preferred_element_type=F32)


def call(body, out_shape, grid, in_specs, out_specs, scratch=(), flops=0, moved=0, prefetch=0, alias=None,
         vmem=VMEM_LIMIT):
    return pl.pallas_call(
        body,
        out_shape=out_shape,
        grid_spec=pltpu.PrefetchScalarGridSpec(
            num_scalar_prefetch=prefetch,
            grid=grid,
            in_specs=in_specs,
            out_specs=out_specs,
            scratch_shapes=scratch,
        ),
        input_output_aliases=alias or {},
        compiler_params=pltpu.CompilerParams(vmem_limit_bytes=vmem),
        cost_estimate=pl.CostEstimate(flops=flops, bytes_accessed=moved, transcendentals=0),
    )


def whole(shape):
    return pl.BlockSpec(shape, lambda *_: (0,) * len(shape), pipeline_mode=pl.Buffered(1))


def lane_of(rows):
    return lax.broadcasted_iota(jnp.int32, (rows, LANES), 1)


def three_terms(column):
    high = column.astype(BF16).astype(F32)
    rest = column - high
    mid = rest.astype(BF16).astype(F32)
    return high, mid, rest - mid


def put_terms(base, column, lane, first):
    high, mid, low = three_terms(column)
    base = jnp.where(lane == first, high, base)
    base = jnp.where(lane == first + 1, mid, base)
    return jnp.where(lane == first + 2, low, base)


def build_weights(place_ref, piece_refs, stage_ref, w_ref, wo_ref):
    core, z, y, x = (place_ref[n] for n in range(4))
    for swapped in range(2):
        near_a, far_a, near_b, far_b = piece_refs[4 * swapped : 4 * swapped + 4]
        to = jnp.bitwise_xor(core, swapped)
        for dy in range(2):
            for dx in range(2):
                for k in range(4):
                    block = lax.rem(z + 4 - k, 4) * 4 + (y ^ dy) * 2 + (x ^ dx)
                    row = pl.multiple_of(block * 64, 64)
                    stage_ref[to, pl.ds(row, 32), :] = (far_a if dy else near_a)[4 * dx + k]
                    stage_ref[to, pl.ds(row + 32, 32), :] = (far_b if dx else near_b)[4 * dy + k]
    n_q, n_k = HEADS * HEAD // 2, KV_HEADS * HEAD // 2
    for j in range(2):
        w_ref[:, n_q * j : n_q * (j + 1)] = stage_ref[j, :, :n_q]
        for part in range(2):
            to, at = 2 * n_q + n_k * (2 * part + j), n_q + n_k * part
            w_ref[:, to : to + n_k] = stage_ref[j, :, at : at + n_k]
        half = wo_ref.shape[1] // 2
        wo_ref[:, half * j : half * (j + 1)] = stage_ref[j, :, PACK - half :]
    w_ref[:, QKV:] = jnp.zeros((w_ref.shape[0], QKV_PAD - QKV), BF16)


def projections(xp, scale, w_ref, gain_ref, cos_ref, sa_ref, sb_ref, aq_ref, ak_ref,
                xp_ref, a_ref, q_ref, k_ref, v_ref):
    a = (xp * scale * gain_ref[:1]).astype(BF16)
    xp_ref[...] = xp.astype(BF16)
    a_ref[...] = a
    t = mm(a, w_ref[...])
    lane = lane_of(t.shape[0])
    low = lane < HEAD
    cos, sa, sb, aq, ak = cos_ref[...], sa_ref[...], sb_ref[...], aq_ref[...], ak_ref[...]
    for pair in range((HEADS + KV_HEADS) // 2):
        tt = t[:, LANES * pair : LANES * (pair + 1)]
        rot = tt * cos + pltpu.roll(tt, 32, 1) * sa + pltpu.roll(tt, 96, 1) * sb
        for half in range(2):
            head = 2 * pair + half
            val = rot if half == 0 else pltpu.roll(rot, 64, 1)
            if head < HEADS:
                q_ref[head] = jnp.where(low, val * HEAD ** -0.5, aq).astype(BF16)
            else:
                k_ref[head - HEADS] = jnp.where(low, val, ak).astype(BF16)
    av = jnp.where(lane < HEAD + 3, -1.0, 0.0)
    for head in range(KV_HEADS):
        first = (HEADS + KV_HEADS) * HEAD + LANES * (head // 2)
        tt = t[:, first : first + LANES]
        val = tt if head % 2 == 0 else pltpu.roll(tt, 64, 1)
        v_ref[head] = jnp.where(low, val, av).astype(BF16)


def own_or_other(place_ref, own_ref, other_ref):
    first = pl.program_id(0) < pl.num_programs(0) // 2
    mine = first == (place_ref[0] == 0)
    return jnp.where(mine, own_ref[...], other_ref[...])


def pre_body(width, place_ref, own_ref, other_ref, e_ref, *refs):
    pieces, refs = refs[:8], refs[8:]
    *rest, w_ref, wo_ref, gain_ref, stage_ref = refs

    @pl.when(pl.program_id(0) == 0)
    def _():
        build_weights(place_ref, pieces, stage_ref, w_ref, wo_ref)
        gain_ref[...] = stage_ref[0, :, 768:896].astype(F32).T[32:40]

    xp = mm_tn(own_or_other(place_ref, own_ref, other_ref), e_ref[:width, :])
    scale = lax.rsqrt(jnp.sum(xp * xp, axis=-1, keepdims=True) / width + EPSILON)
    projections(xp, scale, w_ref, gain_ref, *rest)


def halves_specs(rows, width, block):
    steps = rows // block
    return [pl.BlockSpec((width, block), lambda i, *_: (0, i % steps))] * 2


def pre_attention(place, own, other, spread, pieces, cos, sa, sb, aq, ak, block=512):
    width, half = own.shape
    seq, wide = 2 * half, spread.shape[1]
    rows = lambda n: pl.BlockSpec((block, n), lambda i, *_: (i, 0))
    heads = lambda n: pl.BlockSpec((n, block, LANES), lambda i, *_: (0, i, 0))
    return call(
        functools.partial(pre_body, width),
        [
            jax.ShapeDtypeStruct((seq, wide), BF16),
            jax.ShapeDtypeStruct((seq, wide), BF16),
            jax.ShapeDtypeStruct((HEADS, seq, LANES), BF16),
            jax.ShapeDtypeStruct((KV_HEADS, seq, LANES), BF16),
            jax.ShapeDtypeStruct((KV_HEADS, seq, LANES), BF16),
            jax.ShapeDtypeStruct((wide, QKV_PAD), BF16),
            jax.ShapeDtypeStruct((wide, wide), BF16),
            jax.ShapeDtypeStruct((8, wide), F32),
        ],
        (seq // block,),
        halves_specs(half, width, block)
        + [whole(spread.shape)]
        + [whole(w.shape) for w in pieces]
        + [rows(LANES)] * 5,
        [rows(wide), rows(wide), heads(HEADS), heads(KV_HEADS), heads(KV_HEADS)]
        + [whole((wide, QKV_PAD)), whole((wide, wide)), whole((8, wide))],
        scratch=[pltpu.VMEM((2, wide, PACK), BF16)],
        flops=2 * seq * wide * (width + QKV_PAD),
        moved=20_000_000,
        prefetch=1,
    )(place, own, other, spread, *pieces, cos, sa, sb, aq, ak)


def attend_body(block, q_ref, k_ref, v_ref, o_ref, q2_ref):
    seq = k_ref.shape[1]
    rows = GROUP * block
    below = lax.broadcasted_iota(jnp.int32, (block, block), 0) >= lax.broadcasted_iota(
        jnp.int32, (block, block), 1
    )
    below = jnp.concatenate([below.astype(F32)] * GROUP, axis=0) > 0.5
    lane = lane_of(rows)
    for i in range(seq // block):
        span = slice(block * i, block * (i + 1))
        q = q_ref[:, span, :].reshape(rows, LANES)
        s_in = jnp.where(below, mm_nt(q, k_ref[0, span, :]), MASKED)
        top = jnp.max(s_in, axis=-1, keepdims=True)
        if i:
            s_left = mm_nt(q, k_ref[0, : block * i, :])
            top = jnp.maximum(top, jnp.max(s_left, axis=-1, keepdims=True))
        ext = mm(jnp.exp(s_in - top).astype(BF16), v_ref[0, span, :])
        if i:
            ext = ext + mm(jnp.exp(s_left - top).astype(BF16), v_ref[0, : block * i, :])
        total = -ext[:, HEAD : HEAD + 1]
        o = ext / total
        o = jnp.where(lane < HEAD, o, pltpu.roll(o, 64, 1))
        o_ref[:, span, :] = o.reshape(GROUP, block, LANES).astype(BF16)
        q2 = put_terms(q.astype(F32), top + jnp.log(total), lane, HEAD + DOCS)
        q2_ref[:, span, :] = q2.reshape(GROUP, block, LANES).astype(BF16)


def attend(q, k, v, block=256):
    seq = q.shape[1]
    group = pl.BlockSpec((GROUP, seq, LANES), lambda n: (n, 0, 0))
    one = pl.BlockSpec((1, seq, LANES), lambda n: (n, 0, 0))
    shape = jax.ShapeDtypeStruct(q.shape, BF16)
    return call(
        functools.partial(attend_body, block),
        [shape, shape],
        (KV_HEADS,),
        [group, one, one],
        [group, group],
        flops=4 * HEADS * seq * seq * LANES,
        moved=15_000_000,
    )(q, k, v)


def attend_back_body(block, q_ref, k_ref, v_ref, do_ref, cos_ref, sa_ref, sb_ref,
                     dq_ref, dk_ref, dv_ref, acc_ref):
    seq = k_ref.shape[1]
    above = lax.broadcasted_iota(jnp.int32, (block, block), 0) <= lax.broadcasted_iota(
        jnp.int32, (block, block), 1
    )
    lane = lane_of(seq)

    def unrotate(t, span):
        rows = span.stop - span.start
        rot = (
            t * cos_ref[span, :]
            - pltpu.roll(t, 32, 1) * sa_ref[span, :]
            - pltpu.roll(t, 96, 1) * sb_ref[span, :]
        )
        return twice(rot, rows)

    def twice(t, rows):
        return jnp.where(lane[:rows] < HEAD, t, pltpu.roll(t, 64, 1)).astype(BF16)

    for j in range(seq // block):
        span = slice(block * j, block * (j + 1))
        k, v = k_ref[0, span, :], v_ref[0, span, :]
        dk = jnp.zeros((block, LANES), F32)
        dv = jnp.zeros((block, LANES), F32)
        for g in range(GROUP):
            q, do = q_ref[g, block * j :, :], do_ref[g, block * j :, :]
            p = jnp.exp(mm_nt(k, q))
            inner = jnp.where(above, p[:, :block], 0.0)
            p = inner if p.shape[1] == block else jnp.concatenate([inner, p[:, block:]], axis=1)
            ds = (p * mm_nt(v, do)).astype(BF16)
            dv = dv + mm(p.astype(BF16), do)
            dk = dk + mm(ds, q)
            dq = mm_tn(ds, k)
            if j == 0:
                acc_ref[g] = dq
            else:
                acc_ref[g, block * j :, :] += dq
        dk_ref[0, span, :] = unrotate(dk, span)
        dv_ref[0, span, :] = twice(dv, block)
    for g in range(GROUP):
        dq_ref[g] = unrotate(acc_ref[g] * HEAD ** -0.5, slice(0, seq))


def attend_back(q, k, v, do, cos, sa, sb, first, count, block=256):
    seq = q.shape[1]
    group = lambda at: pl.BlockSpec((GROUP, seq, LANES), lambda n: (n + at, 0, 0))
    one = lambda at: pl.BlockSpec((1, seq, LANES), lambda n: (n + at, 0, 0))
    return call(
        functools.partial(attend_back_body, block),
        [
            jax.ShapeDtypeStruct((GROUP * count, seq, LANES), BF16),
            jax.ShapeDtypeStruct((count, seq, LANES), BF16),
            jax.ShapeDtypeStruct((count, seq, LANES), BF16),
        ],
        (count,),
        [group(first), one(first), one(first), group(first)] + [whole((seq, LANES))] * 3,
        [group(0), one(0), one(0)],
        scratch=[pltpu.VMEM((GROUP, seq, LANES), F32)],
        flops=10 * GROUP * count * seq * seq * LANES,
        moved=4_000_000 * count,
    )(q, k, v, do, cos, sa, sb)


def pairs_to(ref, get, heads, first=0):
    for pair in range((heads + 1) // 2):
        left = get(2 * pair)
        lane = lane_of(left.shape[0])
        right = get(2 * pair + 1).astype(F32) if 2 * pair + 1 < heads else 0.0
        both = jnp.where(lane < HEAD, left.astype(F32), right)
        ref[:, first + LANES * pair : first + LANES * (pair + 1)] = both.astype(BF16)


def mid_body(width, place_ref, o_ref, own_ref, other_ref, e_ref, u_ref, wo_ref, xp_ref, gain_ref,
             op_ref, m_ref, b_ref, df_ref):
    flat = jnp.concatenate([o_ref[head] for head in range(HEADS)], axis=1)
    op = mm_nt(flat, u_ref[: wo_ref.shape[0], :]).astype(BF16)
    op_ref[...] = op
    m = xp_ref[...].astype(F32) + mm(op, wo_ref[...])
    m_ref[...] = m
    scale = lax.rsqrt(jnp.sum(m * m, axis=-1, keepdims=True) / width + EPSILON)
    b_ref[...] = (m * scale * gain_ref[1:2]).astype(BF16)
    ct = own_or_other(place_ref, own_ref, other_ref)
    df_ref[...] = mm_tn(ct, e_ref[:width, :]).astype(BF16)


def middle(place, o, own, other, spread, unpack, w_out, xp, gain, block=512):
    width, half = own.shape
    seq, wide = 2 * half, spread.shape[1]
    rows = lambda n: pl.BlockSpec((block, n), lambda i, *_: (i, 0))
    return call(
        functools.partial(mid_body, width),
        [
            jax.ShapeDtypeStruct((seq, wide), BF16),
            jax.ShapeDtypeStruct((seq, wide), F32),
            jax.ShapeDtypeStruct((seq, wide), BF16),
            jax.ShapeDtypeStruct((seq, wide), BF16),
        ],
        (seq // block,),
        [
            pl.BlockSpec((HEADS, block, LANES), lambda i, *_: (0, i, 0)),
            *halves_specs(half, width, block),
            whole(spread.shape),
            whole(unpack.shape),
            whole(w_out.shape),
            rows(wide),
            whole((8, wide)),
        ],
        [rows(wide)] * 4,
        flops=2 * seq * wide * 4 * wide,
        moved=22_000_000,
        prefetch=1,
    )(place, o, own, other, spread, unpack, w_out, xp, gain)


def ffn_body(turn, place_ref, b_ref, df_ref, *refs):
    near_g, far_g, near_u, far_u = refs[:4]
    downs, refs = (refs[4:8], refs[8:12]), refs[12:]
    before, refs = refs[: 4 * turn], refs[4 * turn :]
    out_ref, db_ref, gu_ref, d_send, d_keep, wg_ref, wu_ref, wd_ref, *carry = refs
    s = pl.program_id(0)
    core, z_me, y_me, x_me = (place_ref[n] for n in range(4))
    chunk = wg_ref.shape[1]
    half = core if turn else 1 - core

    def carried(n):
        return pltpu.make_async_copy(before[2 + n], carry[n], carry[2 + n])

    if turn:

        @pl.when(s == 0)
        def _():
            carried(0).start()
            carried(1).start()

    @pl.when(s == 0)
    def _():
        rows = downs[0][0].shape[2]
        for swapped in range(2):
            for k in range(4):
                z = lax.rem(z_me + 4 - k, 4)

                @pl.when(z // 2 == half)
                def _():
                    ref = downs[swapped][k]
                    for q in range(2):
                        col = pl.multiple_of(2 * chunk * (core ^ swapped) + chunk * q, chunk)
                        for dy in range(2):
                            for dx in range(2):
                                block = lax.rem(z, 2) * 4 + (y_me ^ dy) * 2 + (x_me ^ dx)
                                row = pl.multiple_of(rows * block, 16)
                                piece = ref[q, 2 * dx + dy if q else 2 * dy + dx]
                                wd_ref[pl.ds(row, rows), pl.ds(col, chunk)] = piece

    for dy in range(2):
        for dx in range(2):
            for k in range(4):
                block = lax.rem(z_me + 4 - k, 4) * 4 + (y_me ^ dy) * 2 + (x_me ^ dx)
                row = pl.multiple_of(block * 64, 64)
                wg_ref[pl.ds(row, 64), :] = (far_g if dy else near_g)[4 * dx + k]
                wu_ref[pl.ds(row, 64), :] = (far_u if dx else near_u)[4 * dy + k]

    b, df = b_ref[...], df_ref[...]
    wg, wu = wg_ref[...], wu_ref[...]
    wd = wd_ref[pl.ds(pl.multiple_of(chunk * s, chunk), chunk), :]
    gate = mm(b, wg)
    upper = mm(b, wu)
    sig = jax.nn.sigmoid(gate)
    act = gate * sig
    z = (act * upper).astype(BF16)
    dz = mm_nt(df, wd)
    dg = (dz * upper * sig * (1.0 + gate * (1.0 - sig))).astype(BF16)
    du = (dz * act).astype(BF16)

    @pl.when(s == 0)
    def _():
        out_ref[...] = mm(z, wd)
        db_ref[...] = mm_nt(dg, wg) + mm_nt(du, wu)

    @pl.when(s > 0)
    def _():
        out_ref[...] += mm(z, wd)
        db_ref[...] += mm_nt(dg, wg) + mm_nt(du, wu)

    if turn:

        @pl.when(s == pl.num_programs(0) - 1)
        def _():
            carried(0).wait()
            carried(1).wait()
            out_ref[...] += carry[0][...]
            db_ref[...] += carry[1][...]

    gu_ref[:, :64] = mm_tn(b, dg).astype(BF16).reshape(gu_ref.shape[0], 64, chunk)
    gu_ref[:, 64:] = mm_tn(b, du).astype(BF16).reshape(gu_ref.shape[0], 64, chunk)
    side = df.shape[1] // 2
    for ref, j in ((d_send, 1 - core), (d_keep, core)):
        dwd = mm_tn(z, df_ref[:, pl.ds(pl.multiple_of(side * j, side), side)]).astype(BF16)
        ref[0] = dwd[:, :chunk]
        ref[1] = dwd[:, chunk:]


def feed_forward(place, b, df, columns, downs, turn, before=()):
    seq, wide = b.shape
    blocks, chunks, chunk = 16, 5, 256
    half_of = lambda place: place[0] if turn else 1 - place[0]
    d_shape = jax.ShapeDtypeStruct((2, 2 * chunks * chunk, chunk), BF16)
    d_spec = pl.BlockSpec((2, chunk, chunk), lambda s, place: (0, half_of(place) * chunks + s, 0))
    return call(
        functools.partial(ffn_body, turn),
        [
            jax.ShapeDtypeStruct((seq, wide), F32),
            jax.ShapeDtypeStruct((seq, wide), F32),
            jax.ShapeDtypeStruct((blocks, 128 * chunks, chunk), BF16),
            d_shape,
            d_shape,
        ],
        (chunks,),
        [whole(b.shape), whole(df.shape)]
        + [pl.BlockSpec((blocks // 2, 64, chunk), lambda s, place: (0, s, 0))] * 4
        + [whole(t.shape) for t in downs]
        + [pl.BlockSpec(memory_space=pl.ANY)] * len(before),
        [
            whole((seq, wide)),
            whole((seq, wide)),
            pl.BlockSpec((blocks, 128, chunk), lambda s, place: (0, s, 0)),
            d_spec,
            d_spec,
        ],
        scratch=[
            pltpu.VMEM((wide, chunk), BF16),
            pltpu.VMEM((wide, chunk), BF16),
            pltpu.VMEM((chunks * chunk, wide), BF16),
        ]
        + turn * [pltpu.VMEM((seq, wide), F32)] * 2
        + turn * [pltpu.SemaphoreType.DMA] * 2,
        flops=18 * seq * wide * chunks * chunk,
        moved=40_000_000,
        prefetch=1,
        alias={15: 3, 16: 4} if before else None,
    )(place, b, df, *columns, *downs, *before)


def token_block(steps):
    def at(i, place):
        return jnp.where(i < steps // 2, (1 - place[0]) * (steps // 2) + i, place[0] * (steps // 2) + i - steps // 2)

    return at


def token_specs(steps, block, width):
    half = steps // 2
    return [
        pl.BlockSpec((width, block), lambda i, place: (0, jnp.minimum(i, half - 1))),
        pl.BlockSpec((1, width, block), lambda i, place: (place[0], 0, jnp.maximum(i - half, 0))),
    ]


def put_tokens(send_ref, keep_ref, value):
    early = pl.program_id(0) < pl.num_programs(0) // 2

    @pl.when(early)
    def _():
        send_ref[...] = value.astype(send_ref.dtype)

    @pl.when(jnp.logical_not(early))
    def _():
        keep_ref[0] = value.astype(keep_ref.dtype)


def post_body(width, place_ref, m_ref, acc_ref, db_ref, df_ref, gain_ref, e_ref, u_ref,
              sum_ref, wo_ref, op_ref,
              send_ref, keep_ref, em_ref, do_ref, dwo_send, dwo_keep, dgain_ref, da_ref):
    i = pl.program_id(0)
    m, db = m_ref[...], db_ref[...]
    out = (m + acc_ref[...]).astype(BF16)
    put_tokens(send_ref, keep_ref, mm_nt(e_ref[:width, :], out))
    scale = lax.rsqrt(jnp.sum(m * m, axis=-1, keepdims=True) / width + EPSILON)
    n = m * scale
    c = db * gain_ref[1:2]
    mean = jnp.sum(c * n, axis=-1, keepdims=True) / width
    em = df_ref[...].astype(F32) + scale * (c - n * mean)
    em_ref[...] = em
    da = em.astype(BF16)
    dgain = jnp.sum(db * n, axis=0, keepdims=True)
    block = m.shape[0]
    late = pl.num_programs(0) // 2
    at = jnp.where(i < late, (1 - place_ref[0]) * late + i, place_ref[0] * late + i - late)
    rows = pl.ds(pl.multiple_of(block * at, block), block)
    da_ref[rows, :] = da

    @pl.when(i == 0)
    def _():
        dgain_ref[...] = dgain

    @pl.when(i > 0)
    def _():
        dgain_ref[...] += dgain

    do = mm_nt(da, wo_ref[...]).astype(BF16)
    product = do.astype(F32) * op_ref[rows, :].astype(F32)
    high = product.astype(BF16)
    low = (product - high.astype(F32)).astype(BF16)
    delta = mm(high, sum_ref[...]) + mm(low, sum_ref[...])
    full = jnp.concatenate([do] + [t.astype(BF16) for t in three_terms(delta)], axis=1)
    do = mm(full, u_ref[...]).astype(BF16)
    for head in range(HEADS):
        do_ref[head] = do[:, LANES * head : LANES * (head + 1)]

    @pl.when(i == pl.num_programs(0) - 1)
    def _():
        half = da_ref.shape[1] // 2
        for ref, j in ((dwo_send, 1 - place_ref[0]), (dwo_keep, place_ref[0])):
            dwo = mm_tn(op_ref[...], da_ref[:, pl.ds(pl.multiple_of(half * j, half), half)]).astype(BF16)
            for q in range(2):
                ref[q] = dwo[:, 256 * q : 256 * (q + 1)].reshape(ref.shape[1:])


def after(place, m, acc, db, df, gain, spread, unpack, delta_sum, w_out, op, width, block=512):
    seq, wide = m.shape
    blocks = 16
    steps = seq // block
    at = token_block(steps)
    rows = lambda n: pl.BlockSpec((block, n), lambda i, place: (at(i, place), 0))
    heads = pl.BlockSpec((HEADS, block, LANES), lambda i, place: (0, at(i, place), 0))
    dwo_shape = (2, blocks, wide // blocks, 256)
    consts = (gain, spread, unpack, delta_sum, w_out, op)
    return call(
        functools.partial(post_body, width),
        [
            jax.ShapeDtypeStruct((width, seq // 2), BF16),
            jax.ShapeDtypeStruct((2, width, seq // 2), BF16),
            jax.ShapeDtypeStruct((seq, wide), F32),
            jax.ShapeDtypeStruct((HEADS, seq, LANES), BF16),
            jax.ShapeDtypeStruct(dwo_shape, BF16),
            jax.ShapeDtypeStruct(dwo_shape, BF16),
            jax.ShapeDtypeStruct((1, wide), F32),
        ],
        (steps,),
        [rows(wide)] * 4 + [whole(t.shape) for t in consts],
        token_specs(steps, block, width)
        + [rows(wide), heads, whole(dwo_shape), whole(dwo_shape), whole((1, wide))],
        scratch=[pltpu.VMEM((seq, wide), BF16)],
        flops=2 * seq * wide * 6 * wide,
        moved=40_000_000,
        prefetch=1,
    )(place, m, acc, db, df, *consts)


def weights_body(place_ref, dq_ref, dk_ref, dv_ref, a_ref, w_ref, gain_ref,
                 dgain_ref, flat_ref, send_ref, keep_ref, dw_acc, part_ref, all_ref):
    i = pl.program_id(0)
    heads = HEADS + KV_HEADS

    pairs_to(flat_ref, lambda h: dq_ref[h] if h < HEADS else dk_ref[h - HEADS], heads)
    pairs_to(flat_ref, lambda h: dv_ref[h], KV_HEADS, heads * HEAD)
    block = flat_ref.shape[0]
    all_ref[pl.ds(pl.multiple_of(block * i, block), block), :] = flat_ref[...]

    @pl.when(i == pl.num_programs(0) - 1)
    def _():
        wide = dw_acc.shape[0]
        dw_acc[...] = mm_tn(a_ref[...], all_ref[...])
        total = jnp.sum(dw_acc[...] * w_ref[...].astype(F32), axis=-1, keepdims=True)
        column = lambda row: jnp.broadcast_to(row, (LANES, wide)).T
        gain = column(gain_ref[:1])
        attn = jnp.broadcast_to(total, (wide, LANES)) / jnp.where(gain == 0.0, 1.0, gain)
        lane = lane_of(wide)
        gains = jnp.where(lane == 32, attn, 0.0) + jnp.where(lane == 33, column(dgain_ref[...]), 0.0)
        n_q, n_k = HEADS * HEAD // 2, KV_HEADS * HEAD // 2
        for j in range(2):
            part_ref[:, 768:] = gains.astype(BF16)
            part_ref[:, :n_q] = dw_acc[:, n_q * j : n_q * (j + 1)].astype(BF16)
            for part in range(2):
                at, to = 2 * n_q + n_k * (2 * part + j), n_q + n_k * part
                part_ref[:, to : to + n_k] = dw_acc[:, at : at + n_k].astype(BF16)
            for ref, here in ((keep_ref, place_ref[0] == j), (send_ref, place_ref[0] != j)):

                @pl.when(here)
                def _():
                    ref[...] = part_ref[...].reshape(ref.shape)


def projections_back(place, parts, a, w_qkv, gain, dgain_ffn, block=256):
    seq, wide = a.shape
    blocks = 16
    rows = lambda n: pl.BlockSpec((block, n), lambda i, *_: (i, 0))
    heads = lambda t: pl.BlockSpec((t.shape[0], block, LANES), lambda i, *_: (0, i, 0))
    shape = (blocks, wide // blocks, 896)
    return call(
        weights_body,
        [
            jax.ShapeDtypeStruct((seq, QKV_PAD), BF16),
            jax.ShapeDtypeStruct(shape, BF16),
            jax.ShapeDtypeStruct(shape, BF16),
        ],
        (seq // block,),
        [heads(t) for t in parts] + [whole(a.shape), whole(w_qkv.shape), whole((8, wide)), whole((1, wide))],
        [rows(QKV_PAD), whole(shape), whole(shape)],
        scratch=[
            pltpu.VMEM((wide, QKV_PAD), F32),
            pltpu.VMEM((wide, 896), BF16),
            pltpu.VMEM((seq, QKV_PAD), BF16),
        ],
        flops=2 * seq * wide * QKV_PAD,
        moved=20_000_000,
        prefetch=1,
    )(place, *parts, a, w_qkv, gain, dgain_ffn)


def input_body(width, place_ref, flat_ref, w_ref, xp_ref, em_ref, gain_ref, e_ref, send_ref, keep_ref):
    da = mm_nt(flat_ref[...], w_ref[...])
    xp = xp_ref[...].astype(F32)
    scale = lax.rsqrt(jnp.sum(xp * xp, axis=-1, keepdims=True) / width + EPSILON)
    n = xp * scale
    c = da * gain_ref[:1]
    mean = jnp.sum(c * n, axis=-1, keepdims=True) / width
    grad = em_ref[...] + scale * (c - n * mean)
    put_tokens(send_ref, keep_ref, mm_nt(e_ref[:width, :], grad.astype(BF16)))


def input_back(place, flat, w_qkv, xp, em, gain, spread, width, block=512):
    seq, wide = xp.shape
    steps = seq // block
    at = token_block(steps)
    rows = lambda n: pl.BlockSpec((block, n), lambda i, place: (at(i, place), 0))
    return call(
        functools.partial(input_body, width),
        [
            jax.ShapeDtypeStruct((width, seq // 2), BF16),
            jax.ShapeDtypeStruct((2, width, seq // 2), F32),
        ],
        (steps,),
        [rows(QKV_PAD), whole(w_qkv.shape), rows(wide), rows(wide), whole((8, wide)), whole(spread.shape)],
        token_specs(steps, block, width),
        flops=2 * seq * wide * (QKV_PAD + 2 * width),
        moved=20_000_000,
        prefetch=1,
    )(place, flat, w_qkv, xp, em, gain, spread)


def begin_body(reader, n_in, place_ref, *refs):
    ins, outs = refs[:n_in], refs[n_in:]
    _, _, y, x = (place_ref[n] for n in range(4))
    for side in range(2):
        mine = y if side else x
        for other in range(2):
            for ref, bit in ((outs[2 * side], 1 - mine), (outs[2 * side + 1], mine)):
                block = 2 * bit + other if side else 2 * other + bit
                for row, keep, got in reader(ins, side, block):
                    ref[other, row : row + keep.shape[0]] = add(keep, got)


def begin(place, arrays, reader, rows, count=4):
    n = arrays[0].shape[-1]

    def spec(t):
        lead = t.shape[:-3]
        return pl.BlockSpec((*lead, 4, *t.shape[-2:]), lambda i, place: (0,) * len(lead) + (i, 0, 0))

    shape = jax.ShapeDtypeStruct((2 * count, rows, n), BF16)
    return call(
        functools.partial(begin_body, reader, len(arrays)),
        [shape] * 4,
        (count,),
        [spec(t) for t in arrays],
        [pl.BlockSpec((2, rows, n), lambda i, place: (i, 0, 0))] * 4,
        flops=1,
        moved=16 * count * rows * n * 6,
        prefetch=1,
        vmem=VMEM_SMALL,
    )(place, *arrays)


def turn_body(place_ref, *refs):
    y, x = place_ref[2], place_ref[3]
    for side in range(2):
        keep, got = refs[2 * side : 2 * side + 2]
        mine = x if side else y
        for ref, bit in ((refs[4 + 2 * side], 1 - mine), (refs[5 + 2 * side], mine)):
            ref[0] = add(keep[bit], got[bit])


def turn(place, keeps, gots):
    blocks, rows, n = keeps[0].shape
    shape = jax.ShapeDtypeStruct((blocks // 2, rows, n), BF16)
    return call(
        turn_body,
        [shape] * 4,
        (blocks // 2,),
        [pl.BlockSpec((2, rows, n), lambda i, place: (i, 0, 0))] * 4,
        [pl.BlockSpec((1, rows, n), lambda i, place: (i, 0, 0))] * 4,
        flops=1,
        moved=blocks * rows * n * 12,
        prefetch=1,
        vmem=VMEM_SMALL,
    )(place, keeps[0], gots[0], keeps[1], gots[1])


def climb_body(place_ref, a_keep, a_got, b_keep, b_got, total_ref, *sent):
    for step in range(4):
        block = lax.rem(place_ref[1] + step, 4)
        for side, (keep, got) in enumerate(((a_keep, a_got), (b_keep, b_got))):
            value = keep[block].astype(F32) + got[block].astype(F32)
            if step:
                sent[step - 1][side] = value.astype(BF16)
            else:
                total_ref[side] = value


def climb(place, keeps, gots):
    _, rows, n = keeps[0].shape
    return call(
        climb_body,
        [jax.ShapeDtypeStruct((2, rows, n), F32)] + [jax.ShapeDtypeStruct((2, rows, n), BF16)] * 3,
        (1,),
        [whole(keeps[0].shape)] * 4,
        [whole((2, rows, n))] * 4,
        flops=1,
        moved=rows * n * 50,
        prefetch=1,
        vmem=VMEM_SMALL,
    )(place, keeps[0], gots[0], keeps[1], gots[1])


def unpack_matrix(width, blocks, wide):
    per, step = width // blocks, wide // blocks
    col = jnp.arange(WIDE_HEADS, dtype=jnp.int32)
    feature = col // LANES * HEAD + col % LANES
    place = jnp.where(col % LANES < HEAD, feature // per * step + feature % per, -1)
    term = col % LANES - HEAD
    place = jnp.where((term >= 0) & (term < 3), wide + term * LANES + col // LANES, place)
    return (jnp.arange(wide + 3 * LANES, dtype=jnp.int32)[:, None] == place[None, :]).astype(BF16)


def delta_matrix(width, blocks, wide):
    per, step = width // blocks, wide // blocks
    row = jnp.arange(wide, dtype=jnp.int32)
    head = jnp.where(row % step < per, (row // step * per + row % step) // HEAD, -1)
    return (head[:, None] == jnp.arange(LANES, dtype=jnp.int32)[None, :]).astype(BF16)


def spread_matrix(width, blocks, wide):
    row = jnp.arange(wide, dtype=jnp.int32)
    per, step = width // blocks, wide // blocks
    place = (row // per) * step + row % per
    hit = (place[:, None] == jnp.arange(wide, dtype=jnp.int32)[None, :]) & (row < width)[:, None]
    return hit.astype(BF16)


def tables(positions, segments):
    lane = jnp.arange(LANES, dtype=jnp.int32)
    frequency = 10000.0 ** (-((lane % 32).astype(F32) * 2.0 / HEAD))
    angles = positions.astype(F32)[:, None] * frequency[None, :]
    cos, sin = jnp.cos(angles), jnp.sin(angles)
    high = (lane % HEAD >= 32)[None, :]
    sa = jnp.where(high, sin, 0.0)
    sb = jnp.where(high, 0.0, -sin)
    doc = (lane - HEAD)[None, :]
    mine = segments[:, None] == doc
    in_doc = (doc >= 0) & (doc < DOCS)
    aq = jnp.where(mine & in_doc, MASKED, 0.0)
    ak = jnp.where(in_doc & ~mine, 1.0, 0.0)
    ak = jnp.where((doc >= DOCS) & (doc < DOCS + 3), -1.0, ak)
    return cos, sa, sb, aq, ak


def pad_rows(w, blocks, step=64):
    per = w.shape[0] // blocks
    return jnp.pad(w.reshape(blocks, per, w.shape[1]), ((0, 0), (0, step - per), (0, 0)))


def pad_cols(w, blocks, step=64):
    per = w.shape[1] // blocks
    w = jnp.pad(w.reshape(w.shape[0], blocks, per), ((0, 0), (0, 0), (0, step - per)))
    return w.reshape(w.shape[0], blocks * step)


def cut_rows(w, per):
    return w[:, :per].reshape(w.shape[0] * per, w.shape[2])


def cut_cols(w, per, step=64):
    blocks = w.shape[1] // step
    return w.reshape(w.shape[0], blocks, step)[:, :, :per].reshape(w.shape[0], blocks * per)


def chunked(w, chunk=256):
    blocks, rows, cols = w.shape
    w = w.reshape(blocks, rows, cols // chunk, chunk).transpose(0, 2, 1, 3)
    return w.reshape(blocks, cols // chunk * rows, chunk)


def joined(w, rows):
    blocks, total, chunk = w.shape
    w = w.reshape(blocks, total // rows, rows, chunk).transpose(0, 2, 1, 3)
    return w.reshape(blocks, rows, total // rows * chunk)


def pack_half(w_gate, w_up, w_down, blocks, groups):
    down = pad_cols(w_down, groups)
    down = down.reshape(blocks, w_down.shape[0] // blocks, 2, -1).transpose(0, 2, 1, 3)
    columns = [chunked(pad_rows(w_gate, blocks)), chunked(pad_rows(w_up, blocks))]
    return jnp.concatenate(columns, axis=1), down


def add(left, right):
    return (left.astype(F32) + right.astype(F32)).astype(BF16)


def swap(x):
    return lax.ppermute(x, "ctx", [(0, 1), (1, 0)])


def across(x, bit, count):
    return lax.ppermute(x, "dp", [(i, i ^ (1 << bit)) for i in range(count)])


def pick(x, index, axis=0):
    return lax.dynamic_index_in_dim(x, index, axis, keepdims=False)


def tie(value, *others):
    return lax.optimization_barrier((value, *others))[0]


def tie_all(values, *others):
    return lax.optimization_barrier((*values, *others))[: len(values)]


def along_z(x, step, count):
    return lax.ppermute(x, "dp", [(i, (i + 4 * step) % count) for i in range(count)])


def rise(x, count):
    return [x] + [along_z(x, k, count) for k in (1, 2, 3)]


def spread_first(stack, count):
    half = stack.shape[1] // 2
    first, second = stack[:, :half], stack[:, half:]
    return first, across(first, 0, count), second, across(second, 1, count)


def spread_second(first, first_got, second, second_got, count):
    first, second = jnp.concatenate([first, first_got]), jnp.concatenate([second, second_got])
    return first, across(first, 1, count), second, across(second, 0, count)


def pieces_of(whole_one):
    n = whole_one.shape[1] // 2
    cube = whole_one.reshape(4, 2, 2, 2 * n, -1)
    cube = jnp.stack([cube[(4 - k) % 4] for k in range(4)])
    first, second = cube[:, :, :, :n], cube[:, :, :, n:]
    first, second = first.transpose(1, 2, 0, 3, 4), second.transpose(2, 1, 0, 3, 4)
    flat = lambda t: t.reshape(8, n, -1)
    return flat(first[0]), flat(first[1]), flat(second[0]), flat(second[1])


def downs_of(whole_one):
    cube = whole_one.reshape(4, 2, 2, 2, *whole_one.shape[2:])
    result = []
    for k in range(4):
        first, second = cube[(4 - k) % 4, :, :, 0], cube[(4 - k) % 4, :, :, 1].transpose(1, 0, 2, 3)
        result.append(jnp.stack([first, second]).reshape(2, 4, *whole_one.shape[2:]))
    return result


class RowSum:
    def __init__(self, place, count, arrays, reader, rows):
        self.place, self.count = place, count
        a_sent, a_kept, b_sent, b_kept = begin(place, arrays, reader, rows)
        self.sent, self.kept = [a_sent, b_sent], [a_kept, b_kept]

    def move(self):
        self.got = [across(self.sent[0], 0, self.count), across(self.sent[1], 1, self.count)]

    def wait(self, other):
        self.got = list(lax.optimization_barrier((*self.got, other))[:-1])

    def turn(self, other):
        self.wait(other)
        a_sent, a_kept, b_sent, b_kept = turn(self.place, self.kept, self.got)
        self.sent, self.kept = [a_sent, b_sent], [a_kept, b_kept]

    def move_again(self):
        self.got = [across(self.sent[0], 1, self.count), across(self.sent[1], 0, self.count)]

    def climb(self, other):
        self.wait(other)
        self.kept, *self.sent = climb(self.place, self.kept, self.got)

    def start_up(self):
        return along_z(self.sent[1], 1, self.count)

    def start_down(self):
        return along_z(self.sent[2], 3, self.count)

    def go_up(self, got):
        return along_z(add(self.sent[0], got), 1, self.count)

    def move_up(self):
        return [along_z(self.sent[k - 1], k, self.count) for k in (1, 2, 3)]

    def total(self, *gots):
        total = self.kept
        for got in gots:
            total = total + got.astype(F32)
        return total


def read_rows(ins, side, block):
    half = ins[0].shape[1] // 2
    rows = slice(half * side, half * (side + 1))
    return [(0, ins[0][block, rows], ins[1][block, rows])]


def read_quarters(ins, side, block):
    first = ins[0].shape[2]
    return [(0, ins[0][side, block], ins[1][side, block]), (first, ins[2][side, block], ins[3][side, block])]


def put_other(both, got, core):
    return lax.dynamic_update_slice(both, got[None], (1 - core, 0, 0))


def shards_of_two(inputs, segment_ids, positions, w_query, w_key, w_value, w_out, w_gate, w_up,
                  w_down, gain_attn, gain_ffn, cotangent):
    count = lax.axis_size("dp")
    me, core = lax.axis_index("dp"), lax.axis_index("ctx")
    place = (core, me // 4, (me >> 1) & 1, me & 1)
    place_of = jnp.stack(place).astype(jnp.int32)
    per = gain_attn.shape[0]
    width = per * count
    groups = w_out.shape[1] // per
    hidden = w_down.shape[0]
    n_q, n_k = w_query.shape[1], w_key.shape[1]
    n_qkv = n_q + 2 * n_k

    shard = jnp.concatenate(
        [w_query, w_key, w_value, gain_attn[:, None], gain_ffn[:, None]], axis=1
    )
    shard = jnp.pad(shard, ((0, 0), (0, 896 - n_qkv - 2)))
    shard = jnp.concatenate([shard, pad_cols(w_out, groups)], axis=1)
    shard = jnp.pad(shard, ((0, 64 - per), (0, 0)))
    columns, down = pack_half(w_gate, w_up, w_down, 1, groups)
    columns, down = columns[0], down[0]

    level = rise(shard, count)
    d_first, d_second = down[:1], down[1:]
    d_first = jnp.concatenate([d_first, across(d_first, 0, count)])
    d_second = jnp.concatenate([d_second, across(d_second, 1, count)])
    d_first = jnp.concatenate([d_first, across(d_first, 1, count)])
    d_second = jnp.concatenate([d_second, across(d_second, 0, count)])
    down = jnp.stack([d_first, d_second])
    stack = tie(jnp.stack(level), down)
    part = spread_first(stack, count)
    c_level = rise(tie(columns, stack), count)
    near_far = spread_second(*tie_all(part, c_level[1]), count)
    near_far = tie_all(near_far, *c_level[2:])
    pieces = near_far + tuple(swap(t) for t in near_far)
    c_level = tie_all(c_level, near_far[0])
    c_part = spread_first(jnp.stack(c_level), count)
    down = tie(down, *c_level)
    down_next = along_z(down, 1, count)

    def halves(x):
        x = jnp.swapaxes(x[:, 0], 1, 2)
        return pick(x, core), swap(pick(x, 1 - core))

    wide = count * 64
    spread, unpack = spread_matrix(width, count, wide), unpack_matrix(width, count, wide)
    delta_sum = delta_matrix(width, count, wide)
    cos, sa, sb, aq, ak = tables(pick(positions[:, 0], core), pick(segment_ids[:, 0], core))
    xp, a, q, k, v, w_qkv, w_o, gains = pre_attention(
        place_of, *halves(inputs), spread, tie_all(pieces, c_part[0], c_part[2], down), cos, sa, sb, aq, ak
    )
    columns = spread_second(*tie_all(c_part, q), count)
    near_got = [swap(t) for t in columns[::2]]
    down_next = tie(down_next, q)
    down_prev, down_far = along_z(down, 3, count), along_z(down_next, 1, count)
    down_got = [swap(t) for t in (down, down_next)]
    q = tie(q, *columns[::2], down_next)
    o, q2 = attend(q, k, v)
    columns = list(columns)
    columns[1], columns[3], down_prev, down_far = tie_all((columns[1], columns[3], down_prev, down_far), o)
    o = tie(o, columns[1], columns[3], down_prev, down_far)
    far_got = [swap(t) for t in columns[1::2]]
    down_got += [swap(down_far), swap(down_prev)]
    op, m, b, df = middle(
        place_of, o, *halves(cotangent), spread, unpack, w_o, xp, gains
    )
    downs = [down, down_next, down_far, down_prev] + down_got
    other = (near_got[0], far_got[0], near_got[1], far_got[1])

    acc0, db0, gu_send, d_send, d_keep = feed_forward(place_of, b, df, other, downs, 0)
    gu_got = swap(gu_send)
    acc, db, gu_keep, d_send, d_keep = feed_forward(
        place_of, tie(b, gu_send), df, columns, downs, 1, (d_send, d_keep, acc0, db0)
    )
    one = RowSum(place_of, count, (gu_keep, tie(gu_got, acc)), read_rows, 320)
    one.move()
    blocked = lambda t: t.reshape(2, count, hidden, 256)
    d_got = swap(d_send)
    m = tie(m, *one.sent, d_send)
    out_send, outs, em, do, o_send, o_keep, dgf = after(
        place_of, m, acc, db, df, gains, spread, unpack, delta_sum, w_o, op, width
    )
    o_got = swap(o_send)
    one.turn(em)
    one.move_again()
    two = RowSum(
        place_of, count, (blocked(d_keep), blocked(tie(d_got, em)), o_keep, o_got), read_quarters, 224
    )
    two.move()
    do = tie(do, *one.sent, *two.sent)
    parts = attend_back(q2, k, v, do, cos, sa, sb, 0, KV_HEADS)
    outs = put_other(outs, tie(swap(out_send), parts[0]), core)
    one.climb(parts[0])
    up, down = one.start_up(), one.start_down()
    two.turn(parts[0])
    two.move_again()
    a = tie(a, *one.sent, *two.sent)
    flat, p_send, p_keep = projections_back(place_of, parts, a, w_qkv, gains, dgf)
    up, down, *two.got = tie_all((up, down, *two.got), flat)
    p_got = swap(tie(p_send, up))
    two.climb(flat)
    one_up, one_down, two_up = one.go_up(up), down, two.start_up()
    three = RowSum(place_of, count, (p_keep, p_got), read_rows, 32)
    three.move()
    flat = tie(flat, *two.sent, *three.sent)
    gi_send, gis = input_back(place_of, flat, w_qkv, xp, em, gains, spread, width)
    *three.got, one_up, two_up = tie_all((*three.got, one_up, two_up), gis)
    gi_got = swap(tie(gi_send, one_up))
    three.turn(one_up)
    three.move_again()
    two_up, two_down = two.go_up(two_up), two.start_down()
    gis = put_other(gis, gi_got.astype(F32), core)
    first = one.total(one_up, one_down)
    three.climb(first)
    last_got = three.move_up()
    second, third = two.total(two_up, two_down), three.total(*last_got)
    third = third.reshape(64, 896)[:per]
    gu = first.reshape(5, 2, 64, 256)
    wide_of = lambda t: t.transpose(1, 0, 2).reshape(t.shape[1], -1)
    tokens = lambda t: jnp.swapaxes(t, 1, 2)[:, None]
    return (
        tokens(outs),
        tokens(gis),
        third[:, :n_q],
        third[:, n_q : n_q + n_k],
        third[:, n_q + n_k : n_qkv],
        cut_cols(wide_of(second[:, 160:])[:per], per),
        wide_of(gu[:, 0])[:per],
        wide_of(gu[:, 1])[:per],
        cut_cols(wide_of(second[:, :160]), per),
        third[:, n_qkv],
        third[:, n_qkv + 1],
    )


def shards_of_many(inputs, segment_ids, positions, w_query, w_key, w_value, w_out, w_gate, w_up,
                   w_down, gain_attn, gain_ffn, cotangent):
    count, cores = lax.axis_size("dp"), lax.axis_size("ctx")
    core = lax.axis_index("ctx")
    share = cores // MICRO
    per = gain_attn.shape[0]
    width = per * count

    def gathered(w):
        return lax.all_gather(lax.all_gather(w, "dp", axis=0, tiled=True), "ctx", axis=1, tiled=True)

    full = [gathered(w) for w in (w_query, w_key, w_value, w_out, w_gate, w_up, w_down)]
    gain_pair = lax.all_gather(jnp.stack([gain_attn, gain_ffn]), "dp", axis=1, tiled=True)
    w_o, w_g, w_u, w_d = full[3:]
    half = lambda w, j: w[:, w.shape[1] // 2 * j : w.shape[1] // 2 * (j + 1)]
    packs = [pack_half(half(w_g, j), half(w_u, j), half(w_d, j), count, count // 2) for j in range(2)]
    columns = [pieces_of(p[0]) for p in packs]
    downs = [t for p in packs for t in downs_of(p[1])]
    pieces = []
    for j in range(2):
        parts = [half(w, j) for w in full[:3]] + [gain_pair.T]
        part = jnp.concatenate(parts, axis=1)
        part = jnp.pad(part, ((0, 0), (0, 896 - part.shape[1])))
        part = jnp.concatenate([part, pad_cols(half(w_o, j), count // 2)], axis=1)
        pieces += pieces_of(pad_rows(part, count))
    which = core // share

    def sequence(x):
        whole_one = pick(lax.all_gather(x[:, 0], "ctx", axis=1, tiled=True), which).T
        return whole_one[:, : whole_one.shape[1] // 2], whole_one[:, whole_one.shape[1] // 2 :]

    place = jnp.zeros((4,), jnp.int32)
    wide = count * 64
    spread, unpack = spread_matrix(width, count, wide), unpack_matrix(width, count, wide)
    delta_sum = delta_matrix(width, count, wide)
    cos, sa, sb, aq, ak = tables(pick(positions[:, 0], which), pick(segment_ids[:, 0], which))
    xp, a, q, k, v, w_qkv, w_o, gains = pre_attention(
        place, *sequence(inputs), spread, pieces, cos, sa, sb, aq, ak
    )
    o, q2 = attend(q, k, v)
    op, m, b, df = middle(place, o, *sequence(cotangent), spread, unpack, w_o, xp, gains)
    acc0, db0, gu_send, d_send, d_keep = feed_forward(place, b, df, columns[1], downs, 0)
    acc, db, gu_keep, d_send, d_keep = feed_forward(
        place, b, df, columns[0], downs, 1, (d_send, d_keep, acc0, db0)
    )
    out_send, outs, em, do, o_send, o_keep, dgf = after(
        place, m, acc, db, df, gains, spread, unpack, delta_sum, w_o, op, width
    )
    parts = attend_back(q2, k, v, do, cos, sa, sb, 0, KV_HEADS)
    flat, p_send, p_keep = projections_back(place, parts, a, w_qkv, gains, dgf)
    gi_send, gis = input_back(place, flat, w_qkv, xp, em, gains, spread, width)

    parts = [cut_rows(p, per) for p in (p_keep, p_send)]
    n_q, n_k = HEADS * HEAD // 2, KV_HEADS * HEAD // 2
    both = lambda at, n: jnp.concatenate([p[:, at : at + n] for p in parts], axis=1)
    side = lambda t: jnp.concatenate([t[0], t[1]], axis=-1)

    def wide_of(index):
        every = []
        for t in (gu_keep, gu_send):
            t = t.reshape(count, 5, 2, 64, 256)[:, :, index]
            every.append(cut_rows(t.transpose(0, 2, 1, 3).reshape(count, 64, -1), per))
        return jnp.concatenate(every, axis=1)

    grads = [
        both(0, n_q),
        both(n_q * 1, n_k),
        both(n_q + n_k, n_k),
        cut_cols(cut_rows(jnp.concatenate([side(o_keep), side(o_send)], axis=-1), per), per),
        wide_of(0),
        wide_of(1),
        cut_cols(
            jnp.concatenate([side(d_keep), side(d_send)], axis=-1),
            per,
        ),
    ]

    def summed(g):
        g = lax.psum_scatter(g * (1.0 / share), "dp", scatter_dimension=0, tiled=True)
        return lax.psum_scatter(g, "ctx", scatter_dimension=1, tiled=True).astype(F32)

    sums = [summed(g.astype(BF16)) for g in grads]
    dgain = parts[0][:, 2 * n_k + n_q : 2 * n_k + n_q + 2].astype(F32).T * (1.0 / share)
    dgain = lax.psum_scatter(lax.psum(dgain, "ctx"), "dp", scatter_dimension=1, tiled=True)

    def tokens(seq):
        rows = seq.shape[0] // cores
        every = lax.all_gather(seq, "ctx", axis=0, tiled=False)
        return lax.dynamic_slice_in_dim(every[::share], core * rows, rows, axis=1)[:, None]

    out = jnp.concatenate([outs[0], out_send], axis=1).T
    gi = jnp.concatenate([gis[0], gi_send.astype(F32)], axis=1).T
    return (tokens(out), tokens(gi), *sums, dgain[0], dgain[1])


def solution(mesh):
    two = mesh.shape["ctx"] == MICRO and mesh.shape["dp"] == 16
    matrices = (P("dp", "ctx"),) * 7 + (P("dp"), P("dp"))
    tokens = P(None, "dp", "ctx", None)
    return jax.shard_map(
        shards_of_two if two else shards_of_many,
        mesh=mesh,
        in_specs=(tokens, P(None, "dp", None), P(None, "dp", None)) + matrices + (tokens,),
        out_specs=(tokens, tokens) + matrices,
        check_vma=False,
    )
```

```python
import functools

import jax
import jax.numpy as jnp
from jax import lax
from jax.experimental import pallas as pl
from jax.experimental.pallas import tpu as pltpu
from jax.sharding import PartitionSpec as P

HEADS = 15
KV_HEADS = 5
HEAD = 64
MICRO = 2
GROUP = 3
DOCS = 4

EPSILON = 1e-05
MASKED = -1e30
LANES = 128
QKV = (HEADS + 2 * KV_HEADS) * HEAD
QKV_PAD = 1664
VMEM_LIMIT = 56 * 1024 * 1024
PACK = 1408
VMEM_SMALL = 24 * 1024 * 1024
WIDE_HEADS = HEADS * LANES
F32 = jnp.float32
BF16 = jnp.bfloat16


def up(value, step):
    return -(-value // step) * step


def mm(left, right):
    return lax.dot_general(left, right, (((1,), (0,)), ((), ())), preferred_element_type=F32)


def mm_nt(left, right):
    return lax.dot_general(left, right, (((1,), (1,)), ((), ())), preferred_element_type=F32)


def mm_tn(left, right):
    return lax.dot_general(left, right, (((0,), (0,)), ((), ())), preferred_element_type=F32)


def call(body, out_shape, grid, in_specs, out_specs, scratch=(), flops=0, moved=0, prefetch=0, alias=None,
         vmem=VMEM_LIMIT):
    return pl.pallas_call(
        body,
        out_shape=out_shape,
        grid_spec=pltpu.PrefetchScalarGridSpec(
            num_scalar_prefetch=prefetch,
            grid=grid,
            in_specs=in_specs,
            out_specs=out_specs,
            scratch_shapes=scratch,
        ),
        input_output_aliases=alias or {},
        compiler_params=pltpu.CompilerParams(vmem_limit_bytes=vmem),
        cost_estimate=pl.CostEstimate(flops=flops, bytes_accessed=moved, transcendentals=0),
    )


def whole(shape):
    return pl.BlockSpec(shape, lambda *_: (0,) * len(shape), pipeline_mode=pl.Buffered(1))


def lane_of(rows):
    return lax.broadcasted_iota(jnp.int32, (rows, LANES), 1)


def three_terms(column):
    high = column.astype(BF16).astype(F32)
    rest = column - high
    mid = rest.astype(BF16).astype(F32)
    return high, mid, rest - mid


def put_terms(base, column, lane, first):
    high, mid, low = three_terms(column)
    base = jnp.where(lane == first, high, base)
    base = jnp.where(lane == first + 1, mid, base)
    return jnp.where(lane == first + 2, low, base)


def build_weights(place_ref, piece_refs, stage_ref, w_ref, wo_ref):
    core, z, y, x = (place_ref[n] for n in range(4))
    for swapped in range(2):
        near_a, far_a, near_b, far_b = piece_refs[4 * swapped : 4 * swapped + 4]
        to = jnp.bitwise_xor(core, swapped)
        for dy in range(2):
            for dx in range(2):
                for k in range(4):
                    block = lax.rem(z + 4 - k, 4) * 4 + (y ^ dy) * 2 + (x ^ dx)
                    row = pl.multiple_of(block * 64, 64)
                    stage_ref[to, pl.ds(row, 32), :] = (far_a if dy else near_a)[4 * dx + k]
                    stage_ref[to, pl.ds(row + 32, 32), :] = (far_b if dx else near_b)[4 * dy + k]
    n_q, n_k = HEADS * HEAD // 2, KV_HEADS * HEAD // 2
    for j in range(2):
        w_ref[:, n_q * j : n_q * (j + 1)] = stage_ref[j, :, :n_q]
        for part in range(2):
            to, at = 2 * n_q + n_k * (2 * part + j), n_q + n_k * part
            w_ref[:, to : to + n_k] = stage_ref[j, :, at : at + n_k]
        half = wo_ref.shape[1] // 2
        wo_ref[:, half * j : half * (j + 1)] = stage_ref[j, :, PACK - half :]
    w_ref[:, QKV:] = jnp.zeros((w_ref.shape[0], QKV_PAD - QKV), BF16)


def projections(xp, scale, w_ref, gain_ref, cos_ref, sa_ref, sb_ref, aq_ref, ak_ref,
                xp_ref, a_ref, q_ref, k_ref, v_ref):
    a = (xp * scale * gain_ref[:1]).astype(BF16)
    xp_ref[...] = xp.astype(BF16)
    a_ref[...] = a
    t = mm(a, w_ref[...])
    lane = lane_of(t.shape[0])
    low = lane < HEAD
    cos, sa, sb, aq, ak = cos_ref[...], sa_ref[...], sb_ref[...], aq_ref[...], ak_ref[...]
    for pair in range((HEADS + KV_HEADS) // 2):
        tt = t[:, LANES * pair : LANES * (pair + 1)]
        rot = tt * cos + pltpu.roll(tt, 32, 1) * sa + pltpu.roll(tt, 96, 1) * sb
        for half in range(2):
            head = 2 * pair + half
            val = rot if half == 0 else pltpu.roll(rot, 64, 1)
            if head < HEADS:
                q_ref[head] = jnp.where(low, val * HEAD ** -0.5, aq).astype(BF16)
            else:
                k_ref[head - HEADS] = jnp.where(low, val, ak).astype(BF16)
    av = jnp.where(lane < HEAD + 3, -1.0, 0.0)
    for head in range(KV_HEADS):
        first = (HEADS + KV_HEADS) * HEAD + LANES * (head // 2)
        tt = t[:, first : first + LANES]
        val = tt if head % 2 == 0 else pltpu.roll(tt, 64, 1)
        v_ref[head] = jnp.where(low, val, av).astype(BF16)


def own_or_other(place_ref, own_ref, other_ref):
    first = pl.program_id(0) < pl.num_programs(0) // 2
    mine = first == (place_ref[0] == 0)
    return jnp.where(mine, own_ref[...], other_ref[...])


def pre_body(width, place_ref, own_ref, other_ref, e_ref, *refs):
    pieces, refs = refs[:8], refs[8:]
    *rest, w_ref, wo_ref, gain_ref, stage_ref = refs

    @pl.when(pl.program_id(0) == 0)
    def _():
        build_weights(place_ref, pieces, stage_ref, w_ref, wo_ref)
        gain_ref[...] = stage_ref[0, :, 768:896].astype(F32).T[32:40]

    xp = mm_tn(own_or_other(place_ref, own_ref, other_ref), e_ref[:width, :])
    scale = lax.rsqrt(jnp.sum(xp * xp, axis=-1, keepdims=True) / width + EPSILON)
    projections(xp, scale, w_ref, gain_ref, *rest)


def halves_specs(rows, width, block):
    steps = rows // block
    return [pl.BlockSpec((width, block), lambda i, *_: (0, i % steps))] * 2


def pre_attention(place, own, other, spread, pieces, cos, sa, sb, aq, ak, block=512):
    width, half = own.shape
    seq, wide = 2 * half, spread.shape[1]
    rows = lambda n: pl.BlockSpec((block, n), lambda i, *_: (i, 0))
    heads = lambda n: pl.BlockSpec((n, block, LANES), lambda i, *_: (0, i, 0))
    return call(
        functools.partial(pre_body, width),
        [
            jax.ShapeDtypeStruct((seq, wide), BF16),
            jax.ShapeDtypeStruct((seq, wide), BF16),
            jax.ShapeDtypeStruct((HEADS, seq, LANES), BF16),
            jax.ShapeDtypeStruct((KV_HEADS, seq, LANES), BF16),
            jax.ShapeDtypeStruct((KV_HEADS, seq, LANES), BF16),
            jax.ShapeDtypeStruct((wide, QKV_PAD), BF16),
            jax.ShapeDtypeStruct((wide, wide), BF16),
            jax.ShapeDtypeStruct((8, wide), F32),
        ],
        (seq // block,),
        halves_specs(half, width, block)
        + [whole(spread.shape)]
        + [whole(w.shape) for w in pieces]
        + [rows(LANES)] * 5,
        [rows(wide), rows(wide), heads(HEADS), heads(KV_HEADS), heads(KV_HEADS)]
        + [whole((wide, QKV_PAD)), whole((wide, wide)), whole((8, wide))],
        scratch=[pltpu.VMEM((2, wide, PACK), BF16)],
        flops=2 * seq * wide * (width + QKV_PAD),
        moved=20_000_000,
        prefetch=1,
    )(place, own, other, spread, *pieces, cos, sa, sb, aq, ak)


def attend_body(block, q_ref, k_ref, v_ref, o_ref, q2_ref):
    seq = k_ref.shape[1]
    rows = GROUP * block
    below = lax.broadcasted_iota(jnp.int32, (block, block), 0) >= lax.broadcasted_iota(
        jnp.int32, (block, block), 1
    )
    below = jnp.concatenate([below.astype(F32)] * GROUP, axis=0) > 0.5
    lane = lane_of(rows)
    for i in range(seq // block):
        span = slice(block * i, block * (i + 1))
        q = q_ref[:, span, :].reshape(rows, LANES)
        s_in = jnp.where(below, mm_nt(q, k_ref[0, span, :]), MASKED)
        top = jnp.max(s_in, axis=-1, keepdims=True)
        if i:
            s_left = mm_nt(q, k_ref[0, : block * i, :])
            top = jnp.maximum(top, jnp.max(s_left, axis=-1, keepdims=True))
        ext = mm(jnp.exp(s_in - top).astype(BF16), v_ref[0, span, :])
        if i:
            ext = ext + mm(jnp.exp(s_left - top).astype(BF16), v_ref[0, : block * i, :])
        total = -ext[:, HEAD : HEAD + 1]
        o = ext / total
        o = jnp.where(lane < HEAD, o, pltpu.roll(o, 64, 1))
        o_ref[:, span, :] = o.reshape(GROUP, block, LANES).astype(BF16)
        q2 = put_terms(q.astype(F32), top + jnp.log(total), lane, HEAD + DOCS)
        q2_ref[:, span, :] = q2.reshape(GROUP, block, LANES).astype(BF16)


def attend(q, k, v, block=256):
    seq = q.shape[1]
    group = pl.BlockSpec((GROUP, seq, LANES), lambda n: (n, 0, 0))
    one = pl.BlockSpec((1, seq, LANES), lambda n: (n, 0, 0))
    shape = jax.ShapeDtypeStruct(q.shape, BF16)
    return call(
        functools.partial(attend_body, block),
        [shape, shape],
        (KV_HEADS,),
        [group, one, one],
        [group, group],
        flops=4 * HEADS * seq * seq * LANES,
        moved=15_000_000,
    )(q, k, v)


def attend_back_body(block, q_ref, k_ref, v_ref, do_ref, cos_ref, sa_ref, sb_ref,
                     dq_ref, dk_ref, dv_ref, acc_ref):
    seq = k_ref.shape[1]
    above = lax.broadcasted_iota(jnp.int32, (block, block), 0) <= lax.broadcasted_iota(
        jnp.int32, (block, block), 1
    )
    lane = lane_of(seq)

    def unrotate(t, span):
        rows = span.stop - span.start
        rot = (
            t * cos_ref[span, :]
            - pltpu.roll(t, 32, 1) * sa_ref[span, :]
            - pltpu.roll(t, 96, 1) * sb_ref[span, :]
        )
        return twice(rot, rows)

    def twice(t, rows):
        return jnp.where(lane[:rows] < HEAD, t, pltpu.roll(t, 64, 1)).astype(BF16)

    for j in range(seq // block):
        span = slice(block * j, block * (j + 1))
        k, v = k_ref[0, span, :], v_ref[0, span, :]
        dk = jnp.zeros((block, LANES), F32)
        dv = jnp.zeros((block, LANES), F32)
        for g in range(GROUP):
            q, do = q_ref[g, block * j :, :], do_ref[g, block * j :, :]
            p = jnp.exp(mm_nt(k, q))
            inner = jnp.where(above, p[:, :block], 0.0)
            p = inner if p.shape[1] == block else jnp.concatenate([inner, p[:, block:]], axis=1)
            ds = (p * mm_nt(v, do)).astype(BF16)
            dv = dv + mm(p.astype(BF16), do)
            dk = dk + mm(ds, q)
            dq = mm_tn(ds, k)
            if j == 0:
                acc_ref[g] = dq
            else:
                acc_ref[g, block * j :, :] += dq
        dk_ref[0, span, :] = unrotate(dk, span)
        dv_ref[0, span, :] = twice(dv, block)
    for g in range(GROUP):
        dq_ref[g] = unrotate(acc_ref[g] * HEAD ** -0.5, slice(0, seq))


def attend_back(q, k, v, do, cos, sa, sb, first, count, block=256):
    seq = q.shape[1]
    group = lambda at: pl.BlockSpec((GROUP, seq, LANES), lambda n: (n + at, 0, 0))
    one = lambda at: pl.BlockSpec((1, seq, LANES), lambda n: (n + at, 0, 0))
    return call(
        functools.partial(attend_back_body, block),
        [
            jax.ShapeDtypeStruct((GROUP * count, seq, LANES), BF16),
            jax.ShapeDtypeStruct((count, seq, LANES), BF16),
            jax.ShapeDtypeStruct((count, seq, LANES), BF16),
        ],
        (count,),
        [group(first), one(first), one(first), group(first)] + [whole((seq, LANES))] * 3,
        [group(0), one(0), one(0)],
        scratch=[pltpu.VMEM((GROUP, seq, LANES), F32)],
        flops=10 * GROUP * count * seq * seq * LANES,
        moved=4_000_000 * count,
    )(q, k, v, do, cos, sa, sb)


def pairs_to(ref, get, heads, first=0):
    for pair in range((heads + 1) // 2):
        left = get(2 * pair)
        lane = lane_of(left.shape[0])
        right = get(2 * pair + 1).astype(F32) if 2 * pair + 1 < heads else 0.0
        both = jnp.where(lane < HEAD, left.astype(F32), right)
        ref[:, first + LANES * pair : first + LANES * (pair + 1)] = both.astype(BF16)


def mid_body(width, place_ref, o_ref, own_ref, other_ref, e_ref, u_ref, wo_ref, xp_ref, gain_ref,
             op_ref, m_ref, b_ref, df_ref):
    flat = jnp.concatenate([o_ref[head] for head in range(HEADS)], axis=1)
    op = mm_nt(flat, u_ref[: wo_ref.shape[0], :]).astype(BF16)
    op_ref[...] = op
    m = xp_ref[...].astype(F32) + mm(op, wo_ref[...])
    m_ref[...] = m
    scale = lax.rsqrt(jnp.sum(m * m, axis=-1, keepdims=True) / width + EPSILON)
    b_ref[...] = (m * scale * gain_ref[1:2]).astype(BF16)
    ct = own_or_other(place_ref, own_ref, other_ref)
    df_ref[...] = mm_tn(ct, e_ref[:width, :]).astype(BF16)


def middle(place, o, own, other, spread, unpack, w_out, xp, gain, block=512):
    width, half = own.shape
    seq, wide = 2 * half, spread.shape[1]
    rows = lambda n: pl.BlockSpec((block, n), lambda i, *_: (i, 0))
    return call(
        functools.partial(mid_body, width),
        [
            jax.ShapeDtypeStruct((seq, wide), BF16),
            jax.ShapeDtypeStruct((seq, wide), F32),
            jax.ShapeDtypeStruct((seq, wide), BF16),
            jax.ShapeDtypeStruct((seq, wide), BF16),
        ],
        (seq // block,),
        [
            pl.BlockSpec((HEADS, block, LANES), lambda i, *_: (0, i, 0)),
            *halves_specs(half, width, block),
            whole(spread.shape),
            whole(unpack.shape),
            whole(w_out.shape),
            rows(wide),
            whole((8, wide)),
        ],
        [rows(wide)] * 4,
        flops=2 * seq * wide * 4 * wide,
        moved=22_000_000,
        prefetch=1,
    )(place, o, own, other, spread, unpack, w_out, xp, gain)


def ffn_body(turn, place_ref, b_ref, df_ref, *refs):
    gates, ups, downs, refs = refs[:4], refs[4:8], refs[8:24], refs[24:]
    before, refs = refs[: 4 * turn], refs[4 * turn :]
    out_ref, db_ref, gu_ref, d_send, d_keep, wg_ref, wu_ref, wd_ref, down_sem, *carry = refs
    s = pl.program_id(0)
    core, z_me, y_me, x_me = (place_ref[n] for n in range(4))
    chunk = wg_ref.shape[1]
    half = core if turn else 1 - core
    rows = wd_ref.shape[0] // 8

    def carried(n):
        return pltpu.make_async_copy(before[2 + n], carry[n], carry[2 + n])

    def down_copies():
        for swapped in range(2):
            for q in range(2):
                for near in range(4):
                    for up_z in range(2):
                        k = lax.rem(z_me + 4 - (2 * half + up_z), 4)
                        block = up_z * 4 + (y_me ^ (near // 2)) * 2 + (x_me ^ (near % 2))
                        row = pl.multiple_of(rows * block, 16)
                        col = pl.multiple_of(2 * chunk * (core ^ swapped) + chunk * q, chunk)
                        ref = downs[8 * swapped + 4 * q + near]
                        yield pltpu.make_async_copy(
                            ref.at[k, pl.ds(ref.shape[1] - rows, rows), :],
                            wd_ref.at[pl.ds(row, rows), pl.ds(col, chunk)],
                            down_sem.at[16 * swapped + 8 * q + 2 * near + up_z],
                        )

    @pl.when(s == 0)
    def _():
        for copy in down_copies():
            copy.start()
        if turn:
            carried(0).start()
            carried(1).start()

    for near in range(4):
        for k in range(4):
            block = lax.rem(z_me + 4 - k, 4) * 4 + (y_me ^ (near // 2)) * 2 + (x_me ^ (near % 2))
            row = pl.multiple_of(block * 64, 64)
            wg_ref[pl.ds(row, 64), :] = gates[near][k]
            wu_ref[pl.ds(row, 64), :] = ups[near][k]

    b, df = b_ref[...], df_ref[...]
    wg, wu = wg_ref[...], wu_ref[...]
    gate = mm(b, wg)
    upper = mm(b, wu)

    @pl.when(s == 0)
    def _():
        for copy in down_copies():
            copy.wait()

    wd = wd_ref[pl.ds(pl.multiple_of(chunk * s, chunk), chunk), :]
    sig = jax.nn.sigmoid(gate)
    act = gate * sig
    z = (act * upper).astype(BF16)
    dz = mm_nt(df, wd)
    dg = (dz * upper * (sig + act * (1.0 - sig))).astype(BF16)
    du = (dz * act).astype(BF16)

    @pl.when(s == 0)
    def _():
        out_ref[...] = mm(z, wd)
        db_ref[...] = mm_nt(dg, wg) + mm_nt(du, wu)

    @pl.when(s > 0)
    def _():
        out_ref[...] += mm(z, wd)
        db_ref[...] += mm_nt(dg, wg) + mm_nt(du, wu)

    if turn:

        @pl.when(s == pl.num_programs(0) - 1)
        def _():
            carried(0).wait()
            carried(1).wait()
            out_ref[...] += carry[0][...]
            db_ref[...] += carry[1][...]

    gu_ref[:, :64] = mm_tn(b, dg).astype(BF16).reshape(gu_ref.shape[0], 64, chunk)
    gu_ref[:, 64:] = mm_tn(b, du).astype(BF16).reshape(gu_ref.shape[0], 64, chunk)
    side = df.shape[1] // 2
    for ref, j in ((d_send, 1 - core), (d_keep, core)):
        dwd = mm_tn(z, df_ref[:, pl.ds(pl.multiple_of(side * j, side), side)]).astype(BF16)
        ref[0] = dwd[:, :chunk]
        ref[1] = dwd[:, chunk:]


def feed_forward(place, b, df, mine, other, turn, before=()):
    seq, wide = b.shape
    blocks, chunks, chunk = 16, 5, 256
    columns = mine if turn else other
    any_spec = pl.BlockSpec(memory_space=pl.ANY)
    half_of = lambda place: place[0] if turn else 1 - place[0]
    d_shape = jax.ShapeDtypeStruct((2, 2 * chunks * chunk, chunk), BF16)
    d_spec = pl.BlockSpec((2, chunk, chunk), lambda s, place: (0, half_of(place) * chunks + s, 0))
    return call(
        functools.partial(ffn_body, turn),
        [
            jax.ShapeDtypeStruct((seq, wide), F32),
            jax.ShapeDtypeStruct((seq, wide), F32),
            jax.ShapeDtypeStruct((blocks, 128 * chunks, chunk), BF16),
            d_shape,
            d_shape,
        ],
        (chunks,),
        [whole(b.shape), whole(df.shape)]
        + [pl.BlockSpec((4, 64, chunk), lambda s, place: (0, s, 0))] * 8
        + [any_spec] * (16 + len(before)),
        [
            whole((seq, wide)),
            whole((seq, wide)),
            pl.BlockSpec((blocks, 128, chunk), lambda s, place: (0, s, 0)),
            d_spec,
            d_spec,
        ],
        scratch=[
            pltpu.VMEM((wide, chunk), BF16),
            pltpu.VMEM((wide, chunk), BF16),
            pltpu.VMEM((chunks * chunk, wide), BF16),
            pltpu.SemaphoreType.DMA((32,)),
        ]
        + turn * [pltpu.VMEM((seq, wide), F32)] * 2
        + turn * [pltpu.SemaphoreType.DMA] * 2,
        flops=18 * seq * wide * chunks * chunk,
        moved=40_000_000,
        prefetch=1,
        alias={27: 3, 28: 4} if before else None,
    )(place, b, df, *columns, *mine, *other, *before)


def token_block(steps):
    def at(i, place):
        return jnp.where(i < steps // 2, (1 - place[0]) * (steps // 2) + i, place[0] * (steps // 2) + i - steps // 2)

    return at


def token_specs(steps, block, width):
    half = steps // 2
    return [
        pl.BlockSpec((width, block), lambda i, place: (0, jnp.minimum(i, half - 1))),
        pl.BlockSpec((1, width, block), lambda i, place: (place[0], 0, jnp.maximum(i - half, 0))),
    ]


def put_tokens(send_ref, keep_ref, value):
    early = pl.program_id(0) < pl.num_programs(0) // 2

    @pl.when(early)
    def _():
        send_ref[...] = value.astype(send_ref.dtype)

    @pl.when(jnp.logical_not(early))
    def _():
        keep_ref[0] = value.astype(keep_ref.dtype)


def post_body(width, place_ref, m_ref, acc_ref, db_ref, df_ref, gain_ref, e_ref, u_ref,
              sum_ref, wo_ref, op_ref,
              send_ref, keep_ref, em_ref, do_ref, dwo_send, dwo_keep, dgain_ref, da_ref):
    i = pl.program_id(0)
    m, db = m_ref[...], db_ref[...]
    out = (m + acc_ref[...]).astype(BF16)
    put_tokens(send_ref, keep_ref, mm_nt(e_ref[:width, :], out))
    scale = lax.rsqrt(jnp.sum(m * m, axis=-1, keepdims=True) / width + EPSILON)
    n = m * scale
    c = db * gain_ref[1:2]
    mean = jnp.sum(c * n, axis=-1, keepdims=True) / width
    em = df_ref[...].astype(F32) + scale * (c - n * mean)
    em_ref[...] = em
    da = em.astype(BF16)
    dgain = jnp.sum(db * n, axis=0, keepdims=True)
    block = m.shape[0]
    late = pl.num_programs(0) // 2
    at = jnp.where(i < late, (1 - place_ref[0]) * late + i, place_ref[0] * late + i - late)
    rows = pl.ds(pl.multiple_of(block * at, block), block)
    da_ref[rows, :] = da

    @pl.when(i == 0)
    def _():
        dgain_ref[...] = dgain

    @pl.when(i > 0)
    def _():
        dgain_ref[...] += dgain

    do = mm_nt(da, wo_ref[...]).astype(BF16)
    product = do.astype(F32) * op_ref[rows, :].astype(F32)
    high = product.astype(BF16)
    low = (product - high.astype(F32)).astype(BF16)
    delta = mm(high, sum_ref[...]) + mm(low, sum_ref[...])
    full = jnp.concatenate([do] + [t.astype(BF16) for t in three_terms(delta)], axis=1)
    do = mm(full, u_ref[...]).astype(BF16)
    for head in range(HEADS):
        do_ref[head] = do[:, LANES * head : LANES * (head + 1)]

    @pl.when(i == pl.num_programs(0) - 1)
    def _():
        half = da_ref.shape[1] // 2
        for ref, j in ((dwo_send, 1 - place_ref[0]), (dwo_keep, place_ref[0])):
            dwo = mm_tn(op_ref[...], da_ref[:, pl.ds(pl.multiple_of(half * j, half), half)]).astype(BF16)
            for q in range(2):
                ref[q] = dwo[:, 256 * q : 256 * (q + 1)].reshape(ref.shape[1:])


def after(place, m, acc, db, df, gain, spread, unpack, delta_sum, w_out, op, width, block=512):
    seq, wide = m.shape
    blocks = 16
    steps = seq // block
    at = token_block(steps)
    rows = lambda n: pl.BlockSpec((block, n), lambda i, place: (at(i, place), 0))
    heads = pl.BlockSpec((HEADS, block, LANES), lambda i, place: (0, at(i, place), 0))
    dwo_shape = (2, blocks, wide // blocks, 256)
    consts = (gain, spread, unpack, delta_sum, w_out, op)
    return call(
        functools.partial(post_body, width),
        [
            jax.ShapeDtypeStruct((width, seq // 2), BF16),
            jax.ShapeDtypeStruct((2, width, seq // 2), BF16),
            jax.ShapeDtypeStruct((seq, wide), F32),
            jax.ShapeDtypeStruct((HEADS, seq, LANES), BF16),
            jax.ShapeDtypeStruct(dwo_shape, BF16),
            jax.ShapeDtypeStruct(dwo_shape, BF16),
            jax.ShapeDtypeStruct((1, wide), F32),
        ],
        (steps,),
        [rows(wide)] * 4 + [whole(t.shape) for t in consts],
        token_specs(steps, block, width)
        + [rows(wide), heads, whole(dwo_shape), whole(dwo_shape), whole((1, wide))],
        scratch=[pltpu.VMEM((seq, wide), BF16)],
        flops=2 * seq * wide * 6 * wide,
        moved=40_000_000,
        prefetch=1,
    )(place, m, acc, db, df, *consts)


def weights_body(place_ref, dq_ref, dk_ref, dv_ref, a_ref, w_ref, gain_ref,
                 dgain_ref, flat_ref, send_ref, keep_ref, dw_acc, part_ref, all_ref):
    i = pl.program_id(0)
    heads = HEADS + KV_HEADS

    pairs_to(flat_ref, lambda h: dq_ref[h] if h < HEADS else dk_ref[h - HEADS], heads)
    pairs_to(flat_ref, lambda h: dv_ref[h], KV_HEADS, heads * HEAD)
    block = flat_ref.shape[0]
    all_ref[pl.ds(pl.multiple_of(block * i, block), block), :] = flat_ref[...]

    @pl.when(i == pl.num_programs(0) - 1)
    def _():
        wide = dw_acc.shape[0]
        dw_acc[...] = mm_tn(a_ref[...], all_ref[...])
        total = jnp.sum(dw_acc[...] * w_ref[...].astype(F32), axis=-1, keepdims=True)
        column = lambda row: jnp.broadcast_to(row, (LANES, wide)).T
        gain = column(gain_ref[:1])
        attn = jnp.broadcast_to(total, (wide, LANES)) / jnp.where(gain == 0.0, 1.0, gain)
        lane = lane_of(wide)
        gains = jnp.where(lane == 32, attn, 0.0) + jnp.where(lane == 33, column(dgain_ref[...]), 0.0)
        n_q, n_k = HEADS * HEAD // 2, KV_HEADS * HEAD // 2
        for j in range(2):
            part_ref[:, 768:] = gains.astype(BF16)
            part_ref[:, :n_q] = dw_acc[:, n_q * j : n_q * (j + 1)].astype(BF16)
            for part in range(2):
                at, to = 2 * n_q + n_k * (2 * part + j), n_q + n_k * part
                part_ref[:, to : to + n_k] = dw_acc[:, at : at + n_k].astype(BF16)
            for ref, here in ((keep_ref, place_ref[0] == j), (send_ref, place_ref[0] != j)):

                @pl.when(here)
                def _():
                    ref[...] = part_ref[...].reshape(ref.shape)


def projections_back(place, parts, a, w_qkv, gain, dgain_ffn, block=256):
    seq, wide = a.shape
    blocks = 16
    rows = lambda n: pl.BlockSpec((block, n), lambda i, *_: (i, 0))
    heads = lambda t: pl.BlockSpec((t.shape[0], block, LANES), lambda i, *_: (0, i, 0))
    shape = (blocks, wide // blocks, 896)
    return call(
        weights_body,
        [
            jax.ShapeDtypeStruct((seq, QKV_PAD), BF16),
            jax.ShapeDtypeStruct(shape, BF16),
            jax.ShapeDtypeStruct(shape, BF16),
        ],
        (seq // block,),
        [heads(t) for t in parts] + [whole(a.shape), whole(w_qkv.shape), whole((8, wide)), whole((1, wide))],
        [rows(QKV_PAD), whole(shape), whole(shape)],
        scratch=[
            pltpu.VMEM((wide, QKV_PAD), F32),
            pltpu.VMEM((wide, 896), BF16),
            pltpu.VMEM((seq, QKV_PAD), BF16),
        ],
        flops=2 * seq * wide * QKV_PAD,
        moved=20_000_000,
        prefetch=1,
    )(place, *parts, a, w_qkv, gain, dgain_ffn)


def input_body(width, place_ref, flat_ref, w_ref, xp_ref, em_ref, gain_ref, e_ref, send_ref, keep_ref):
    da = mm_nt(flat_ref[...], w_ref[...])
    xp = xp_ref[...].astype(F32)
    scale = lax.rsqrt(jnp.sum(xp * xp, axis=-1, keepdims=True) / width + EPSILON)
    n = xp * scale
    c = da * gain_ref[:1]
    mean = jnp.sum(c * n, axis=-1, keepdims=True) / width
    grad = em_ref[...] + scale * (c - n * mean)
    put_tokens(send_ref, keep_ref, mm_nt(e_ref[:width, :], grad.astype(BF16)))


def input_back(place, flat, w_qkv, xp, em, gain, spread, width, block=512):
    seq, wide = xp.shape
    steps = seq // block
    at = token_block(steps)
    rows = lambda n: pl.BlockSpec((block, n), lambda i, place: (at(i, place), 0))
    return call(
        functools.partial(input_body, width),
        [
            jax.ShapeDtypeStruct((width, seq // 2), BF16),
            jax.ShapeDtypeStruct((2, width, seq // 2), F32),
        ],
        (steps,),
        [rows(QKV_PAD), whole(w_qkv.shape), rows(wide), rows(wide), whole((8, wide)), whole(spread.shape)],
        token_specs(steps, block, width),
        flops=2 * seq * wide * (QKV_PAD + 2 * width),
        moved=20_000_000,
        prefetch=1,
    )(place, flat, w_qkv, xp, em, gain, spread)


def begin_body(reader, n_in, place_ref, *refs):
    ins, outs = refs[:n_in], refs[n_in:]
    _, _, y, x = (place_ref[n] for n in range(4))
    for side in range(2):
        mine = y if side else x
        for other in range(2):
            for ref, bit in ((outs[2 * side], 1 - mine), (outs[2 * side + 1], mine)):
                block = 2 * bit + other if side else 2 * other + bit
                for row, keep, got in reader(ins, side, block):
                    ref[other, row : row + keep.shape[0]] = add(keep, got)


def begin(place, arrays, reader, rows, count=4):
    n = arrays[0].shape[-1]

    def spec(t):
        lead = t.shape[:-3]
        return pl.BlockSpec((*lead, 4, *t.shape[-2:]), lambda i, place: (0,) * len(lead) + (i, 0, 0))

    shape = jax.ShapeDtypeStruct((2 * count, rows, n), BF16)
    return call(
        functools.partial(begin_body, reader, len(arrays)),
        [shape] * 4,
        (count,),
        [spec(t) for t in arrays],
        [pl.BlockSpec((2, rows, n), lambda i, place: (i, 0, 0))] * 4,
        flops=1,
        moved=16 * count * rows * n * 6,
        prefetch=1,
        vmem=VMEM_SMALL,
    )(place, *arrays)


def turn_body(place_ref, *refs):
    y, x = place_ref[2], place_ref[3]
    for side in range(2):
        keep, got = refs[2 * side : 2 * side + 2]
        mine = x if side else y
        for ref, bit in ((refs[4 + 2 * side], 1 - mine), (refs[5 + 2 * side], mine)):
            ref[0] = add(keep[bit], got[bit])


def turn(place, keeps, gots):
    blocks, rows, n = keeps[0].shape
    shape = jax.ShapeDtypeStruct((blocks // 2, rows, n), BF16)
    return call(
        turn_body,
        [shape] * 4,
        (blocks // 2,),
        [pl.BlockSpec((2, rows, n), lambda i, place: (i, 0, 0))] * 4,
        [pl.BlockSpec((1, rows, n), lambda i, place: (i, 0, 0))] * 4,
        flops=1,
        moved=blocks * rows * n * 12,
        prefetch=1,
        vmem=VMEM_SMALL,
    )(place, keeps[0], gots[0], keeps[1], gots[1])


def climb_body(place_ref, a_keep, a_got, b_keep, b_got, total_ref, *sent):
    for step in range(4):
        block = lax.rem(place_ref[1] + step, 4)
        for side, (keep, got) in enumerate(((a_keep, a_got), (b_keep, b_got))):
            value = keep[block].astype(F32) + got[block].astype(F32)
            if step:
                sent[step - 1][side] = value.astype(BF16)
            else:
                total_ref[side] = value


def climb(place, keeps, gots):
    _, rows, n = keeps[0].shape
    return call(
        climb_body,
        [jax.ShapeDtypeStruct((2, rows, n), F32)] + [jax.ShapeDtypeStruct((2, rows, n), BF16)] * 3,
        (1,),
        [whole(keeps[0].shape)] * 4,
        [whole((2, rows, n))] * 4,
        flops=1,
        moved=rows * n * 50,
        prefetch=1,
        vmem=VMEM_SMALL,
    )(place, keeps[0], gots[0], keeps[1], gots[1])


def unpack_matrix(width, blocks, wide):
    per, step = width // blocks, wide // blocks
    col = jnp.arange(WIDE_HEADS, dtype=jnp.int32)
    feature = col // LANES * HEAD + col % LANES
    place = jnp.where(col % LANES < HEAD, feature // per * step + feature % per, -1)
    term = col % LANES - HEAD
    place = jnp.where((term >= 0) & (term < 3), wide + term * LANES + col // LANES, place)
    return (jnp.arange(wide + 3 * LANES, dtype=jnp.int32)[:, None] == place[None, :]).astype(BF16)


def delta_matrix(width, blocks, wide):
    per, step = width // blocks, wide // blocks
    row = jnp.arange(wide, dtype=jnp.int32)
    head = jnp.where(row % step < per, (row // step * per + row % step) // HEAD, -1)
    return (head[:, None] == jnp.arange(LANES, dtype=jnp.int32)[None, :]).astype(BF16)


def spread_matrix(width, blocks, wide):
    row = jnp.arange(wide, dtype=jnp.int32)
    per, step = width // blocks, wide // blocks
    place = (row // per) * step + row % per
    hit = (place[:, None] == jnp.arange(wide, dtype=jnp.int32)[None, :]) & (row < width)[:, None]
    return hit.astype(BF16)


def tables(positions, segments):
    lane = jnp.arange(LANES, dtype=jnp.int32)
    frequency = 10000.0 ** (-((lane % 32).astype(F32) * 2.0 / HEAD))
    angles = positions.astype(F32)[:, None] * frequency[None, :]
    cos, sin = jnp.cos(angles), jnp.sin(angles)
    high = (lane % HEAD >= 32)[None, :]
    sa = jnp.where(high, sin, 0.0)
    sb = jnp.where(high, 0.0, -sin)
    doc = (lane - HEAD)[None, :]
    mine = segments[:, None] == doc
    in_doc = (doc >= 0) & (doc < DOCS)
    aq = jnp.where(mine & in_doc, MASKED, 0.0)
    ak = jnp.where(in_doc & ~mine, 1.0, 0.0)
    ak = jnp.where((doc >= DOCS) & (doc < DOCS + 3), -1.0, ak)
    return cos, sa, sb, aq, ak


def pad_rows(w, blocks, step=64):
    per = w.shape[0] // blocks
    return jnp.pad(w.reshape(blocks, per, w.shape[1]), ((0, 0), (0, step - per), (0, 0)))


def pad_cols(w, blocks, step=64):
    per = w.shape[1] // blocks
    w = jnp.pad(w.reshape(w.shape[0], blocks, per), ((0, 0), (0, 0), (0, step - per)))
    return w.reshape(w.shape[0], blocks * step)


def cut_rows(w, per):
    return w[:, :per].reshape(w.shape[0] * per, w.shape[2])


def cut_cols(w, per, step=64):
    blocks = w.shape[1] // step
    return w.reshape(w.shape[0], blocks, step)[:, :, :per].reshape(w.shape[0], blocks * per)


def chunked(w, chunk=256):
    blocks, rows, cols = w.shape
    w = w.reshape(blocks, rows, cols // chunk, chunk).transpose(0, 2, 1, 3)
    return w.reshape(blocks, cols // chunk * rows, chunk)


def joined(w, rows):
    blocks, total, chunk = w.shape
    w = w.reshape(blocks, total // rows, rows, chunk).transpose(0, 2, 1, 3)
    return w.reshape(blocks, rows, total // rows * chunk)


def pack_half(w_gate, w_up, w_down, blocks, groups):
    down = pad_cols(w_down, groups)
    down = down.reshape(blocks, w_down.shape[0] // blocks, down.shape[1])
    gate, upper = chunked(pad_rows(w_gate, blocks)), chunked(pad_rows(w_up, blocks))
    return jnp.concatenate([gate, down[:, :, :256], upper, down[:, :, 256:]], axis=1)


def add(left, right):
    return (left.astype(F32) + right.astype(F32)).astype(BF16)


def swap(x):
    return lax.ppermute(x, "ctx", [(0, 1), (1, 0)])


def across(x, bit, count):
    return lax.ppermute(x, "dp", [(i, i ^ (1 << bit)) for i in range(count)])


def pick(x, index, axis=0):
    return lax.dynamic_index_in_dim(x, index, axis, keepdims=False)


def tie(value, *others):
    return lax.optimization_barrier((value, *others))[0]


def tie_all(values, *others):
    return lax.optimization_barrier((*values, *others))[: len(values)]


def along_z(x, step, count):
    return lax.ppermute(x, "dp", [(i, (i + 4 * step) % count) for i in range(count)])


def rise(x, count):
    return [x] + [along_z(x, k, count) for k in (1, 2, 3)]


def spread_first(stack, count):
    half = stack.shape[1] // 2
    first, second = stack[:, :half], stack[:, half:]
    return first, across(first, 0, count), second, across(second, 1, count)


def spread_second(first, first_got, second, second_got, count):
    first, second = jnp.concatenate([first, first_got]), jnp.concatenate([second, second_got])
    return first, across(first, 1, count), second, across(second, 0, count)


def pieces_of(whole_one):
    n = whole_one.shape[1] // 2
    cube = whole_one.reshape(4, 2, 2, 2 * n, -1)
    cube = jnp.stack([cube[(4 - k) % 4] for k in range(4)])
    first, second = cube[:, :, :, :n], cube[:, :, :, n:]
    first, second = first.transpose(1, 2, 0, 3, 4), second.transpose(2, 1, 0, 3, 4)
    flat = lambda t: t.reshape(8, n, -1)
    return flat(first[0]), flat(first[1]), flat(second[0]), flat(second[1])


def fine_pieces_of(whole_one):
    n = whole_one.shape[1] // 2
    cube = whole_one.reshape(4, 2, 2, 2 * n, -1)
    cube = jnp.stack([cube[(4 - k) % 4] for k in range(4)])
    near = [cube[:, dy, dx] for dy in range(2) for dx in range(2)]
    return [t[:, :n] for t in near] + [t[:, n:] for t in near]


class RowSum:
    def __init__(self, place, count, arrays, reader, rows):
        self.place, self.count = place, count
        a_sent, a_kept, b_sent, b_kept = begin(place, arrays, reader, rows)
        self.sent, self.kept = [a_sent, b_sent], [a_kept, b_kept]

    def move(self):
        self.got = [across(self.sent[0], 0, self.count), across(self.sent[1], 1, self.count)]

    def wait(self, other):
        self.got = list(lax.optimization_barrier((*self.got, other))[:-1])

    def turn(self, other):
        self.wait(other)
        a_sent, a_kept, b_sent, b_kept = turn(self.place, self.kept, self.got)
        self.sent, self.kept = [a_sent, b_sent], [a_kept, b_kept]

    def move_again(self):
        self.got = [across(self.sent[0], 1, self.count), across(self.sent[1], 0, self.count)]

    def climb(self, other):
        self.wait(other)
        self.kept, *self.sent = climb(self.place, self.kept, self.got)

    def start_up(self):
        return along_z(self.sent[1], 1, self.count)

    def start_down(self):
        return along_z(self.sent[2], 3, self.count)

    def go_up(self, got):
        return along_z(add(self.sent[0], got), 1, self.count)

    def move_up(self):
        return [along_z(self.sent[k - 1], k, self.count) for k in (1, 2, 3)]

    def total(self, *gots):
        total = self.kept
        for got in gots:
            total = total + got.astype(F32)
        return total


def read_rows(ins, side, block):
    half = ins[0].shape[1] // 2
    rows = slice(half * side, half * (side + 1))
    return [(0, ins[0][block, rows], ins[1][block, rows])]


def read_quarters(ins, side, block):
    first = ins[0].shape[2]
    return [(0, ins[0][side, block], ins[1][side, block]), (first, ins[2][side, block], ins[3][side, block])]


def put_other(both, got, core):
    return lax.dynamic_update_slice(both, got[None], (1 - core, 0, 0))


def shards_of_two(inputs, segment_ids, positions, w_query, w_key, w_value, w_out, w_gate, w_up,
                  w_down, gain_attn, gain_ffn, cotangent):
    count = lax.axis_size("dp")
    me, core = lax.axis_index("dp"), lax.axis_index("ctx")
    place = (core, me // 4, (me >> 1) & 1, me & 1)
    place_of = jnp.stack(place).astype(jnp.int32)
    per = gain_attn.shape[0]
    width = per * count
    groups = w_out.shape[1] // per
    hidden = w_down.shape[0]
    n_q, n_k = w_query.shape[1], w_key.shape[1]
    n_qkv = n_q + 2 * n_k

    shard = jnp.concatenate(
        [w_query, w_key, w_value, gain_attn[:, None], gain_ffn[:, None]], axis=1
    )
    shard = jnp.pad(shard, ((0, 0), (0, 896 - n_qkv - 2)))
    shard = jnp.concatenate([shard, pad_cols(w_out, groups)], axis=1)
    shard = jnp.pad(shard, ((0, 64 - per), (0, 0)))
    packed = pack_half(w_gate, w_up, w_down, 1, groups)[0]
    wide = count * 64
    spread, unpack = spread_matrix(width, count, wide), unpack_matrix(width, count, wide)
    delta_sum = delta_matrix(width, count, wide)
    table = tables(pick(positions[:, 0], core), pick(segment_ids[:, 0], core))

    level = rise(shard, count)
    stack = tie(jnp.stack(level), spread, unpack, delta_sum, *table)
    part = spread_first(stack, count)
    packed = tie(packed, stack)
    up = along_z(packed, 1, count)
    part = tie_all(part, up)
    near_far = spread_second(*part, count)
    up = tie(up, part[0])
    up_two, down = along_z(up, 1, count), along_z(packed, 3, count)
    near_far = tie_all(near_far, up_two, down)
    pieces = near_far + tuple(swap(t) for t in near_far)
    packs = jnp.stack(tie_all((packed, up, up_two, down), near_far[0]))
    half = packs.shape[1] // 2
    a00, b00 = packs[:, :half], packs[:, half:]
    a01, b10 = across(a00, 0, count), across(b00, 1, count)

    def halves(x):
        x = jnp.swapaxes(x[:, 0], 1, 2)
        return pick(x, core), swap(pick(x, 1 - core))

    x_own, x_other = halves(inputs)
    ct_own, ct_other = halves(cotangent)
    pieces = tie_all(pieces, a00, b00)
    xp, a, q, k, v, w_qkv, w_o, gains = pre_attention(place_of, x_own, x_other, spread, pieces, *table)
    a01, b10, ct_other, a00, b00 = tie_all((a01, b10, ct_other, a00, b00), q)
    a10, b01 = across(a00, 1, count), across(b00, 0, count)
    got = [swap(a00), swap(b00), swap(a01)]
    q = tie(q, a01, b10, ct_other)
    o, q2 = attend(q, k, v)
    a10, b01, *got = tie_all((a10, b01, *got), o)
    a11, b11 = across(tie(a01, a10), 1, count), across(tie(b10, a10), 0, count)
    got += [swap(b10), swap(a10), swap(b01)]
    op, m, b, df = middle(
        place_of, tie(o, a10, b01, *got[:3]), ct_own, ct_other, spread, unpack, w_o, xp, gains
    )
    a11, b11, *got = tie_all((a11, b11, *got), b)
    mine = [a00, a01, a10, a11, b00, b01, b10, b11]
    other = [got[0], got[2], got[4], swap(a11), got[1], got[5], got[3], swap(b11)]

    acc0, db0, gu_send, d_send, d_keep = feed_forward(place_of, b, df, mine, other, 0)
    gu_got = swap(gu_send)
    acc, db, gu_keep, d_send, d_keep = feed_forward(
        place_of, tie(b, gu_send), df, mine, other, 1, (d_send, d_keep, acc0, db0)
    )
    one = RowSum(place_of, count, (gu_keep, tie(gu_got, acc)), read_rows, 320)
    one.move()
    blocked = lambda t: t.reshape(2, count, hidden, 256)
    d_got = swap(d_send)
    m = tie(m, *one.sent, d_send)
    out_send, outs, em, do, o_send, o_keep, dgf = after(
        place_of, m, acc, db, df, gains, spread, unpack, delta_sum, w_o, op, width
    )
    o_got = swap(o_send)
    one.turn(em)
    one.move_again()
    two = RowSum(
        place_of, count, (blocked(d_keep), blocked(tie(d_got, em)), o_keep, o_got), read_quarters, 224
    )
    two.move()
    do = tie(do, *one.sent, *two.sent)
    parts = attend_back(q2, k, v, do, *table[:3], 0, KV_HEADS)
    outs = put_other(outs, tie(swap(out_send), parts[0]), core)
    one.climb(parts[0])
    up, down = one.start_up(), one.start_down()
    two.turn(parts[0])
    two.move_again()
    a = tie(a, *one.sent, *two.sent)
    flat, p_send, p_keep = projections_back(place_of, parts, a, w_qkv, gains, dgf)
    up, down, *two.got = tie_all((up, down, *two.got), flat)
    p_got = swap(tie(p_send, up))
    two.climb(flat)
    one_up, one_down, two_up = one.go_up(up), down, two.start_up()
    three = RowSum(place_of, count, (p_keep, p_got), read_rows, 32)
    three.move()
    flat = tie(flat, *two.sent, *three.sent)
    gi_send, gis = input_back(place_of, flat, w_qkv, xp, em, gains, spread, width)
    *three.got, one_up, two_up = tie_all((*three.got, one_up, two_up), gis)
    gi_got = swap(tie(gi_send, one_up))
    three.turn(one_up)
    three.move_again()
    two_up, two_down = two.go_up(two_up), two.start_down()
    gis = put_other(gis, gi_got.astype(F32), core)
    first = one.total(one_up, one_down)
    three.climb(first)
    last_got = three.move_up()
    second, third = two.total(two_up, two_down), three.total(*last_got)
    third = third.reshape(64, 896)[:per]
    gu = first.reshape(5, 2, 64, 256)
    wide_of = lambda t: t.transpose(1, 0, 2).reshape(t.shape[1], -1)
    tokens = lambda t: jnp.swapaxes(t, 1, 2)[:, None]
    return (
        tokens(outs),
        tokens(gis),
        third[:, :n_q],
        third[:, n_q : n_q + n_k],
        third[:, n_q + n_k : n_qkv],
        cut_cols(wide_of(second[:, 160:])[:per], per),
        wide_of(gu[:, 0])[:per],
        wide_of(gu[:, 1])[:per],
        cut_cols(wide_of(second[:, :160]), per),
        third[:, n_qkv],
        third[:, n_qkv + 1],
    )


def shards_of_many(inputs, segment_ids, positions, w_query, w_key, w_value, w_out, w_gate, w_up,
                   w_down, gain_attn, gain_ffn, cotangent):
    count, cores = lax.axis_size("dp"), lax.axis_size("ctx")
    core = lax.axis_index("ctx")
    share = cores // MICRO
    per = gain_attn.shape[0]
    width = per * count

    def gathered(w):
        return lax.all_gather(lax.all_gather(w, "dp", axis=0, tiled=True), "ctx", axis=1, tiled=True)

    full = [gathered(w) for w in (w_query, w_key, w_value, w_out, w_gate, w_up, w_down)]
    gain_pair = lax.all_gather(jnp.stack([gain_attn, gain_ffn]), "dp", axis=1, tiled=True)
    w_o, w_g, w_u, w_d = full[3:]
    half = lambda w, j: w[:, w.shape[1] // 2 * j : w.shape[1] // 2 * (j + 1)]
    packs = [pack_half(half(w_g, j), half(w_u, j), half(w_d, j), count, count // 2) for j in range(2)]
    mine, other = (fine_pieces_of(p) for p in packs)
    pieces = []
    for j in range(2):
        parts = [half(w, j) for w in full[:3]] + [gain_pair.T]
        part = jnp.concatenate(parts, axis=1)
        part = jnp.pad(part, ((0, 0), (0, 896 - part.shape[1])))
        part = jnp.concatenate([part, pad_cols(half(w_o, j), count // 2)], axis=1)
        pieces += pieces_of(pad_rows(part, count))
    which = core // share

    def sequence(x):
        whole_one = pick(lax.all_gather(x[:, 0], "ctx", axis=1, tiled=True), which).T
        return whole_one[:, : whole_one.shape[1] // 2], whole_one[:, whole_one.shape[1] // 2 :]

    place = jnp.zeros((4,), jnp.int32)
    wide = count * 64
    spread, unpack = spread_matrix(width, count, wide), unpack_matrix(width, count, wide)
    delta_sum = delta_matrix(width, count, wide)
    cos, sa, sb, aq, ak = tables(pick(positions[:, 0], which), pick(segment_ids[:, 0], which))
    xp, a, q, k, v, w_qkv, w_o, gains = pre_attention(
        place, *sequence(inputs), spread, pieces, cos, sa, sb, aq, ak
    )
    o, q2 = attend(q, k, v)
    op, m, b, df = middle(place, o, *sequence(cotangent), spread, unpack, w_o, xp, gains)
    acc0, db0, gu_send, d_send, d_keep = feed_forward(place, b, df, mine, other, 0)
    acc, db, gu_keep, d_send, d_keep = feed_forward(
        place, b, df, mine, other, 1, (d_send, d_keep, acc0, db0)
    )
    out_send, outs, em, do, o_send, o_keep, dgf = after(
        place, m, acc, db, df, gains, spread, unpack, delta_sum, w_o, op, width
    )
    parts = attend_back(q2, k, v, do, cos, sa, sb, 0, KV_HEADS)
    flat, p_send, p_keep = projections_back(place, parts, a, w_qkv, gains, dgf)
    gi_send, gis = input_back(place, flat, w_qkv, xp, em, gains, spread, width)

    parts = [cut_rows(p, per) for p in (p_keep, p_send)]
    n_q, n_k = HEADS * HEAD // 2, KV_HEADS * HEAD // 2
    both = lambda at, n: jnp.concatenate([p[:, at : at + n] for p in parts], axis=1)
    side = lambda t: jnp.concatenate([t[0], t[1]], axis=-1)

    def wide_of(index):
        every = []
        for t in (gu_keep, gu_send):
            t = t.reshape(count, 5, 2, 64, 256)[:, :, index]
            every.append(cut_rows(t.transpose(0, 2, 1, 3).reshape(count, 64, -1), per))
        return jnp.concatenate(every, axis=1)

    grads = [
        both(0, n_q),
        both(n_q * 1, n_k),
        both(n_q + n_k, n_k),
        cut_cols(cut_rows(jnp.concatenate([side(o_keep), side(o_send)], axis=-1), per), per),
        wide_of(0),
        wide_of(1),
        cut_cols(
            jnp.concatenate([side(d_keep), side(d_send)], axis=-1),
            per,
        ),
    ]

    def summed(g):
        g = lax.psum_scatter(g * (1.0 / share), "dp", scatter_dimension=0, tiled=True)
        return lax.psum_scatter(g, "ctx", scatter_dimension=1, tiled=True).astype(F32)

    sums = [summed(g.astype(BF16)) for g in grads]
    dgain = parts[0][:, 2 * n_k + n_q : 2 * n_k + n_q + 2].astype(F32).T * (1.0 / share)
    dgain = lax.psum_scatter(lax.psum(dgain, "ctx"), "dp", scatter_dimension=1, tiled=True)

    def tokens(seq):
        rows = seq.shape[0] // cores
        every = lax.all_gather(seq, "ctx", axis=0, tiled=False)
        return lax.dynamic_slice_in_dim(every[::share], core * rows, rows, axis=1)[:, None]

    out = jnp.concatenate([outs[0], out_send], axis=1).T
    gi = jnp.concatenate([gis[0], gi_send.astype(F32)], axis=1).T
    return (tokens(out), tokens(gi), *sums, dgain[0], dgain[1])


def solution(mesh):
    two = mesh.shape["ctx"] == MICRO and mesh.shape["dp"] == 16
    matrices = (P("dp", "ctx"),) * 7 + (P("dp"), P("dp"))
    tokens = P(None, "dp", "ctx", None)
    return jax.shard_map(
        shards_of_two if two else shards_of_many,
        mesh=mesh,
        in_specs=(tokens, P(None, "dp", None), P(None, "dp", None)) + matrices + (tokens,),
        out_specs=(tokens, tokens) + matrices,
        check_vma=False,
    )
```

```python
import functools

import jax
import jax.numpy as jnp
from jax import lax
from jax.experimental import pallas as pl
from jax.experimental.pallas import tpu as pltpu
from jax.sharding import PartitionSpec as P

HEADS = 15
KV_HEADS = 5
HEAD = 64
MICRO = 2
GROUP = 3
DOCS = 4

EPSILON = 1e-05
MASKED = -1e30
LANES = 128
QKV = (HEADS + 2 * KV_HEADS) * HEAD
QKV_PAD = 1664
VMEM_LIMIT = 56 * 1024 * 1024
PACK = 1408
VMEM_SMALL = 24 * 1024 * 1024
WIDE_HEADS = HEADS * LANES
F32 = jnp.float32
BF16 = jnp.bfloat16


def up(value, step):
    return -(-value // step) * step


def mm(left, right):
    return lax.dot_general(left, right, (((1,), (0,)), ((), ())), preferred_element_type=F32)


def mm_nt(left, right):
    return lax.dot_general(left, right, (((1,), (1,)), ((), ())), preferred_element_type=F32)


def mm_tn(left, right):
    return lax.dot_general(left, right, (((0,), (0,)), ((), ())), preferred_element_type=F32)


def call(body, out_shape, grid, in_specs, out_specs, scratch=(), flops=0, moved=0, prefetch=0, alias=None,
         vmem=VMEM_LIMIT):
    return pl.pallas_call(
        body,
        out_shape=out_shape,
        grid_spec=pltpu.PrefetchScalarGridSpec(
            num_scalar_prefetch=prefetch,
            grid=grid,
            in_specs=in_specs,
            out_specs=out_specs,
            scratch_shapes=scratch,
        ),
        input_output_aliases=alias or {},
        compiler_params=pltpu.CompilerParams(vmem_limit_bytes=vmem),
        cost_estimate=pl.CostEstimate(flops=flops, bytes_accessed=moved, transcendentals=0),
    )


def whole(shape):
    return pl.BlockSpec(shape, lambda *_: (0,) * len(shape), pipeline_mode=pl.Buffered(1))


def lane_of(rows):
    return lax.broadcasted_iota(jnp.int32, (rows, LANES), 1)


def three_terms(column):
    high = column.astype(BF16).astype(F32)
    rest = column - high
    mid = rest.astype(BF16).astype(F32)
    return high, mid, rest - mid


def put_terms(base, column, lane, first):
    high, mid, low = three_terms(column)
    base = jnp.where(lane == first, high, base)
    base = jnp.where(lane == first + 1, mid, base)
    return jnp.where(lane == first + 2, low, base)


def build_weights(place_ref, piece_refs, stage_ref, w_ref, wo_ref):
    core, z, y, x = (place_ref[n] for n in range(4))
    for swapped in range(2):
        near_a, far_a, near_b, far_b = piece_refs[4 * swapped : 4 * swapped + 4]
        to = jnp.bitwise_xor(core, swapped)
        for dy in range(2):
            for dx in range(2):
                for k in range(4):
                    block = lax.rem(z + 4 - k, 4) * 4 + (y ^ dy) * 2 + (x ^ dx)
                    row = pl.multiple_of(block * 64, 64)
                    stage_ref[to, pl.ds(row, 32), :] = (far_a if dy else near_a)[4 * dx + k]
                    stage_ref[to, pl.ds(row + 32, 32), :] = (far_b if dx else near_b)[4 * dy + k]
    n_q, n_k = HEADS * HEAD // 2, KV_HEADS * HEAD // 2
    for j in range(2):
        w_ref[:, n_q * j : n_q * (j + 1)] = stage_ref[j, :, :n_q]
        for part in range(2):
            to, at = 2 * n_q + n_k * (2 * part + j), n_q + n_k * part
            w_ref[:, to : to + n_k] = stage_ref[j, :, at : at + n_k]
        half = wo_ref.shape[1] // 2
        wo_ref[:, half * j : half * (j + 1)] = stage_ref[j, :, PACK - half :]
    w_ref[:, QKV:] = jnp.zeros((w_ref.shape[0], QKV_PAD - QKV), BF16)


def projections(xp, scale, w_ref, gain_ref, cos_ref, sa_ref, sb_ref, aq_ref, ak_ref,
                xp_ref, a_ref, q_ref, k_ref, v_ref):
    a = (xp * scale * gain_ref[:1]).astype(BF16)
    xp_ref[...] = xp.astype(BF16)
    a_ref[...] = a
    t = mm(a, w_ref[...])
    lane = lane_of(t.shape[0])
    low = lane < HEAD
    cos, sa, sb, aq, ak = cos_ref[...], sa_ref[...], sb_ref[...], aq_ref[...], ak_ref[...]
    for pair in range((HEADS + KV_HEADS) // 2):
        tt = t[:, LANES * pair : LANES * (pair + 1)]
        rot = tt * cos + pltpu.roll(tt, 32, 1) * sa + pltpu.roll(tt, 96, 1) * sb
        for half in range(2):
            head = 2 * pair + half
            val = rot if half == 0 else pltpu.roll(rot, 64, 1)
            if head < HEADS:
                q_ref[head] = jnp.where(low, val * HEAD ** -0.5, aq).astype(BF16)
            else:
                k_ref[head - HEADS] = jnp.where(low, val, ak).astype(BF16)
    av = jnp.where(lane < HEAD + 3, -1.0, 0.0)
    for head in range(KV_HEADS):
        first = (HEADS + KV_HEADS) * HEAD + LANES * (head // 2)
        tt = t[:, first : first + LANES]
        val = tt if head % 2 == 0 else pltpu.roll(tt, 64, 1)
        v_ref[head] = jnp.where(low, val, av).astype(BF16)


def own_or_other(place_ref, own_ref, other_ref):
    first = pl.program_id(0) < pl.num_programs(0) // 2
    mine = first == (place_ref[0] == 0)
    return jnp.where(mine, own_ref[...], other_ref[...])


def pre_body(width, place_ref, own_ref, other_ref, e_ref, *refs):
    pieces, refs = refs[:8], refs[8:]
    *rest, w_ref, wo_ref, gain_ref, stage_ref = refs

    @pl.when(pl.program_id(0) == 0)
    def _():
        build_weights(place_ref, pieces, stage_ref, w_ref, wo_ref)
        gain_ref[...] = stage_ref[0, :, 768:896].astype(F32).T[32:40]

    xp = mm_tn(own_or_other(place_ref, own_ref, other_ref), e_ref[:width, :])
    scale = lax.rsqrt(jnp.sum(xp * xp, axis=-1, keepdims=True) / width + EPSILON)
    projections(xp, scale, w_ref, gain_ref, *rest)


def halves_specs(rows, width, block):
    steps = rows // block
    return [pl.BlockSpec((width, block), lambda i, *_: (0, i % steps))] * 2


def pre_attention(place, own, other, spread, pieces, cos, sa, sb, aq, ak, block=512):
    width, half = own.shape
    seq, wide = 2 * half, spread.shape[1]
    rows = lambda n: pl.BlockSpec((block, n), lambda i, *_: (i, 0))
    heads = lambda n: pl.BlockSpec((n, block, LANES), lambda i, *_: (0, i, 0))
    return call(
        functools.partial(pre_body, width),
        [
            jax.ShapeDtypeStruct((seq, wide), BF16),
            jax.ShapeDtypeStruct((seq, wide), BF16),
            jax.ShapeDtypeStruct((HEADS, seq, LANES), BF16),
            jax.ShapeDtypeStruct((KV_HEADS, seq, LANES), BF16),
            jax.ShapeDtypeStruct((KV_HEADS, seq, LANES), BF16),
            jax.ShapeDtypeStruct((wide, QKV_PAD), BF16),
            jax.ShapeDtypeStruct((wide, wide), BF16),
            jax.ShapeDtypeStruct((8, wide), F32),
        ],
        (seq // block,),
        halves_specs(half, width, block)
        + [whole(spread.shape)]
        + [whole(w.shape) for w in pieces]
        + [rows(LANES)] * 5,
        [rows(wide), rows(wide), heads(HEADS), heads(KV_HEADS), heads(KV_HEADS)]
        + [whole((wide, QKV_PAD)), whole((wide, wide)), whole((8, wide))],
        scratch=[pltpu.VMEM((2, wide, PACK), BF16)],
        flops=2 * seq * wide * (width + QKV_PAD),
        moved=20_000_000,
        prefetch=1,
    )(place, own, other, spread, *pieces, cos, sa, sb, aq, ak)


def attend_body(block, q_ref, k_ref, v_ref, o_ref, q2_ref):
    seq = k_ref.shape[1]
    rows = GROUP * block
    below = lax.broadcasted_iota(jnp.int32, (block, block), 0) >= lax.broadcasted_iota(
        jnp.int32, (block, block), 1
    )
    below = jnp.concatenate([below.astype(F32)] * GROUP, axis=0) > 0.5
    lane = lane_of(rows)
    for i in range(seq // block):
        span = slice(block * i, block * (i + 1))
        q = q_ref[:, span, :].reshape(rows, LANES)
        s_in = jnp.where(below, mm_nt(q, k_ref[0, span, :]), MASKED)
        top = jnp.max(s_in, axis=-1, keepdims=True)
        if i:
            s_left = mm_nt(q, k_ref[0, : block * i, :])
            top = jnp.maximum(top, jnp.max(s_left, axis=-1, keepdims=True))
        ext = mm(jnp.exp(s_in - top).astype(BF16), v_ref[0, span, :])
        if i:
            ext = ext + mm(jnp.exp(s_left - top).astype(BF16), v_ref[0, : block * i, :])
        total = -ext[:, HEAD : HEAD + 1]
        o = ext / total
        o = jnp.where(lane < HEAD, o, pltpu.roll(o, 64, 1))
        o_ref[:, span, :] = o.reshape(GROUP, block, LANES).astype(BF16)
        q2 = put_terms(q.astype(F32), top + jnp.log(total), lane, HEAD + DOCS)
        q2_ref[:, span, :] = q2.reshape(GROUP, block, LANES).astype(BF16)


def attend(q, k, v, block=256):
    seq = q.shape[1]
    group = pl.BlockSpec((GROUP, seq, LANES), lambda n: (n, 0, 0))
    one = pl.BlockSpec((1, seq, LANES), lambda n: (n, 0, 0))
    shape = jax.ShapeDtypeStruct(q.shape, BF16)
    return call(
        functools.partial(attend_body, block),
        [shape, shape],
        (KV_HEADS,),
        [group, one, one],
        [group, group],
        flops=4 * HEADS * seq * seq * LANES,
        moved=15_000_000,
    )(q, k, v)


def attend_back_body(block, q_ref, k_ref, v_ref, do_ref, delta_ref, cos_ref, sa_ref, sb_ref,
                     dq_ref, dk_ref, dv_ref, acc_ref):
    seq = k_ref.shape[1]
    above = lax.broadcasted_iota(jnp.int32, (block, block), 0) <= lax.broadcasted_iota(
        jnp.int32, (block, block), 1
    )
    lane = lane_of(seq)

    def unrotate(t, span):
        rows = span.stop - span.start
        rot = (
            t * cos_ref[span, :]
            - pltpu.roll(t, 32, 1) * sa_ref[span, :]
            - pltpu.roll(t, 96, 1) * sb_ref[span, :]
        )
        return twice(rot, rows)

    def twice(t, rows):
        return jnp.where(lane[:rows] < HEAD, t, pltpu.roll(t, 64, 1)).astype(BF16)

    for j in range(seq // block):
        span = slice(block * j, block * (j + 1))
        k, v = k_ref[0, span, :], v_ref[0, span, :]
        dk = jnp.zeros((block, LANES), F32)
        dv = jnp.zeros((block, LANES), F32)
        for g in range(GROUP):
            q, do = q_ref[g, block * j :, :], do_ref[g, block * j :, :]
            p = jnp.exp(mm_nt(k, q))
            inner = jnp.where(above, p[:, :block], 0.0)
            p = inner if p.shape[1] == block else jnp.concatenate([inner, p[:, block:]], axis=1)
            ds = (p * (mm_nt(v, do) - delta_ref[g : g + 1, block * j :])).astype(BF16)
            dv = dv + mm(p.astype(BF16), do)
            dk = dk + mm(ds, q)
            dq = mm_tn(ds, k)
            if j == 0:
                acc_ref[g] = dq
            else:
                acc_ref[g, block * j :, :] += dq
        dk_ref[0, span, :] = unrotate(dk, span)
        dv_ref[0, span, :] = twice(dv, block)
    for g in range(GROUP):
        dq_ref[g] = unrotate(acc_ref[g] * HEAD ** -0.5, slice(0, seq))


def attend_back(q, k, v, do, delta, cos, sa, sb, first, count, block=256):
    seq = q.shape[1]
    group = lambda at: pl.BlockSpec((GROUP, seq, LANES), lambda n: (n + at, 0, 0))
    one = lambda at: pl.BlockSpec((1, seq, LANES), lambda n: (n + at, 0, 0))
    return call(
        functools.partial(attend_back_body, block),
        [
            jax.ShapeDtypeStruct((GROUP * count, seq, LANES), BF16),
            jax.ShapeDtypeStruct((count, seq, LANES), BF16),
            jax.ShapeDtypeStruct((count, seq, LANES), BF16),
        ],
        (count,),
        [group(first), one(first), one(first), group(first)]
        + [pl.BlockSpec((8, seq), lambda n: (n + first, 0))]
        + [whole((seq, LANES))] * 3,
        [group(0), one(0), one(0)],
        scratch=[pltpu.VMEM((GROUP, seq, LANES), F32)],
        flops=10 * GROUP * count * seq * seq * LANES,
        moved=4_000_000 * count,
    )(q, k, v, do, delta, cos, sa, sb)


def pairs_to(ref, get, heads, first=0):
    for pair in range((heads + 1) // 2):
        left = get(2 * pair)
        lane = lane_of(left.shape[0])
        right = get(2 * pair + 1).astype(F32) if 2 * pair + 1 < heads else 0.0
        both = jnp.where(lane < HEAD, left.astype(F32), right)
        ref[:, first + LANES * pair : first + LANES * (pair + 1)] = both.astype(BF16)


def mid_body(width, place_ref, o_ref, own_ref, other_ref, e_ref, u_ref, wo_ref, xp_ref, gain_ref,
             op_ref, m_ref, b_ref, df_ref):
    flat = jnp.concatenate([o_ref[head] for head in range(HEADS)], axis=1)
    op = mm_nt(flat, u_ref[...]).astype(BF16)
    op_ref[...] = op
    m = xp_ref[...].astype(F32) + mm(op, wo_ref[...])
    m_ref[...] = m
    scale = lax.rsqrt(jnp.sum(m * m, axis=-1, keepdims=True) / width + EPSILON)
    b_ref[...] = (m * scale * gain_ref[1:2]).astype(BF16)
    ct = own_or_other(place_ref, own_ref, other_ref)
    df_ref[...] = mm_tn(ct, e_ref[:width, :]).astype(BF16)


def middle(place, o, own, other, spread, unpack, w_out, xp, gain, block=512):
    width, half = own.shape
    seq, wide = 2 * half, spread.shape[1]
    rows = lambda n: pl.BlockSpec((block, n), lambda i, *_: (i, 0))
    return call(
        functools.partial(mid_body, width),
        [
            jax.ShapeDtypeStruct((seq, wide), BF16),
            jax.ShapeDtypeStruct((seq, wide), F32),
            jax.ShapeDtypeStruct((seq, wide), BF16),
            jax.ShapeDtypeStruct((seq, wide), BF16),
        ],
        (seq // block,),
        [
            pl.BlockSpec((HEADS, block, LANES), lambda i, *_: (0, i, 0)),
            *halves_specs(half, width, block),
            whole(spread.shape),
            whole(unpack.shape),
            whole(w_out.shape),
            rows(wide),
            whole((8, wide)),
        ],
        [rows(wide)] * 4,
        flops=2 * seq * wide * 4 * wide,
        moved=22_000_000,
        prefetch=1,
    )(place, o, own, other, spread, unpack, w_out, xp, gain)


def ffn_body(turn, place_ref, b_ref, df_ref, *refs):
    gates, ups, downs, refs = refs[:4], refs[4:8], refs[8:24], refs[24:]
    before, refs = refs[: 4 * turn], refs[4 * turn :]
    out_ref, db_ref, gu_ref, d_send, d_keep, wg_ref, wu_ref, wd_ref, down_sem, *carry = refs
    s = pl.program_id(0)
    core, z_me, y_me, x_me = (place_ref[n] for n in range(4))
    chunk = wg_ref.shape[1]
    half = core if turn else 1 - core
    rows = wd_ref.shape[0] // 8

    def carried(n):
        return pltpu.make_async_copy(before[2 + n], carry[n], carry[2 + n])

    def down_copies():
        for swapped in range(2):
            for q in range(2):
                for near in range(4):
                    for up_z in range(2):
                        k = lax.rem(z_me + 4 - (2 * half + up_z), 4)
                        block = up_z * 4 + (y_me ^ (near // 2)) * 2 + (x_me ^ (near % 2))
                        row = pl.multiple_of(rows * block, 16)
                        col = pl.multiple_of(2 * chunk * (core ^ swapped) + chunk * q, chunk)
                        ref = downs[8 * swapped + 4 * q + near]
                        yield pltpu.make_async_copy(
                            ref.at[k, pl.ds(ref.shape[1] - rows, rows), :],
                            wd_ref.at[pl.ds(row, rows), pl.ds(col, chunk)],
                            down_sem.at[16 * swapped + 8 * q + 2 * near + up_z],
                        )

    @pl.when(s == 0)
    def _():
        for copy in down_copies():
            copy.start()
        out_ref[...] = jnp.zeros_like(out_ref)
        db_ref[...] = jnp.zeros_like(db_ref)
        if turn:
            carried(0).start()
            carried(1).start()

    for near in range(4):
        for k in range(4):
            block = lax.rem(z_me + 4 - k, 4) * 4 + (y_me ^ (near // 2)) * 2 + (x_me ^ (near % 2))
            row = pl.multiple_of(block * 64, 64)
            wg_ref[pl.ds(row, 64), :] = gates[near][k]
            wu_ref[pl.ds(row, 64), :] = ups[near][k]

    @pl.when(s == 0)
    def _():
        for copy in down_copies():
            copy.wait()

    b, df = b_ref[...], df_ref[...]
    wg, wu = wg_ref[...], wu_ref[...]
    wd = wd_ref[pl.ds(pl.multiple_of(chunk * s, chunk), chunk), :]
    gate = mm(b, wg)
    upper = mm(b, wu)
    sig = jax.nn.sigmoid(gate)
    act = gate * sig
    z = (act * upper).astype(BF16)
    dz = mm_nt(df, wd)
    dg = (dz * upper * (sig + act * (1.0 - sig))).astype(BF16)
    du = (dz * act).astype(BF16)

    out_ref[...] += mm(z, wd)
    db_ref[...] += mm_nt(dg, wg) + mm_nt(du, wu)

    if turn:

        @pl.when(s == pl.num_programs(0) - 1)
        def _():
            carried(0).wait()
            carried(1).wait()
            out_ref[...] += carry[0][...]
            db_ref[...] += carry[1][...]

    gu_ref[:, :64] = mm_tn(b, dg).astype(BF16).reshape(gu_ref.shape[0], 64, chunk)
    gu_ref[:, 64:] = mm_tn(b, du).astype(BF16).reshape(gu_ref.shape[0], 64, chunk)
    side = df.shape[1] // 2
    for ref, j in ((d_send, 1 - core), (d_keep, core)):
        dwd = mm_tn(z, df_ref[:, pl.ds(pl.multiple_of(side * j, side), side)]).astype(BF16)
        ref[0] = dwd[:, :chunk]
        ref[1] = dwd[:, chunk:]


def feed_forward(place, b, df, mine, other, turn, before=()):
    seq, wide = b.shape
    blocks, chunks, chunk = 16, 5, 256
    columns = mine if turn else other
    any_spec = pl.BlockSpec(memory_space=pl.ANY)
    half_of = lambda place: place[0] if turn else 1 - place[0]
    d_shape = jax.ShapeDtypeStruct((2, 2 * chunks * chunk, chunk), BF16)
    d_spec = pl.BlockSpec((2, chunk, chunk), lambda s, place: (0, half_of(place) * chunks + s, 0))
    return call(
        functools.partial(ffn_body, turn),
        [
            jax.ShapeDtypeStruct((seq, wide), F32),
            jax.ShapeDtypeStruct((seq, wide), F32),
            jax.ShapeDtypeStruct((blocks, 128 * chunks, chunk), BF16),
            d_shape,
            d_shape,
        ],
        (chunks,),
        [whole(b.shape), whole(df.shape)]
        + [pl.BlockSpec((4, 64, chunk), lambda s, place: (0, s, 0))] * 8
        + [any_spec] * (16 + len(before)),
        [
            whole((seq, wide)),
            whole((seq, wide)),
            pl.BlockSpec((blocks, 128, chunk), lambda s, place: (0, s, 0)),
            d_spec,
            d_spec,
        ],
        scratch=[
            pltpu.VMEM((wide, chunk), BF16),
            pltpu.VMEM((wide, chunk), BF16),
            pltpu.VMEM((chunks * chunk, wide), BF16),
            pltpu.SemaphoreType.DMA((32,)),
        ]
        + turn * [pltpu.VMEM((seq, wide), F32)] * 2
        + turn * [pltpu.SemaphoreType.DMA] * 2,
        flops=18 * seq * wide * chunks * chunk,
        moved=40_000_000,
        prefetch=1,
        alias={27: 3, 28: 4} if before else None,
    )(place, b, df, *columns, *mine, *other, *before)


def token_block(steps):
    def at(i, place):
        return jnp.where(i < steps // 2, (1 - place[0]) * (steps // 2) + i, place[0] * (steps // 2) + i - steps // 2)

    return at


def token_specs(steps, block, width):
    half = steps // 2
    return [
        pl.BlockSpec((width, block), lambda i, place: (0, jnp.minimum(i, half - 1))),
        pl.BlockSpec((1, width, block), lambda i, place: (place[0], 0, jnp.maximum(i - half, 0))),
    ]


def put_tokens(send_ref, keep_ref, value):
    early = pl.program_id(0) < pl.num_programs(0) // 2

    @pl.when(early)
    def _():
        send_ref[...] = value.astype(send_ref.dtype)

    @pl.when(jnp.logical_not(early))
    def _():
        keep_ref[0] = value.astype(keep_ref.dtype)


def post_body(width, place_ref, m_ref, db_ref, df_ref, gain_ref, u_ref,
              sum_ref, wo_ref, op_ref,
              em_ref, do_ref, delta_ref, dwo_send, dwo_keep, dgain_ref, da_ref):
    i = pl.program_id(0)
    m, db = m_ref[...], db_ref[...]
    scale = lax.rsqrt(jnp.sum(m * m, axis=-1, keepdims=True) / width + EPSILON)
    n = m * scale
    c = db * gain_ref[1:2]
    mean = jnp.sum(c * n, axis=-1, keepdims=True) / width
    em = df_ref[...].astype(F32) + scale * (c - n * mean)
    em_ref[...] = em
    da = em.astype(BF16)
    dgain = jnp.sum(db * n, axis=0, keepdims=True)
    block = m.shape[0]
    rows = pl.ds(pl.multiple_of(block * i, block), block)
    da_ref[rows, :] = da

    @pl.when(i == 0)
    def _():
        dgain_ref[...] = dgain

    @pl.when(i > 0)
    def _():
        dgain_ref[...] += dgain

    do = mm_nt(da, wo_ref[...]).astype(BF16)
    product = do.astype(F32) * op_ref[rows, :].astype(F32)
    high = product.astype(BF16)
    low = (product - high.astype(F32)).astype(BF16)
    delta_ref[...] = mm_nt(sum_ref[...], high) + mm_nt(sum_ref[...], low)
    do = mm(do, u_ref[...]).astype(BF16)
    for head in range(HEADS):
        do_ref[head] = do[:, LANES * head : LANES * (head + 1)]

    @pl.when(i == pl.num_programs(0) - 1)
    def _():
        half = da_ref.shape[1] // 2
        for ref, j in ((dwo_send, 1 - place_ref[0]), (dwo_keep, place_ref[0])):
            dwo = mm_tn(op_ref[...], da_ref[:, pl.ds(pl.multiple_of(half * j, half), half)]).astype(BF16)
            for q in range(2):
                ref[q] = dwo[:, 256 * q : 256 * (q + 1)].reshape(ref.shape[1:])


def after(place, m, db, df, gain, unpack, delta_sum, w_out, op, width, block=512):
    seq, wide = m.shape
    blocks = 16
    steps = seq // block
    rows = lambda n: pl.BlockSpec((block, n), lambda i, place: (i, 0))
    heads = pl.BlockSpec((HEADS, block, LANES), lambda i, place: (0, i, 0))
    dwo_shape = (2, blocks, wide // blocks, 256)
    consts = (gain, unpack, delta_sum, w_out, op)
    return call(
        functools.partial(post_body, width),
        [
            jax.ShapeDtypeStruct((seq, wide), F32),
            jax.ShapeDtypeStruct((HEADS, seq, LANES), BF16),
            jax.ShapeDtypeStruct((8 * KV_HEADS, seq), F32),
            jax.ShapeDtypeStruct(dwo_shape, BF16),
            jax.ShapeDtypeStruct(dwo_shape, BF16),
            jax.ShapeDtypeStruct((1, wide), F32),
        ],
        (steps,),
        [rows(wide)] * 3 + [whole(t.shape) for t in consts],
        [
            rows(wide),
            heads,
            pl.BlockSpec((8 * KV_HEADS, block), lambda i, place: (0, i)),
            whole(dwo_shape),
            whole(dwo_shape),
            whole((1, wide)),
        ],
        scratch=[pltpu.VMEM((seq, wide), BF16)],
        flops=2 * seq * wide * 6 * wide,
        moved=40_000_000,
        prefetch=1,
    )(place, m, db, df, *consts)


def finish_body(width, place_ref, m_ref, acc_ref, e_ref, send_ref, keep_ref):
    out = (m_ref[...] + acc_ref[...]).astype(BF16)
    put_tokens(send_ref, keep_ref, mm_nt(e_ref[:width, :], out))


def finish(place, m, acc, spread, width, block=256):
    seq, wide = m.shape
    steps = seq // block
    at = token_block(steps)
    rows = lambda n: pl.BlockSpec((block, n), lambda i, place: (at(i, place), 0))
    return call(
        functools.partial(finish_body, width),
        [
            jax.ShapeDtypeStruct((width, seq // 2), BF16),
            jax.ShapeDtypeStruct((2, width, seq // 2), BF16),
        ],
        (steps,),
        [rows(wide), rows(wide), whole(spread.shape)],
        token_specs(steps, block, width),
        flops=2 * seq * wide * wide,
        moved=16_000_000,
        prefetch=1,
    )(place, m, acc, spread)


def weights_body(place_ref, dq_ref, dk_ref, dv_ref, a_ref, w_ref, gain_ref,
                 dgain_ref, flat_ref, send_ref, keep_ref, dw_acc, part_ref, all_ref):
    i = pl.program_id(0)
    heads = HEADS + KV_HEADS

    pairs_to(flat_ref, lambda h: dq_ref[h] if h < HEADS else dk_ref[h - HEADS], heads)
    pairs_to(flat_ref, lambda h: dv_ref[h], KV_HEADS, heads * HEAD)
    block = flat_ref.shape[0]
    all_ref[pl.ds(pl.multiple_of(block * i, block), block), :] = flat_ref[...]

    @pl.when(i == pl.num_programs(0) - 1)
    def _():
        wide = dw_acc.shape[0]
        dw_acc[...] = mm_tn(a_ref[...], all_ref[...])
        total = jnp.sum(dw_acc[...] * w_ref[...].astype(F32), axis=-1, keepdims=True)
        column = lambda row: jnp.broadcast_to(row, (LANES, wide)).T
        gain = column(gain_ref[:1])
        attn = jnp.broadcast_to(total, (wide, LANES)) / jnp.where(gain == 0.0, 1.0, gain)
        lane = lane_of(wide)
        gains = jnp.where(lane == 32, attn, 0.0) + jnp.where(lane == 33, column(dgain_ref[...]), 0.0)
        n_q, n_k = HEADS * HEAD // 2, KV_HEADS * HEAD // 2
        for j in range(2):
            part_ref[:, 768:] = gains.astype(BF16)
            part_ref[:, :n_q] = dw_acc[:, n_q * j : n_q * (j + 1)].astype(BF16)
            for part in range(2):
                at, to = 2 * n_q + n_k * (2 * part + j), n_q + n_k * part
                part_ref[:, to : to + n_k] = dw_acc[:, at : at + n_k].astype(BF16)
            for ref, here in ((keep_ref, place_ref[0] == j), (send_ref, place_ref[0] != j)):

                @pl.when(here)
                def _():
                    ref[...] = part_ref[...].reshape(ref.shape)


def projections_back(place, parts, a, w_qkv, gain, dgain_ffn, block=256):
    seq, wide = a.shape
    blocks = 16
    rows = lambda n: pl.BlockSpec((block, n), lambda i, *_: (i, 0))
    heads = lambda t: pl.BlockSpec((t.shape[0], block, LANES), lambda i, *_: (0, i, 0))
    shape = (blocks, wide // blocks, 896)
    return call(
        weights_body,
        [
            jax.ShapeDtypeStruct((seq, QKV_PAD), BF16),
            jax.ShapeDtypeStruct(shape, BF16),
            jax.ShapeDtypeStruct(shape, BF16),
        ],
        (seq // block,),
        [heads(t) for t in parts] + [whole(a.shape), whole(w_qkv.shape), whole((8, wide)), whole((1, wide))],
        [rows(QKV_PAD), whole(shape), whole(shape)],
        scratch=[
            pltpu.VMEM((wide, QKV_PAD), F32),
            pltpu.VMEM((wide, 896), BF16),
            pltpu.VMEM((seq, QKV_PAD), BF16),
        ],
        flops=2 * seq * wide * QKV_PAD,
        moved=20_000_000,
        prefetch=1,
    )(place, *parts, a, w_qkv, gain, dgain_ffn)


def input_body(width, keep, place_ref, flat_ref, w_ref, xp_ref, em_ref, gain_ref, e_ref, *refs):
    got_ref, to_ref = refs if keep else (None, refs[0])
    i = pl.program_id(0)
    steps = pl.num_programs(0) // (2 if keep else 1)

    def work():
        da = mm_nt(flat_ref[...], w_ref[...])
        xp = xp_ref[...].astype(F32)
        scale = lax.rsqrt(jnp.sum(xp * xp, axis=-1, keepdims=True) / width + EPSILON)
        n = xp * scale
        c = da * gain_ref[:1]
        mean = jnp.sum(c * n, axis=-1, keepdims=True) / width
        grad = em_ref[...] + scale * (c - n * mean)
        return mm_nt(e_ref[:width, :], grad.astype(BF16))

    if keep:

        @pl.when(i < steps)
        def _():
            to_ref[0] = work()

        @pl.when(i >= steps)
        def _():
            to_ref[0] = got_ref[...].astype(F32)

    else:
        to_ref[...] = work().astype(BF16)


def input_back(place, flat, w_qkv, xp, em, gain, spread, width, got=None, block=256):
    seq, wide = xp.shape
    steps = seq // 2 // block
    keep = got is not None
    token = lambda i, place: (place[0] if keep else 1 - place[0]) * steps + jnp.minimum(i, steps - 1)
    rows = lambda n: pl.BlockSpec((block, n), lambda i, place: (token(i, place), 0))
    ins = [rows(QKV_PAD), whole(w_qkv.shape), rows(wide), rows(wide), whole((8, wide)), whole(spread.shape)]
    if keep:
        ins.append(pl.BlockSpec((width, block), lambda i, place: (0, jnp.maximum(i - steps, 0))))
        shape = jax.ShapeDtypeStruct((2, width, seq // 2), F32)
        half = lambda i, place: jnp.where(i < steps, place[0], 1 - place[0])
        out = pl.BlockSpec((1, width, block), lambda i, place: (half(i, place), 0, lax.rem(i, steps)))
    else:
        shape = jax.ShapeDtypeStruct((width, seq // 2), BF16)
        out = pl.BlockSpec((width, block), lambda i, place: (0, i))
    return call(
        functools.partial(input_body, width, keep),
        [shape],
        (steps * (2 if keep else 1),),
        ins,
        [out],
        flops=seq * wide * (QKV_PAD + width),
        moved=10_000_000,
        prefetch=1,
    )(place, flat, w_qkv, xp, em, gain, spread, *([got] if keep else []))[0]


def begin_body(reader, n_in, place_ref, *refs):
    ins, outs = refs[:n_in], refs[n_in:]
    _, _, y, x = (place_ref[n] for n in range(4))
    for side in range(2):
        mine = y if side else x
        for other in range(2):
            for ref, bit in ((outs[2 * side], 1 - mine), (outs[2 * side + 1], mine)):
                block = 2 * bit + other if side else 2 * other + bit
                for row, keep, got in reader(ins, side, block):
                    ref[other, row : row + keep.shape[0]] = add(keep, got)


def begin(place, arrays, reader, rows, count=4):
    n = arrays[0].shape[-1]

    def spec(t):
        lead = t.shape[:-3]
        return pl.BlockSpec((*lead, 4, *t.shape[-2:]), lambda i, place: (0,) * len(lead) + (i, 0, 0))

    shape = jax.ShapeDtypeStruct((2 * count, rows, n), BF16)
    return call(
        functools.partial(begin_body, reader, len(arrays)),
        [shape] * 4,
        (count,),
        [spec(t) for t in arrays],
        [pl.BlockSpec((2, rows, n), lambda i, place: (i, 0, 0))] * 4,
        flops=1,
        moved=16 * count * rows * n * 6,
        prefetch=1,
        vmem=VMEM_SMALL,
    )(place, *arrays)


def turn_body(place_ref, *refs):
    y, x = place_ref[2], place_ref[3]
    for side in range(2):
        keep, got = refs[2 * side : 2 * side + 2]
        mine = x if side else y
        for ref, bit in ((refs[4 + 2 * side], 1 - mine), (refs[5 + 2 * side], mine)):
            ref[0] = add(keep[bit], got[bit])


def turn(place, keeps, gots):
    blocks, rows, n = keeps[0].shape
    shape = jax.ShapeDtypeStruct((blocks // 2, rows, n), BF16)
    return call(
        turn_body,
        [shape] * 4,
        (blocks // 2,),
        [pl.BlockSpec((2, rows, n), lambda i, place: (i, 0, 0))] * 4,
        [pl.BlockSpec((1, rows, n), lambda i, place: (i, 0, 0))] * 4,
        flops=1,
        moved=blocks * rows * n * 12,
        prefetch=1,
        vmem=VMEM_SMALL,
    )(place, keeps[0], gots[0], keeps[1], gots[1])


def climb_body(place_ref, a_keep, a_got, b_keep, b_got, total_ref, *sent):
    for step in range(4):
        block = lax.rem(place_ref[1] + step, 4)
        for side, (keep, got) in enumerate(((a_keep, a_got), (b_keep, b_got))):
            value = keep[block].astype(F32) + got[block].astype(F32)
            if step:
                sent[step - 1][side] = value.astype(BF16)
            else:
                total_ref[side] = value


def climb(place, keeps, gots):
    _, rows, n = keeps[0].shape
    return call(
        climb_body,
        [jax.ShapeDtypeStruct((2, rows, n), F32)] + [jax.ShapeDtypeStruct((2, rows, n), BF16)] * 3,
        (1,),
        [whole(keeps[0].shape)] * 4,
        [whole((2, rows, n))] * 4,
        flops=1,
        moved=rows * n * 50,
        prefetch=1,
        vmem=VMEM_SMALL,
    )(place, keeps[0], gots[0], keeps[1], gots[1])


def unpack_matrix(width, blocks, wide):
    per, step = width // blocks, wide // blocks
    col = jnp.arange(WIDE_HEADS, dtype=jnp.int32)
    feature = col // LANES * HEAD + col % LANES
    place = jnp.where(col % LANES < HEAD, feature // per * step + feature % per, -1)
    return (jnp.arange(wide, dtype=jnp.int32)[:, None] == place[None, :]).astype(BF16)


def delta_matrix(width, blocks, wide):
    per, step = width // blocks, wide // blocks
    col = jnp.arange(wide, dtype=jnp.int32)
    head = jnp.where(col % step < per, (col // step * per + col % step) // HEAD, -1)
    row = jnp.arange(8 * KV_HEADS, dtype=jnp.int32)
    mine = jnp.where(row % 8 < GROUP, row // 8 * GROUP + row % 8, -2)
    return (mine[:, None] == head[None, :]).astype(BF16)


def spread_matrix(width, blocks, wide):
    row = jnp.arange(wide, dtype=jnp.int32)
    per, step = width // blocks, wide // blocks
    place = (row // per) * step + row % per
    hit = (place[:, None] == jnp.arange(wide, dtype=jnp.int32)[None, :]) & (row < width)[:, None]
    return hit.astype(BF16)


def tables(positions, segments):
    lane = jnp.arange(LANES, dtype=jnp.int32)
    frequency = 10000.0 ** (-((lane % 32).astype(F32) * 2.0 / HEAD))
    angles = positions.astype(F32)[:, None] * frequency[None, :]
    cos, sin = jnp.cos(angles), jnp.sin(angles)
    high = (lane % HEAD >= 32)[None, :]
    sa = jnp.where(high, sin, 0.0)
    sb = jnp.where(high, 0.0, -sin)
    doc = (lane - HEAD)[None, :]
    mine = segments[:, None] == doc
    in_doc = (doc >= 0) & (doc < DOCS)
    aq = jnp.where(mine & in_doc, MASKED, 0.0)
    ak = jnp.where(in_doc & ~mine, 1.0, 0.0)
    ak = jnp.where((doc >= DOCS) & (doc < DOCS + 3), -1.0, ak)
    return cos, sa, sb, aq, ak


def pad_rows(w, blocks, step=64):
    per = w.shape[0] // blocks
    return jnp.pad(w.reshape(blocks, per, w.shape[1]), ((0, 0), (0, step - per), (0, 0)))


def pad_cols(w, blocks, step=64):
    per = w.shape[1] // blocks
    w = jnp.pad(w.reshape(w.shape[0], blocks, per), ((0, 0), (0, 0), (0, step - per)))
    return w.reshape(w.shape[0], blocks * step)


def cut_rows(w, per):
    return w[:, :per].reshape(w.shape[0] * per, w.shape[2])


def cut_cols(w, per, step=64):
    blocks = w.shape[1] // step
    return w.reshape(w.shape[0], blocks, step)[:, :, :per].reshape(w.shape[0], blocks * per)


def chunked(w, chunk=256):
    blocks, rows, cols = w.shape
    w = w.reshape(blocks, rows, cols // chunk, chunk).transpose(0, 2, 1, 3)
    return w.reshape(blocks, cols // chunk * rows, chunk)


def joined(w, rows):
    blocks, total, chunk = w.shape
    w = w.reshape(blocks, total // rows, rows, chunk).transpose(0, 2, 1, 3)
    return w.reshape(blocks, rows, total // rows * chunk)


def pack_half(w_gate, w_up, w_down, blocks, groups):
    down = pad_cols(w_down, groups)
    down = down.reshape(blocks, w_down.shape[0] // blocks, down.shape[1])
    gate, upper = chunked(pad_rows(w_gate, blocks)), chunked(pad_rows(w_up, blocks))
    return jnp.concatenate([gate, down[:, :, :256], upper, down[:, :, 256:]], axis=1)


def add(left, right):
    return (left.astype(F32) + right.astype(F32)).astype(BF16)


def swap(x):
    return lax.ppermute(x, "ctx", [(0, 1), (1, 0)])


def across(x, bit, count):
    return lax.ppermute(x, "dp", [(i, i ^ (1 << bit)) for i in range(count)])


def pick(x, index, axis=0):
    return lax.dynamic_index_in_dim(x, index, axis, keepdims=False)


def tie(value, *others):
    return lax.optimization_barrier((value, *others))[0]


def tie_all(values, *others):
    return lax.optimization_barrier((*values, *others))[: len(values)]


def along_z(x, step, count):
    return lax.ppermute(x, "dp", [(i, (i + 4 * step) % count) for i in range(count)])


def rise(x, count):
    return [x] + [along_z(x, k, count) for k in (1, 2, 3)]


def spread_first(stack, count):
    half = stack.shape[1] // 2
    first, second = stack[:, :half], stack[:, half:]
    return first, across(first, 0, count), second, across(second, 1, count)


def spread_second(first, first_got, second, second_got, count):
    first, second = jnp.concatenate([first, first_got]), jnp.concatenate([second, second_got])
    return first, across(first, 1, count), second, across(second, 0, count)


def pieces_of(whole_one):
    n = whole_one.shape[1] // 2
    cube = whole_one.reshape(4, 2, 2, 2 * n, -1)
    cube = jnp.stack([cube[(4 - k) % 4] for k in range(4)])
    first, second = cube[:, :, :, :n], cube[:, :, :, n:]
    first, second = first.transpose(1, 2, 0, 3, 4), second.transpose(2, 1, 0, 3, 4)
    flat = lambda t: t.reshape(8, n, -1)
    return flat(first[0]), flat(first[1]), flat(second[0]), flat(second[1])


def fine_pieces_of(whole_one):
    n = whole_one.shape[1] // 2
    cube = whole_one.reshape(4, 2, 2, 2 * n, -1)
    cube = jnp.stack([cube[(4 - k) % 4] for k in range(4)])
    near = [cube[:, dy, dx] for dy in range(2) for dx in range(2)]
    return [t[:, :n] for t in near] + [t[:, n:] for t in near]


class RowSum:
    def __init__(self, place, count, arrays, reader, rows):
        self.place, self.count = place, count
        a_sent, a_kept, b_sent, b_kept = begin(place, arrays, reader, rows)
        self.sent, self.kept = [a_sent, b_sent], [a_kept, b_kept]

    def move(self):
        self.got = [across(self.sent[0], 0, self.count), across(self.sent[1], 1, self.count)]

    def wait(self, other):
        self.got = list(lax.optimization_barrier((*self.got, other))[:-1])

    def turn(self, other):
        self.wait(other)
        a_sent, a_kept, b_sent, b_kept = turn(self.place, self.kept, self.got)
        self.sent, self.kept = [a_sent, b_sent], [a_kept, b_kept]

    def move_again(self):
        self.got = [across(self.sent[0], 1, self.count), across(self.sent[1], 0, self.count)]

    def climb(self, other):
        self.wait(other)
        self.kept, *self.sent = climb(self.place, self.kept, self.got)

    def start_up(self):
        return along_z(self.sent[1], 1, self.count)

    def start_down(self):
        return along_z(self.sent[2], 3, self.count)

    def go_up(self, got):
        return along_z(add(self.sent[0], got), 1, self.count)

    def move_up(self):
        return [along_z(self.sent[k - 1], k, self.count) for k in (1, 2, 3)]

    def total(self, *gots):
        total = self.kept
        for got in gots:
            total = total + got.astype(F32)
        return total


def read_rows(ins, side, block):
    half = ins[0].shape[1] // 2
    rows = slice(half * side, half * (side + 1))
    return [(0, ins[0][block, rows], ins[1][block, rows])]


def read_quarters(ins, side, block):
    first = ins[0].shape[2]
    return [(0, ins[0][side, block], ins[1][side, block]), (first, ins[2][side, block], ins[3][side, block])]


def put_other(both, got, core):
    return lax.dynamic_update_slice(both, got[None], (1 - core, 0, 0))


def shards_of_two(inputs, segment_ids, positions, w_query, w_key, w_value, w_out, w_gate, w_up,
                  w_down, gain_attn, gain_ffn, cotangent):
    count = lax.axis_size("dp")
    me, core = lax.axis_index("dp"), lax.axis_index("ctx")
    place = (core, me // 4, (me >> 1) & 1, me & 1)
    place_of = jnp.stack(place).astype(jnp.int32)
    per = gain_attn.shape[0]
    width = per * count
    groups = w_out.shape[1] // per
    hidden = w_down.shape[0]
    n_q, n_k = w_query.shape[1], w_key.shape[1]
    n_qkv = n_q + 2 * n_k

    shard = jnp.concatenate(
        [w_query, w_key, w_value, gain_attn[:, None], gain_ffn[:, None]], axis=1
    )
    shard = jnp.pad(shard, ((0, 0), (0, 896 - n_qkv - 2)))
    shard = jnp.concatenate([shard, pad_cols(w_out, groups)], axis=1)
    shard = jnp.pad(shard, ((0, 64 - per), (0, 0)))
    packed = pack_half(w_gate, w_up, w_down, 1, groups)[0]

    def halves(x):
        x = jnp.swapaxes(x[:, 0], 1, 2)
        return pick(x, core), swap(pick(x, 1 - core))

    wide = count * 64
    spread, unpack = spread_matrix(width, count, wide), unpack_matrix(width, count, wide)
    delta_sum = delta_matrix(width, count, wide)
    table = tables(pick(positions[:, 0], core), pick(segment_ids[:, 0], core))

    level = rise(shard, count)
    x_own, x_other = halves(inputs)
    ct_own, ct_other = halves(cotangent)
    stack = tie(jnp.stack(level), spread, delta_sum, *table, x_other, ct_other)
    part = spread_first(stack, count)
    packed = tie(packed, stack)
    up, down = along_z(packed, 1, count), along_z(packed, 3, count)
    near_far = spread_second(*tie_all(part, unpack), count)
    up, down = tie_all((up, down), part[0])
    up_two = along_z(up, 1, count)
    near_far = tie_all(near_far, up_two, down)
    pieces = near_far + tuple(swap(t) for t in near_far)
    packs = jnp.stack(tie_all((packed, up, up_two, down), near_far[0]))
    half = packs.shape[1] // 2
    a00, b00 = packs[:, :half], packs[:, half:]
    a01, b10 = across(a00, 0, count), across(b00, 1, count)

    pieces = tie_all(pieces, a00, b00)
    xp, a, q, k, v, w_qkv, w_o, gains = pre_attention(place_of, x_own, x_other, spread, pieces, *table)
    a01, b10, a00, b00 = tie_all((a01, b10, a00, b00), q)
    a10, b01 = across(a00, 1, count), across(b00, 0, count)
    got = [swap(a00), swap(b00), swap(a01)]
    q = tie(q, a01, b10)
    o, q2 = attend(q, k, v)
    a10, b01, *got = tie_all((a10, b01, *got), o)
    a11, b11 = across(tie(a01, a10), 1, count), across(tie(b10, a10), 0, count)
    got += [swap(b10), swap(a10), swap(b01)]
    op, m, b, df = middle(
        place_of, tie(o, a10, b01, *got[:3]), ct_own, ct_other, spread, unpack, w_o, xp, gains
    )
    a11, b11, *got = tie_all((a11, b11, *got), b)
    mine = [a00, a01, a10, a11, b00, b01, b10, b11]
    other = [got[0], got[2], got[4], swap(a11), got[1], got[5], got[3], swap(b11)]

    acc0, db0, gu_send, d_send, d_keep = feed_forward(place_of, b, df, mine, other, 0)
    gu_got = swap(gu_send)
    acc, db, gu_keep, d_send, d_keep = feed_forward(
        place_of, tie(b, gu_send), df, mine, other, 1, (d_send, d_keep, acc0, db0)
    )
    one = RowSum(place_of, count, (gu_keep, tie(gu_got, acc)), read_rows, 320)
    one.move()
    blocked = lambda t: t.reshape(2, count, hidden, 256)
    d_got = swap(d_send)
    m = tie(m, *one.sent, d_send)
    em, do, delta, o_send, o_keep, dgf = after(place_of, m, db, df, gains, unpack, delta_sum, w_o, op, width)
    o_got = swap(o_send)
    one.turn(em)
    one.move_again()
    two = RowSum(
        place_of, count, (blocked(d_keep), blocked(tie(d_got, em)), o_keep, o_got), read_quarters, 224
    )
    two.move()
    do = tie(do, *one.sent, *two.sent)
    parts = attend_back(q2, k, v, do, delta, *table[:3], 0, KV_HEADS)
    one.climb(parts[0])
    up, down = one.start_up(), one.start_down()
    two.turn(parts[0])
    two.move_again()
    a = tie(a, *one.sent, *two.sent)
    flat, p_send, p_keep = projections_back(place_of, parts, a, w_qkv, gains, dgf)
    up, down, *two.got = tie_all((up, down, *two.got), flat)
    p_got = swap(tie(p_send, up))
    two.climb(flat)
    one_up, one_down, two_up = one.go_up(up), down, two.start_up()
    three = RowSum(place_of, count, (p_keep, p_got), read_rows, 32)
    three.move()
    flat = tie(flat, *two.sent, *three.sent)
    gi_send = input_back(place_of, flat, w_qkv, xp, em, gains, spread, width)
    *three.got, one_up, two_up = tie_all((*three.got, one_up, two_up), gi_send)
    gi_got = swap(tie(gi_send, one_up))
    three.turn(one_up)
    three.move_again()
    two_up, two_down = two.go_up(two_up), two.start_down()
    out_send, outs = finish(place_of, tie(m, *three.sent), acc, spread, width)
    *three.got, gi_got = tie_all((*three.got, gi_got), outs)
    three.climb(gi_got)
    last_got = three.move_up()
    out_got = swap(out_send)
    gis = input_back(place_of, tie(flat, *three.sent, out_send), w_qkv, xp, em, gains, spread, width, gi_got)
    last_got = tie_all(last_got, gis)
    outs = put_other(outs, tie(out_got, gis), core)
    first = one.total(one_up, one_down)
    second, third = two.total(two_up, two_down), three.total(*last_got)
    third = third.reshape(64, 896)[:per]
    gu = first.reshape(5, 2, 64, 256)
    wide_of = lambda t: t.transpose(1, 0, 2).reshape(t.shape[1], -1)
    tokens = lambda t: jnp.swapaxes(t, 1, 2)[:, None]
    return (
        tokens(outs),
        tokens(gis),
        third[:, :n_q],
        third[:, n_q : n_q + n_k],
        third[:, n_q + n_k : n_qkv],
        cut_cols(wide_of(second[:, 160:])[:per], per),
        wide_of(gu[:, 0])[:per],
        wide_of(gu[:, 1])[:per],
        cut_cols(wide_of(second[:, :160]), per),
        third[:, n_qkv],
        third[:, n_qkv + 1],
    )


def shards_of_many(inputs, segment_ids, positions, w_query, w_key, w_value, w_out, w_gate, w_up,
                   w_down, gain_attn, gain_ffn, cotangent):
    count, cores = lax.axis_size("dp"), lax.axis_size("ctx")
    core = lax.axis_index("ctx")
    share = cores // MICRO
    per = gain_attn.shape[0]
    width = per * count

    def gathered(w):
        return lax.all_gather(lax.all_gather(w, "dp", axis=0, tiled=True), "ctx", axis=1, tiled=True)

    full = [gathered(w) for w in (w_query, w_key, w_value, w_out, w_gate, w_up, w_down)]
    gain_pair = lax.all_gather(jnp.stack([gain_attn, gain_ffn]), "dp", axis=1, tiled=True)
    w_o, w_g, w_u, w_d = full[3:]
    half = lambda w, j: w[:, w.shape[1] // 2 * j : w.shape[1] // 2 * (j + 1)]
    packs = [pack_half(half(w_g, j), half(w_u, j), half(w_d, j), count, count // 2) for j in range(2)]
    mine, other = (fine_pieces_of(p) for p in packs)
    pieces = []
    for j in range(2):
        parts = [half(w, j) for w in full[:3]] + [gain_pair.T]
        part = jnp.concatenate(parts, axis=1)
        part = jnp.pad(part, ((0, 0), (0, 896 - part.shape[1])))
        part = jnp.concatenate([part, pad_cols(half(w_o, j), count // 2)], axis=1)
        pieces += pieces_of(pad_rows(part, count))
    which = core // share

    def sequence(x):
        whole_one = pick(lax.all_gather(x[:, 0], "ctx", axis=1, tiled=True), which).T
        return whole_one[:, : whole_one.shape[1] // 2], whole_one[:, whole_one.shape[1] // 2 :]

    place = jnp.zeros((4,), jnp.int32)
    wide = count * 64
    spread, unpack = spread_matrix(width, count, wide), unpack_matrix(width, count, wide)
    delta_sum = delta_matrix(width, count, wide)
    cos, sa, sb, aq, ak = tables(pick(positions[:, 0], which), pick(segment_ids[:, 0], which))
    xp, a, q, k, v, w_qkv, w_o, gains = pre_attention(
        place, *sequence(inputs), spread, pieces, cos, sa, sb, aq, ak
    )
    o, q2 = attend(q, k, v)
    op, m, b, df = middle(place, o, *sequence(cotangent), spread, unpack, w_o, xp, gains)
    acc0, db0, gu_send, d_send, d_keep = feed_forward(place, b, df, mine, other, 0)
    acc, db, gu_keep, d_send, d_keep = feed_forward(
        place, b, df, mine, other, 1, (d_send, d_keep, acc0, db0)
    )
    em, do, delta, o_send, o_keep, dgf = after(place, m, db, df, gains, unpack, delta_sum, w_o, op, width)
    out_send, outs = finish(place, m, acc, spread, width)
    parts = attend_back(q2, k, v, do, delta, cos, sa, sb, 0, KV_HEADS)
    flat, p_send, p_keep = projections_back(place, parts, a, w_qkv, gains, dgf)
    gi_send = input_back(place, flat, w_qkv, xp, em, gains, spread, width)
    gis = input_back(place, flat, w_qkv, xp, em, gains, spread, width, gi_send)

    parts = [cut_rows(p, per) for p in (p_keep, p_send)]
    n_q, n_k = HEADS * HEAD // 2, KV_HEADS * HEAD // 2
    both = lambda at, n: jnp.concatenate([p[:, at : at + n] for p in parts], axis=1)
    side = lambda t: jnp.concatenate([t[0], t[1]], axis=-1)

    def wide_of(index):
        every = []
        for t in (gu_keep, gu_send):
            t = t.reshape(count, 5, 2, 64, 256)[:, :, index]
            every.append(cut_rows(t.transpose(0, 2, 1, 3).reshape(count, 64, -1), per))
        return jnp.concatenate(every, axis=1)

    grads = [
        both(0, n_q),
        both(n_q * 1, n_k),
        both(n_q + n_k, n_k),
        cut_cols(cut_rows(jnp.concatenate([side(o_keep), side(o_send)], axis=-1), per), per),
        wide_of(0),
        wide_of(1),
        cut_cols(
            jnp.concatenate([side(d_keep), side(d_send)], axis=-1),
            per,
        ),
    ]

    def summed(g):
        g = lax.psum_scatter(g * (1.0 / share), "dp", scatter_dimension=0, tiled=True)
        return lax.psum_scatter(g, "ctx", scatter_dimension=1, tiled=True).astype(F32)

    sums = [summed(g.astype(BF16)) for g in grads]
    dgain = parts[0][:, 2 * n_k + n_q : 2 * n_k + n_q + 2].astype(F32).T * (1.0 / share)
    dgain = lax.psum_scatter(lax.psum(dgain, "ctx"), "dp", scatter_dimension=1, tiled=True)

    def tokens(seq):
        rows = seq.shape[0] // cores
        every = lax.all_gather(seq, "ctx", axis=0, tiled=False)
        return lax.dynamic_slice_in_dim(every[::share], core * rows, rows, axis=1)[:, None]

    out = jnp.concatenate([outs[0], out_send], axis=1).T
    gi = jnp.concatenate([gis[0], gi_send.astype(F32)], axis=1).T
    return (tokens(out), tokens(gi), *sums, dgain[0], dgain[1])


def solution(mesh):
    two = mesh.shape["ctx"] == MICRO and mesh.shape["dp"] == 16
    matrices = (P("dp", "ctx"),) * 7 + (P("dp"), P("dp"))
    tokens = P(None, "dp", "ctx", None)
    return jax.shard_map(
        shards_of_two if two else shards_of_many,
        mesh=mesh,
        in_specs=(tokens, P(None, "dp", None), P(None, "dp", None)) + matrices + (tokens,),
        out_specs=(tokens, tokens) + matrices,
        check_vma=False,
    )
```

```python
import functools

import jax
import jax.numpy as jnp
from jax import lax
from jax.experimental import pallas as pl
from jax.experimental.pallas import tpu as pltpu
from jax.sharding import PartitionSpec as P

HEADS = 15
KV_HEADS = 5
HEAD = 64
MICRO = 2
GROUP = 3
DOCS = 4

EPSILON = 1e-05
MASKED = -1e30
LANES = 128
QKV = (HEADS + 2 * KV_HEADS) * HEAD
QKV_PAD = 1664
PACK = 1408
MIB = 1024 * 1024
WIDE_HEADS = HEADS * LANES
F32 = jnp.float32
BF16 = jnp.bfloat16


def up(value, step):
    return -(-value // step) * step


def mm(left, right):
    return lax.dot_general(left, right, (((1,), (0,)), ((), ())), preferred_element_type=F32)


def mm_nt(left, right):
    return lax.dot_general(left, right, (((1,), (1,)), ((), ())), preferred_element_type=F32)


def mm_tn(left, right):
    return lax.dot_general(left, right, (((0,), (0,)), ((), ())), preferred_element_type=F32)


def call(body, out_shape, grid, in_specs, out_specs, scratch=(), flops=0, moved=0, prefetch=0, alias=None,
         vmem=8):
    return pl.pallas_call(
        body,
        out_shape=out_shape,
        grid_spec=pltpu.PrefetchScalarGridSpec(
            num_scalar_prefetch=prefetch,
            grid=grid,
            in_specs=in_specs,
            out_specs=out_specs,
            scratch_shapes=scratch,
        ),
        input_output_aliases=alias or {},
        compiler_params=pltpu.CompilerParams(vmem_limit_bytes=vmem * MIB),
        cost_estimate=pl.CostEstimate(flops=flops, bytes_accessed=moved, transcendentals=0),
    )


def whole(shape):
    return pl.BlockSpec(shape, lambda *_: (0,) * len(shape), pipeline_mode=pl.Buffered(1))


def lane_of(rows):
    return lax.broadcasted_iota(jnp.int32, (rows, LANES), 1)


def three_terms(column):
    high = column.astype(BF16).astype(F32)
    rest = column - high
    mid = rest.astype(BF16).astype(F32)
    return high, mid, rest - mid


def put_terms(base, column, lane, first):
    high, mid, low = three_terms(column)
    base = jnp.where(lane == first, high, base)
    base = jnp.where(lane == first + 1, mid, base)
    return jnp.where(lane == first + 2, low, base)


def build_weights(place_ref, piece_refs, stage_ref, w_ref, wo_ref):
    core, z, y, x = (place_ref[n] for n in range(4))
    for swapped in range(2):
        near_a, far_a, near_b, far_b = piece_refs[4 * swapped : 4 * swapped + 4]
        to = jnp.bitwise_xor(core, swapped)
        for dy in range(2):
            for dx in range(2):
                for k in range(4):
                    block = lax.rem(z + 4 - k, 4) * 4 + (y ^ dy) * 2 + (x ^ dx)
                    row = pl.multiple_of(block * 64, 64)
                    stage_ref[to, pl.ds(row, 32), :] = (far_a if dy else near_a)[4 * dx + k]
                    stage_ref[to, pl.ds(row + 32, 32), :] = (far_b if dx else near_b)[4 * dy + k]
    n_q, n_k = HEADS * HEAD // 2, KV_HEADS * HEAD // 2
    for j in range(2):
        w_ref[:, n_q * j : n_q * (j + 1)] = stage_ref[j, :, :n_q]
        for part in range(2):
            to, at = 2 * n_q + n_k * (2 * part + j), n_q + n_k * part
            w_ref[:, to : to + n_k] = stage_ref[j, :, at : at + n_k]
        half = wo_ref.shape[1] // 2
        wo_ref[:, half * j : half * (j + 1)] = stage_ref[j, :, PACK - half :]
    w_ref[:, QKV:] = jnp.zeros((w_ref.shape[0], QKV_PAD - QKV), BF16)


def projections(xp, scale, w_ref, gain_ref, cos_ref, sa_ref, sb_ref, aq_ref, ak_ref,
                xp_ref, a_ref, q_ref, k_ref, v_ref):
    a = (xp * scale * gain_ref[:1]).astype(BF16)
    xp_ref[...] = xp.astype(BF16)
    a_ref[...] = a
    t = mm(a, w_ref[...])
    lane = lane_of(t.shape[0])
    low = lane < HEAD
    cos, sa, sb, aq, ak = cos_ref[...], sa_ref[...], sb_ref[...], aq_ref[...], ak_ref[...]
    for pair in range((HEADS + KV_HEADS) // 2):
        tt = t[:, LANES * pair : LANES * (pair + 1)]
        rot = tt * cos + pltpu.roll(tt, 32, 1) * sa + pltpu.roll(tt, 96, 1) * sb
        for half in range(2):
            head = 2 * pair + half
            val = rot if half == 0 else pltpu.roll(rot, 64, 1)
            if head < HEADS:
                q_ref[head] = jnp.where(low, val * HEAD ** -0.5, aq).astype(BF16)
            else:
                k_ref[head - HEADS] = jnp.where(low, val, ak).astype(BF16)
    av = jnp.where(lane < HEAD + 3, -1.0, 0.0)
    for head in range(KV_HEADS):
        first = (HEADS + KV_HEADS) * HEAD + LANES * (head // 2)
        tt = t[:, first : first + LANES]
        val = tt if head % 2 == 0 else pltpu.roll(tt, 64, 1)
        v_ref[head] = jnp.where(low, val, av).astype(BF16)


def own_or_other(place_ref, own_ref, other_ref):
    first = pl.program_id(0) < pl.num_programs(0) // 2
    mine = first == (place_ref[0] == 0)
    return jnp.where(mine, own_ref[...], other_ref[...])


def pre_body(width, place_ref, own_ref, other_ref, e_ref, *refs):
    pieces, refs = refs[:8], refs[8:]
    *rest, w_ref, wo_ref, gain_ref, stage_ref = refs

    @pl.when(pl.program_id(0) == 0)
    def _():
        build_weights(place_ref, pieces, stage_ref, w_ref, wo_ref)
        gain_ref[...] = stage_ref[0, :, 768:896].astype(F32).T[32:40]

    xp = mm_tn(own_or_other(place_ref, own_ref, other_ref), e_ref[:width, :])
    scale = lax.rsqrt(jnp.sum(xp * xp, axis=-1, keepdims=True) / width + EPSILON)
    projections(xp, scale, w_ref, gain_ref, *rest)


def halves_specs(rows, width, block):
    steps = rows // block
    return [pl.BlockSpec((width, block), lambda i, *_: (0, i % steps))] * 2


def pre_attention(place, own, other, spread, pieces, cos, sa, sb, aq, ak, block=512):
    width, half = own.shape
    seq, wide = 2 * half, spread.shape[1]
    rows = lambda n: pl.BlockSpec((block, n), lambda i, *_: (i, 0))
    heads = lambda n: pl.BlockSpec((n, block, LANES), lambda i, *_: (0, i, 0))
    return call(
        functools.partial(pre_body, width),
        [
            jax.ShapeDtypeStruct((seq, wide), BF16),
            jax.ShapeDtypeStruct((seq, wide), BF16),
            jax.ShapeDtypeStruct((HEADS, seq, LANES), BF16),
            jax.ShapeDtypeStruct((KV_HEADS, seq, LANES), BF16),
            jax.ShapeDtypeStruct((KV_HEADS, seq, LANES), BF16),
            jax.ShapeDtypeStruct((wide, QKV_PAD), BF16),
            jax.ShapeDtypeStruct((wide, wide), BF16),
            jax.ShapeDtypeStruct((8, wide), F32),
        ],
        (seq // block,),
        halves_specs(half, width, block)
        + [whole(spread.shape)]
        + [whole(w.shape) for w in pieces]
        + [rows(LANES)] * 5,
        [rows(wide), rows(wide), heads(HEADS), heads(KV_HEADS), heads(KV_HEADS)]
        + [whole((wide, QKV_PAD)), whole((wide, wide)), whole((8, wide))],
        scratch=[pltpu.VMEM((2, wide, PACK), BF16)],
        flops=2 * seq * wide * (width + QKV_PAD),
        moved=20_000_000,
        vmem=56,
        prefetch=1,
    )(place, own, other, spread, *pieces, cos, sa, sb, aq, ak)


def attend_body(block, q_ref, k_ref, v_ref, o_ref, q2_ref):
    seq = k_ref.shape[1]
    rows = GROUP * block
    below = lax.broadcasted_iota(jnp.int32, (block, block), 0) >= lax.broadcasted_iota(
        jnp.int32, (block, block), 1
    )
    below = jnp.concatenate([below.astype(F32)] * GROUP, axis=0) > 0.5
    lane = lane_of(rows)
    for i in range(seq // block):
        span = slice(block * i, block * (i + 1))
        q = q_ref[:, span, :].reshape(rows, LANES)
        s_in = jnp.where(below, mm_nt(q, k_ref[0, span, :]), MASKED)
        top = jnp.max(s_in, axis=-1, keepdims=True)
        if i:
            s_left = mm_nt(q, k_ref[0, : block * i, :])
            top = jnp.maximum(top, jnp.max(s_left, axis=-1, keepdims=True))
        ext = mm(jnp.exp(s_in - top).astype(BF16), v_ref[0, span, :])
        if i:
            ext = ext + mm(jnp.exp(s_left - top).astype(BF16), v_ref[0, : block * i, :])
        total = -ext[:, HEAD : HEAD + 1]
        o = ext / total
        o = jnp.where(lane < HEAD, o, pltpu.roll(o, 64, 1))
        o_ref[:, span, :] = o.reshape(GROUP, block, LANES).astype(BF16)
        q2 = put_terms(q.astype(F32), top + jnp.log(total), lane, HEAD + DOCS)
        q2_ref[:, span, :] = q2.reshape(GROUP, block, LANES).astype(BF16)


def attend(q, k, v, block=256):
    seq = q.shape[1]
    group = pl.BlockSpec((GROUP, seq, LANES), lambda n: (n, 0, 0))
    one = pl.BlockSpec((1, seq, LANES), lambda n: (n, 0, 0))
    shape = jax.ShapeDtypeStruct(q.shape, BF16)
    return call(
        functools.partial(attend_body, block),
        [shape, shape],
        (KV_HEADS,),
        [group, one, one],
        [group, group],
        flops=4 * HEADS * seq * seq * LANES,
        moved=15_000_000,
        vmem=56,
    )(q, k, v)


def attend_back_body(block, q_ref, k_ref, v_ref, do_ref, delta_ref, cos_ref, sa_ref, sb_ref,
                     dq_ref, dk_ref, dv_ref, acc_ref):
    seq = k_ref.shape[1]
    above = lax.broadcasted_iota(jnp.int32, (block, block), 0) <= lax.broadcasted_iota(
        jnp.int32, (block, block), 1
    )
    lane = lane_of(seq)

    def unrotate(t, span):
        rows = span.stop - span.start
        rot = (
            t * cos_ref[span, :]
            - pltpu.roll(t, 32, 1) * sa_ref[span, :]
            - pltpu.roll(t, 96, 1) * sb_ref[span, :]
        )
        return twice(rot, rows)

    def twice(t, rows):
        return jnp.where(lane[:rows] < HEAD, t, pltpu.roll(t, 64, 1)).astype(BF16)

    for j in range(seq // block):
        span = slice(block * j, block * (j + 1))
        k, v = k_ref[0, span, :], v_ref[0, span, :]
        dk = jnp.zeros((block, LANES), F32)
        dv = jnp.zeros((block, LANES), F32)
        for g in range(GROUP):
            q, do = q_ref[g, block * j :, :], do_ref[g, block * j :, :]
            p = jnp.exp(mm_nt(k, q))
            inner = jnp.where(above, p[:, :block], 0.0)
            p = inner if p.shape[1] == block else jnp.concatenate([inner, p[:, block:]], axis=1)
            ds = (p * (mm_nt(v, do) - delta_ref[g : g + 1, block * j :])).astype(BF16)
            dv = dv + mm(p.astype(BF16), do)
            dk = dk + mm(ds, q)
            dq = mm_tn(ds, k)
            if j == 0:
                acc_ref[g] = dq
            else:
                acc_ref[g, block * j :, :] += dq
        dk_ref[0, span, :] = unrotate(dk, span)
        dv_ref[0, span, :] = twice(dv, block)
    for g in range(GROUP):
        dq_ref[g] = unrotate(acc_ref[g] * HEAD ** -0.5, slice(0, seq))


def attend_back(q, k, v, do, delta, cos, sa, sb, first, count, block=256):
    seq = q.shape[1]
    group = lambda at: pl.BlockSpec((GROUP, seq, LANES), lambda n: (n + at, 0, 0))
    one = lambda at: pl.BlockSpec((1, seq, LANES), lambda n: (n + at, 0, 0))
    return call(
        functools.partial(attend_back_body, block),
        [
            jax.ShapeDtypeStruct((GROUP * count, seq, LANES), BF16),
            jax.ShapeDtypeStruct((count, seq, LANES), BF16),
            jax.ShapeDtypeStruct((count, seq, LANES), BF16),
        ],
        (count,),
        [group(first), one(first), one(first), group(first)]
        + [pl.BlockSpec((8, seq), lambda n: (n + first, 0))]
        + [whole((seq, LANES))] * 3,
        [group(0), one(0), one(0)],
        scratch=[pltpu.VMEM((GROUP, seq, LANES), F32)],
        flops=10 * GROUP * count * seq * seq * LANES,
        moved=4_000_000 * count,
        vmem=12,
    )(q, k, v, do, delta, cos, sa, sb)


def pairs_to(ref, get, heads, first=0):
    for pair in range((heads + 1) // 2):
        left = get(2 * pair)
        lane = lane_of(left.shape[0])
        right = get(2 * pair + 1).astype(F32) if 2 * pair + 1 < heads else 0.0
        both = jnp.where(lane < HEAD, left.astype(F32), right)
        ref[:, first + LANES * pair : first + LANES * (pair + 1)] = both.astype(BF16)


def mid_body(width, place_ref, o_ref, own_ref, other_ref, e_ref, u_ref, wo_ref, xp_ref, gain_ref,
             op_ref, m_ref, b_ref, df_ref):
    flat = jnp.concatenate([o_ref[head] for head in range(HEADS)], axis=1)
    op = mm_nt(flat, u_ref[...]).astype(BF16)
    op_ref[...] = op
    m = xp_ref[...].astype(F32) + mm(op, wo_ref[...])
    m_ref[...] = m
    scale = lax.rsqrt(jnp.sum(m * m, axis=-1, keepdims=True) / width + EPSILON)
    b_ref[...] = (m * scale * gain_ref[1:2]).astype(BF16)
    ct = own_or_other(place_ref, own_ref, other_ref)
    df_ref[...] = mm_tn(ct, e_ref[:width, :]).astype(BF16)


def middle(place, o, own, other, spread, unpack, w_out, xp, gain, block=512):
    width, half = own.shape
    seq, wide = 2 * half, spread.shape[1]
    rows = lambda n: pl.BlockSpec((block, n), lambda i, *_: (i, 0))
    return call(
        functools.partial(mid_body, width),
        [
            jax.ShapeDtypeStruct((seq, wide), BF16),
            jax.ShapeDtypeStruct((seq, wide), F32),
            jax.ShapeDtypeStruct((seq, wide), BF16),
            jax.ShapeDtypeStruct((seq, wide), BF16),
        ],
        (seq // block,),
        [
            pl.BlockSpec((HEADS, block, LANES), lambda i, *_: (0, i, 0)),
            *halves_specs(half, width, block),
            whole(spread.shape),
            whole(unpack.shape),
            whole(w_out.shape),
            rows(wide),
            whole((8, wide)),
        ],
        [rows(wide)] * 4,
        flops=2 * seq * wide * 4 * wide,
        moved=22_000_000,
        vmem=56,
        prefetch=1,
    )(place, o, own, other, spread, unpack, w_out, xp, gain)


def ffn_body(turn, place_ref, b_ref, df_ref, *refs):
    gates, ups, downs, refs = refs[:4], refs[4:8], refs[8:24], refs[24:]
    before, refs = refs[: 4 * turn], refs[4 * turn :]
    out_ref, db_ref, gu_ref, d_send, d_keep, wg_ref, wu_ref, wd_ref, down_sem, *carry = refs
    s = pl.program_id(0)
    core, z_me, y_me, x_me = (place_ref[n] for n in range(4))
    chunk = wg_ref.shape[1]
    half = core if turn else 1 - core
    rows = wd_ref.shape[0] // 8

    def carried(n):
        return pltpu.make_async_copy(before[2 + n], carry[n], carry[2 + n])

    def down_copies():
        for swapped in range(2):
            for q in range(2):
                for near in range(4):
                    for up_z in range(2):
                        k = lax.rem(z_me + 4 - (2 * half + up_z), 4)
                        block = up_z * 4 + (y_me ^ (near // 2)) * 2 + (x_me ^ (near % 2))
                        row = pl.multiple_of(rows * block, 16)
                        col = pl.multiple_of(2 * chunk * (core ^ swapped) + chunk * q, chunk)
                        ref = downs[8 * swapped + 4 * q + near]
                        yield pltpu.make_async_copy(
                            ref.at[k, pl.ds(ref.shape[1] - rows, rows), :],
                            wd_ref.at[pl.ds(row, rows), pl.ds(col, chunk)],
                            down_sem.at[16 * swapped + 8 * q + 2 * near + up_z],
                        )

    @pl.when(s == 0)
    def _():
        for copy in down_copies():
            copy.start()
        out_ref[...] = jnp.zeros_like(out_ref)
        db_ref[...] = jnp.zeros_like(db_ref)
        if turn:
            carried(0).start()
            carried(1).start()

    for near in range(4):
        for k in range(4):
            block = lax.rem(z_me + 4 - k, 4) * 4 + (y_me ^ (near // 2)) * 2 + (x_me ^ (near % 2))
            row = pl.multiple_of(block * 64, 64)
            wg_ref[pl.ds(row, 64), :] = gates[near][k]
            wu_ref[pl.ds(row, 64), :] = ups[near][k]

    @pl.when(s == 0)
    def _():
        for copy in down_copies():
            copy.wait()

    b, df = b_ref[...], df_ref[...]
    wg, wu = wg_ref[...], wu_ref[...]
    wd = wd_ref[pl.ds(pl.multiple_of(chunk * s, chunk), chunk), :]
    gate = mm(b, wg)
    upper = mm(b, wu)
    sig = jax.nn.sigmoid(gate)
    act = gate * sig
    z = (act * upper).astype(BF16)
    dz = mm_nt(df, wd)
    dg = (dz * upper * (sig + act * (1.0 - sig))).astype(BF16)
    du = (dz * act).astype(BF16)

    out_ref[...] += mm(z, wd)
    db_ref[...] += mm_nt(dg, wg) + mm_nt(du, wu)

    if turn:

        @pl.when(s == pl.num_programs(0) - 1)
        def _():
            carried(0).wait()
            carried(1).wait()
            out_ref[...] += carry[0][...]
            db_ref[...] += carry[1][...]

    gu_ref[:, :64] = mm_tn(b, dg).astype(BF16).reshape(gu_ref.shape[0], 64, chunk)
    gu_ref[:, 64:] = mm_tn(b, du).astype(BF16).reshape(gu_ref.shape[0], 64, chunk)
    side = df.shape[1] // 2
    for ref, j in ((d_send, 1 - core), (d_keep, core)):
        dwd = mm_tn(z, df_ref[:, pl.ds(pl.multiple_of(side * j, side), side)]).astype(BF16)
        ref[0] = dwd[:, :chunk]
        ref[1] = dwd[:, chunk:]


def feed_forward(place, b, df, mine, other, turn, before=()):
    seq, wide = b.shape
    blocks, chunks, chunk = 16, 5, 256
    columns = mine if turn else other
    any_spec = pl.BlockSpec(memory_space=pltpu.HBM)
    half_of = lambda place: place[0] if turn else 1 - place[0]
    d_shape = jax.ShapeDtypeStruct((2, 2 * chunks * chunk, chunk), BF16)
    d_spec = pl.BlockSpec((2, chunk, chunk), lambda s, place: (0, half_of(place) * chunks + s, 0))
    return call(
        functools.partial(ffn_body, turn),
        [
            jax.ShapeDtypeStruct((seq, wide), F32),
            jax.ShapeDtypeStruct((seq, wide), F32),
            jax.ShapeDtypeStruct((blocks, 128 * chunks, chunk), BF16),
            d_shape,
            d_shape,
        ],
        (chunks,),
        [whole(b.shape), whole(df.shape)]
        + [pl.BlockSpec((4, 64, chunk), lambda s, place: (0, s, 0))] * 8
        + [any_spec] * (16 + len(before)),
        [
            whole((seq, wide)),
            whole((seq, wide)),
            pl.BlockSpec((blocks, 128, chunk), lambda s, place: (0, s, 0)),
            d_spec,
            d_spec,
        ],
        scratch=[
            pltpu.VMEM((wide, chunk), BF16),
            pltpu.VMEM((wide, chunk), BF16),
            pltpu.VMEM((chunks * chunk, wide), BF16),
            pltpu.SemaphoreType.DMA((32,)),
        ]
        + turn * [pltpu.VMEM((seq, wide), F32)] * 2
        + turn * [pltpu.SemaphoreType.DMA] * 2,
        flops=18 * seq * wide * chunks * chunk,
        moved=40_000_000,
        vmem=56,
        prefetch=1,
        alias={27: 3, 28: 4} if before else None,
    )(place, b, df, *columns, *mine, *other, *before)


def token_block(steps):
    def at(i, place):
        return jnp.where(i < steps // 2, (1 - place[0]) * (steps // 2) + i, place[0] * (steps // 2) + i - steps // 2)

    return at


def token_specs(steps, block, width):
    half = steps // 2
    return [
        pl.BlockSpec((width, block), lambda i, place: (0, jnp.minimum(i, half - 1))),
        pl.BlockSpec((1, width, block), lambda i, place: (place[0], 0, jnp.maximum(i - half, 0))),
    ]


def put_tokens(send_ref, keep_ref, value):
    early = pl.program_id(0) < pl.num_programs(0) // 2

    @pl.when(early)
    def _():
        send_ref[...] = value.astype(send_ref.dtype)

    @pl.when(jnp.logical_not(early))
    def _():
        keep_ref[0] = value.astype(keep_ref.dtype)


def post_body(width, place_ref, m_ref, db_ref, df_ref, gain_ref, u_ref,
              sum_ref, wo_ref, op_ref,
              em_ref, do_ref, delta_ref, dwo_send, dwo_keep, dgain_ref, da_ref):
    i = pl.program_id(0)
    m, db = m_ref[...], db_ref[...]
    scale = lax.rsqrt(jnp.sum(m * m, axis=-1, keepdims=True) / width + EPSILON)
    n = m * scale
    c = db * gain_ref[1:2]
    mean = jnp.sum(c * n, axis=-1, keepdims=True) / width
    em = df_ref[...].astype(F32) + scale * (c - n * mean)
    em_ref[...] = em
    da = em.astype(BF16)
    dgain = jnp.sum(db * n, axis=0, keepdims=True)
    block = m.shape[0]
    rows = pl.ds(pl.multiple_of(block * i, block), block)
    da_ref[rows, :] = da

    @pl.when(i == 0)
    def _():
        dgain_ref[...] = dgain

    @pl.when(i > 0)
    def _():
        dgain_ref[...] += dgain

    do = mm_nt(da, wo_ref[...]).astype(BF16)
    product = do.astype(F32) * op_ref[rows, :].astype(F32)
    high = product.astype(BF16)
    low = (product - high.astype(F32)).astype(BF16)
    delta_ref[...] = mm_nt(sum_ref[...], high) + mm_nt(sum_ref[...], low)
    do = mm(do, u_ref[...]).astype(BF16)
    for head in range(HEADS):
        do_ref[head] = do[:, LANES * head : LANES * (head + 1)]

    @pl.when(i == pl.num_programs(0) - 1)
    def _():
        half = da_ref.shape[1] // 2
        for ref, j in ((dwo_send, 1 - place_ref[0]), (dwo_keep, place_ref[0])):
            dwo = mm_tn(op_ref[...], da_ref[:, pl.ds(pl.multiple_of(half * j, half), half)]).astype(BF16)
            for q in range(2):
                ref[q] = dwo[:, 256 * q : 256 * (q + 1)].reshape(ref.shape[1:])


def after(place, m, db, df, gain, unpack, delta_sum, w_out, op, width, block=512):
    seq, wide = m.shape
    blocks = 16
    steps = seq // block
    rows = lambda n: pl.BlockSpec((block, n), lambda i, place: (i, 0))
    heads = pl.BlockSpec((HEADS, block, LANES), lambda i, place: (0, i, 0))
    dwo_shape = (2, blocks, wide // blocks, 256)
    consts = (gain, unpack, delta_sum, w_out, op)
    return call(
        functools.partial(post_body, width),
        [
            jax.ShapeDtypeStruct((seq, wide), F32),
            jax.ShapeDtypeStruct((HEADS, seq, LANES), BF16),
            jax.ShapeDtypeStruct((8 * KV_HEADS, seq), F32),
            jax.ShapeDtypeStruct(dwo_shape, BF16),
            jax.ShapeDtypeStruct(dwo_shape, BF16),
            jax.ShapeDtypeStruct((1, wide), F32),
        ],
        (steps,),
        [rows(wide)] * 3 + [whole(t.shape) for t in consts],
        [
            rows(wide),
            heads,
            pl.BlockSpec((8 * KV_HEADS, block), lambda i, place: (0, i)),
            whole(dwo_shape),
            whole(dwo_shape),
            whole((1, wide)),
        ],
        scratch=[pltpu.VMEM((seq, wide), BF16)],
        flops=2 * seq * wide * 6 * wide,
        moved=40_000_000,
        vmem=56,
        prefetch=1,
    )(place, m, db, df, *consts)


def finish_body(width, place_ref, m_ref, acc_ref, e_ref, send_ref, keep_ref):
    out = (m_ref[...] + acc_ref[...]).astype(BF16)
    put_tokens(send_ref, keep_ref, mm_nt(e_ref[:width, :], out))


def finish(place, m, acc, spread, width, block=256):
    seq, wide = m.shape
    steps = seq // block
    at = token_block(steps)
    rows = lambda n: pl.BlockSpec((block, n), lambda i, place: (at(i, place), 0))
    return call(
        functools.partial(finish_body, width),
        [
            jax.ShapeDtypeStruct((width, seq // 2), BF16),
            jax.ShapeDtypeStruct((2, width, seq // 2), BF16),
        ],
        (steps,),
        [rows(wide), rows(wide), whole(spread.shape)],
        token_specs(steps, block, width),
        flops=2 * seq * wide * wide,
        moved=16_000_000,
        vmem=8,
        prefetch=1,
    )(place, m, acc, spread)


def weights_body(place_ref, dq_ref, dk_ref, dv_ref, a_ref, w_ref, gain_ref,
                 dgain_ref, flat_ref, send_ref, keep_ref, dw_acc, part_ref, all_ref):
    i = pl.program_id(0)
    heads = HEADS + KV_HEADS

    pairs_to(flat_ref, lambda h: dq_ref[h] if h < HEADS else dk_ref[h - HEADS], heads)
    pairs_to(flat_ref, lambda h: dv_ref[h], KV_HEADS, heads * HEAD)
    block = flat_ref.shape[0]
    all_ref[pl.ds(pl.multiple_of(block * i, block), block), :] = flat_ref[...]

    @pl.when(i == pl.num_programs(0) - 1)
    def _():
        wide = dw_acc.shape[0]
        dw_acc[...] = mm_tn(a_ref[...], all_ref[...])
        total = jnp.sum(dw_acc[...] * w_ref[...].astype(F32), axis=-1, keepdims=True)
        column = lambda row: jnp.broadcast_to(row, (LANES, wide)).T
        gain = column(gain_ref[:1])
        attn = jnp.broadcast_to(total, (wide, LANES)) / jnp.where(gain == 0.0, 1.0, gain)
        lane = lane_of(wide)
        gains = jnp.where(lane == 32, attn, 0.0) + jnp.where(lane == 33, column(dgain_ref[...]), 0.0)
        n_q, n_k = HEADS * HEAD // 2, KV_HEADS * HEAD // 2
        for j in range(2):
            part_ref[:, 768:] = gains.astype(BF16)
            part_ref[:, :n_q] = dw_acc[:, n_q * j : n_q * (j + 1)].astype(BF16)
            for part in range(2):
                at, to = 2 * n_q + n_k * (2 * part + j), n_q + n_k * part
                part_ref[:, to : to + n_k] = dw_acc[:, at : at + n_k].astype(BF16)
            for ref, here in ((keep_ref, place_ref[0] == j), (send_ref, place_ref[0] != j)):

                @pl.when(here)
                def _():
                    ref[...] = part_ref[...].reshape(ref.shape)


def projections_back(place, parts, a, w_qkv, gain, dgain_ffn, block=256):
    seq, wide = a.shape
    blocks = 16
    rows = lambda n: pl.BlockSpec((block, n), lambda i, *_: (i, 0))
    heads = lambda t: pl.BlockSpec((t.shape[0], block, LANES), lambda i, *_: (0, i, 0))
    shape = (blocks, wide // blocks, 896)
    return call(
        weights_body,
        [
            jax.ShapeDtypeStruct((seq, QKV_PAD), BF16),
            jax.ShapeDtypeStruct(shape, BF16),
            jax.ShapeDtypeStruct(shape, BF16),
        ],
        (seq // block,),
        [heads(t) for t in parts] + [whole(a.shape), whole(w_qkv.shape), whole((8, wide)), whole((1, wide))],
        [rows(QKV_PAD), whole(shape), whole(shape)],
        scratch=[
            pltpu.VMEM((wide, QKV_PAD), F32),
            pltpu.VMEM((wide, 896), BF16),
            pltpu.VMEM((seq, QKV_PAD), BF16),
        ],
        flops=2 * seq * wide * QKV_PAD,
        moved=20_000_000,
        vmem=28,
        prefetch=1,
    )(place, *parts, a, w_qkv, gain, dgain_ffn)


def input_body(width, keep, place_ref, flat_ref, w_ref, xp_ref, em_ref, gain_ref, e_ref, *refs):
    got_ref, to_ref = refs if keep else (None, refs[0])
    i = pl.program_id(0)
    steps = pl.num_programs(0) // (2 if keep else 1)

    def work():
        da = mm_nt(flat_ref[...], w_ref[...])
        xp = xp_ref[...].astype(F32)
        scale = lax.rsqrt(jnp.sum(xp * xp, axis=-1, keepdims=True) / width + EPSILON)
        n = xp * scale
        c = da * gain_ref[:1]
        mean = jnp.sum(c * n, axis=-1, keepdims=True) / width
        grad = em_ref[...] + scale * (c - n * mean)
        return mm_nt(e_ref[:width, :], grad.astype(BF16))

    if keep:

        @pl.when(i < steps)
        def _():
            to_ref[0] = work()

        @pl.when(i >= steps)
        def _():
            to_ref[0] = got_ref[...].astype(F32)

    else:
        to_ref[...] = work().astype(BF16)


def input_back(place, flat, w_qkv, xp, em, gain, spread, width, got=None, block=256):
    seq, wide = xp.shape
    steps = seq // 2 // block
    keep = got is not None
    token = lambda i, place: (place[0] if keep else 1 - place[0]) * steps + jnp.minimum(i, steps - 1)
    rows = lambda n: pl.BlockSpec((block, n), lambda i, place: (token(i, place), 0))
    ins = [rows(QKV_PAD), whole(w_qkv.shape), rows(wide), rows(wide), whole((8, wide)), whole(spread.shape)]
    if keep:
        ins.append(pl.BlockSpec((width, block), lambda i, place: (0, jnp.maximum(i - steps, 0))))
        shape = jax.ShapeDtypeStruct((2, width, seq // 2), F32)
        half = lambda i, place: jnp.where(i < steps, place[0], 1 - place[0])
        out = pl.BlockSpec((1, width, block), lambda i, place: (half(i, place), 0, lax.rem(i, steps)))
    else:
        shape = jax.ShapeDtypeStruct((width, seq // 2), BF16)
        out = pl.BlockSpec((width, block), lambda i, place: (0, i))
    return call(
        functools.partial(input_body, width, keep),
        [shape],
        (steps * (2 if keep else 1),),
        ins,
        [out],
        flops=seq * wide * (QKV_PAD + width),
        moved=10_000_000,
        vmem=56 if keep else 8,
        prefetch=1,
    )(place, flat, w_qkv, xp, em, gain, spread, *([got] if keep else []))[0]


def begin_body(reader, n_in, place_ref, *refs):
    ins, outs = refs[:n_in], refs[n_in:]
    _, _, y, x = (place_ref[n] for n in range(4))
    for side in range(2):
        mine = y if side else x
        for other in range(2):
            for ref, bit in ((outs[2 * side], 1 - mine), (outs[2 * side + 1], mine)):
                block = 2 * bit + other if side else 2 * other + bit
                for row, keep, got in reader(ins, side, block):
                    ref[other, row : row + keep.shape[0]] = add(keep, got)


def begin(place, arrays, reader, rows, count=4):
    n = arrays[0].shape[-1]

    def spec(t):
        lead = t.shape[:-3]
        return pl.BlockSpec((*lead, 4, *t.shape[-2:]), lambda i, place: (0,) * len(lead) + (i, 0, 0))

    shape = jax.ShapeDtypeStruct((2 * count, rows, n), BF16)
    return call(
        functools.partial(begin_body, reader, len(arrays)),
        [shape] * 4,
        (count,),
        [spec(t) for t in arrays],
        [pl.BlockSpec((2, rows, n), lambda i, place: (i, 0, 0))] * 4,
        flops=1,
        moved=16 * count * rows * n * 6,
        vmem=24,
        prefetch=1,
    )(place, *arrays)


def turn_body(place_ref, *refs):
    y, x = place_ref[2], place_ref[3]
    for side in range(2):
        keep, got = refs[2 * side : 2 * side + 2]
        mine = x if side else y
        for ref, bit in ((refs[4 + 2 * side], 1 - mine), (refs[5 + 2 * side], mine)):
            ref[0] = add(keep[bit], got[bit])


def turn(place, keeps, gots):
    blocks, rows, n = keeps[0].shape
    shape = jax.ShapeDtypeStruct((blocks // 2, rows, n), BF16)
    return call(
        turn_body,
        [shape] * 4,
        (blocks // 2,),
        [pl.BlockSpec((2, rows, n), lambda i, place: (i, 0, 0))] * 4,
        [pl.BlockSpec((1, rows, n), lambda i, place: (i, 0, 0))] * 4,
        flops=1,
        moved=blocks * rows * n * 12,
        vmem=24,
        prefetch=1,
    )(place, keeps[0], gots[0], keeps[1], gots[1])


def climb_body(place_ref, a_keep, a_got, b_keep, b_got, total_ref, *sent):
    for step in range(4):
        block = lax.rem(place_ref[1] + step, 4)
        for side, (keep, got) in enumerate(((a_keep, a_got), (b_keep, b_got))):
            value = keep[block].astype(F32) + got[block].astype(F32)
            if step:
                sent[step - 1][side] = value.astype(BF16)
            else:
                total_ref[side] = value


def climb(place, keeps, gots):
    _, rows, n = keeps[0].shape
    return call(
        climb_body,
        [jax.ShapeDtypeStruct((2, rows, n), F32)] + [jax.ShapeDtypeStruct((2, rows, n), BF16)] * 3,
        (1,),
        [whole(keeps[0].shape)] * 4,
        [whole((2, rows, n))] * 4,
        flops=1,
        moved=rows * n * 50,
        vmem=24,
        prefetch=1,
    )(place, keeps[0], gots[0], keeps[1], gots[1])


def unpack_matrix(width, blocks, wide):
    per, step = width // blocks, wide // blocks
    col = jnp.arange(WIDE_HEADS, dtype=jnp.int32)
    feature = col // LANES * HEAD + col % LANES
    place = jnp.where(col % LANES < HEAD, feature // per * step + feature % per, -1)
    return (jnp.arange(wide, dtype=jnp.int32)[:, None] == place[None, :]).astype(BF16)


def delta_matrix(width, blocks, wide):
    per, step = width // blocks, wide // blocks
    col = jnp.arange(wide, dtype=jnp.int32)
    head = jnp.where(col % step < per, (col // step * per + col % step) // HEAD, -1)
    row = jnp.arange(8 * KV_HEADS, dtype=jnp.int32)
    mine = jnp.where(row % 8 < GROUP, row // 8 * GROUP + row % 8, -2)
    return (mine[:, None] == head[None, :]).astype(BF16)


def spread_matrix(width, blocks, wide):
    row = jnp.arange(wide, dtype=jnp.int32)
    per, step = width // blocks, wide // blocks
    place = (row // per) * step + row % per
    hit = (place[:, None] == jnp.arange(wide, dtype=jnp.int32)[None, :]) & (row < width)[:, None]
    return hit.astype(BF16)


def tables(positions, segments):
    lane = jnp.arange(LANES, dtype=jnp.int32)
    frequency = 10000.0 ** (-((lane % 32).astype(F32) * 2.0 / HEAD))
    angles = positions.astype(F32)[:, None] * frequency[None, :]
    cos, sin = jnp.cos(angles), jnp.sin(angles)
    high = (lane % HEAD >= 32)[None, :]
    sa = jnp.where(high, sin, 0.0)
    sb = jnp.where(high, 0.0, -sin)
    doc = (lane - HEAD)[None, :]
    mine = segments[:, None] == doc
    in_doc = (doc >= 0) & (doc < DOCS)
    aq = jnp.where(mine & in_doc, MASKED, 0.0)
    ak = jnp.where(in_doc & ~mine, 1.0, 0.0)
    ak = jnp.where((doc >= DOCS) & (doc < DOCS + 3), -1.0, ak)
    return cos, sa, sb, aq, ak


def pad_rows(w, blocks, step=64):
    per = w.shape[0] // blocks
    return jnp.pad(w.reshape(blocks, per, w.shape[1]), ((0, 0), (0, step - per), (0, 0)))


def pad_cols(w, blocks, step=64):
    per = w.shape[1] // blocks
    w = jnp.pad(w.reshape(w.shape[0], blocks, per), ((0, 0), (0, 0), (0, step - per)))
    return w.reshape(w.shape[0], blocks * step)


def cut_rows(w, per):
    return w[:, :per].reshape(w.shape[0] * per, w.shape[2])


def cut_cols(w, per, step=64):
    blocks = w.shape[1] // step
    return w.reshape(w.shape[0], blocks, step)[:, :, :per].reshape(w.shape[0], blocks * per)


def chunked(w, chunk=256):
    blocks, rows, cols = w.shape
    w = w.reshape(blocks, rows, cols // chunk, chunk).transpose(0, 2, 1, 3)
    return w.reshape(blocks, cols // chunk * rows, chunk)


def joined(w, rows):
    blocks, total, chunk = w.shape
    w = w.reshape(blocks, total // rows, rows, chunk).transpose(0, 2, 1, 3)
    return w.reshape(blocks, rows, total // rows * chunk)


def pack_half(w_gate, w_up, w_down, blocks, groups):
    down = pad_cols(w_down, groups)
    down = down.reshape(blocks, w_down.shape[0] // blocks, down.shape[1])
    gate, upper = chunked(pad_rows(w_gate, blocks)), chunked(pad_rows(w_up, blocks))
    return jnp.concatenate([gate, down[:, :, :256], upper, down[:, :, 256:]], axis=1)


def add(left, right):
    return (left.astype(F32) + right.astype(F32)).astype(BF16)


def swap(x):
    return lax.ppermute(x, "ctx", [(0, 1), (1, 0)])


def across(x, bit, count):
    return lax.ppermute(x, "dp", [(i, i ^ (1 << bit)) for i in range(count)])


def pick(x, index, axis=0):
    return lax.dynamic_index_in_dim(x, index, axis, keepdims=False)


def tie(value, *others):
    return lax.optimization_barrier((value, *others))[0]


def tie_all(values, *others):
    return lax.optimization_barrier((*values, *others))[: len(values)]


def along_z(x, step, count):
    return lax.ppermute(x, "dp", [(i, (i + 4 * step) % count) for i in range(count)])


def rise(x, count):
    return [x] + [along_z(x, k, count) for k in (1, 2, 3)]


def spread_first(stack, count):
    half = stack.shape[1] // 2
    first, second = stack[:, :half], stack[:, half:]
    return first, across(first, 0, count), second, across(second, 1, count)


def spread_second(first, first_got, second, second_got, count):
    first, second = jnp.concatenate([first, first_got]), jnp.concatenate([second, second_got])
    return first, across(first, 1, count), second, across(second, 0, count)


def pieces_of(whole_one):
    n = whole_one.shape[1] // 2
    cube = whole_one.reshape(4, 2, 2, 2 * n, -1)
    cube = jnp.stack([cube[(4 - k) % 4] for k in range(4)])
    first, second = cube[:, :, :, :n], cube[:, :, :, n:]
    first, second = first.transpose(1, 2, 0, 3, 4), second.transpose(2, 1, 0, 3, 4)
    flat = lambda t: t.reshape(8, n, -1)
    return flat(first[0]), flat(first[1]), flat(second[0]), flat(second[1])


def fine_pieces_of(whole_one):
    n = whole_one.shape[1] // 2
    cube = whole_one.reshape(4, 2, 2, 2 * n, -1)
    cube = jnp.stack([cube[(4 - k) % 4] for k in range(4)])
    near = [cube[:, dy, dx] for dy in range(2) for dx in range(2)]
    return [t[:, :n] for t in near] + [t[:, n:] for t in near]


class RowSum:
    def __init__(self, place, count, arrays, reader, rows):
        self.place, self.count = place, count
        a_sent, a_kept, b_sent, b_kept = begin(place, arrays, reader, rows)
        self.sent, self.kept = [a_sent, b_sent], [a_kept, b_kept]

    def move(self):
        self.got = [across(self.sent[0], 0, self.count), across(self.sent[1], 1, self.count)]

    def wait(self, other):
        self.got = list(lax.optimization_barrier((*self.got, other))[:-1])

    def turn(self, other):
        self.wait(other)
        a_sent, a_kept, b_sent, b_kept = turn(self.place, self.kept, self.got)
        self.sent, self.kept = [a_sent, b_sent], [a_kept, b_kept]

    def move_again(self):
        self.got = [across(self.sent[0], 1, self.count), across(self.sent[1], 0, self.count)]

    def climb(self, other):
        self.wait(other)
        self.kept, *self.sent = climb(self.place, self.kept, self.got)

    def start_up(self):
        return along_z(self.sent[1], 1, self.count)

    def start_down(self):
        return along_z(self.sent[2], 3, self.count)

    def go_up(self, got):
        return along_z(add(self.sent[0], got), 1, self.count)

    def move_up(self):
        return [along_z(self.sent[k - 1], k, self.count) for k in (1, 2, 3)]

    def total(self, *gots):
        total = self.kept
        for got in gots:
            total = total + got.astype(F32)
        return total


def read_rows(ins, side, block):
    half = ins[0].shape[1] // 2
    rows = slice(half * side, half * (side + 1))
    return [(0, ins[0][block, rows], ins[1][block, rows])]


def read_quarters(ins, side, block):
    first = ins[0].shape[2]
    return [(0, ins[0][side, block], ins[1][side, block]), (first, ins[2][side, block], ins[3][side, block])]


def put_other(both, got, core):
    return lax.dynamic_update_slice(both, got[None], (1 - core, 0, 0))


def shards_of_two(inputs, segment_ids, positions, w_query, w_key, w_value, w_out, w_gate, w_up,
                  w_down, gain_attn, gain_ffn, cotangent):
    count = lax.axis_size("dp")
    me, core = lax.axis_index("dp"), lax.axis_index("ctx")
    place = (core, me // 4, (me >> 1) & 1, me & 1)
    place_of = jnp.stack(place).astype(jnp.int32)
    per = gain_attn.shape[0]
    width = per * count
    groups = w_out.shape[1] // per
    hidden = w_down.shape[0]
    n_q, n_k = w_query.shape[1], w_key.shape[1]
    n_qkv = n_q + 2 * n_k

    shard = jnp.concatenate(
        [w_query, w_key, w_value, gain_attn[:, None], gain_ffn[:, None]], axis=1
    )
    shard = jnp.pad(shard, ((0, 0), (0, 896 - n_qkv - 2)))
    shard = jnp.concatenate([shard, pad_cols(w_out, groups)], axis=1)
    shard = jnp.pad(shard, ((0, 64 - per), (0, 0)))
    packed = pack_half(w_gate, w_up, w_down, 1, groups)[0]

    def halves(x):
        x = jnp.swapaxes(x[:, 0], 1, 2)
        return pick(x, core), swap(pick(x, 1 - core))

    wide = count * 64
    spread, unpack = spread_matrix(width, count, wide), unpack_matrix(width, count, wide)
    delta_sum = delta_matrix(width, count, wide)
    table = tables(pick(positions[:, 0], core), pick(segment_ids[:, 0], core))

    level = rise(shard, count)
    x_own, x_other = halves(inputs)
    ct_own, ct_other = halves(cotangent)
    stack = tie(jnp.stack(level), packed, x_other, ct_other)
    part = spread_first(stack, count)
    packed = tie(packed, stack)
    up, down = along_z(packed, 1, count), along_z(packed, 3, count)
    near_far = spread_second(*part, count)
    up, down = tie_all((up, down), part[0])
    up_two = along_z(up, 1, count)
    near_far = tie_all(near_far, up_two, down, spread, delta_sum, unpack, *table)
    pieces = near_far + tuple(swap(t) for t in near_far)
    packs = jnp.stack(tie_all((packed, up, up_two, down), near_far[0]))
    half = packs.shape[1] // 2
    a00, b00 = packs[:, :half], packs[:, half:]
    a01, b10 = across(a00, 0, count), across(b00, 1, count)

    pieces = tie_all(pieces, a00, b00)
    xp, a, q, k, v, w_qkv, w_o, gains = pre_attention(place_of, x_own, x_other, spread, pieces, *table)
    a01, b10, a00, b00 = tie_all((a01, b10, a00, b00), q)
    a10, b01 = across(a00, 1, count), across(b00, 0, count)
    got = [swap(a00), swap(b00), swap(a01)]
    q = tie(q, a01, b10)
    o, q2 = attend(q, k, v)
    a10, b01, *got = tie_all((a10, b01, *got), o)
    a11, b11 = across(tie(a01, a10), 1, count), across(tie(b10, a10), 0, count)
    got += [swap(b10), swap(a10), swap(b01)]
    op, m, b, df = middle(
        place_of, tie(o, a10, b01, *got[:3]), ct_own, ct_other, spread, unpack, w_o, xp, gains
    )
    a11, b11, *got = tie_all((a11, b11, *got), b)
    mine = [a00, a01, a10, a11, b00, b01, b10, b11]
    other = [got[0], got[2], got[4], swap(a11), got[1], got[5], got[3], swap(b11)]

    acc0, db0, gu_send, d_send, d_keep = feed_forward(place_of, b, df, mine, other, 0)
    gu_got = swap(gu_send)
    acc, db, gu_keep, d_send, d_keep = feed_forward(
        place_of, tie(b, gu_send), df, mine, other, 1, (d_send, d_keep, acc0, db0)
    )
    one = RowSum(place_of, count, (gu_keep, tie(gu_got, acc)), read_rows, 320)
    one.move()
    blocked = lambda t: t.reshape(2, count, hidden, 256)
    d_got = swap(d_send)
    m = tie(m, *one.sent, d_send)
    em, do, delta, o_send, o_keep, dgf = after(place_of, m, db, df, gains, unpack, delta_sum, w_o, op, width)
    o_got = swap(o_send)
    one.turn(em)
    one.move_again()
    two = RowSum(
        place_of, count, (blocked(d_keep), blocked(tie(d_got, em)), o_keep, o_got), read_quarters, 224
    )
    two.move()
    do = tie(do, *one.sent, *two.sent)
    parts = attend_back(q2, k, v, do, delta, *table[:3], 0, KV_HEADS)
    one.climb(parts[0])
    up, down = one.start_up(), one.start_down()
    two.turn(parts[0])
    two.move_again()
    a = tie(a, *one.sent, *two.sent)
    flat, p_send, p_keep = projections_back(place_of, parts, a, w_qkv, gains, dgf)
    up, down, *two.got = tie_all((up, down, *two.got), flat)
    p_got = swap(tie(p_send, up))
    two.climb(flat)
    one_up, one_down, two_up = one.go_up(up), down, two.start_up()
    three = RowSum(place_of, count, (p_keep, p_got), read_rows, 32)
    three.move()
    flat = tie(flat, *two.sent, *three.sent)
    gi_send = input_back(place_of, flat, w_qkv, xp, em, gains, spread, width)
    *three.got, one_up, two_up = tie_all((*three.got, one_up, two_up), gi_send)
    three.turn(gi_send)
    three.move_again()
    gi_got = swap(tie(gi_send, *three.sent))
    two_up = two.go_up(tie(two_up, *three.sent))
    two.sent[2] = tie(two.sent[2], *three.sent)
    two_down = two.start_down()
    out_send, outs = finish(place_of, tie(m, *three.sent), acc, spread, width)
    first = tie(one.total(one_up, one_down), outs)
    *three.got, gi_got, two_up = tie_all((*three.got, gi_got, two_up), outs)
    three.climb(gi_got)
    last_got = three.move_up()
    out_got = swap(out_send)
    gis = input_back(place_of, tie(flat, *three.sent, out_send), w_qkv, xp, em, gains, spread, width, gi_got)
    last_got = tie_all(last_got, gis)
    outs = put_other(outs, tie(out_got, gis), core)
    second, third = two.total(two_up, two_down), three.total(*last_got)
    third = third.reshape(64, 896)[:per]
    gu = first.reshape(5, 2, 64, 256)
    wide_of = lambda t: t.transpose(1, 0, 2).reshape(t.shape[1], -1)
    tokens = lambda t: jnp.swapaxes(t, 1, 2)[:, None]
    return (
        tokens(outs),
        tokens(gis),
        third[:, :n_q],
        third[:, n_q : n_q + n_k],
        third[:, n_q + n_k : n_qkv],
        cut_cols(wide_of(second[:, 160:])[:per], per),
        wide_of(gu[:, 0])[:per],
        wide_of(gu[:, 1])[:per],
        cut_cols(wide_of(second[:, :160]), per),
        third[:, n_qkv],
        third[:, n_qkv + 1],
    )


def shards_of_many(inputs, segment_ids, positions, w_query, w_key, w_value, w_out, w_gate, w_up,
                   w_down, gain_attn, gain_ffn, cotangent):
    count, cores = lax.axis_size("dp"), lax.axis_size("ctx")
    core = lax.axis_index("ctx")
    share = cores // MICRO
    per = gain_attn.shape[0]
    width = per * count

    def gathered(w):
        return lax.all_gather(lax.all_gather(w, "dp", axis=0, tiled=True), "ctx", axis=1, tiled=True)

    full = [gathered(w) for w in (w_query, w_key, w_value, w_out, w_gate, w_up, w_down)]
    gain_pair = lax.all_gather(jnp.stack([gain_attn, gain_ffn]), "dp", axis=1, tiled=True)
    w_o, w_g, w_u, w_d = full[3:]
    half = lambda w, j: w[:, w.shape[1] // 2 * j : w.shape[1] // 2 * (j + 1)]
    packs = [pack_half(half(w_g, j), half(w_u, j), half(w_d, j), count, count // 2) for j in range(2)]
    mine, other = (fine_pieces_of(p) for p in packs)
    pieces = []
    for j in range(2):
        parts = [half(w, j) for w in full[:3]] + [gain_pair.T]
        part = jnp.concatenate(parts, axis=1)
        part = jnp.pad(part, ((0, 0), (0, 896 - part.shape[1])))
        part = jnp.concatenate([part, pad_cols(half(w_o, j), count // 2)], axis=1)
        pieces += pieces_of(pad_rows(part, count))
    which = core // share

    def sequence(x):
        whole_one = pick(lax.all_gather(x[:, 0], "ctx", axis=1, tiled=True), which).T
        return whole_one[:, : whole_one.shape[1] // 2], whole_one[:, whole_one.shape[1] // 2 :]

    place = jnp.zeros((4,), jnp.int32)
    wide = count * 64
    spread, unpack = spread_matrix(width, count, wide), unpack_matrix(width, count, wide)
    delta_sum = delta_matrix(width, count, wide)
    cos, sa, sb, aq, ak = tables(pick(positions[:, 0], which), pick(segment_ids[:, 0], which))
    xp, a, q, k, v, w_qkv, w_o, gains = pre_attention(
        place, *sequence(inputs), spread, pieces, cos, sa, sb, aq, ak
    )
    o, q2 = attend(q, k, v)
    op, m, b, df = middle(place, o, *sequence(cotangent), spread, unpack, w_o, xp, gains)
    acc0, db0, gu_send, d_send, d_keep = feed_forward(place, b, df, mine, other, 0)
    acc, db, gu_keep, d_send, d_keep = feed_forward(
        place, b, df, mine, other, 1, (d_send, d_keep, acc0, db0)
    )
    em, do, delta, o_send, o_keep, dgf = after(place, m, db, df, gains, unpack, delta_sum, w_o, op, width)
    out_send, outs = finish(place, m, acc, spread, width)
    parts = attend_back(q2, k, v, do, delta, cos, sa, sb, 0, KV_HEADS)
    flat, p_send, p_keep = projections_back(place, parts, a, w_qkv, gains, dgf)
    gi_send = input_back(place, flat, w_qkv, xp, em, gains, spread, width)
    gis = input_back(place, flat, w_qkv, xp, em, gains, spread, width, gi_send)

    parts = [cut_rows(p, per) for p in (p_keep, p_send)]
    n_q, n_k = HEADS * HEAD // 2, KV_HEADS * HEAD // 2
    both = lambda at, n: jnp.concatenate([p[:, at : at + n] for p in parts], axis=1)
    side = lambda t: jnp.concatenate([t[0], t[1]], axis=-1)

    def wide_of(index):
        every = []
        for t in (gu_keep, gu_send):
            t = t.reshape(count, 5, 2, 64, 256)[:, :, index]
            every.append(cut_rows(t.transpose(0, 2, 1, 3).reshape(count, 64, -1), per))
        return jnp.concatenate(every, axis=1)

    grads = [
        both(0, n_q),
        both(n_q * 1, n_k),
        both(n_q + n_k, n_k),
        cut_cols(cut_rows(jnp.concatenate([side(o_keep), side(o_send)], axis=-1), per), per),
        wide_of(0),
        wide_of(1),
        cut_cols(
            jnp.concatenate([side(d_keep), side(d_send)], axis=-1),
            per,
        ),
    ]

    def summed(g):
        g = lax.psum_scatter(g * (1.0 / share), "dp", scatter_dimension=0, tiled=True)
        return lax.psum_scatter(g, "ctx", scatter_dimension=1, tiled=True).astype(F32)

    sums = [summed(g.astype(BF16)) for g in grads]
    dgain = parts[0][:, 2 * n_k + n_q : 2 * n_k + n_q + 2].astype(F32).T * (1.0 / share)
    dgain = lax.psum_scatter(lax.psum(dgain, "ctx"), "dp", scatter_dimension=1, tiled=True)

    def tokens(seq):
        rows = seq.shape[0] // cores
        every = lax.all_gather(seq, "ctx", axis=0, tiled=False)
        return lax.dynamic_slice_in_dim(every[::share], core * rows, rows, axis=1)[:, None]

    out = jnp.concatenate([outs[0], out_send], axis=1).T
    gi = jnp.concatenate([gis[0], gi_send.astype(F32)], axis=1).T
    return (tokens(out), tokens(gi), *sums, dgain[0], dgain[1])


def solution(mesh):
    two = mesh.shape["ctx"] == MICRO and mesh.shape["dp"] == 16
    matrices = (P("dp", "ctx"),) * 7 + (P("dp"), P("dp"))
    tokens = P(None, "dp", "ctx", None)
    return jax.shard_map(
        shards_of_two if two else shards_of_many,
        mesh=mesh,
        in_specs=(tokens, P(None, "dp", None), P(None, "dp", None)) + matrices + (tokens,),
        out_specs=(tokens, tokens) + matrices,
        check_vma=False,
    )
```

```python
import functools

import jax
import jax.numpy as jnp
from jax import lax
from jax.experimental import pallas as pl
from jax.experimental.pallas import tpu as pltpu
from jax.sharding import PartitionSpec as P

HEADS = 15
KV_HEADS = 5
HEAD = 64
MICRO = 2
GROUP = 3
DOCS = 4

EPSILON = 1e-05
MASKED = -1e30
LANES = 128
QKV = (HEADS + 2 * KV_HEADS) * HEAD
QKV_PAD = 1664
PACK = 1408
MIB = 1024 * 1024
WIDE_HEADS = HEADS * LANES
F32 = jnp.float32
BF16 = jnp.bfloat16


def up(value, step):
    return -(-value // step) * step


def mm(left, right):
    return lax.dot_general(left, right, (((1,), (0,)), ((), ())), preferred_element_type=F32)


def mm_nt(left, right):
    return lax.dot_general(left, right, (((1,), (1,)), ((), ())), preferred_element_type=F32)


def mm_tn(left, right):
    return lax.dot_general(left, right, (((0,), (0,)), ((), ())), preferred_element_type=F32)


def call(body, out_shape, grid, in_specs, out_specs, scratch=(), flops=0, moved=0, prefetch=0, alias=None,
         vmem=8):
    return pl.pallas_call(
        body,
        out_shape=out_shape,
        grid_spec=pltpu.PrefetchScalarGridSpec(
            num_scalar_prefetch=prefetch,
            grid=grid,
            in_specs=in_specs,
            out_specs=out_specs,
            scratch_shapes=scratch,
        ),
        input_output_aliases=alias or {},
        compiler_params=pltpu.CompilerParams(vmem_limit_bytes=vmem * MIB),
        cost_estimate=pl.CostEstimate(flops=flops, bytes_accessed=moved, transcendentals=0),
    )


def whole(shape):
    return pl.BlockSpec(shape, lambda *_: (0,) * len(shape), pipeline_mode=pl.Buffered(1))


def lane_of(rows):
    return lax.broadcasted_iota(jnp.int32, (rows, LANES), 1)


def three_terms(column):
    high = column.astype(BF16).astype(F32)
    rest = column - high
    mid = rest.astype(BF16).astype(F32)
    return high, mid, rest - mid


def put_terms(base, column, lane, first):
    high, mid, low = three_terms(column)
    base = jnp.where(lane == first, high, base)
    base = jnp.where(lane == first + 1, mid, base)
    return jnp.where(lane == first + 2, low, base)


def build_weights(place_ref, piece_refs, stage_ref, w_ref, wo_ref):
    core, z, y, x = (place_ref[n] for n in range(4))
    for swapped in range(2):
        near_a, far_a, near_b, far_b = piece_refs[4 * swapped : 4 * swapped + 4]
        to = jnp.bitwise_xor(core, swapped)
        for dy in range(2):
            for dx in range(2):
                for k in range(4):
                    block = lax.rem(z + 4 - k, 4) * 4 + (y ^ dy) * 2 + (x ^ dx)
                    row = pl.multiple_of(block * 64, 64)
                    stage_ref[to, pl.ds(row, 32), :] = (far_a if dy else near_a)[4 * dx + k]
                    stage_ref[to, pl.ds(row + 32, 32), :] = (far_b if dx else near_b)[4 * dy + k]
    n_q, n_k = HEADS * HEAD // 2, KV_HEADS * HEAD // 2
    for j in range(2):
        w_ref[:, n_q * j : n_q * (j + 1)] = stage_ref[j, :, :n_q]
        for part in range(2):
            to, at = 2 * n_q + n_k * (2 * part + j), n_q + n_k * part
            w_ref[:, to : to + n_k] = stage_ref[j, :, at : at + n_k]
        half = wo_ref.shape[1] // 2
        wo_ref[:, half * j : half * (j + 1)] = stage_ref[j, :, PACK - half :]
    w_ref[:, QKV:] = jnp.zeros((w_ref.shape[0], QKV_PAD - QKV), BF16)


def projections(xp, scale, w_ref, gain_ref, cos_ref, sa_ref, sb_ref, aq_ref, ak_ref,
                xp_ref, a_ref, q_ref, k_ref, v_ref):
    a = (xp * scale * gain_ref[:1]).astype(BF16)
    xp_ref[...] = xp.astype(BF16)
    a_ref[...] = a
    t = mm(a, w_ref[...])
    lane = lane_of(t.shape[0])
    low = lane < HEAD
    cos, sa, sb, aq, ak = cos_ref[...], sa_ref[...], sb_ref[...], aq_ref[...], ak_ref[...]
    for pair in range((HEADS + KV_HEADS) // 2):
        tt = t[:, LANES * pair : LANES * (pair + 1)]
        rot = tt * cos + pltpu.roll(tt, 32, 1) * sa + pltpu.roll(tt, 96, 1) * sb
        for half in range(2):
            head = 2 * pair + half
            val = rot if half == 0 else pltpu.roll(rot, 64, 1)
            if head < HEADS:
                q_ref[head] = jnp.where(low, val * HEAD ** -0.5, aq).astype(BF16)
            else:
                k_ref[head - HEADS] = jnp.where(low, val, ak).astype(BF16)
    av = jnp.where(lane < HEAD + 3, -1.0, 0.0)
    for head in range(KV_HEADS):
        first = (HEADS + KV_HEADS) * HEAD + LANES * (head // 2)
        tt = t[:, first : first + LANES]
        val = tt if head % 2 == 0 else pltpu.roll(tt, 64, 1)
        v_ref[head] = jnp.where(low, val, av).astype(BF16)


def own_or_other(place_ref, own_ref, other_ref):
    first = pl.program_id(0) < pl.num_programs(0) // 2
    mine = first == (place_ref[0] == 0)
    return jnp.where(mine, own_ref[...], other_ref[...])


def pre_body(width, place_ref, own_ref, other_ref, e_ref, *refs):
    pieces, refs = refs[:8], refs[8:]
    *rest, w_ref, wo_ref, gain_ref, stage_ref = refs

    @pl.when(pl.program_id(0) == 0)
    def _():
        build_weights(place_ref, pieces, stage_ref, w_ref, wo_ref)
        gain_ref[...] = jnp.zeros_like(gain_ref)
        step = stage_ref.shape[1] // 16
        for block in range(16):
            end = step * (block + 1)
            tail = stage_ref[0, end - 16 : end, :step].astype(F32)
            gain_ref[:2, end - step : end] = tail[12:14]

    xp = mm_tn(own_or_other(place_ref, own_ref, other_ref), e_ref[:width, :])
    scale = lax.rsqrt(jnp.sum(xp * xp, axis=-1, keepdims=True) / width + EPSILON)
    projections(xp, scale, w_ref, gain_ref, *rest)


def halves_specs(rows, width, block):
    steps = rows // block
    return [pl.BlockSpec((width, block), lambda i, *_: (0, i % steps))] * 2


def pre_attention(place, own, other, spread, pieces, cos, sa, sb, aq, ak, block=512):
    width, half = own.shape
    seq, wide = 2 * half, spread.shape[1]
    rows = lambda n: pl.BlockSpec((block, n), lambda i, *_: (i, 0))
    heads = lambda n: pl.BlockSpec((n, block, LANES), lambda i, *_: (0, i, 0))
    return call(
        functools.partial(pre_body, width),
        [
            jax.ShapeDtypeStruct((seq, wide), BF16),
            jax.ShapeDtypeStruct((seq, wide), BF16),
            jax.ShapeDtypeStruct((HEADS, seq, LANES), BF16),
            jax.ShapeDtypeStruct((KV_HEADS, seq, LANES), BF16),
            jax.ShapeDtypeStruct((KV_HEADS, seq, LANES), BF16),
            jax.ShapeDtypeStruct((wide, QKV_PAD), BF16),
            jax.ShapeDtypeStruct((wide, wide), BF16),
            jax.ShapeDtypeStruct((8, wide), F32),
        ],
        (seq // block,),
        halves_specs(half, width, block)
        + [whole(spread.shape)]
        + [whole(w.shape) for w in pieces]
        + [rows(LANES)] * 5,
        [rows(wide), rows(wide), heads(HEADS), heads(KV_HEADS), heads(KV_HEADS)]
        + [whole((wide, QKV_PAD)), whole((wide, wide)), whole((8, wide))],
        scratch=[pltpu.VMEM((2, wide, PACK), BF16)],
        flops=2 * seq * wide * (width + QKV_PAD),
        moved=20_000_000,
        vmem=56,
        prefetch=1,
    )(place, own, other, spread, *pieces, cos, sa, sb, aq, ak)


def attend_body(block, q_ref, k_ref, v_ref, o_ref, q2_ref):
    seq = k_ref.shape[1]
    rows = GROUP * block
    below = lax.broadcasted_iota(jnp.int32, (block, block), 0) >= lax.broadcasted_iota(
        jnp.int32, (block, block), 1
    )
    below = jnp.concatenate([below.astype(F32)] * GROUP, axis=0) > 0.5
    lane = lane_of(rows)
    for i in range(seq // block):
        span = slice(block * i, block * (i + 1))
        q = q_ref[:, span, :].reshape(rows, LANES)
        s_in = jnp.where(below, mm_nt(q, k_ref[0, span, :]), MASKED)
        top = jnp.max(s_in, axis=-1, keepdims=True)
        if i:
            s_left = mm_nt(q, k_ref[0, : block * i, :])
            top = jnp.maximum(top, jnp.max(s_left, axis=-1, keepdims=True))
        ext = mm(jnp.exp(s_in - top).astype(BF16), v_ref[0, span, :])
        if i:
            ext = ext + mm(jnp.exp(s_left - top).astype(BF16), v_ref[0, : block * i, :])
        total = -ext[:, HEAD : HEAD + 1]
        o = ext / total
        o = jnp.where(lane < HEAD, o, pltpu.roll(o, 64, 1))
        o_ref[:, span, :] = o.reshape(GROUP, block, LANES).astype(BF16)
        q2 = put_terms(q.astype(F32), top + jnp.log(total), lane, HEAD + DOCS)
        q2_ref[:, span, :] = q2.reshape(GROUP, block, LANES).astype(BF16)


def attend(q, k, v, block=256):
    seq = q.shape[1]
    group = pl.BlockSpec((GROUP, seq, LANES), lambda n: (n, 0, 0))
    one = pl.BlockSpec((1, seq, LANES), lambda n: (n, 0, 0))
    shape = jax.ShapeDtypeStruct(q.shape, BF16)
    return call(
        functools.partial(attend_body, block),
        [shape, shape],
        (KV_HEADS,),
        [group, one, one],
        [group, group],
        flops=4 * HEADS * seq * seq * LANES,
        moved=15_000_000,
        vmem=56,
    )(q, k, v)


def attend_back_body(block, q_ref, k_ref, v_ref, do_ref, delta_ref, cos_ref, sa_ref, sb_ref,
                     dq_ref, dk_ref, dv_ref, acc_ref):
    seq = k_ref.shape[1]
    above = lax.broadcasted_iota(jnp.int32, (block, block), 0) <= lax.broadcasted_iota(
        jnp.int32, (block, block), 1
    )
    lane = lane_of(seq)

    def unrotate(t, span):
        rows = span.stop - span.start
        rot = (
            t * cos_ref[span, :]
            - pltpu.roll(t, 32, 1) * sa_ref[span, :]
            - pltpu.roll(t, 96, 1) * sb_ref[span, :]
        )
        return twice(rot, rows)

    def twice(t, rows):
        return jnp.where(lane[:rows] < HEAD, t, pltpu.roll(t, 64, 1)).astype(BF16)

    for j in range(seq // block):
        span = slice(block * j, block * (j + 1))
        k, v = k_ref[0, span, :], v_ref[0, span, :]
        dk = jnp.zeros((block, LANES), F32)
        dv = jnp.zeros((block, LANES), F32)
        for g in range(GROUP):
            q, do = q_ref[g, block * j :, :], do_ref[g, block * j :, :]
            p = jnp.exp(mm_nt(k, q))
            inner = jnp.where(above, p[:, :block], 0.0)
            p = inner if p.shape[1] == block else jnp.concatenate([inner, p[:, block:]], axis=1)
            ds = (p * (mm_nt(v, do) - delta_ref[g : g + 1, block * j :])).astype(BF16)
            dv = dv + mm(p.astype(BF16), do)
            dk = dk + mm(ds, q)
            dq = mm_tn(ds, k)
            if j == 0:
                acc_ref[g] = dq
            else:
                acc_ref[g, block * j :, :] += dq
        dk_ref[0, span, :] = unrotate(dk, span)
        dv_ref[0, span, :] = twice(dv, block)
    for g in range(GROUP):
        dq_ref[g] = unrotate(acc_ref[g] * HEAD ** -0.5, slice(0, seq))


def attend_back(q, k, v, do, delta, cos, sa, sb, first, count, block=256):
    seq = q.shape[1]
    group = lambda at: pl.BlockSpec((GROUP, seq, LANES), lambda n: (n + at, 0, 0))
    one = lambda at: pl.BlockSpec((1, seq, LANES), lambda n: (n + at, 0, 0))
    return call(
        functools.partial(attend_back_body, block),
        [
            jax.ShapeDtypeStruct((GROUP * count, seq, LANES), BF16),
            jax.ShapeDtypeStruct((count, seq, LANES), BF16),
            jax.ShapeDtypeStruct((count, seq, LANES), BF16),
        ],
        (count,),
        [group(first), one(first), one(first), group(first)]
        + [pl.BlockSpec((8, seq), lambda n: (n + first, 0))]
        + [whole((seq, LANES))] * 3,
        [group(0), one(0), one(0)],
        scratch=[pltpu.VMEM((GROUP, seq, LANES), F32)],
        flops=10 * GROUP * count * seq * seq * LANES,
        moved=4_000_000 * count,
        vmem=12,
    )(q, k, v, do, delta, cos, sa, sb)


def pairs_to(ref, get, heads, first=0):
    for pair in range((heads + 1) // 2):
        left = get(2 * pair)
        lane = lane_of(left.shape[0])
        right = get(2 * pair + 1).astype(F32) if 2 * pair + 1 < heads else 0.0
        both = jnp.where(lane < HEAD, left.astype(F32), right)
        ref[:, first + LANES * pair : first + LANES * (pair + 1)] = both.astype(BF16)


def mid_body(width, place_ref, o_ref, own_ref, other_ref, e_ref, u_ref, wo_ref, xp_ref, gain_ref,
             op_ref, m_ref, b_ref, df_ref):
    flat = jnp.concatenate([o_ref[head] for head in range(HEADS)], axis=1)
    op = mm_nt(flat, u_ref[...]).astype(BF16)
    op_ref[...] = op
    m = xp_ref[...].astype(F32) + mm(op, wo_ref[...])
    m_ref[...] = m
    scale = lax.rsqrt(jnp.sum(m * m, axis=-1, keepdims=True) / width + EPSILON)
    b_ref[...] = (m * scale * gain_ref[1:2]).astype(BF16)
    ct = own_or_other(place_ref, own_ref, other_ref)
    df_ref[...] = mm_tn(ct, e_ref[:width, :]).astype(BF16)


def middle(place, o, own, other, spread, unpack, w_out, xp, gain, block=512):
    width, half = own.shape
    seq, wide = 2 * half, spread.shape[1]
    rows = lambda n: pl.BlockSpec((block, n), lambda i, *_: (i, 0))
    return call(
        functools.partial(mid_body, width),
        [
            jax.ShapeDtypeStruct((seq, wide), BF16),
            jax.ShapeDtypeStruct((seq, wide), F32),
            jax.ShapeDtypeStruct((seq, wide), BF16),
            jax.ShapeDtypeStruct((seq, wide), BF16),
        ],
        (seq // block,),
        [
            pl.BlockSpec((HEADS, block, LANES), lambda i, *_: (0, i, 0)),
            *halves_specs(half, width, block),
            whole(spread.shape),
            whole(unpack.shape),
            whole(w_out.shape),
            rows(wide),
            whole((8, wide)),
        ],
        [rows(wide)] * 4,
        flops=2 * seq * wide * 4 * wide,
        moved=22_000_000,
        vmem=56,
        prefetch=1,
    )(place, o, own, other, spread, unpack, w_out, xp, gain)


def ffn_body(turn, place_ref, b_ref, df_ref, *refs):
    gates, ups, downs, refs = refs[:4], refs[4:8], refs[8:24], refs[24:]
    before, refs = refs[: 4 * turn], refs[4 * turn :]
    out_ref, db_ref, gu_ref, d_send, d_keep, wg_ref, wu_ref, wd_ref, down_sem, *carry = refs
    s = pl.program_id(0)
    core, z_me, y_me, x_me = (place_ref[n] for n in range(4))
    chunk = wg_ref.shape[1]
    half = core if turn else 1 - core
    rows = wd_ref.shape[0] // 8

    def carried(n):
        return pltpu.make_async_copy(before[2 + n], carry[n], carry[2 + n])

    def down_copies():
        for swapped in range(2):
            for q in range(2):
                for near in range(4):
                    for up_z in range(2):
                        k = lax.rem(z_me + 4 - (2 * half + up_z), 4)
                        block = up_z * 4 + (y_me ^ (near // 2)) * 2 + (x_me ^ (near % 2))
                        row = pl.multiple_of(rows * block, 16)
                        col = pl.multiple_of(2 * chunk * (core ^ swapped) + chunk * q, chunk)
                        ref = downs[8 * swapped + 4 * q + near]
                        yield pltpu.make_async_copy(
                            ref.at[k, pl.ds(ref.shape[1] - rows, rows), :],
                            wd_ref.at[pl.ds(row, rows), pl.ds(col, chunk)],
                            down_sem.at[16 * swapped + 8 * q + 2 * near + up_z],
                        )

    @pl.when(s == 0)
    def _():
        for copy in down_copies():
            copy.start()
        out_ref[...] = jnp.zeros_like(out_ref)
        db_ref[...] = jnp.zeros_like(db_ref)
        if turn:
            carried(0).start()
            carried(1).start()

    for near in range(4):
        for k in range(4):
            block = lax.rem(z_me + 4 - k, 4) * 4 + (y_me ^ (near // 2)) * 2 + (x_me ^ (near % 2))
            row = pl.multiple_of(block * 64, 64)
            wg_ref[pl.ds(row, 64), :] = gates[near][k]
            wu_ref[pl.ds(row, 64), :] = ups[near][k]

    @pl.when(s == 0)
    def _():
        for copy in down_copies():
            copy.wait()

    b, df = b_ref[...], df_ref[...]
    wg, wu = wg_ref[...], wu_ref[...]
    wd = wd_ref[pl.ds(pl.multiple_of(chunk * s, chunk), chunk), :]
    gate = mm(b, wg)
    upper = mm(b, wu)
    sig = jax.nn.sigmoid(gate)
    act = gate * sig
    z = (act * upper).astype(BF16)
    dz = mm_nt(df, wd)
    dg = (dz * upper * (sig + act * (1.0 - sig))).astype(BF16)
    du = (dz * act).astype(BF16)

    out_ref[...] += mm(z, wd)
    db_ref[...] += mm_nt(dg, wg) + mm_nt(du, wu)

    if turn:

        @pl.when(s == pl.num_programs(0) - 1)
        def _():
            carried(0).wait()
            carried(1).wait()
            out_ref[...] += carry[0][...]
            db_ref[...] += carry[1][...]

    gu_ref[:, :64] = mm_tn(b, dg).astype(BF16).reshape(gu_ref.shape[0], 64, chunk)
    gu_ref[:, 64:] = mm_tn(b, du).astype(BF16).reshape(gu_ref.shape[0], 64, chunk)
    side = df.shape[1] // 2
    for ref, j in ((d_send, 1 - core), (d_keep, core)):
        dwd = mm_tn(z, df_ref[:, pl.ds(pl.multiple_of(side * j, side), side)]).astype(BF16)
        ref[0] = dwd[:, :chunk]
        ref[1] = dwd[:, chunk:]


def feed_forward(place, b, df, mine, other, turn, before=()):
    seq, wide = b.shape
    blocks, chunks, chunk = 16, 5, 256
    columns = mine if turn else other
    any_spec = pl.BlockSpec(memory_space=pltpu.HBM)
    half_of = lambda place: place[0] if turn else 1 - place[0]
    d_shape = jax.ShapeDtypeStruct((2, 2 * chunks * chunk, chunk), BF16)
    d_spec = pl.BlockSpec((2, chunk, chunk), lambda s, place: (0, half_of(place) * chunks + s, 0))
    return call(
        functools.partial(ffn_body, turn),
        [
            jax.ShapeDtypeStruct((seq, wide), F32),
            jax.ShapeDtypeStruct((seq, wide), F32),
            jax.ShapeDtypeStruct((blocks, 128 * chunks, chunk), BF16),
            d_shape,
            d_shape,
        ],
        (chunks,),
        [whole(b.shape), whole(df.shape)]
        + [pl.BlockSpec((4, 64, chunk), lambda s, place: (0, s, 0))] * 8
        + [any_spec] * (16 + len(before)),
        [
            whole((seq, wide)),
            whole((seq, wide)),
            pl.BlockSpec((blocks, 128, chunk), lambda s, place: (0, s, 0)),
            d_spec,
            d_spec,
        ],
        scratch=[
            pltpu.VMEM((wide, chunk), BF16),
            pltpu.VMEM((wide, chunk), BF16),
            pltpu.VMEM((chunks * chunk, wide), BF16),
            pltpu.SemaphoreType.DMA((32,)),
        ]
        + turn * [pltpu.VMEM((seq, wide), F32)] * 2
        + turn * [pltpu.SemaphoreType.DMA] * 2,
        flops=18 * seq * wide * chunks * chunk,
        moved=40_000_000,
        vmem=56,
        prefetch=1,
        alias={27: 3, 28: 4} if before else None,
    )(place, b, df, *columns, *mine, *other, *before)


def token_block(steps):
    def at(i, place):
        return jnp.where(i < steps // 2, (1 - place[0]) * (steps // 2) + i, place[0] * (steps // 2) + i - steps // 2)

    return at


def token_specs(steps, block, width):
    half = steps // 2
    return [
        pl.BlockSpec((width, block), lambda i, place: (0, jnp.minimum(i, half - 1))),
        pl.BlockSpec((1, width, block), lambda i, place: (place[0], 0, jnp.maximum(i - half, 0))),
    ]


def put_tokens(send_ref, keep_ref, value):
    early = pl.program_id(0) < pl.num_programs(0) // 2

    @pl.when(early)
    def _():
        send_ref[...] = value.astype(send_ref.dtype)

    @pl.when(jnp.logical_not(early))
    def _():
        keep_ref[0] = value.astype(keep_ref.dtype)


def post_body(width, place_ref, m_ref, db_ref, df_ref, gain_ref, u_ref,
              sum_ref, wo_ref, op_ref,
              em_ref, do_ref, delta_ref, dwo_send, dwo_keep, dgain_ref, da_ref):
    i = pl.program_id(0)
    m, db = m_ref[...], db_ref[...]
    scale = lax.rsqrt(jnp.sum(m * m, axis=-1, keepdims=True) / width + EPSILON)
    n = m * scale
    c = db * gain_ref[1:2]
    mean = jnp.sum(c * n, axis=-1, keepdims=True) / width
    em = df_ref[...].astype(F32) + scale * (c - n * mean)
    em_ref[...] = em
    da = em.astype(BF16)
    dgain = jnp.sum(db * n, axis=0, keepdims=True)
    block = m.shape[0]
    rows = pl.ds(pl.multiple_of(block * i, block), block)
    da_ref[rows, :] = da

    @pl.when(i == 0)
    def _():
        dgain_ref[...] = dgain

    @pl.when(i > 0)
    def _():
        dgain_ref[...] += dgain

    do = mm_nt(da, wo_ref[...]).astype(BF16)
    product = do.astype(F32) * op_ref[rows, :].astype(F32)
    high = product.astype(BF16)
    low = (product - high.astype(F32)).astype(BF16)
    delta_ref[...] = mm_nt(sum_ref[...], high) + mm_nt(sum_ref[...], low)
    do = mm(do, u_ref[...]).astype(BF16)
    for head in range(HEADS):
        do_ref[head] = do[:, LANES * head : LANES * (head + 1)]

    @pl.when(i == pl.num_programs(0) - 1)
    def _():
        half = da_ref.shape[1] // 2
        for ref, j in ((dwo_send, 1 - place_ref[0]), (dwo_keep, place_ref[0])):
            dwo = mm_tn(op_ref[...], da_ref[:, pl.ds(pl.multiple_of(half * j, half), half)]).astype(BF16)
            for q in range(2):
                ref[q] = dwo[:, 256 * q : 256 * (q + 1)].reshape(ref.shape[1:])


def after(place, m, db, df, gain, unpack, delta_sum, w_out, op, width, block=512):
    seq, wide = m.shape
    blocks = 16
    steps = seq // block
    rows = lambda n: pl.BlockSpec((block, n), lambda i, place: (i, 0))
    heads = pl.BlockSpec((HEADS, block, LANES), lambda i, place: (0, i, 0))
    dwo_shape = (2, blocks, wide // blocks, 256)
    consts = (gain, unpack, delta_sum, w_out, op)
    return call(
        functools.partial(post_body, width),
        [
            jax.ShapeDtypeStruct((seq, wide), F32),
            jax.ShapeDtypeStruct((HEADS, seq, LANES), BF16),
            jax.ShapeDtypeStruct((8 * KV_HEADS, seq), F32),
            jax.ShapeDtypeStruct(dwo_shape, BF16),
            jax.ShapeDtypeStruct(dwo_shape, BF16),
            jax.ShapeDtypeStruct((1, wide), F32),
        ],
        (steps,),
        [rows(wide)] * 3 + [whole(t.shape) for t in consts],
        [
            rows(wide),
            heads,
            pl.BlockSpec((8 * KV_HEADS, block), lambda i, place: (0, i)),
            whole(dwo_shape),
            whole(dwo_shape),
            whole((1, wide)),
        ],
        scratch=[pltpu.VMEM((seq, wide), BF16)],
        flops=2 * seq * wide * 6 * wide,
        moved=40_000_000,
        vmem=56,
        prefetch=1,
    )(place, m, db, df, *consts)


def finish_body(width, place_ref, m_ref, acc_ref, e_ref, send_ref, keep_ref):
    out = (m_ref[...] + acc_ref[...]).astype(BF16)
    put_tokens(send_ref, keep_ref, mm_nt(e_ref[:width, :], out))


def finish(place, m, acc, spread, width, block=256):
    seq, wide = m.shape
    steps = seq // block
    at = token_block(steps)
    rows = lambda n: pl.BlockSpec((block, n), lambda i, place: (at(i, place), 0))
    return call(
        functools.partial(finish_body, width),
        [
            jax.ShapeDtypeStruct((width, seq // 2), BF16),
            jax.ShapeDtypeStruct((2, width, seq // 2), BF16),
        ],
        (steps,),
        [rows(wide), rows(wide), whole(spread.shape)],
        token_specs(steps, block, width),
        flops=2 * seq * wide * wide,
        moved=16_000_000,
        vmem=8,
        prefetch=1,
    )(place, m, acc, spread)


def weights_body(place_ref, dq_ref, dk_ref, dv_ref, a_ref, w_ref, gain_ref,
                 dgain_ref, flat_ref, send_ref, keep_ref, dw_acc, part_ref, all_ref):
    i = pl.program_id(0)
    heads = HEADS + KV_HEADS

    pairs_to(flat_ref, lambda h: dq_ref[h] if h < HEADS else dk_ref[h - HEADS], heads)
    pairs_to(flat_ref, lambda h: dv_ref[h], KV_HEADS, heads * HEAD)
    block = flat_ref.shape[0]
    all_ref[pl.ds(pl.multiple_of(block * i, block), block), :] = flat_ref[...]

    @pl.when(i == pl.num_programs(0) - 1)
    def _():
        wide = dw_acc.shape[0]
        dw_acc[...] = mm_tn(a_ref[...], all_ref[...])
        total = jnp.sum(dw_acc[...] * w_ref[...].astype(F32), axis=-1, keepdims=True)
        column = lambda row: jnp.broadcast_to(row, (LANES, wide)).T
        gain = column(gain_ref[:1])
        attn = jnp.broadcast_to(total, (wide, LANES)) / jnp.where(gain == 0.0, 1.0, gain)
        lane = lane_of(wide)
        gains = jnp.where(lane == 32, attn, 0.0) + jnp.where(lane == 33, column(dgain_ref[...]), 0.0)
        n_q, n_k = HEADS * HEAD // 2, KV_HEADS * HEAD // 2
        for j in range(2):
            part_ref[:, 768:] = gains.astype(BF16)
            part_ref[:, :n_q] = dw_acc[:, n_q * j : n_q * (j + 1)].astype(BF16)
            for part in range(2):
                at, to = 2 * n_q + n_k * (2 * part + j), n_q + n_k * part
                part_ref[:, to : to + n_k] = dw_acc[:, at : at + n_k].astype(BF16)
            for ref, here in ((keep_ref, place_ref[0] == j), (send_ref, place_ref[0] != j)):

                @pl.when(here)
                def _():
                    ref[...] = part_ref[...].reshape(ref.shape)


def projections_back(place, parts, a, w_qkv, gain, dgain_ffn, block=256):
    seq, wide = a.shape
    blocks = 16
    rows = lambda n: pl.BlockSpec((block, n), lambda i, *_: (i, 0))
    heads = lambda t: pl.BlockSpec((t.shape[0], block, LANES), lambda i, *_: (0, i, 0))
    shape = (blocks, wide // blocks, 896)
    return call(
        weights_body,
        [
            jax.ShapeDtypeStruct((seq, QKV_PAD), BF16),
            jax.ShapeDtypeStruct(shape, BF16),
            jax.ShapeDtypeStruct(shape, BF16),
        ],
        (seq // block,),
        [heads(t) for t in parts] + [whole(a.shape), whole(w_qkv.shape), whole((8, wide)), whole((1, wide))],
        [rows(QKV_PAD), whole(shape), whole(shape)],
        scratch=[
            pltpu.VMEM((wide, QKV_PAD), F32),
            pltpu.VMEM((wide, 896), BF16),
            pltpu.VMEM((seq, QKV_PAD), BF16),
        ],
        flops=2 * seq * wide * QKV_PAD,
        moved=20_000_000,
        vmem=28,
        prefetch=1,
    )(place, *parts, a, w_qkv, gain, dgain_ffn)


def input_body(width, keep, place_ref, flat_ref, w_ref, xp_ref, em_ref, gain_ref, e_ref, *refs):
    got_ref, to_ref = refs if keep else (None, refs[0])
    i = pl.program_id(0)
    steps = pl.num_programs(0) // (2 if keep else 1)

    def work():
        da = mm_nt(flat_ref[...], w_ref[...])
        xp = xp_ref[...].astype(F32)
        scale = lax.rsqrt(jnp.sum(xp * xp, axis=-1, keepdims=True) / width + EPSILON)
        n = xp * scale
        c = da * gain_ref[:1]
        mean = jnp.sum(c * n, axis=-1, keepdims=True) / width
        grad = em_ref[...] + scale * (c - n * mean)
        return mm_nt(e_ref[:width, :], grad.astype(BF16))

    if keep:

        @pl.when(i < steps)
        def _():
            to_ref[0] = work()

        @pl.when(i >= steps)
        def _():
            to_ref[0] = got_ref[...].astype(F32)

    else:
        to_ref[...] = work().astype(BF16)


def input_back(place, flat, w_qkv, xp, em, gain, spread, width, got=None, block=256):
    seq, wide = xp.shape
    steps = seq // 2 // block
    keep = got is not None
    token = lambda i, place: (place[0] if keep else 1 - place[0]) * steps + jnp.minimum(i, steps - 1)
    rows = lambda n: pl.BlockSpec((block, n), lambda i, place: (token(i, place), 0))
    ins = [rows(QKV_PAD), whole(w_qkv.shape), rows(wide), rows(wide), whole((8, wide)), whole(spread.shape)]
    if keep:
        ins.append(pl.BlockSpec((width, block), lambda i, place: (0, jnp.maximum(i - steps, 0))))
        shape = jax.ShapeDtypeStruct((2, width, seq // 2), F32)
        half = lambda i, place: jnp.where(i < steps, place[0], 1 - place[0])
        out = pl.BlockSpec((1, width, block), lambda i, place: (half(i, place), 0, lax.rem(i, steps)))
    else:
        shape = jax.ShapeDtypeStruct((width, seq // 2), BF16)
        out = pl.BlockSpec((width, block), lambda i, place: (0, i))
    return call(
        functools.partial(input_body, width, keep),
        [shape],
        (steps * (2 if keep else 1),),
        ins,
        [out],
        flops=seq * wide * (QKV_PAD + width),
        moved=10_000_000,
        vmem=56 if keep else 8,
        prefetch=1,
    )(place, flat, w_qkv, xp, em, gain, spread, *([got] if keep else []))[0]


def begin_body(reader, n_in, place_ref, *refs):
    ins, outs = refs[:n_in], refs[n_in:]
    _, _, y, x = (place_ref[n] for n in range(4))
    for side in range(2):
        mine = y if side else x
        for other in range(2):
            for ref, bit in ((outs[2 * side], 1 - mine), (outs[2 * side + 1], mine)):
                block = 2 * bit + other if side else 2 * other + bit
                for row, keep, got in reader(ins, side, block):
                    ref[other, row : row + keep.shape[0]] = add(keep, got)


def begin(place, arrays, reader, rows, count=4):
    n = arrays[0].shape[-1]

    def spec(t):
        lead = t.shape[:-3]
        return pl.BlockSpec((*lead, 4, *t.shape[-2:]), lambda i, place: (0,) * len(lead) + (i, 0, 0))

    shape = jax.ShapeDtypeStruct((2 * count, rows, n), BF16)
    return call(
        functools.partial(begin_body, reader, len(arrays)),
        [shape] * 4,
        (count,),
        [spec(t) for t in arrays],
        [pl.BlockSpec((2, rows, n), lambda i, place: (i, 0, 0))] * 4,
        flops=1,
        moved=16 * count * rows * n * 6,
        vmem=24,
        prefetch=1,
    )(place, *arrays)


def turn_body(place_ref, *refs):
    y, x = place_ref[2], place_ref[3]
    for side in range(2):
        keep, got = refs[2 * side : 2 * side + 2]
        mine = x if side else y
        for ref, bit in ((refs[4 + 2 * side], 1 - mine), (refs[5 + 2 * side], mine)):
            ref[0] = add(keep[bit], got[bit])


def turn(place, keeps, gots):
    blocks, rows, n = keeps[0].shape
    shape = jax.ShapeDtypeStruct((blocks // 2, rows, n), BF16)
    return call(
        turn_body,
        [shape] * 4,
        (blocks // 2,),
        [pl.BlockSpec((2, rows, n), lambda i, place: (i, 0, 0))] * 4,
        [pl.BlockSpec((1, rows, n), lambda i, place: (i, 0, 0))] * 4,
        flops=1,
        moved=blocks * rows * n * 12,
        vmem=24,
        prefetch=1,
    )(place, keeps[0], gots[0], keeps[1], gots[1])


def climb_body(place_ref, a_keep, a_got, b_keep, b_got, total_ref, *sent):
    for step in range(4):
        block = lax.rem(place_ref[1] + step, 4)
        for side, (keep, got) in enumerate(((a_keep, a_got), (b_keep, b_got))):
            value = keep[block].astype(F32) + got[block].astype(F32)
            if step:
                sent[step - 1][side] = value.astype(BF16)
            else:
                total_ref[side] = value


def climb(place, keeps, gots):
    _, rows, n = keeps[0].shape
    return call(
        climb_body,
        [jax.ShapeDtypeStruct((2, rows, n), F32)] + [jax.ShapeDtypeStruct((2, rows, n), BF16)] * 3,
        (1,),
        [whole(keeps[0].shape)] * 4,
        [whole((2, rows, n))] * 4,
        flops=1,
        moved=rows * n * 50,
        vmem=24,
        prefetch=1,
    )(place, keeps[0], gots[0], keeps[1], gots[1])


def unpack_matrix(width, blocks, wide):
    per, step = width // blocks, wide // blocks
    col = jnp.arange(WIDE_HEADS, dtype=jnp.int32)
    feature = col // LANES * HEAD + col % LANES
    place = jnp.where(col % LANES < HEAD, feature // per * step + feature % per, -1)
    return (jnp.arange(wide, dtype=jnp.int32)[:, None] == place[None, :]).astype(BF16)


def delta_matrix(width, blocks, wide):
    per, step = width // blocks, wide // blocks
    col = jnp.arange(wide, dtype=jnp.int32)
    head = jnp.where(col % step < per, (col // step * per + col % step) // HEAD, -1)
    row = jnp.arange(8 * KV_HEADS, dtype=jnp.int32)
    mine = jnp.where(row % 8 < GROUP, row // 8 * GROUP + row % 8, -2)
    return (mine[:, None] == head[None, :]).astype(BF16)


def spread_matrix(width, blocks, wide):
    row = jnp.arange(wide, dtype=jnp.int32)
    per, step = width // blocks, wide // blocks
    place = (row // per) * step + row % per
    hit = (place[:, None] == jnp.arange(wide, dtype=jnp.int32)[None, :]) & (row < width)[:, None]
    return hit.astype(BF16)


def tables(positions, segments):
    lane = jnp.arange(LANES, dtype=jnp.int32)
    frequency = 10000.0 ** (-((lane % 32).astype(F32) * 2.0 / HEAD))
    angles = positions.astype(F32)[:, None] * frequency[None, :]
    cos, sin = jnp.cos(angles), jnp.sin(angles)
    high = (lane % HEAD >= 32)[None, :]
    sa = jnp.where(high, sin, 0.0)
    sb = jnp.where(high, 0.0, -sin)
    doc = (lane - HEAD)[None, :]
    mine = segments[:, None] == doc
    in_doc = (doc >= 0) & (doc < DOCS)
    aq = jnp.where(mine & in_doc, MASKED, 0.0)
    ak = jnp.where(in_doc & ~mine, 1.0, 0.0)
    ak = jnp.where((doc >= DOCS) & (doc < DOCS + 3), -1.0, ak)
    return cos, sa, sb, aq, ak


def pad_rows(w, blocks, step=64):
    per = w.shape[0] // blocks
    return jnp.pad(w.reshape(blocks, per, w.shape[1]), ((0, 0), (0, step - per), (0, 0)))


def pad_cols(w, blocks, step=64):
    per = w.shape[1] // blocks
    w = jnp.pad(w.reshape(w.shape[0], blocks, per), ((0, 0), (0, 0), (0, step - per)))
    return w.reshape(w.shape[0], blocks * step)


def cut_rows(w, per):
    return w[:, :per].reshape(w.shape[0] * per, w.shape[2])


def cut_cols(w, per, step=64):
    blocks = w.shape[1] // step
    return w.reshape(w.shape[0], blocks, step)[:, :, :per].reshape(w.shape[0], blocks * per)


def chunked(w, chunk=256):
    blocks, rows, cols = w.shape
    w = w.reshape(blocks, rows, cols // chunk, chunk).transpose(0, 2, 1, 3)
    return w.reshape(blocks, cols // chunk * rows, chunk)


def joined(w, rows):
    blocks, total, chunk = w.shape
    w = w.reshape(blocks, total // rows, rows, chunk).transpose(0, 2, 1, 3)
    return w.reshape(blocks, rows, total // rows * chunk)


def pack_half(w_gate, w_up, w_down, blocks, groups):
    down = pad_cols(w_down, groups)
    down = down.reshape(blocks, w_down.shape[0] // blocks, down.shape[1])
    gate, upper = chunked(pad_rows(w_gate, blocks)), chunked(pad_rows(w_up, blocks))
    return jnp.concatenate([gate, down[:, :, :256], upper, down[:, :, 256:]], axis=1)


def add(left, right):
    return (left.astype(F32) + right.astype(F32)).astype(BF16)


def swap(x):
    return lax.ppermute(x, "ctx", [(0, 1), (1, 0)])


def across(x, bit, count):
    return lax.ppermute(x, "dp", [(i, i ^ (1 << bit)) for i in range(count)])


def pick(x, index, axis=0):
    return lax.dynamic_index_in_dim(x, index, axis, keepdims=False)


def tie(value, *others):
    return lax.optimization_barrier((value, *others))[0]


def tie_all(values, *others):
    return lax.optimization_barrier((*values, *others))[: len(values)]


def along_z(x, step, count):
    return lax.ppermute(x, "dp", [(i, (i + 4 * step) % count) for i in range(count)])


def rise(x, count):
    return [x] + [along_z(x, k, count) for k in (1, 2, 3)]


def spread_first(stack, count):
    half = stack.shape[1] // 2
    first, second = stack[:, :half], stack[:, half:]
    return first, across(first, 0, count), second, across(second, 1, count)


def spread_second(first, first_got, second, second_got, count):
    first, second = jnp.concatenate([first, first_got]), jnp.concatenate([second, second_got])
    return first, across(first, 1, count), second, across(second, 0, count)


def pieces_of(whole_one):
    n = whole_one.shape[1] // 2
    cube = whole_one.reshape(4, 2, 2, 2 * n, -1)
    cube = jnp.stack([cube[(4 - k) % 4] for k in range(4)])
    first, second = cube[:, :, :, :n], cube[:, :, :, n:]
    first, second = first.transpose(1, 2, 0, 3, 4), second.transpose(2, 1, 0, 3, 4)
    flat = lambda t: t.reshape(8, n, -1)
    return flat(first[0]), flat(first[1]), flat(second[0]), flat(second[1])


def fine_pieces_of(whole_one):
    n = whole_one.shape[1] // 2
    cube = whole_one.reshape(4, 2, 2, 2 * n, -1)
    cube = jnp.stack([cube[(4 - k) % 4] for k in range(4)])
    near = [cube[:, dy, dx] for dy in range(2) for dx in range(2)]
    return [t[:, :n] for t in near] + [t[:, n:] for t in near]


class RowSum:
    def __init__(self, place, count, arrays, reader, rows):
        self.place, self.count = place, count
        a_sent, a_kept, b_sent, b_kept = begin(place, arrays, reader, rows)
        self.sent, self.kept = [a_sent, b_sent], [a_kept, b_kept]

    def move(self):
        self.got = [across(self.sent[0], 0, self.count), across(self.sent[1], 1, self.count)]

    def wait(self, other):
        self.got = list(lax.optimization_barrier((*self.got, other))[:-1])

    def turn(self, other):
        self.wait(other)
        a_sent, a_kept, b_sent, b_kept = turn(self.place, self.kept, self.got)
        self.sent, self.kept = [a_sent, b_sent], [a_kept, b_kept]

    def move_again(self):
        self.got = [across(self.sent[0], 1, self.count), across(self.sent[1], 0, self.count)]

    def climb(self, other):
        self.wait(other)
        self.kept, *self.sent = climb(self.place, self.kept, self.got)

    def start_up(self):
        return along_z(self.sent[1], 1, self.count)

    def start_down(self):
        return along_z(self.sent[2], 3, self.count)

    def go_up(self, got):
        return along_z(add(self.sent[0], got), 1, self.count)

    def move_up(self):
        return [along_z(self.sent[k - 1], k, self.count) for k in (1, 2, 3)]

    def total(self, *gots):
        total = self.kept
        for got in gots:
            total = total + got.astype(F32)
        return total


def read_rows(ins, side, block):
    half = ins[0].shape[1] // 2
    rows = slice(half * side, half * (side + 1))
    return [(0, ins[0][block, rows], ins[1][block, rows])]


def read_quarters(ins, side, block):
    first = ins[0].shape[2]
    return [(0, ins[0][side, block], ins[1][side, block]), (first, ins[2][side, block], ins[3][side, block])]


def put_other(both, got, core):
    return lax.dynamic_update_slice(both, got[None], (1 - core, 0, 0))


def shards_of_two(inputs, segment_ids, positions, w_query, w_key, w_value, w_out, w_gate, w_up,
                  w_down, gain_attn, gain_ffn, cotangent):
    count = lax.axis_size("dp")
    me, core = lax.axis_index("dp"), lax.axis_index("ctx")
    place = (core, me // 4, (me >> 1) & 1, me & 1)
    place_of = jnp.stack(place).astype(jnp.int32)
    per = gain_attn.shape[0]
    width = per * count
    groups = w_out.shape[1] // per
    hidden = w_down.shape[0]
    n_q, n_k = w_query.shape[1], w_key.shape[1]
    n_qkv = n_q + 2 * n_k

    shard = jnp.concatenate([w_query, w_key, w_value], axis=1)
    shard = jnp.concatenate([jnp.pad(shard, ((0, 0), (0, 896 - n_qkv))), pad_cols(w_out, groups)], axis=1)
    gain_rows = jnp.pad(jnp.stack([gain_attn, gain_ffn]), ((0, 62 - per), (0, PACK - per)))
    shard = jnp.concatenate([shard, gain_rows])
    packed = pack_half(w_gate, w_up, w_down, 1, groups)[0]

    def halves(x):
        x = jnp.swapaxes(x[:, 0], 1, 2)
        return pick(x, core), swap(pick(x, 1 - core))

    wide = count * 64
    spread, unpack = spread_matrix(width, count, wide), unpack_matrix(width, count, wide)
    delta_sum = delta_matrix(width, count, wide)
    table = tables(pick(positions[:, 0], core), pick(segment_ids[:, 0], core))

    level = rise(shard, count)
    x_own, x_other = halves(inputs)
    ct_own, ct_other = halves(cotangent)
    stack = tie(jnp.stack(level), packed, x_other, ct_other)
    part = spread_first(stack, count)
    packed = tie(packed, stack)
    up, down = along_z(packed, 1, count), along_z(packed, 3, count)
    near_far = spread_second(*part, count)
    up, down = tie_all((up, down), part[0])
    up_two = along_z(up, 1, count)
    near_far = tie_all(near_far, up_two, down, spread, delta_sum, unpack, *table)
    pieces = near_far + tuple(swap(t) for t in near_far)
    packs = jnp.stack(tie_all((packed, up, up_two, down), near_far[0]))
    half = packs.shape[1] // 2
    a00, b00 = packs[:, :half], packs[:, half:]
    a01, b10 = across(a00, 0, count), across(b00, 1, count)

    pieces = tie_all(pieces, a00, b00)
    xp, a, q, k, v, w_qkv, w_o, gains = pre_attention(place_of, x_own, x_other, spread, pieces, *table)
    a01, b10, a00, b00 = tie_all((a01, b10, a00, b00), q)
    a10, b01 = across(a00, 1, count), across(b00, 0, count)
    got = [swap(a00), swap(b00), swap(a01)]
    q = tie(q, a01, b10)
    o, q2 = attend(q, k, v)
    a10, b01, *got = tie_all((a10, b01, *got), o)
    a11, b11 = across(tie(a01, a10), 1, count), across(tie(b10, a10), 0, count)
    got += [swap(b10), swap(a10), swap(b01)]
    op, m, b, df = middle(
        place_of, tie(o, a10, b01, *got[:3]), ct_own, ct_other, spread, unpack, w_o, xp, gains
    )
    a11, b11, *got = tie_all((a11, b11, *got), b)
    mine = [a00, a01, a10, a11, b00, b01, b10, b11]
    other = [got[0], got[2], got[4], swap(a11), got[1], got[5], got[3], swap(b11)]

    acc0, db0, gu_send, d_send, d_keep = feed_forward(place_of, b, df, mine, other, 0)
    gu_got = swap(gu_send)
    acc, db, gu_keep, d_send, d_keep = feed_forward(
        place_of, tie(b, gu_send), df, mine, other, 1, (d_send, d_keep, acc0, db0)
    )
    one = RowSum(place_of, count, (gu_keep, tie(gu_got, acc)), read_rows, 320)
    one.move()
    blocked = lambda t: t.reshape(2, count, hidden, 256)
    d_got = swap(d_send)
    m = tie(m, *one.sent, d_send)
    em, do, delta, o_send, o_keep, dgf = after(place_of, m, db, df, gains, unpack, delta_sum, w_o, op, width)
    o_got = swap(o_send)
    one.turn(em)
    one.move_again()
    two = RowSum(
        place_of, count, (blocked(d_keep), blocked(tie(d_got, em)), o_keep, o_got), read_quarters, 224
    )
    two.move()
    do = tie(do, *one.sent, *two.sent)
    parts = attend_back(q2, k, v, do, delta, *table[:3], 0, KV_HEADS)
    one.climb(parts[0])
    up, down = one.start_up(), one.start_down()
    two.turn(parts[0])
    two.move_again()
    a = tie(a, *one.sent, *two.sent)
    flat, p_send, p_keep = projections_back(place_of, parts, a, w_qkv, gains, dgf)
    up, down, *two.got = tie_all((up, down, *two.got), flat)
    p_got = swap(tie(p_send, up))
    two.climb(flat)
    one_up, one_down, two_up = one.go_up(up), down, two.start_up()
    three = RowSum(place_of, count, (p_keep, p_got), read_rows, 32)
    three.move()
    flat = tie(flat, *two.sent, *three.sent)
    gi_send = input_back(place_of, flat, w_qkv, xp, em, gains, spread, width)
    out_send, outs = finish(place_of, tie(m, gi_send), acc, spread, width)
    *three.got, one_up, two_up = tie_all((*three.got, one_up, two_up), outs)
    three.turn(outs)
    three.move_again()
    gi_got, out_got = swap(tie(gi_send, *three.sent)), swap(tie(out_send, *three.sent))
    two_up = two.go_up(tie(two_up, *three.sent))
    two.sent[2] = tie(two.sent[2], *three.sent)
    two_down = two.start_down()
    first = tie(one.total(one_up, one_down), *three.sent)
    wide_of = lambda t: t.transpose(1, 0, 2).reshape(t.shape[1], -1)
    gu = first.reshape(5, 2, 64, 256)
    gate, upper = wide_of(gu[:, 0])[:per], wide_of(gu[:, 1])[:per]
    outs = put_other(outs, out_got, core)
    *three.got, gi_got, two_up = tie_all((*three.got, gi_got, two_up), outs, gate, upper)
    three.climb(gi_got)
    last_got = three.move_up()
    gis = input_back(place_of, tie(flat, *three.sent), w_qkv, xp, em, gains, spread, width, gi_got)
    last_got = tie_all(last_got, gis)
    second, third = two.total(two_up, two_down), three.total(*last_got)
    third = third.reshape(64, 896)[:per]
    tokens = lambda t: jnp.swapaxes(t, 1, 2)[:, None]
    return (
        tokens(outs),
        tokens(gis),
        third[:, :n_q],
        third[:, n_q : n_q + n_k],
        third[:, n_q + n_k : n_qkv],
        cut_cols(wide_of(second[:, 160:])[:per], per),
        gate,
        upper,
        cut_cols(wide_of(second[:, :160]), per),
        third[:, n_qkv],
        third[:, n_qkv + 1],
    )


def shards_of_many(inputs, segment_ids, positions, w_query, w_key, w_value, w_out, w_gate, w_up,
                   w_down, gain_attn, gain_ffn, cotangent):
    count, cores = lax.axis_size("dp"), lax.axis_size("ctx")
    core = lax.axis_index("ctx")
    share = cores // MICRO
    per = gain_attn.shape[0]
    width = per * count

    def gathered(w):
        return lax.all_gather(lax.all_gather(w, "dp", axis=0, tiled=True), "ctx", axis=1, tiled=True)

    full = [gathered(w) for w in (w_query, w_key, w_value, w_out, w_gate, w_up, w_down)]
    gain_pair = lax.all_gather(jnp.stack([gain_attn, gain_ffn]), "dp", axis=1, tiled=True)
    w_o, w_g, w_u, w_d = full[3:]
    half = lambda w, j: w[:, w.shape[1] // 2 * j : w.shape[1] // 2 * (j + 1)]
    packs = [pack_half(half(w_g, j), half(w_u, j), half(w_d, j), count, count // 2) for j in range(2)]
    mine, other = (fine_pieces_of(p) for p in packs)
    pieces = []
    for j in range(2):
        part = jnp.concatenate([half(w, j) for w in full[:3]], axis=1)
        part = jnp.pad(part, ((0, 0), (0, 896 - part.shape[1])))
        part = jnp.concatenate([part, pad_cols(half(w_o, j), count // 2)], axis=1)
        part = pad_rows(part, count)
        part = part.at[:, per : per + 2, :per].set(gain_pair.reshape(2, count, per).transpose(1, 0, 2))
        pieces += pieces_of(part)
    which = core // share

    def sequence(x):
        whole_one = pick(lax.all_gather(x[:, 0], "ctx", axis=1, tiled=True), which).T
        return whole_one[:, : whole_one.shape[1] // 2], whole_one[:, whole_one.shape[1] // 2 :]

    place = jnp.zeros((4,), jnp.int32)
    wide = count * 64
    spread, unpack = spread_matrix(width, count, wide), unpack_matrix(width, count, wide)
    delta_sum = delta_matrix(width, count, wide)
    cos, sa, sb, aq, ak = tables(pick(positions[:, 0], which), pick(segment_ids[:, 0], which))
    xp, a, q, k, v, w_qkv, w_o, gains = pre_attention(
        place, *sequence(inputs), spread, pieces, cos, sa, sb, aq, ak
    )
    o, q2 = attend(q, k, v)
    op, m, b, df = middle(place, o, *sequence(cotangent), spread, unpack, w_o, xp, gains)
    acc0, db0, gu_send, d_send, d_keep = feed_forward(place, b, df, mine, other, 0)
    acc, db, gu_keep, d_send, d_keep = feed_forward(
        place, b, df, mine, other, 1, (d_send, d_keep, acc0, db0)
    )
    em, do, delta, o_send, o_keep, dgf = after(place, m, db, df, gains, unpack, delta_sum, w_o, op, width)
    out_send, outs = finish(place, m, acc, spread, width)
    parts = attend_back(q2, k, v, do, delta, cos, sa, sb, 0, KV_HEADS)
    flat, p_send, p_keep = projections_back(place, parts, a, w_qkv, gains, dgf)
    gi_send = input_back(place, flat, w_qkv, xp, em, gains, spread, width)
    gis = input_back(place, flat, w_qkv, xp, em, gains, spread, width, gi_send)

    parts = [cut_rows(p, per) for p in (p_keep, p_send)]
    n_q, n_k = HEADS * HEAD // 2, KV_HEADS * HEAD // 2
    both = lambda at, n: jnp.concatenate([p[:, at : at + n] for p in parts], axis=1)
    side = lambda t: jnp.concatenate([t[0], t[1]], axis=-1)

    def wide_of(index):
        every = []
        for t in (gu_keep, gu_send):
            t = t.reshape(count, 5, 2, 64, 256)[:, :, index]
            every.append(cut_rows(t.transpose(0, 2, 1, 3).reshape(count, 64, -1), per))
        return jnp.concatenate(every, axis=1)

    grads = [
        both(0, n_q),
        both(n_q * 1, n_k),
        both(n_q + n_k, n_k),
        cut_cols(cut_rows(jnp.concatenate([side(o_keep), side(o_send)], axis=-1), per), per),
        wide_of(0),
        wide_of(1),
        cut_cols(
            jnp.concatenate([side(d_keep), side(d_send)], axis=-1),
            per,
        ),
    ]

    def summed(g):
        g = lax.psum_scatter(g * (1.0 / share), "dp", scatter_dimension=0, tiled=True)
        return lax.psum_scatter(g, "ctx", scatter_dimension=1, tiled=True).astype(F32)

    sums = [summed(g.astype(BF16)) for g in grads]
    dgain = parts[0][:, 2 * n_k + n_q : 2 * n_k + n_q + 2].astype(F32).T * (1.0 / share)
    dgain = lax.psum_scatter(lax.psum(dgain, "ctx"), "dp", scatter_dimension=1, tiled=True)

    def tokens(seq):
        rows = seq.shape[0] // cores
        every = lax.all_gather(seq, "ctx", axis=0, tiled=False)
        return lax.dynamic_slice_in_dim(every[::share], core * rows, rows, axis=1)[:, None]

    out = jnp.concatenate([outs[0], out_send], axis=1).T
    gi = jnp.concatenate([gis[0], gi_send.astype(F32)], axis=1).T
    return (tokens(out), tokens(gi), *sums, dgain[0], dgain[1])


def solution(mesh):
    two = mesh.shape["ctx"] == MICRO and mesh.shape["dp"] == 16
    matrices = (P("dp", "ctx"),) * 7 + (P("dp"), P("dp"))
    tokens = P(None, "dp", "ctx", None)
    return jax.shard_map(
        shards_of_two if two else shards_of_many,
        mesh=mesh,
        in_specs=(tokens, P(None, "dp", None), P(None, "dp", None)) + matrices + (tokens,),
        out_specs=(tokens, tokens) + matrices,
        check_vma=False,
    )
```

```python
import functools

import jax
import jax.numpy as jnp
from jax import lax
from jax.experimental import pallas as pl
from jax.experimental.pallas import tpu as pltpu
from jax.sharding import PartitionSpec as P

HEADS = 15
KV_HEADS = 5
HEAD = 64
MICRO = 2
GROUP = 3
DOCS = 4

EPSILON = 1e-05
MASKED = -1e30
LANES = 128
QKV = (HEADS + 2 * KV_HEADS) * HEAD
QKV_PAD = 1664
PACK = 1408
MIB = 1024 * 1024
WIDE_HEADS = HEADS * LANES
F32 = jnp.float32
BF16 = jnp.bfloat16


def up(value, step):
    return -(-value // step) * step


def mm(left, right):
    return lax.dot_general(left, right, (((1,), (0,)), ((), ())), preferred_element_type=F32)


def mm_nt(left, right):
    return lax.dot_general(left, right, (((1,), (1,)), ((), ())), preferred_element_type=F32)


def mm_tn(left, right):
    return lax.dot_general(left, right, (((0,), (0,)), ((), ())), preferred_element_type=F32)


def call(body, out_shape, grid, in_specs, out_specs, scratch=(), flops=0, moved=0, prefetch=0, alias=None,
         vmem=8):
    return pl.pallas_call(
        body,
        out_shape=out_shape,
        grid_spec=pltpu.PrefetchScalarGridSpec(
            num_scalar_prefetch=prefetch,
            grid=grid,
            in_specs=in_specs,
            out_specs=out_specs,
            scratch_shapes=scratch,
        ),
        input_output_aliases=alias or {},
        compiler_params=pltpu.CompilerParams(vmem_limit_bytes=vmem * MIB),
        cost_estimate=pl.CostEstimate(flops=flops, bytes_accessed=moved, transcendentals=0),
    )


def whole(shape):
    return pl.BlockSpec(shape, lambda *_: (0,) * len(shape), pipeline_mode=pl.Buffered(1))


def lane_of(rows):
    return lax.broadcasted_iota(jnp.int32, (rows, LANES), 1)


def three_terms(column):
    high = column.astype(BF16).astype(F32)
    rest = column - high
    mid = rest.astype(BF16).astype(F32)
    return high, mid, rest - mid


def put_terms(base, column, lane, first):
    high, mid, low = three_terms(column)
    base = jnp.where(lane == first, high, base)
    base = jnp.where(lane == first + 1, mid, base)
    return jnp.where(lane == first + 2, low, base)


def build_weights(place_ref, piece_refs, stage_ref, w_ref, wo_ref):
    core, z, y, x = (place_ref[n] for n in range(4))
    for swapped in range(2):
        near_a, far_a, near_b, far_b = piece_refs[4 * swapped : 4 * swapped + 4]
        to = jnp.bitwise_xor(core, swapped)
        for dy in range(2):
            for dx in range(2):
                for k in range(4):
                    block = lax.rem(z + 4 - k, 4) * 4 + (y ^ dy) * 2 + (x ^ dx)
                    row = pl.multiple_of(block * 64, 64)
                    stage_ref[to, pl.ds(row, 32), :] = (far_a if dy else near_a)[4 * dx + k]
                    stage_ref[to, pl.ds(row + 32, 32), :] = (far_b if dx else near_b)[4 * dy + k]
    n_q, n_k = HEADS * HEAD // 2, KV_HEADS * HEAD // 2
    for j in range(2):
        w_ref[:, n_q * j : n_q * (j + 1)] = stage_ref[j, :, :n_q]
        for part in range(2):
            to, at = 2 * n_q + n_k * (2 * part + j), n_q + n_k * part
            w_ref[:, to : to + n_k] = stage_ref[j, :, at : at + n_k]
        half = wo_ref.shape[1] // 2
        wo_ref[:, half * j : half * (j + 1)] = stage_ref[j, :, PACK - half :]
    w_ref[:, QKV:] = jnp.zeros((w_ref.shape[0], QKV_PAD - QKV), BF16)


def projections(xp, scale, w_ref, gain_ref, cos_ref, sa_ref, sb_ref, aq_ref, ak_ref,
                xp_ref, a_ref, q_ref, k_ref, v_ref):
    a = (xp * scale * gain_ref[:1]).astype(BF16)
    xp_ref[...] = xp.astype(BF16)
    a_ref[...] = a
    t = mm(a, w_ref[...])
    lane = lane_of(t.shape[0])
    low = lane < HEAD
    cos, sa, sb, aq, ak = cos_ref[...], sa_ref[...], sb_ref[...], aq_ref[...], ak_ref[...]
    for pair in range((HEADS + KV_HEADS) // 2):
        tt = t[:, LANES * pair : LANES * (pair + 1)]
        rot = tt * cos + pltpu.roll(tt, 32, 1) * sa + pltpu.roll(tt, 96, 1) * sb
        for half in range(2):
            head = 2 * pair + half
            val = rot if half == 0 else pltpu.roll(rot, 64, 1)
            if head < HEADS:
                q_ref[head] = jnp.where(low, val * HEAD ** -0.5, aq).astype(BF16)
            else:
                k_ref[head - HEADS] = jnp.where(low, val, ak).astype(BF16)
    av = jnp.where(lane < HEAD + 3, -1.0, 0.0)
    for head in range(KV_HEADS):
        first = (HEADS + KV_HEADS) * HEAD + LANES * (head // 2)
        tt = t[:, first : first + LANES]
        val = tt if head % 2 == 0 else pltpu.roll(tt, 64, 1)
        v_ref[head] = jnp.where(low, val, av).astype(BF16)


def own_or_other(place_ref, own_ref, other_ref):
    first = pl.program_id(0) < pl.num_programs(0) // 2
    mine = first == (place_ref[0] == 0)
    return jnp.where(mine, own_ref[...], other_ref[...])


def pre_body(width, place_ref, own_ref, other_ref, e_ref, *refs):
    pieces, refs = refs[:8], refs[8:]
    *rest, w_ref, wo_ref, gain_ref, stage_ref = refs

    @pl.when(pl.program_id(0) == 0)
    def _():
        build_weights(place_ref, pieces, stage_ref, w_ref, wo_ref)
        gain_ref[...] = jnp.zeros_like(gain_ref)
        step = stage_ref.shape[1] // 16
        for block in range(16):
            end = step * (block + 1)
            tail = stage_ref[0, end - 16 : end, :step].astype(F32)
            gain_ref[:2, end - step : end] = tail[12:14]

    xp = mm_tn(own_or_other(place_ref, own_ref, other_ref), e_ref[:width, :])
    scale = lax.rsqrt(jnp.sum(xp * xp, axis=-1, keepdims=True) / width + EPSILON)
    projections(xp, scale, w_ref, gain_ref, *rest)


def halves_specs(rows, width, block):
    steps = rows // block
    return [pl.BlockSpec((width, block), lambda i, *_: (0, i % steps))] * 2


def pre_attention(place, own, other, spread, pieces, cos, sa, sb, aq, ak, block=512):
    width, half = own.shape
    seq, wide = 2 * half, spread.shape[1]
    rows = lambda n: pl.BlockSpec((block, n), lambda i, *_: (i, 0))
    heads = lambda n: pl.BlockSpec((n, block, LANES), lambda i, *_: (0, i, 0))
    return call(
        functools.partial(pre_body, width),
        [
            jax.ShapeDtypeStruct((seq, wide), BF16),
            jax.ShapeDtypeStruct((seq, wide), BF16),
            jax.ShapeDtypeStruct((HEADS, seq, LANES), BF16),
            jax.ShapeDtypeStruct((KV_HEADS, seq, LANES), BF16),
            jax.ShapeDtypeStruct((KV_HEADS, seq, LANES), BF16),
            jax.ShapeDtypeStruct((wide, QKV_PAD), BF16),
            jax.ShapeDtypeStruct((wide, wide), BF16),
            jax.ShapeDtypeStruct((8, wide), F32),
        ],
        (seq // block,),
        halves_specs(half, width, block)
        + [whole(spread.shape)]
        + [whole(w.shape) for w in pieces]
        + [rows(LANES)] * 5,
        [rows(wide), rows(wide), heads(HEADS), heads(KV_HEADS), heads(KV_HEADS)]
        + [whole((wide, QKV_PAD)), whole((wide, wide)), whole((8, wide))],
        scratch=[pltpu.VMEM((2, wide, PACK), BF16)],
        flops=2 * seq * wide * (width + QKV_PAD),
        moved=20_000_000,
        vmem=56,
        prefetch=1,
    )(place, own, other, spread, *pieces, cos, sa, sb, aq, ak)


def attend_body(block, q_ref, k_ref, v_ref, o_ref, q2_ref):
    seq = k_ref.shape[1]
    rows = GROUP * block
    below = lax.broadcasted_iota(jnp.int32, (block, block), 0) >= lax.broadcasted_iota(
        jnp.int32, (block, block), 1
    )
    below = jnp.concatenate([below.astype(F32)] * GROUP, axis=0) > 0.5
    lane = lane_of(rows)
    for i in range(seq // block):
        span = slice(block * i, block * (i + 1))
        q = q_ref[:, span, :].reshape(rows, LANES)
        s_in = jnp.where(below, mm_nt(q, k_ref[0, span, :]), MASKED)
        top = jnp.max(s_in, axis=-1, keepdims=True)
        if i:
            s_left = mm_nt(q, k_ref[0, : block * i, :])
            top = jnp.maximum(top, jnp.max(s_left, axis=-1, keepdims=True))
        ext = mm(jnp.exp(s_in - top).astype(BF16), v_ref[0, span, :])
        if i:
            ext = ext + mm(jnp.exp(s_left - top).astype(BF16), v_ref[0, : block * i, :])
        total = -ext[:, HEAD : HEAD + 1]
        o = ext / total
        o = jnp.where(lane < HEAD, o, pltpu.roll(o, 64, 1))
        o_ref[:, span, :] = o.reshape(GROUP, block, LANES).astype(BF16)
        q2 = put_terms(q.astype(F32), top + jnp.log(total), lane, HEAD + DOCS)
        q2_ref[:, span, :] = q2.reshape(GROUP, block, LANES).astype(BF16)


def attend(q, k, v, block=256):
    seq = q.shape[1]
    group = pl.BlockSpec((GROUP, seq, LANES), lambda n: (n, 0, 0))
    one = pl.BlockSpec((1, seq, LANES), lambda n: (n, 0, 0))
    shape = jax.ShapeDtypeStruct(q.shape, BF16)
    return call(
        functools.partial(attend_body, block),
        [shape, shape],
        (KV_HEADS,),
        [group, one, one],
        [group, group],
        flops=4 * HEADS * seq * seq * LANES,
        moved=15_000_000,
        vmem=56,
    )(q, k, v)


def attend_back_body(block, q_ref, k_ref, v_ref, do_ref, delta_ref, cos_ref, sa_ref, sb_ref,
                     dq_ref, dk_ref, dv_ref, acc_ref):
    seq = k_ref.shape[1]
    above = lax.broadcasted_iota(jnp.int32, (block, block), 0) <= lax.broadcasted_iota(
        jnp.int32, (block, block), 1
    )
    lane = lane_of(seq)

    def unrotate(t, span):
        rows = span.stop - span.start
        rot = (
            t * cos_ref[span, :]
            - pltpu.roll(t, 32, 1) * sa_ref[span, :]
            - pltpu.roll(t, 96, 1) * sb_ref[span, :]
        )
        return twice(rot, rows)

    def twice(t, rows):
        return jnp.where(lane[:rows] < HEAD, t, pltpu.roll(t, 64, 1)).astype(BF16)

    for j in range(seq // block):
        span = slice(block * j, block * (j + 1))
        k, v = k_ref[0, span, :], v_ref[0, span, :]
        dk = jnp.zeros((block, LANES), F32)
        dv = jnp.zeros((block, LANES), F32)
        for g in range(GROUP):
            q, do = q_ref[g, block * j :, :], do_ref[g, block * j :, :]
            p = jnp.exp(mm_nt(k, q))
            inner = jnp.where(above, p[:, :block], 0.0)
            p = inner if p.shape[1] == block else jnp.concatenate([inner, p[:, block:]], axis=1)
            ds = (p * (mm_nt(v, do) - delta_ref[g : g + 1, block * j :])).astype(BF16)
            dv = dv + mm(p.astype(BF16), do)
            dk = dk + mm(ds, q)
            dq = mm_tn(ds, k)
            if j == 0:
                acc_ref[g] = dq
            else:
                acc_ref[g, block * j :, :] += dq
        dk_ref[0, span, :] = unrotate(dk, span)
        dv_ref[0, span, :] = twice(dv, block)
    for g in range(GROUP):
        dq_ref[g] = unrotate(acc_ref[g] * HEAD ** -0.5, slice(0, seq))


def attend_back(q, k, v, do, delta, cos, sa, sb, first, count, block=256):
    seq = q.shape[1]
    group = lambda at: pl.BlockSpec((GROUP, seq, LANES), lambda n: (n + at, 0, 0))
    one = lambda at: pl.BlockSpec((1, seq, LANES), lambda n: (n + at, 0, 0))
    return call(
        functools.partial(attend_back_body, block),
        [
            jax.ShapeDtypeStruct((GROUP * count, seq, LANES), BF16),
            jax.ShapeDtypeStruct((count, seq, LANES), BF16),
            jax.ShapeDtypeStruct((count, seq, LANES), BF16),
        ],
        (count,),
        [group(first), one(first), one(first), group(first)]
        + [pl.BlockSpec((8, seq), lambda n: (n + first, 0))]
        + [whole((seq, LANES))] * 3,
        [group(0), one(0), one(0)],
        scratch=[pltpu.VMEM((GROUP, seq, LANES), F32)],
        flops=10 * GROUP * count * seq * seq * LANES,
        moved=4_000_000 * count,
        vmem=12,
    )(q, k, v, do, delta, cos, sa, sb)


def pairs_to(ref, get, heads, first=0):
    for pair in range((heads + 1) // 2):
        left = get(2 * pair)
        lane = lane_of(left.shape[0])
        right = get(2 * pair + 1).astype(F32) if 2 * pair + 1 < heads else 0.0
        both = jnp.where(lane < HEAD, left.astype(F32), right)
        ref[:, first + LANES * pair : first + LANES * (pair + 1)] = both.astype(BF16)


def mid_body(width, place_ref, o_ref, own_ref, other_ref, e_ref, u_ref, wo_ref, xp_ref, gain_ref,
             op_ref, m_ref, b_ref, df_ref):
    flat = jnp.concatenate([o_ref[head] for head in range(HEADS)], axis=1)
    op = mm_nt(flat, u_ref[...]).astype(BF16)
    op_ref[...] = op
    m = xp_ref[...].astype(F32) + mm(op, wo_ref[...])
    m_ref[...] = m
    scale = lax.rsqrt(jnp.sum(m * m, axis=-1, keepdims=True) / width + EPSILON)
    b_ref[...] = (m * scale * gain_ref[1:2]).astype(BF16)
    ct = own_or_other(place_ref, own_ref, other_ref)
    df_ref[...] = mm_tn(ct, e_ref[:width, :]).astype(BF16)


def middle(place, o, own, other, spread, unpack, w_out, xp, gain, block=512):
    width, half = own.shape
    seq, wide = 2 * half, spread.shape[1]
    rows = lambda n: pl.BlockSpec((block, n), lambda i, *_: (i, 0))
    return call(
        functools.partial(mid_body, width),
        [
            jax.ShapeDtypeStruct((seq, wide), BF16),
            jax.ShapeDtypeStruct((seq, wide), F32),
            jax.ShapeDtypeStruct((seq, wide), BF16),
            jax.ShapeDtypeStruct((seq, wide), BF16),
        ],
        (seq // block,),
        [
            pl.BlockSpec((HEADS, block, LANES), lambda i, *_: (0, i, 0)),
            *halves_specs(half, width, block),
            whole(spread.shape),
            whole(unpack.shape),
            whole(w_out.shape),
            rows(wide),
            whole((8, wide)),
        ],
        [rows(wide)] * 4,
        flops=2 * seq * wide * 4 * wide,
        moved=22_000_000,
        vmem=56,
        prefetch=1,
    )(place, o, own, other, spread, unpack, w_out, xp, gain)


def ffn_body(turn, place_ref, b_ref, df_ref, *refs):
    gates, ups, downs, refs = refs[:4], refs[4:8], refs[8:24], refs[24:]
    before, refs = refs[: 4 * turn], refs[4 * turn :]
    out_ref, db_ref, gu_ref, d_send, d_keep, wg_ref, wu_ref, wd_ref, down_sem, *carry = refs
    s = pl.program_id(0)
    core, z_me, y_me, x_me = (place_ref[n] for n in range(4))
    chunk = wg_ref.shape[1]
    half = core if turn else 1 - core
    rows = wd_ref.shape[0] // 8

    def carried(n):
        return pltpu.make_async_copy(before[2 + n], carry[n], carry[2 + n])

    def down_copies():
        for swapped in range(2):
            for q in range(2):
                for near in range(4):
                    for up_z in range(2):
                        k = lax.rem(z_me + 4 - (2 * half + up_z), 4)
                        block = up_z * 4 + (y_me ^ (near // 2)) * 2 + (x_me ^ (near % 2))
                        row = pl.multiple_of(rows * block, 16)
                        col = pl.multiple_of(2 * chunk * (core ^ swapped) + chunk * q, chunk)
                        ref = downs[8 * swapped + 4 * q + near]
                        yield pltpu.make_async_copy(
                            ref.at[k, pl.ds(ref.shape[1] - rows, rows), :],
                            wd_ref.at[pl.ds(row, rows), pl.ds(col, chunk)],
                            down_sem.at[16 * swapped + 8 * q + 2 * near + up_z],
                        )

    @pl.when(s == 0)
    def _():
        for copy in down_copies():
            copy.start()
        out_ref[...] = jnp.zeros_like(out_ref)
        db_ref[...] = jnp.zeros_like(db_ref)
        if turn:
            carried(0).start()
            carried(1).start()

    for near in range(4):
        for k in range(4):
            block = lax.rem(z_me + 4 - k, 4) * 4 + (y_me ^ (near // 2)) * 2 + (x_me ^ (near % 2))
            row = pl.multiple_of(block * 64, 64)
            wg_ref[pl.ds(row, 64), :] = gates[near][k]
            wu_ref[pl.ds(row, 64), :] = ups[near][k]

    @pl.when(s == 0)
    def _():
        for copy in down_copies():
            copy.wait()

    b, df = b_ref[...], df_ref[...]
    wg, wu = wg_ref[...], wu_ref[...]
    wd = wd_ref[pl.ds(pl.multiple_of(chunk * s, chunk), chunk), :]
    gate = mm(b, wg)
    upper = mm(b, wu)
    sig = jax.nn.sigmoid(gate)
    act = gate * sig
    z = (act * upper).astype(BF16)
    dz = mm_nt(df, wd)
    dg = (dz * upper * (sig + act * (1.0 - sig))).astype(BF16)
    du = (dz * act).astype(BF16)

    out_ref[...] += mm(z, wd)
    db_ref[...] += mm_nt(dg, wg) + mm_nt(du, wu)

    if turn:

        @pl.when(s == pl.num_programs(0) - 1)
        def _():
            carried(0).wait()
            carried(1).wait()
            out_ref[...] += carry[0][...]
            db_ref[...] += carry[1][...]

    gu_ref[:, :64] = mm_tn(b, dg).astype(BF16).reshape(gu_ref.shape[0], 64, chunk)
    gu_ref[:, 64:] = mm_tn(b, du).astype(BF16).reshape(gu_ref.shape[0], 64, chunk)
    side = df.shape[1] // 2
    for ref, j in ((d_send, 1 - core), (d_keep, core)):
        dwd = mm_tn(z, df_ref[:, pl.ds(pl.multiple_of(side * j, side), side)]).astype(BF16)
        ref[0] = dwd[:, :chunk]
        ref[1] = dwd[:, chunk:]


def feed_forward(place, b, df, mine, other, turn, before=()):
    seq, wide = b.shape
    blocks, chunks, chunk = 16, 5, 256
    columns = mine if turn else other
    any_spec = pl.BlockSpec(memory_space=pltpu.HBM)
    half_of = lambda place: place[0] if turn else 1 - place[0]
    d_shape = jax.ShapeDtypeStruct((2, 2 * chunks * chunk, chunk), BF16)
    d_spec = pl.BlockSpec((2, chunk, chunk), lambda s, place: (0, half_of(place) * chunks + s, 0))
    return call(
        functools.partial(ffn_body, turn),
        [
            jax.ShapeDtypeStruct((seq, wide), F32),
            jax.ShapeDtypeStruct((seq, wide), F32),
            jax.ShapeDtypeStruct((blocks, 128 * chunks, chunk), BF16),
            d_shape,
            d_shape,
        ],
        (chunks,),
        [whole(b.shape), whole(df.shape)]
        + [pl.BlockSpec((4, 64, chunk), lambda s, place: (0, s, 0))] * 8
        + [any_spec] * (16 + len(before)),
        [
            whole((seq, wide)),
            whole((seq, wide)),
            pl.BlockSpec((blocks, 128, chunk), lambda s, place: (0, s, 0)),
            d_spec,
            d_spec,
        ],
        scratch=[
            pltpu.VMEM((wide, chunk), BF16),
            pltpu.VMEM((wide, chunk), BF16),
            pltpu.VMEM((chunks * chunk, wide), BF16),
            pltpu.SemaphoreType.DMA((32,)),
        ]
        + turn * [pltpu.VMEM((seq, wide), F32)] * 2
        + turn * [pltpu.SemaphoreType.DMA] * 2,
        flops=18 * seq * wide * chunks * chunk,
        moved=40_000_000,
        vmem=56,
        prefetch=1,
        alias={27: 3, 28: 4} if before else None,
    )(place, b, df, *columns, *mine, *other, *before)


def token_block(steps):
    def at(i, place):
        return jnp.where(i < steps // 2, (1 - place[0]) * (steps // 2) + i, place[0] * (steps // 2) + i - steps // 2)

    return at


def token_specs(steps, block, width):
    half = steps // 2
    return [
        pl.BlockSpec((width, block), lambda i, place: (0, jnp.minimum(i, half - 1))),
        pl.BlockSpec((1, width, block), lambda i, place: (place[0], 0, jnp.maximum(i - half, 0))),
    ]


def put_tokens(send_ref, keep_ref, value):
    early = pl.program_id(0) < pl.num_programs(0) // 2

    @pl.when(early)
    def _():
        send_ref[...] = value.astype(send_ref.dtype)

    @pl.when(jnp.logical_not(early))
    def _():
        keep_ref[0] = value.astype(keep_ref.dtype)


def post_body(width, place_ref, m_ref, db_ref, df_ref, gain_ref, u_ref,
              sum_ref, wo_ref, op_ref,
              em_ref, do_ref, delta_ref, dwo_send, dwo_keep, dgain_ref, da_ref):
    i = pl.program_id(0)
    m, db = m_ref[...], db_ref[...]
    scale = lax.rsqrt(jnp.sum(m * m, axis=-1, keepdims=True) / width + EPSILON)
    n = m * scale
    c = db * gain_ref[1:2]
    mean = jnp.sum(c * n, axis=-1, keepdims=True) / width
    em = df_ref[...].astype(F32) + scale * (c - n * mean)
    em_ref[...] = em
    da = em.astype(BF16)
    dgain = jnp.sum(db * n, axis=0, keepdims=True)
    block = m.shape[0]
    rows = pl.ds(pl.multiple_of(block * i, block), block)
    da_ref[rows, :] = da

    @pl.when(i == 0)
    def _():
        dgain_ref[...] = dgain

    @pl.when(i > 0)
    def _():
        dgain_ref[...] += dgain

    do = mm_nt(da, wo_ref[...]).astype(BF16)
    product = do.astype(F32) * op_ref[rows, :].astype(F32)
    high = product.astype(BF16)
    low = (product - high.astype(F32)).astype(BF16)
    delta_ref[...] = mm_nt(sum_ref[...], high) + mm_nt(sum_ref[...], low)
    do = mm(do, u_ref[...]).astype(BF16)
    for head in range(HEADS):
        do_ref[head] = do[:, LANES * head : LANES * (head + 1)]

    @pl.when(i == pl.num_programs(0) - 1)
    def _():
        half = da_ref.shape[1] // 2
        for ref, j in ((dwo_send, 1 - place_ref[0]), (dwo_keep, place_ref[0])):
            dwo = mm_tn(op_ref[...], da_ref[:, pl.ds(pl.multiple_of(half * j, half), half)]).astype(BF16)
            for q in range(2):
                ref[q] = dwo[:, 256 * q : 256 * (q + 1)].reshape(ref.shape[1:])


def after(place, m, db, df, gain, unpack, delta_sum, w_out, op, width, block=512):
    seq, wide = m.shape
    blocks = 16
    steps = seq // block
    rows = lambda n: pl.BlockSpec((block, n), lambda i, place: (i, 0))
    heads = pl.BlockSpec((HEADS, block, LANES), lambda i, place: (0, i, 0))
    dwo_shape = (2, blocks, wide // blocks, 256)
    consts = (gain, unpack, delta_sum, w_out, op)
    return call(
        functools.partial(post_body, width),
        [
            jax.ShapeDtypeStruct((seq, wide), F32),
            jax.ShapeDtypeStruct((HEADS, seq, LANES), BF16),
            jax.ShapeDtypeStruct((8 * KV_HEADS, seq), F32),
            jax.ShapeDtypeStruct(dwo_shape, BF16),
            jax.ShapeDtypeStruct(dwo_shape, BF16),
            jax.ShapeDtypeStruct((1, wide), F32),
        ],
        (steps,),
        [rows(wide)] * 3 + [whole(t.shape) for t in consts],
        [
            rows(wide),
            heads,
            pl.BlockSpec((8 * KV_HEADS, block), lambda i, place: (0, i)),
            whole(dwo_shape),
            whole(dwo_shape),
            whole((1, wide)),
        ],
        scratch=[pltpu.VMEM((seq, wide), BF16)],
        flops=2 * seq * wide * 6 * wide,
        moved=40_000_000,
        vmem=56,
        prefetch=1,
    )(place, m, db, df, *consts)


def finish_body(width, place_ref, m_ref, acc_ref, e_ref, send_ref, keep_ref):
    out = (m_ref[...] + acc_ref[...]).astype(BF16)
    put_tokens(send_ref, keep_ref, mm_nt(e_ref[:width, :], out))


def finish(place, m, acc, spread, width, block=256):
    seq, wide = m.shape
    steps = seq // block
    at = token_block(steps)
    rows = lambda n: pl.BlockSpec((block, n), lambda i, place: (at(i, place), 0))
    return call(
        functools.partial(finish_body, width),
        [
            jax.ShapeDtypeStruct((width, seq // 2), BF16),
            jax.ShapeDtypeStruct((2, width, seq // 2), BF16),
        ],
        (steps,),
        [rows(wide), rows(wide), whole(spread.shape)],
        token_specs(steps, block, width),
        flops=2 * seq * wide * wide,
        moved=16_000_000,
        vmem=8,
        prefetch=1,
    )(place, m, acc, spread)


def weights_body(place_ref, dq_ref, dk_ref, dv_ref, a_ref, w_ref, gain_ref,
                 dgain_ref, flat_ref, send_ref, keep_ref, dw_acc, part_ref, all_ref):
    i = pl.program_id(0)
    heads = HEADS + KV_HEADS

    pairs_to(flat_ref, lambda h: dq_ref[h] if h < HEADS else dk_ref[h - HEADS], heads)
    pairs_to(flat_ref, lambda h: dv_ref[h], KV_HEADS, heads * HEAD)
    block = flat_ref.shape[0]
    all_ref[pl.ds(pl.multiple_of(block * i, block), block), :] = flat_ref[...]

    @pl.when(i == pl.num_programs(0) - 1)
    def _():
        wide = dw_acc.shape[0]
        dw_acc[...] = mm_tn(a_ref[...], all_ref[...])
        total = jnp.sum(dw_acc[...] * w_ref[...].astype(F32), axis=-1, keepdims=True)
        column = lambda row: jnp.broadcast_to(row, (LANES, wide)).T
        gain = column(gain_ref[:1])
        attn = jnp.broadcast_to(total, (wide, LANES)) / jnp.where(gain == 0.0, 1.0, gain)
        lane = lane_of(wide)
        gains = jnp.where(lane == 32, attn, 0.0) + jnp.where(lane == 33, column(dgain_ref[...]), 0.0)
        n_q, n_k = HEADS * HEAD // 2, KV_HEADS * HEAD // 2
        for j in range(2):
            part_ref[:, 768:] = gains.astype(BF16)
            part_ref[:, :n_q] = dw_acc[:, n_q * j : n_q * (j + 1)].astype(BF16)
            for part in range(2):
                at, to = 2 * n_q + n_k * (2 * part + j), n_q + n_k * part
                part_ref[:, to : to + n_k] = dw_acc[:, at : at + n_k].astype(BF16)
            for ref, here in ((keep_ref, place_ref[0] == j), (send_ref, place_ref[0] != j)):

                @pl.when(here)
                def _():
                    ref[...] = part_ref[...].reshape(ref.shape)


def projections_back(place, parts, a, w_qkv, gain, dgain_ffn, block=256):
    seq, wide = a.shape
    blocks = 16
    rows = lambda n: pl.BlockSpec((block, n), lambda i, *_: (i, 0))
    heads = lambda t: pl.BlockSpec((t.shape[0], block, LANES), lambda i, *_: (0, i, 0))
    shape = (blocks, wide // blocks, 896)
    return call(
        weights_body,
        [
            jax.ShapeDtypeStruct((seq, QKV_PAD), BF16),
            jax.ShapeDtypeStruct(shape, BF16),
            jax.ShapeDtypeStruct(shape, BF16),
        ],
        (seq // block,),
        [heads(t) for t in parts] + [whole(a.shape), whole(w_qkv.shape), whole((8, wide)), whole((1, wide))],
        [rows(QKV_PAD), whole(shape), whole(shape)],
        scratch=[
            pltpu.VMEM((wide, QKV_PAD), F32),
            pltpu.VMEM((wide, 896), BF16),
            pltpu.VMEM((seq, QKV_PAD), BF16),
        ],
        flops=2 * seq * wide * QKV_PAD,
        moved=20_000_000,
        vmem=28,
        prefetch=1,
    )(place, *parts, a, w_qkv, gain, dgain_ffn)


def input_body(width, keep, place_ref, flat_ref, w_ref, xp_ref, em_ref, gain_ref, e_ref, *refs):
    got_ref, to_ref = refs if keep else (None, refs[0])
    i = pl.program_id(0)
    steps = pl.num_programs(0) // (2 if keep else 1)

    def work():
        da = mm_nt(flat_ref[...], w_ref[...])
        xp = xp_ref[...].astype(F32)
        scale = lax.rsqrt(jnp.sum(xp * xp, axis=-1, keepdims=True) / width + EPSILON)
        n = xp * scale
        c = da * gain_ref[:1]
        mean = jnp.sum(c * n, axis=-1, keepdims=True) / width
        grad = em_ref[...] + scale * (c - n * mean)
        return mm_nt(e_ref[:width, :], grad.astype(BF16))

    if keep:

        @pl.when(i < steps)
        def _():
            to_ref[0] = work()

        @pl.when(i >= steps)
        def _():
            to_ref[0] = got_ref[...].astype(F32)

    else:
        to_ref[...] = work().astype(BF16)


def input_back(place, flat, w_qkv, xp, em, gain, spread, width, got=None, block=256):
    seq, wide = xp.shape
    steps = seq // 2 // block
    keep = got is not None
    token = lambda i, place: (place[0] if keep else 1 - place[0]) * steps + jnp.minimum(i, steps - 1)
    rows = lambda n: pl.BlockSpec((block, n), lambda i, place: (token(i, place), 0))
    ins = [rows(QKV_PAD), whole(w_qkv.shape), rows(wide), rows(wide), whole((8, wide)), whole(spread.shape)]
    if keep:
        ins.append(pl.BlockSpec((width, block), lambda i, place: (0, jnp.maximum(i - steps, 0))))
        shape = jax.ShapeDtypeStruct((2, width, seq // 2), F32)
        half = lambda i, place: jnp.where(i < steps, place[0], 1 - place[0])
        out = pl.BlockSpec((1, width, block), lambda i, place: (half(i, place), 0, lax.rem(i, steps)))
    else:
        shape = jax.ShapeDtypeStruct((width, seq // 2), BF16)
        out = pl.BlockSpec((width, block), lambda i, place: (0, i))
    return call(
        functools.partial(input_body, width, keep),
        [shape],
        (steps * (2 if keep else 1),),
        ins,
        [out],
        flops=seq * wide * (QKV_PAD + width),
        moved=10_000_000,
        vmem=56 if keep else 8,
        prefetch=1,
    )(place, flat, w_qkv, xp, em, gain, spread, *([got] if keep else []))[0]


def begin_body(reader, n_in, place_ref, *refs):
    ins, outs = refs[:n_in], refs[n_in:]
    _, _, y, x = (place_ref[n] for n in range(4))
    for side in range(2):
        mine = y if side else x
        for other in range(2):
            for ref, bit in ((outs[2 * side], 1 - mine), (outs[2 * side + 1], mine)):
                block = 2 * bit + other if side else 2 * other + bit
                for row, keep, got in reader(ins, side, block):
                    ref[other, row : row + keep.shape[0]] = add(keep, got)


def begin(place, arrays, reader, rows, count=4):
    n = arrays[0].shape[-1]

    def spec(t):
        lead = t.shape[:-3]
        return pl.BlockSpec((*lead, 4, *t.shape[-2:]), lambda i, place: (0,) * len(lead) + (i, 0, 0))

    shape = jax.ShapeDtypeStruct((2 * count, rows, n), BF16)
    return call(
        functools.partial(begin_body, reader, len(arrays)),
        [shape] * 4,
        (count,),
        [spec(t) for t in arrays],
        [pl.BlockSpec((2, rows, n), lambda i, place: (i, 0, 0))] * 4,
        flops=1,
        moved=16 * count * rows * n * 6,
        vmem=24,
        prefetch=1,
    )(place, *arrays)


def turn_body(place_ref, *refs):
    y, x = place_ref[2], place_ref[3]
    for side in range(2):
        keep, got = refs[2 * side : 2 * side + 2]
        mine = x if side else y
        for ref, bit in ((refs[4 + 2 * side], 1 - mine), (refs[5 + 2 * side], mine)):
            ref[0] = add(keep[bit], got[bit])


def turn(place, keeps, gots):
    blocks, rows, n = keeps[0].shape
    shape = jax.ShapeDtypeStruct((blocks // 2, rows, n), BF16)
    return call(
        turn_body,
        [shape] * 4,
        (blocks // 2,),
        [pl.BlockSpec((2, rows, n), lambda i, place: (i, 0, 0))] * 4,
        [pl.BlockSpec((1, rows, n), lambda i, place: (i, 0, 0))] * 4,
        flops=1,
        moved=blocks * rows * n * 12,
        vmem=24,
        prefetch=1,
    )(place, keeps[0], gots[0], keeps[1], gots[1])


def climb_body(place_ref, a_keep, a_got, b_keep, b_got, total_ref, *sent):
    for step in range(4):
        block = lax.rem(place_ref[1] + step, 4)
        for side, (keep, got) in enumerate(((a_keep, a_got), (b_keep, b_got))):
            value = keep[block].astype(F32) + got[block].astype(F32)
            if step:
                sent[step - 1][side] = value.astype(BF16)
            else:
                total_ref[side] = value


def climb(place, keeps, gots):
    _, rows, n = keeps[0].shape
    return call(
        climb_body,
        [jax.ShapeDtypeStruct((2, rows, n), F32)] + [jax.ShapeDtypeStruct((2, rows, n), BF16)] * 3,
        (1,),
        [whole(keeps[0].shape)] * 4,
        [whole((2, rows, n))] * 4,
        flops=1,
        moved=rows * n * 50,
        vmem=24,
        prefetch=1,
    )(place, keeps[0], gots[0], keeps[1], gots[1])


def unpack_matrix(width, blocks, wide):
    per, step = width // blocks, wide // blocks
    col = jnp.arange(WIDE_HEADS, dtype=jnp.int32)
    feature = col // LANES * HEAD + col % LANES
    place = jnp.where(col % LANES < HEAD, feature // per * step + feature % per, -1)
    return (jnp.arange(wide, dtype=jnp.int32)[:, None] == place[None, :]).astype(BF16)


def delta_matrix(width, blocks, wide):
    per, step = width // blocks, wide // blocks
    col = jnp.arange(wide, dtype=jnp.int32)
    head = jnp.where(col % step < per, (col // step * per + col % step) // HEAD, -1)
    row = jnp.arange(8 * KV_HEADS, dtype=jnp.int32)
    mine = jnp.where(row % 8 < GROUP, row // 8 * GROUP + row % 8, -2)
    return (mine[:, None] == head[None, :]).astype(BF16)


def spread_matrix(width, blocks, wide):
    row = jnp.arange(wide, dtype=jnp.int32)
    per, step = width // blocks, wide // blocks
    place = (row // per) * step + row % per
    hit = (place[:, None] == jnp.arange(wide, dtype=jnp.int32)[None, :]) & (row < width)[:, None]
    return hit.astype(BF16)


def tables(positions, segments):
    lane = jnp.arange(LANES, dtype=jnp.int32)
    frequency = 10000.0 ** (-((lane % 32).astype(F32) * 2.0 / HEAD))
    angles = positions.astype(F32)[:, None] * frequency[None, :]
    cos, sin = jnp.cos(angles), jnp.sin(angles)
    high = (lane % HEAD >= 32)[None, :]
    sa = jnp.where(high, sin, 0.0)
    sb = jnp.where(high, 0.0, -sin)
    doc = (lane - HEAD)[None, :]
    mine = segments[:, None] == doc
    in_doc = (doc >= 0) & (doc < DOCS)
    aq = jnp.where(mine & in_doc, MASKED, 0.0)
    ak = jnp.where(in_doc & ~mine, 1.0, 0.0)
    ak = jnp.where((doc >= DOCS) & (doc < DOCS + 3), -1.0, ak)
    return cos, sa, sb, aq, ak


def pad_rows(w, blocks, step=64):
    per = w.shape[0] // blocks
    return jnp.pad(w.reshape(blocks, per, w.shape[1]), ((0, 0), (0, step - per), (0, 0)))


def pad_cols(w, blocks, step=64):
    per = w.shape[1] // blocks
    w = jnp.pad(w.reshape(w.shape[0], blocks, per), ((0, 0), (0, 0), (0, step - per)))
    return w.reshape(w.shape[0], blocks * step)


def cut_rows(w, per):
    return w[:, :per].reshape(w.shape[0] * per, w.shape[2])


def cut_cols(w, per, step=64):
    blocks = w.shape[1] // step
    return w.reshape(w.shape[0], blocks, step)[:, :, :per].reshape(w.shape[0], blocks * per)


def chunked(w, chunk=256):
    blocks, rows, cols = w.shape
    w = w.reshape(blocks, rows, cols // chunk, chunk).transpose(0, 2, 1, 3)
    return w.reshape(blocks, cols // chunk * rows, chunk)


def joined(w, rows):
    blocks, total, chunk = w.shape
    w = w.reshape(blocks, total // rows, rows, chunk).transpose(0, 2, 1, 3)
    return w.reshape(blocks, rows, total // rows * chunk)


def pack_half(w_gate, w_up, w_down, blocks, groups):
    down = pad_cols(w_down, groups)
    down = down.reshape(blocks, w_down.shape[0] // blocks, down.shape[1])
    gate, upper = chunked(pad_rows(w_gate, blocks)), chunked(pad_rows(w_up, blocks))
    return jnp.concatenate([gate, down[:, :, :256], upper, down[:, :, 256:]], axis=1)


def add(left, right):
    return (left.astype(F32) + right.astype(F32)).astype(BF16)


def swap(x):
    return lax.ppermute(x, "ctx", [(0, 1), (1, 0)])


def across(x, bit, count):
    return lax.ppermute(x, "dp", [(i, i ^ (1 << bit)) for i in range(count)])


def pick(x, index, axis=0):
    return lax.dynamic_index_in_dim(x, index, axis, keepdims=False)


def tie(value, *others):
    return lax.optimization_barrier((value, *others))[0]


def tie_all(values, *others):
    return lax.optimization_barrier((*values, *others))[: len(values)]


def along_z(x, step, count):
    return lax.ppermute(x, "dp", [(i, (i + 4 * step) % count) for i in range(count)])


def rise(x, count):
    return [x] + [along_z(x, k, count) for k in (1, 2, 3)]


def spread_first(stack, count):
    half = stack.shape[1] // 2
    first, second = stack[:, :half], stack[:, half:]
    return first, across(first, 0, count), second, across(second, 1, count)


def spread_second(first, first_got, second, second_got, count):
    first, second = jnp.concatenate([first, first_got]), jnp.concatenate([second, second_got])
    return first, across(first, 1, count), second, across(second, 0, count)


def pieces_of(whole_one):
    n = whole_one.shape[1] // 2
    cube = whole_one.reshape(4, 2, 2, 2 * n, -1)
    cube = jnp.stack([cube[(4 - k) % 4] for k in range(4)])
    first, second = cube[:, :, :, :n], cube[:, :, :, n:]
    first, second = first.transpose(1, 2, 0, 3, 4), second.transpose(2, 1, 0, 3, 4)
    flat = lambda t: t.reshape(8, n, -1)
    return flat(first[0]), flat(first[1]), flat(second[0]), flat(second[1])


def fine_pieces_of(whole_one):
    n = whole_one.shape[1] // 2
    cube = whole_one.reshape(4, 2, 2, 2 * n, -1)
    cube = jnp.stack([cube[(4 - k) % 4] for k in range(4)])
    near = [cube[:, dy, dx] for dy in range(2) for dx in range(2)]
    return [t[:, :n] for t in near] + [t[:, n:] for t in near]


class RowSum:
    def __init__(self, place, count, arrays, reader, rows):
        self.place, self.count = place, count
        a_sent, a_kept, b_sent, b_kept = begin(place, arrays, reader, rows)
        self.sent, self.kept = [a_sent, b_sent], [a_kept, b_kept]

    def move(self):
        self.got = [across(self.sent[0], 0, self.count), across(self.sent[1], 1, self.count)]

    def wait(self, other):
        self.got = list(lax.optimization_barrier((*self.got, other))[:-1])

    def turn(self, other):
        self.wait(other)
        a_sent, a_kept, b_sent, b_kept = turn(self.place, self.kept, self.got)
        self.sent, self.kept = [a_sent, b_sent], [a_kept, b_kept]

    def move_again(self):
        self.got = [across(self.sent[0], 1, self.count), across(self.sent[1], 0, self.count)]

    def climb(self, other):
        self.wait(other)
        self.kept, *self.sent = climb(self.place, self.kept, self.got)

    def start_up(self):
        return along_z(self.sent[1], 1, self.count)

    def start_down(self):
        return along_z(self.sent[2], 3, self.count)

    def go_up(self, got):
        return along_z(add(self.sent[0], got), 1, self.count)

    def move_up(self):
        return [along_z(self.sent[k - 1], k, self.count) for k in (1, 2, 3)]

    def total(self, *gots):
        total = self.kept
        for got in gots:
            total = total + got.astype(F32)
        return total


def read_rows(ins, side, block):
    half = ins[0].shape[1] // 2
    rows = slice(half * side, half * (side + 1))
    return [(0, ins[0][block, rows], ins[1][block, rows])]


def read_quarters(ins, side, block):
    first = ins[0].shape[2]
    return [(0, ins[0][side, block], ins[1][side, block]), (first, ins[2][side, block], ins[3][side, block])]


def put_other(both, got, core):
    return lax.dynamic_update_slice(both, got[None], (1 - core, 0, 0))


def shards_of_two(inputs, segment_ids, positions, w_query, w_key, w_value, w_out, w_gate, w_up,
                  w_down, gain_attn, gain_ffn, cotangent):
    count = lax.axis_size("dp")
    me, core = lax.axis_index("dp"), lax.axis_index("ctx")
    place = (core, me // 4, (me >> 1) & 1, me & 1)
    place_of = jnp.stack(place).astype(jnp.int32)
    per = gain_attn.shape[0]
    width = per * count
    groups = w_out.shape[1] // per
    hidden = w_down.shape[0]
    n_q, n_k = w_query.shape[1], w_key.shape[1]
    n_qkv = n_q + 2 * n_k

    shard = jnp.concatenate([w_query, w_key, w_value], axis=1)
    shard = jnp.concatenate([jnp.pad(shard, ((0, 0), (0, 896 - n_qkv))), pad_cols(w_out, groups)], axis=1)
    gain_rows = jnp.pad(jnp.stack([gain_attn, gain_ffn]), ((0, 62 - per), (0, PACK - per)))
    shard = jnp.concatenate([shard, gain_rows])
    packed = pack_half(w_gate, w_up, w_down, 1, groups)[0]

    def halves(x):
        x = jnp.swapaxes(x[:, 0], 1, 2)
        return pick(x, core), swap(pick(x, 1 - core))

    wide = count * 64
    spread, unpack = spread_matrix(width, count, wide), unpack_matrix(width, count, wide)
    delta_sum = delta_matrix(width, count, wide)
    table = tables(pick(positions[:, 0], core), pick(segment_ids[:, 0], core))

    level = rise(shard, count)
    x_own, x_other = halves(inputs)
    ct_own, ct_other = halves(cotangent)
    stack = tie(jnp.stack(level), packed, x_other, ct_other)
    part = spread_first(stack, count)
    packed = tie(packed, stack)
    up, down = along_z(packed, 1, count), along_z(packed, 3, count)
    near_far = spread_second(*part, count)
    up, down = tie_all((up, down), part[0])
    up_two = along_z(up, 1, count)
    near_far = tie_all(near_far, up_two, down, spread, delta_sum, unpack, *table)
    pieces = near_far + tuple(swap(t) for t in near_far)
    packs = jnp.stack(tie_all((packed, up, up_two, down), near_far[0]))
    half = packs.shape[1] // 2
    a00, b00 = packs[:, :half], packs[:, half:]
    a01, b10 = across(a00, 0, count), across(b00, 1, count)

    pieces = tie_all(pieces, a00, b00)
    xp, a, q, k, v, w_qkv, w_o, gains = pre_attention(place_of, x_own, x_other, spread, pieces, *table)
    a01, b10, a00, b00 = tie_all((a01, b10, a00, b00), q)
    a10, b01 = across(a00, 1, count), across(b00, 0, count)
    got = [swap(a00), swap(b00), swap(a01)]
    q = tie(q, a01, b10)
    o, q2 = attend(q, k, v)
    a10, b01, *got = tie_all((a10, b01, *got), o)
    a11, b11 = across(tie(a01, a10), 1, count), across(tie(b10, a10), 0, count)
    got += [swap(b10), swap(a10), swap(b01)]
    op, m, b, df = middle(
        place_of, tie(o, a10, b01, *got[:3]), ct_own, ct_other, spread, unpack, w_o, xp, gains
    )
    a11, b11, *got = tie_all((a11, b11, *got), b)
    mine = [a00, a01, a10, a11, b00, b01, b10, b11]
    other = [got[0], got[2], got[4], swap(a11), got[1], got[5], got[3], swap(b11)]

    acc0, db0, gu_send, d_send, d_keep = feed_forward(place_of, b, df, mine, other, 0)
    gu_got = swap(gu_send)
    acc, db, gu_keep, d_send, d_keep = feed_forward(
        place_of, tie(b, gu_send), df, mine, other, 1, (d_send, d_keep, acc0, db0)
    )
    one = RowSum(place_of, count, (gu_keep, tie(gu_got, acc)), read_rows, 320)
    one.move()
    blocked = lambda t: t.reshape(2, count, hidden, 256)
    d_got = swap(d_send)
    m = tie(m, *one.sent, d_send)
    em, do, delta, o_send, o_keep, dgf = after(place_of, m, db, df, gains, unpack, delta_sum, w_o, op, width)
    o_got = swap(o_send)
    one.turn(em)
    one.move_again()
    two = RowSum(
        place_of, count, (blocked(d_keep), blocked(tie(d_got, em)), tie(o_keep, *one.sent), o_got), read_quarters, 224
    )
    two.move()
    do = tie(do, *one.sent, *two.sent)
    parts = attend_back(q2, k, v, do, delta, *table[:3], 0, KV_HEADS)
    one.climb(parts[0])
    up, down = one.start_up(), one.start_down()
    two.turn(parts[0])
    two.move_again()
    a = tie(a, *one.sent, *two.sent)
    flat, p_send, p_keep = projections_back(place_of, parts, a, w_qkv, gains, dgf)
    up, down, *two.got = tie_all((up, down, *two.got), flat)
    p_got = swap(tie(p_send, up))
    two.climb(flat)
    one_up, one_down, two_up = one.go_up(up), down, two.start_up()
    three = RowSum(place_of, count, (p_keep, p_got), read_rows, 32)
    three.move()
    flat = tie(flat, *two.sent, *three.sent)
    gi_send = input_back(place_of, flat, w_qkv, xp, em, gains, spread, width)
    out_send, outs = finish(place_of, tie(m, gi_send), acc, spread, width)
    *three.got, one_up, two_up = tie_all((*three.got, one_up, two_up), outs)
    three.turn(outs)
    three.move_again()
    gi_got, out_got = swap(tie(gi_send, *three.sent)), swap(tie(out_send, *three.sent))
    two_up = two.go_up(tie(two_up, *three.sent))
    two.sent[2] = tie(two.sent[2], *three.sent)
    two_down = two.start_down()
    first = tie(one.total(one_up, one_down), *three.sent)
    wide_of = lambda t: t.transpose(1, 0, 2).reshape(t.shape[1], -1)
    gu = first.reshape(5, 2, 64, 256)
    gate, upper = wide_of(gu[:, 0])[:per], wide_of(gu[:, 1])[:per]
    outs = put_other(outs, out_got, core)
    *three.got, gi_got, two_up = tie_all((*three.got, gi_got, two_up), outs, gate, upper)
    three.climb(gi_got)
    last_got = three.move_up()
    gis = input_back(place_of, tie(flat, *three.sent), w_qkv, xp, em, gains, spread, width, gi_got)
    last_got = tie_all(last_got, gis)
    second, third = two.total(two_up, two_down), three.total(*last_got)
    third = third.reshape(64, 896)[:per]
    tokens = lambda t: jnp.swapaxes(t, 1, 2)[:, None]
    return (
        tokens(outs),
        tokens(gis),
        third[:, :n_q],
        third[:, n_q : n_q + n_k],
        third[:, n_q + n_k : n_qkv],
        cut_cols(wide_of(second[:, 160:])[:per], per),
        gate,
        upper,
        cut_cols(wide_of(second[:, :160]), per),
        third[:, n_qkv],
        third[:, n_qkv + 1],
    )


def shards_of_many(inputs, segment_ids, positions, w_query, w_key, w_value, w_out, w_gate, w_up,
                   w_down, gain_attn, gain_ffn, cotangent):
    count, cores = lax.axis_size("dp"), lax.axis_size("ctx")
    core = lax.axis_index("ctx")
    share = cores // MICRO
    per = gain_attn.shape[0]
    width = per * count

    def gathered(w):
        return lax.all_gather(lax.all_gather(w, "dp", axis=0, tiled=True), "ctx", axis=1, tiled=True)

    full = [gathered(w) for w in (w_query, w_key, w_value, w_out, w_gate, w_up, w_down)]
    gain_pair = lax.all_gather(jnp.stack([gain_attn, gain_ffn]), "dp", axis=1, tiled=True)
    w_o, w_g, w_u, w_d = full[3:]
    half = lambda w, j: w[:, w.shape[1] // 2 * j : w.shape[1] // 2 * (j + 1)]
    packs = [pack_half(half(w_g, j), half(w_u, j), half(w_d, j), count, count // 2) for j in range(2)]
    mine, other = (fine_pieces_of(p) for p in packs)
    pieces = []
    for j in range(2):
        part = jnp.concatenate([half(w, j) for w in full[:3]], axis=1)
        part = jnp.pad(part, ((0, 0), (0, 896 - part.shape[1])))
        part = jnp.concatenate([part, pad_cols(half(w_o, j), count // 2)], axis=1)
        part = pad_rows(part, count)
        part = part.at[:, per : per + 2, :per].set(gain_pair.reshape(2, count, per).transpose(1, 0, 2))
        pieces += pieces_of(part)
    which = core // share

    def sequence(x):
        whole_one = pick(lax.all_gather(x[:, 0], "ctx", axis=1, tiled=True), which).T
        return whole_one[:, : whole_one.shape[1] // 2], whole_one[:, whole_one.shape[1] // 2 :]

    place = jnp.zeros((4,), jnp.int32)
    wide = count * 64
    spread, unpack = spread_matrix(width, count, wide), unpack_matrix(width, count, wide)
    delta_sum = delta_matrix(width, count, wide)
    cos, sa, sb, aq, ak = tables(pick(positions[:, 0], which), pick(segment_ids[:, 0], which))
    xp, a, q, k, v, w_qkv, w_o, gains = pre_attention(
        place, *sequence(inputs), spread, pieces, cos, sa, sb, aq, ak
    )
    o, q2 = attend(q, k, v)
    op, m, b, df = middle(place, o, *sequence(cotangent), spread, unpack, w_o, xp, gains)
    acc0, db0, gu_send, d_send, d_keep = feed_forward(place, b, df, mine, other, 0)
    acc, db, gu_keep, d_send, d_keep = feed_forward(
        place, b, df, mine, other, 1, (d_send, d_keep, acc0, db0)
    )
    em, do, delta, o_send, o_keep, dgf = after(place, m, db, df, gains, unpack, delta_sum, w_o, op, width)
    out_send, outs = finish(place, m, acc, spread, width)
    parts = attend_back(q2, k, v, do, delta, cos, sa, sb, 0, KV_HEADS)
    flat, p_send, p_keep = projections_back(place, parts, a, w_qkv, gains, dgf)
    gi_send = input_back(place, flat, w_qkv, xp, em, gains, spread, width)
    gis = input_back(place, flat, w_qkv, xp, em, gains, spread, width, gi_send)

    parts = [cut_rows(p, per) for p in (p_keep, p_send)]
    n_q, n_k = HEADS * HEAD // 2, KV_HEADS * HEAD // 2
    both = lambda at, n: jnp.concatenate([p[:, at : at + n] for p in parts], axis=1)
    side = lambda t: jnp.concatenate([t[0], t[1]], axis=-1)

    def wide_of(index):
        every = []
        for t in (gu_keep, gu_send):
            t = t.reshape(count, 5, 2, 64, 256)[:, :, index]
            every.append(cut_rows(t.transpose(0, 2, 1, 3).reshape(count, 64, -1), per))
        return jnp.concatenate(every, axis=1)

    grads = [
        both(0, n_q),
        both(n_q * 1, n_k),
        both(n_q + n_k, n_k),
        cut_cols(cut_rows(jnp.concatenate([side(o_keep), side(o_send)], axis=-1), per), per),
        wide_of(0),
        wide_of(1),
        cut_cols(
            jnp.concatenate([side(d_keep), side(d_send)], axis=-1),
            per,
        ),
    ]

    def summed(g):
        g = lax.psum_scatter(g * (1.0 / share), "dp", scatter_dimension=0, tiled=True)
        return lax.psum_scatter(g, "ctx", scatter_dimension=1, tiled=True).astype(F32)

    sums = [summed(g.astype(BF16)) for g in grads]
    dgain = parts[0][:, 2 * n_k + n_q : 2 * n_k + n_q + 2].astype(F32).T * (1.0 / share)
    dgain = lax.psum_scatter(lax.psum(dgain, "ctx"), "dp", scatter_dimension=1, tiled=True)

    def tokens(seq):
        rows = seq.shape[0] // cores
        every = lax.all_gather(seq, "ctx", axis=0, tiled=False)
        return lax.dynamic_slice_in_dim(every[::share], core * rows, rows, axis=1)[:, None]

    out = jnp.concatenate([outs[0], out_send], axis=1).T
    gi = jnp.concatenate([gis[0], gi_send.astype(F32)], axis=1).T
    return (tokens(out), tokens(gi), *sums, dgain[0], dgain[1])


def solution(mesh):
    two = mesh.shape["ctx"] == MICRO and mesh.shape["dp"] == 16
    matrices = (P("dp", "ctx"),) * 7 + (P("dp"), P("dp"))
    tokens = P(None, "dp", "ctx", None)
    return jax.shard_map(
        shards_of_two if two else shards_of_many,
        mesh=mesh,
        in_specs=(tokens, P(None, "dp", None), P(None, "dp", None)) + matrices + (tokens,),
        out_specs=(tokens, tokens) + matrices,
        check_vma=False,
    )
```
